32 devices in a mesh: fsdp: 8 (over z, core), grp: 2 (over y), tp: 2 (over x).
Axes of the slice: x: 2, y: 2, z: 4, core: 2. Of those that a mesh axis runs over, the one named last changes fastest.
Arguments:
- hidden_states: bfloat16 [4, 128, 8192], P(None, ('fsdp', 'grp'), 'tp'), may hold values from -6 to 6
- queries: bfloat16 [4, 128, 64, 128], P(None, ('fsdp', 'grp'), 'tp'), as said below
- cache_keys: bfloat16 [128, 768, 8, 128], P(('fsdp', 'grp'), None, 'tp'), as said below
- cache_values: bfloat16 [128, 768, 8, 128], P(('fsdp', 'grp'), None, 'tp'), may hold values from -6 to 6
- cache_lengths: int32 [128], P(('fsdp', 'grp')), may hold values from 2 to 768, as said below
- projection_weight_matrices: bfloat16 [2, 8192, 1024], P(None, None, 'tp'), may hold values from -0.0625 to 0.0625
- factor_down: bfloat16 [2, 8192, 64], P(None, ('fsdp', 'grp')), may hold values from -0.0625 to 0.0625
- factor_up: bfloat16 [2, 64, 1024], P(None, None, ('fsdp', 'grp')), may hold values from -0.375 to 0.375
Outputs:
- merged: bfloat16 [2, 8192, 1024], P(None, None, 'tp')
- attended: bfloat16 [4, 128, 64, 128], P(None, ('fsdp', 'grp'), 'tp')
The draws below stay inside these ranges and needn't reach their ends.
Inputs may be any that keep to these rules, and one draw needn't show every extreme that they name: `cache_lengths`: at least 2; some row has exactly 768. `queries`: real-valued. `cache_keys`: real-valued.
All inputs are finite; a program needn't handle non-finite values.
Results may differ from the reference program's by a relative error of at most 0.0066.
Values may be sent and summed in bfloat16 or wider, within the bound.
No kernel may reach another device: no remote copies, remote signals or barrier semaphores. Data moves between devices by JAX's collectives and lax.ppermute only.
A program may use at most 192 MiB of HBM per device.

```python
import math
import jax
import jax.numpy as jnp
from jax import lax

D = 8192
HQ = 64
KVH = 8
HD = 128
R = 64
STEPS = 4
CTX = 768
KVW = 1024
ROWS = 128


def draw_queries(key, part):
    key = jax.random.fold_in(key, 1)
    values = jax.random.normal(key, (STEPS, ROWS, HQ, HD), jnp.float32)
    return values.astype(jnp.bfloat16)


def draw_cache_keys(key, part):
    key = jax.random.fold_in(key, 2)
    values = jax.random.normal(key, (ROWS, CTX, KVH, HD), jnp.float32)
    return values.astype(jnp.bfloat16)


def draw_cache_lengths(key, part):
    key = jax.random.fold_in(key, 3)
    first, second, third, fourth = jax.random.split(key, 4)
    longer = jax.random.randint(first, (ROWS,), 2, CTX + 1)
    shorter = jax.random.randint(second, (ROWS,), 2, 9)
    pick = jax.random.randint(third, (ROWS,), 0, 2)
    lengths = jnp.where(pick == 0, shorter, longer)
    spot = jax.random.randint(fourth, (), 0, ROWS)
    return jnp.where(jnp.arange(ROWS) == spot, CTX, lengths).astype(jnp.int32)


def block_levels(key, dims, cuts, smallest, largest):
    level, own = 1.0, jax.random.fold_in(key, 6)
    for position, blocks in cuts:
        steps = jnp.exp(jax.random.uniform(jax.random.fold_in(own, position), (blocks,), jnp.float32, smallest / len(cuts), largest / len(cuts)))
        level = level * jnp.repeat(steps, dims[position] // blocks).reshape([-1 if axis == position else 1 for axis in range(len(dims))])
    return level


def bell_draw(rng, extent, width, reach, cuts=(), kind=jnp.bfloat16):
    values = jax.random.normal(rng, extent, jnp.float32) * width
    if len(cuts) > 0:
        values = block_levels(rng, extent, cuts, -0.22, 0.18) * values
    return jnp.clip(values, min=-reach, max=reach).astype(kind)


def setup_inputs(seed: int = 0) -> dict:
    key_list = jax.random.split(jax.random.key(seed), 9)
    hidden_states = bell_draw(key_list[0], (STEPS, ROWS, D), 1.0, 6.0, ((1, 16), (2, 2)))
    queries = draw_queries(jax.random.fold_in(key_list[8], 71), 0)
    cache_keys = draw_cache_keys(jax.random.fold_in(key_list[8], 71), 0)
    cache_values = bell_draw(key_list[3], (ROWS, CTX, KVH, HD), 1.0, 6.0, ((0, 16), (2, 2)))
    cache_lengths = draw_cache_lengths(jax.random.fold_in(key_list[8], 71), 0)
    projection_weight_matrices = bell_draw(key_list[5], (2, D, KVW), D ** -0.5, 0.0625, ((2, 2),))
    factor_down = bell_draw(key_list[6], (2, D, R), D ** -0.5, 0.0625, ((1, 16),))
    factor_up = bell_draw(key_list[7], (2, R, KVW), (4 * R) ** -0.5, 0.375, ((2, 16),))
    return dict(hidden_states=hidden_states, queries=queries, cache_keys=cache_keys, cache_values=cache_values, cache_lengths=cache_lengths, projection_weight_matrices=projection_weight_matrices, factor_down=factor_down, factor_up=factor_up)


ADAPTER_SCALING = 2.0

def attend(queries, cache_keys, cache_values, cache_lengths, new_keys, new_values):
    step_count, row_count, head_count, head_size = queries.shape
    kv_count = cache_keys.shape[2]
    grouped = queries.reshape(step_count, row_count, kv_count, head_count // kv_count, head_size).astype(jnp.float32)
    inverse = 1.0 / math.sqrt(head_size)
    old_scores = jnp.einsum('srkgh,rckh->srkgc', grouped, cache_keys.astype(jnp.float32)) * inverse
    new_scores = jnp.einsum('srkgh,urkh->srkgu', grouped, new_keys.astype(jnp.float32)) * inverse
    places = jnp.arange(cache_keys.shape[1], dtype=jnp.int32)
    filled = places[None, :] < cache_lengths[:, None]
    old_scores = jnp.where(filled[None, :, None, None, :], old_scores, -jnp.inf)
    order = jnp.arange(step_count, dtype=jnp.int32)
    earlier = order[None, :] <= order[:, None]
    new_scores = jnp.where(earlier[:, None, None, None, :], new_scores, -jnp.inf)
    highest = jnp.maximum(lax.optimization_barrier(jnp.max(old_scores, -1)), lax.optimization_barrier(jnp.max(new_scores, -1)))[..., None]
    old_exp = jnp.exp(old_scores - highest)
    new_exp = jnp.exp(new_scores - highest)
    softmax_divisor = (lax.optimization_barrier(jnp.sum(old_exp, -1)) + lax.optimization_barrier(jnp.sum(new_exp, -1)))[..., None]
    old_weights = (old_exp / softmax_divisor).astype(jnp.bfloat16)
    new_weights = (new_exp / softmax_divisor).astype(jnp.bfloat16)
    result = jnp.einsum('srkgc,rckh->srkgh', old_weights.astype(jnp.float32), cache_values.astype(jnp.float32))
    result = result + jnp.einsum('srkgu,urkh->srkgh', new_weights.astype(jnp.float32), new_values.astype(jnp.float32))
    return result.reshape(step_count, row_count, head_count, head_size).astype(jnp.bfloat16)

def reference(hidden_states, queries, cache_keys, cache_values, cache_lengths, projection_weight_matrices, factor_down, factor_up):
    weight_increment = jnp.einsum('kdr,krw->kdw', factor_down.astype(jnp.float32), factor_up.astype(jnp.float32))
    merged = (projection_weight_matrices.astype(jnp.float32) + ADAPTER_SCALING * weight_increment).astype(jnp.bfloat16)
    fresh = jnp.einsum('srd,kdw->ksrw', hidden_states.astype(jnp.float32), merged.astype(jnp.float32)).astype(jnp.bfloat16)
    fresh = fresh.reshape(2, STEPS, ROWS, KVH, HD)
    block = 8

    def one_block(index):
        start = index * block

        def take(array, dim):
            return lax.dynamic_slice_in_dim(array, start, block, dim)
        return attend(take(queries, 1), take(cache_keys, 0), take(cache_values, 0), take(cache_lengths, 0), take(fresh[0], 1), take(fresh[1], 1))
    pieces = lax.map(one_block, jnp.arange(ROWS // block, dtype=jnp.int32))
    attended = pieces.transpose(1, 0, 2, 3, 4).reshape(STEPS, ROWS, HQ, HD)
    return (merged, attended)
```

```python
import functools
import math

import jax
import jax.numpy as jnp
from jax import lax
from jax.experimental import pallas as pl
from jax.experimental.pallas import tpu as pltpu
from jax.sharding import PartitionSpec as P

AXES = ("fsdp", "grp", "tp")
ADAPTER_SCALING = 2.0
LOG2E = math.log2(math.e)
MIB = 1024 * 1024
ANY = pl.BlockSpec(memory_space=pl.ANY)
VMEM = pl.BlockSpec(memory_space=pltpu.VMEM)
SMEM = pl.BlockSpec(memory_space=pltpu.SMEM)


class Layout:
    def __init__(self, mesh):
        self.fsdp, self.grp, self.tp = (mesh.shape[a] for a in AXES)
        self.depth = self.fsdp // 2
        self.ring = self.depth * self.grp
        self.block = self.depth // self.tp

    def flat(self, z, core, g, t):
        return ((z * 2 + core) * self.grp + g) * self.tp + t

    def devices(self):
        for z in range(self.depth):
            for core in range(2):
                for g in range(self.grp):
                    for t in range(self.tp):
                        yield z, core, g, t

    def place(self, z, g):
        return g * self.depth + (z if g % 2 == 0 else self.depth - 1 - z)

    def at(self, position):
        g, z = divmod(position, self.depth)
        return (z if g % 2 == 0 else self.depth - 1 - z), g

    def ring_step(self, step):
        pairs = []
        for z, core, g, t in self.devices():
            to_z, to_g = self.at((self.place(z, g) + step) % self.ring)
            pairs.append((self.flat(z, core, g, t), self.flat(to_z, core, to_g, t)))
        return pairs

    def core_swap(self):
        return [
            (self.flat(z, c, g, t), self.flat(z, 1 - c, g, t)) for z, c, g, t in self.devices()
        ]

    def feature_step(self, step):
        return [
            (self.flat(z, c, g, (t + step) % self.tp), self.flat(z, c, g, t))
            for z, c, g, t in self.devices()
        ]

    def column_step(self, shift, turn):
        pairs = []
        for z, c, g, t in self.devices():
            source = t * self.block + (z % self.block + shift) % self.block
            pairs.append(
                (
                    self.flat(source, c, (g + turn) % self.grp, z // self.block),
                    self.flat(z, c, g, t),
                )
            )
        return pairs


def attend_cache(first, count, sizes, scale, *refs):
    lengths, q_ref, k_hbm, v_hbm = refs[:4]
    o_ref, lse_ref, k_buf, v_buf, bias, sems = refs[-6:]
    steps, _, heads, size = q_ref.shape
    kv = k_hbm.shape[1] // sizes[-1]
    lanes = steps * heads
    width = k_buf.shape[1]

    def by_length(row, act):
        length = lengths[first + row]
        below = 0
        for slots in sizes:

            @pl.when((length > below) & (length <= slots))
            def _():
                act(row, slots, length)

            below = slots

    def copies(row, slots):
        part = pl.ds(0, slots * kv)
        return (
            pltpu.make_async_copy(
                k_hbm.at[first + row, part], k_buf.at[row, part], sems.at[row, 0]
            ),
            pltpu.make_async_copy(
                v_hbm.at[first + row, part], v_buf.at[row, part], sems.at[row, 1]
            ),
        )

    def begin(row, slots, length):
        for copy in copies(row, slots):
            copy.start()

    def compute(row, slots, length):
        k_copy, v_copy = copies(row, slots)
        n = slots * kv
        q = q_ref[:, first + row].reshape(lanes, size)
        k_copy.wait()
        s = lax.dot_general(
            q, k_buf[row, :n], (((1,), (1,)), ((), ())), preferred_element_type=jnp.float32
        )
        column = lax.broadcasted_iota(jnp.int32, (1, n), 1)
        open_slots = jnp.where(column < length * kv, 0.0, -jnp.inf)
        s = s * scale + bias[:, :n] + open_slots
        highest = jnp.max(s, axis=1, keepdims=True)
        p = jnp.exp2(s - highest)
        total = jnp.sum(p, axis=1, keepdims=True)
        v_copy.wait()
        o = jnp.dot(p.astype(jnp.bfloat16), v_buf[row, :n], preferred_element_type=jnp.float32)
        o_ref[:, row] = (o / total).reshape(steps, heads, size)
        lse = highest + jnp.log(total) * LOG2E
        lse_ref[:, row] = jnp.broadcast_to(lse, (lanes, size)).reshape(steps, heads, size)

    for row in range(count):
        by_length(row, begin)
    head = (lax.broadcasted_iota(jnp.int32, (lanes, width), 0) % heads) // (heads // kv)
    slot_head = lax.broadcasted_iota(jnp.int32, (lanes, width), 1) % kv
    bias[...] = jnp.where(head == slot_head, 0.0, -jnp.inf)

    @pl.loop(0, count)
    def _(row):
        by_length(row, compute)


def cache_attention(first, count, lengths, queries, keys, values, slots, after):
    steps, rows, heads, size = queries.shape
    kv = keys.shape[1] // slots
    sizes = (slots // 24, slots // 6, slots // 2, slots)
    scale = LOG2E / math.sqrt(size)
    part = jax.ShapeDtypeStruct((steps, count, heads, size), jnp.float32)
    return pl.pallas_call(
        functools.partial(attend_cache, first, count, sizes, scale),
        out_shape=(part, part),
        in_specs=[SMEM, VMEM, ANY, ANY] + [ANY] * len(after),
        out_specs=(VMEM, VMEM),
        scratch_shapes=[
            pltpu.VMEM((count, slots * kv, size), jnp.bfloat16),
            pltpu.VMEM((count, slots * kv, size), jnp.bfloat16),
            pltpu.VMEM((steps * heads, slots * kv), jnp.float32),
            pltpu.SemaphoreType.DMA((count, 2)),
        ],
        compiler_params=pltpu.CompilerParams(vmem_limit_bytes=32 * MIB),
        cost_estimate=pl.CostEstimate(
            flops=4 * steps * heads * count * slots * kv * size,
            bytes_accessed=4 * count * slots * kv * size,
            transcendentals=steps * heads * count * slots * kv,
        ),
        name="cache_attention",
    )(lengths, queries, keys, values, *after)


def merge_blocks(lay, plan, n_hidden, n_up, has_prev, final, scale, *refs):
    refs = list(refs)

    def take(n):
        out = refs[:n]
        del refs[:n]
        return out

    (w_hbm,) = take(1)
    hidden = take(n_hidden)
    ups = take(n_up)
    downs = [take(len(entry[2])) for entry in plan]
    if has_prev:
        take(1)
        (fresh_in,) = take(1)
    if final:
        (q_ref,) = take(1)
        caches = take(2 * final)
    n_after = len(refs) - 2 - 10
    take(n_after)
    m_hbm, last_out = take(2)
    w_buf, d_buf, h_buf, u_parts, u_buf, fresh, index, w_sems, d_sems, x_sems = refs

    pairs, rank, depth, width = w_buf.shape[1], d_buf.shape[2], w_buf.shape[2], w_buf.shape[3]
    fsdp, grp, tp = (lax.axis_index(a) for a in AXES)
    z, core = fsdp // 2, fsdp % 2
    even = grp % 2 == 0
    place = grp * lay.depth + jnp.where(even, z, lay.depth - 1 - z)

    x_copies = [
        pltpu.make_async_copy(h, h_buf.at[i], x_sems.at[i]) for i, h in enumerate(hidden)
    ]
    for i, up in enumerate(ups):
        flip, rest = i // (n_up // 2), i % (n_up // 2)
        shift, turn = rest // lay.grp, rest % lay.grp
        zz = lax.rem(lax.rem(z, lay.block) + shift, lay.block)
        cc = core if flip == 0 else 1 - core
        slot = (zz * 2 + cc) * lay.grp + lax.rem(grp + turn, lay.grp)
        x_copies.append(pltpu.make_async_copy(up, u_parts.at[slot], x_sems.at[n_hidden + i]))

    w_copies, d_copies = [], []
    for j, (delta, flip, count) in enumerate(plan):
        spot = lax.rem(place + (delta + lay.ring), lay.ring)
        g = spot // lay.depth
        along = lax.rem(spot, lay.depth)
        zz = jnp.where(g % 2 == 0, along, lay.depth - 1 - along)
        cc = 1 - core if flip else core
        index[j] = (zz * 2 + cc) * lay.grp + g
        start = pl.multiple_of(index[j] * depth, depth)
        w_copies.append(
            pltpu.make_async_copy(
                w_hbm.at[:, pl.ds(start, depth), :], w_buf.at[j], w_sems.at[j]
            )
        )
        parts = downs[j]
        if len(parts) == 1:
            d_copies.append(pltpu.make_async_copy(parts[0], d_buf.at[j], d_sems.at[j, 0]))
        else:
            for k, part in enumerate(parts):
                d_copies.append(
                    pltpu.make_async_copy(part, d_buf.at[j, pl.ds(k, 1)], d_sems.at[j, k])
                )
    for copy in x_copies + d_copies + w_copies:
        copy.start()

    if has_prev:
        fresh[...] = fresh_in[...]
    else:
        fresh[...] = jnp.zeros_like(fresh)
    for copy in x_copies:
        copy.wait()
    columns = u_parts.shape[2] // pairs
    for k in range(pairs):
        u_buf[k] = ADAPTER_SCALING * jnp.concatenate(
            [u_parts[i, :, k * columns : (k + 1) * columns] for i in range(n_up)], axis=1
        )
    for copy in d_copies:
        copy.wait()

    def out_copy(j):
        start = pl.multiple_of(index[j] * depth, depth)
        return pltpu.make_async_copy(
            w_buf.at[j], m_hbm.at[:, pl.ds(start, depth), :], w_sems.at[j]
        )

    chunk = min(depth, 256)
    per_lane = lay.fsdp * lay.grp // lay.tp

    @pl.loop(0, len(plan))
    def _(j):
        start = pl.multiple_of(index[j] * depth, depth)
        pltpu.make_async_copy(
            w_hbm.at[:, pl.ds(start, depth), :], w_buf.at[j], w_sems.at[j]
        ).wait()
        block = lax.rem(index[j], per_lane)
        source = lax.rem(index[j] // per_lane - tp + lay.tp, lay.tp)
        for k in range(pairs):
            for low in range(0, depth, chunk):
                rows = slice(low, low + chunk)
                added = lax.dot_general(
                    d_buf[j, k, :, rows],
                    u_buf[k],
                    (((0,), (0,)), ((), ())),
                    preferred_element_type=jnp.float32,
                )
                merged = (w_buf[j, k, rows, :].astype(jnp.float32) + added).astype(jnp.bfloat16)
                w_buf[j, k, rows, :] = merged
                h = h_buf[source, :, pl.ds(pl.multiple_of(block * depth + low, chunk), chunk)]
                fresh[k] += jnp.dot(h, merged, preferred_element_type=jnp.float32)
        out_copy(j).start()

    if final:
        add_new_tokens(q_ref, caches, fresh, last_out, scale)
    else:
        last_out[...] = fresh[...]
    for j in range(len(plan)):
        out_copy(j).wait()


def add_new_tokens(q_ref, caches, fresh, out_ref, scale):
    steps, rows, heads, size = q_ref.shape
    kv = fresh.shape[2] // size
    new = []
    for k in range(2):
        whole = fresh[k].astype(jnp.bfloat16)
        new.append(
            jnp.concatenate([whole[:, g * size : (g + 1) * size] for g in range(kv)], axis=0)
        )
    n = kv * steps * rows
    done = 0
    for o_ref, lse_ref in zip(caches[0::2], caches[1::2]):
        count = o_ref.shape[1]
        total = steps * count * heads
        q = q_ref[:, done : done + count].reshape(total, size)
        s = lax.dot_general(
            q, new[0], (((1,), (1,)), ((), ())), preferred_element_type=jnp.float32
        )
        left = lax.broadcasted_iota(jnp.int32, (total, n), 0)
        right = lax.broadcasted_iota(jnp.int32, (total, n), 1)
        step, row = left // (heads * count), (left // heads) % count + done
        head = (left % heads) // (heads // kv)
        keep = (
            (head == right // (steps * rows))
            & (row == right % rows)
            & ((right // rows) % steps <= step)
        )
        s = jnp.where(keep, s * scale, -jnp.inf)
        lse = lse_ref[...].reshape(total, size)[:, :1]
        highest = jnp.maximum(jnp.max(s, axis=1, keepdims=True), lse)
        p = jnp.exp2(s - highest)
        old = jnp.exp2(lse - highest)
        divisor = jnp.sum(p, axis=1, keepdims=True) + old
        o = old * o_ref[...].reshape(total, size) + jnp.dot(
            p.astype(jnp.bfloat16), new[1], preferred_element_type=jnp.float32
        )
        out_ref[:, done : done + count] = (
            (o / divisor).reshape(steps, count, heads, size).astype(out_ref.dtype)
        )
        done += count


def merge(lay, plan, weights, hidden, ups, downs, prev, final, after):
    pairs, total, width = weights.shape
    rank, depth = downs[0][0].shape[1:]
    tokens = hidden[0].shape[0]
    n = len(plan)
    flat_downs = [d for entry in downs for d in entry]
    operands = [weights] + hidden + ups + flat_downs
    specs = [ANY] * len(operands)
    aliases = {}
    if prev is not None:
        aliases = {len(operands): 0}
        operands += list(prev)
        specs += [ANY, VMEM]
    scale = 0.0
    last = jax.ShapeDtypeStruct((pairs, tokens, width), jnp.float32)
    if final is not None:
        queries, caches = final
        operands += [queries] + caches
        specs += [VMEM] * (1 + len(caches))
        last = jax.ShapeDtypeStruct(queries.shape, jnp.bfloat16)
        scale = LOG2E / math.sqrt(queries.shape[3])
    operands += after
    specs += [ANY] * len(after)
    return pl.pallas_call(
        functools.partial(
            merge_blocks,
            lay,
            [(d, f, e) for (d, f), e in zip(plan, downs)],
            len(hidden),
            len(ups),
            prev is not None,
            0 if final is None else len(final[1]) // 2,
            scale,
        ),
        out_shape=(jax.ShapeDtypeStruct(weights.shape, weights.dtype), last),
        in_specs=specs,
        out_specs=(ANY, VMEM),
        input_output_aliases=aliases,
        scratch_shapes=[
            pltpu.VMEM((n, pairs, depth, width), jnp.bfloat16),
            pltpu.VMEM((n, pairs, rank, depth), jnp.bfloat16),
            pltpu.VMEM((len(hidden),) + hidden[0].shape, jnp.bfloat16),
            pltpu.VMEM((len(ups),) + ups[0].shape, jnp.bfloat16),
            pltpu.VMEM((pairs, rank, width), jnp.bfloat16),
            pltpu.VMEM((pairs, tokens, width), jnp.float32),
            pltpu.SMEM((n,), jnp.int32),
            pltpu.SemaphoreType.DMA((n,)),
            pltpu.SemaphoreType.DMA((n, 2)),
            pltpu.SemaphoreType.DMA((len(hidden) + len(ups),)),
        ],
        compiler_params=pltpu.CompilerParams(vmem_limit_bytes=32 * MIB),
        cost_estimate=pl.CostEstimate(
            flops=2 * n * pairs * depth * width * (rank + tokens),
            bytes_accessed=2 * n * pairs * depth * width * 2,
            transcendentals=0,
        ),
        name="merge_blocks",
    )(*operands)


def shards(
    lay,
    hidden_states,
    queries,
    cache_keys,
    cache_values,
    cache_lengths,
    projection_weight_matrices,
    factor_down,
    factor_up,
):
    send = functools.partial(lax.ppermute, axis_name=AXES)
    steps, rows, features = hidden_states.shape
    slots, kv, size = cache_keys.shape[1:]
    own = jnp.swapaxes(factor_down, 1, 2)
    own_up = jnp.concatenate([factor_up[k] for k in range(factor_up.shape[0])], axis=1)
    tokens = hidden_states.reshape(steps * rows, features)
    keys = cache_keys.reshape(rows, slots * kv, size)
    values = cache_values.reshape(rows, slots * kv, size)
    swap = lay.core_swap()
    ring = {1: lay.ring_step(1), -1: lay.ring_step(-1)}

    arrived = {1: send(own, perm=ring[1]), -1: send(own, perm=ring[-1])}
    partner = send(own, perm=swap)
    ups = [
        send(own_up, perm=lay.column_step(shift, turn))
        for shift in range(lay.block)
        for turn in range(lay.grp)
    ]
    hidden = [tokens] + [send(tokens, perm=lay.feature_step(i)) for i in range(1, lay.tp)]

    entries = [((0, False), [own]), ((0, True), [partner])]
    half = rows // 2
    caches = []
    state = None
    after = []
    last_step = lay.ring // 2
    for step in range(1, last_step + 1):
        if step <= 2:
            caches += cache_attention(
                (step - 1) * half, half, cache_lengths, queries, keys, values, slots, after
            )
            state_now = [caches[-1]]
        else:
            state = merge(
                lay,
                [e[0] for e in entries],
                projection_weight_matrices,
                hidden,
                ups,
                [e[1] for e in entries],
                state,
                None,
                after,
            )
            entries = []
            state_now = [state[1]]
        if step == 1:
            ups = ups + [send(u, perm=swap) for u in ups]
        if step < last_step:
            came = arrived
            if step + 1 < last_step:
                arrived = {d: send(came[d], perm=ring[d]) for d in ring}
            else:
                arrived = {
                    1: send(came[1][:1], perm=ring[1]),
                    -1: send(came[-1][1:], perm=ring[-1]),
                }
            for d in ring:
                entries.append(((-d * step, False), [came[d]]))
                entries.append(((-d * step, True), [send(came[d], perm=swap)]))
            after = [came[1], came[-1]] + state_now
        else:
            came = [arrived[1], arrived[-1]]
            entries.append(((step, False), came))
            entries.append(((step, True), [send(c, perm=swap) for c in came]))
    return tuple(
        merge(
            lay,
            [e[0] for e in entries],
            projection_weight_matrices,
            hidden,
            ups,
            [e[1] for e in entries],
            state,
            (queries, caches),
            [],
        )
    )


def solution(mesh):
    return jax.shard_map(
        functools.partial(shards, Layout(mesh)),
        mesh=mesh,
        in_specs=(
            P(None, ("fsdp", "grp"), "tp"),
            P(None, ("fsdp", "grp"), "tp", None),
            P(("fsdp", "grp"), None, "tp", None),
            P(("fsdp", "grp"), None, "tp", None),
            P(("fsdp", "grp")),
            P(None, None, "tp"),
            P(None, ("fsdp", "grp"), None),
            P(None, None, ("fsdp", "grp")),
        ),
        out_specs=(P(None, None, "tp"), P(None, ("fsdp", "grp"), "tp", None)),
        check_vma=False,
    )
```

```python
import functools
import math

import jax
import jax.numpy as jnp
from jax import lax
from jax.experimental import pallas as pl
from jax.experimental.pallas import tpu as pltpu
from jax.sharding import PartitionSpec as P

AXES = ("fsdp", "grp", "tp")
ADAPTER_SCALING = 2.0
LOG2E = math.log2(math.e)
MIB = 1024 * 1024
ANY = pl.BlockSpec(memory_space=pl.ANY)
HBM = pl.BlockSpec(memory_space=pltpu.HBM)
VMEM = pl.BlockSpec(memory_space=pltpu.VMEM)
SMEM = pl.BlockSpec(memory_space=pltpu.SMEM)


class Layout:
    def __init__(self, mesh):
        self.fsdp, self.grp, self.tp = (mesh.shape[a] for a in AXES)
        self.depth = self.fsdp // 2
        self.ring = self.depth * self.grp
        self.block = self.depth // self.tp

    def flat(self, z, core, g, t):
        return ((z * 2 + core) * self.grp + g) * self.tp + t

    def devices(self):
        for z in range(self.depth):
            for core in range(2):
                for g in range(self.grp):
                    for t in range(self.tp):
                        yield z, core, g, t

    def place(self, z, g):
        return g * self.depth + (z if g % 2 == 0 else self.depth - 1 - z)

    def at(self, position):
        g, z = divmod(position, self.depth)
        return (z if g % 2 == 0 else self.depth - 1 - z), g

    def ring_step(self, step):
        pairs = []
        for z, core, g, t in self.devices():
            to_z, to_g = self.at((self.place(z, g) + step) % self.ring)
            pairs.append((self.flat(z, core, g, t), self.flat(to_z, core, to_g, t)))
        return pairs

    def core_swap(self):
        return [
            (self.flat(z, c, g, t), self.flat(z, 1 - c, g, t)) for z, c, g, t in self.devices()
        ]

    def feature_step(self, step):
        return [
            (self.flat(z, c, g, (t + step) % self.tp), self.flat(z, c, g, t))
            for z, c, g, t in self.devices()
        ]

    def column_step(self, shift, turn):
        pairs = []
        for z, c, g, t in self.devices():
            source = t * self.block + (z % self.block + shift) % self.block
            pairs.append(
                (
                    self.flat(source, c, (g + turn) % self.grp, z // self.block),
                    self.flat(z, c, g, t),
                )
            )
        return pairs


def gate(arrays, token):
    return lax.optimization_barrier((arrays, token))


def pinned(x, space=pltpu.HBM):
    return pltpu.with_memory_space_constraint(x, space)


def sort_rows(lengths, order):
    rows = lengths.shape[0]
    held = [lengths[r] for r in range(rows)]
    for r in range(rows):
        rank = jnp.int32(0)
        for other in range(rows):
            if other != r:
                ahead = held[other] >= held[r] if other < r else held[other] > held[r]
                rank = rank + ahead.astype(jnp.int32)
        order[rank] = r


def attend_cache(part, pairs, sizes, scale, *refs):
    lengths, q_ref, k_hbm, v_hbm, w_hbm = refs[:5]
    o_ref, lse_ref, w_ref, k_buf, v_buf, order, sems, w_sem = refs[-8:]
    steps, _, heads, size = q_ref.shape
    kv = k_hbm.shape[1] // sizes[-1]
    lanes = steps * heads
    sort_rows(lengths, order)

    def by_length(pair, act):
        length = lengths[order[2 * (part * pairs + pair)]]
        below = 0
        for slots in sizes:

            @pl.when((length > below) & (length <= slots))
            def _():
                act(pair, slots)

            below = slots

    def copies(pair, slots):
        span = pl.ds(0, slots * kv)
        made = []
        for i in range(2):
            spot = 2 * pair + i
            row = order[2 * part * pairs + spot]
            made.append(
                [
                    pltpu.make_async_copy(
                        hbm.at[row, span], buf.at[spot, span], sems.at[spot, which]
                    )
                    for which, (hbm, buf) in enumerate(((k_hbm, k_buf), (v_hbm, v_buf)))
                ]
            )
        return made

    def begin(pair, slots):
        for row in copies(pair, slots):
            for copy in row:
                copy.start()

    def compute(pair, slots):
        made = copies(pair, slots)
        n = slots * kv
        lane = min(n, size)
        head = (lax.broadcasted_iota(jnp.int32, (lanes, lane), 0) % heads) // (heads // kv)
        slot_head = lax.broadcasted_iota(jnp.int32, (lanes, lane), 1) % kv
        bias = jnp.where(head == slot_head, 0.0, -jnp.inf)
        bias = jnp.concatenate([bias] * (n // lane), axis=1)
        column = lax.broadcasted_iota(jnp.int32, (1, n), 1)
        scores = []
        for i in range(2):
            spot = 2 * pair + i
            row = order[2 * part * pairs + spot]
            q = q_ref[:, row].reshape(lanes, size)
            made[i][0].wait()
            s = lax.dot_general(
                q, k_buf[spot, :n], (((1,), (1,)), ((), ())), preferred_element_type=jnp.float32
            )
            open_slots = jnp.where(column < lengths[row] * kv, 0.0, -jnp.inf)
            scores.append(s * scale + (bias + open_slots))
        highest = [jnp.max(s, axis=1, keepdims=True) for s in scores]
        weights = [jnp.exp2(s - h) for s, h in zip(scores, highest)]
        totals = [jnp.sum(p, axis=1, keepdims=True) for p in weights]
        for i in range(2):
            spot = 2 * pair + i
            made[i][1].wait()
            o = jnp.dot(
                weights[i].astype(jnp.bfloat16),
                v_buf[spot, :n],
                preferred_element_type=jnp.float32,
            )
            o_ref[spot] = o / totals[i]
            lse = highest[i] + jnp.log(totals[i]) * LOG2E
            lse_ref[spot] = jnp.broadcast_to(lse, (lanes, size))

    for pair in range(pairs):
        by_length(pair, begin)
    w_copy = pltpu.make_async_copy(w_hbm.at[part], w_ref, w_sem)
    w_copy.start()

    @pl.loop(0, pairs)
    def _(pair):
        by_length(pair, compute)

    w_copy.wait()


def cache_attention(part, pairs, lengths, queries, keys, values, weights, slots, after):
    steps, rows, heads, size = queries.shape
    kv = keys.shape[1] // slots
    sizes = (slots // 24, slots // 6, slots // 2, slots)
    scale = LOG2E / math.sqrt(size)
    piece = jax.ShapeDtypeStruct((2 * pairs, steps * heads, size), jnp.float32)
    return pl.pallas_call(
        functools.partial(attend_cache, part, pairs, sizes, scale),
        out_shape=(piece, piece, pltpu.VMEM(weights.shape[1:], weights.dtype)),
        in_specs=[SMEM, VMEM, HBM, HBM, HBM] + [ANY] * len(after),
        out_specs=(VMEM, VMEM, VMEM),
        scratch_shapes=[
            pltpu.VMEM((2 * pairs, slots * kv, size), jnp.bfloat16),
            pltpu.VMEM((2 * pairs, slots * kv, size), jnp.bfloat16),
            pltpu.SMEM((rows,), jnp.int32),
            pltpu.SemaphoreType.DMA((2 * pairs, 2)),
            pltpu.SemaphoreType.DMA,
        ],
        compiler_params=pltpu.CompilerParams(vmem_limit_bytes=24 * MIB),
        cost_estimate=pl.CostEstimate(
            flops=8 * steps * heads * pairs * slots * kv * size,
            bytes_accessed=8 * pairs * slots * kv * size + 2 * weights[0].size,
            transcendentals=2 * steps * heads * pairs * slots * kv,
        ),
        name="cache_attention",
    )(lengths, queries, pinned(keys), pinned(values), pinned(weights), *after)


def merge_blocks(lay, plan, counts, first, last, scale, *refs):
    refs = list(refs)

    def take(n):
        out = refs[:n]
        del refs[:n]
        return out

    weights = take(2)
    downs = [take(n) for _, _, n in plan]
    if first:
        hidden, ups = take(counts[0]), take(counts[1])
    else:
        u_in, h_in, _, fresh_in, low_in = take(5)
    if last:
        lengths, q_ref = take(2)
        caches = [take(2) for _ in range(2)]
    take(len(refs) - (2 if last else 3) - (3 if first else 0) - 2 - (3 if last else 0))
    (m_hbm,) = take(1)
    (out_ref,) = take(1) if last else (None,)
    if first:
        u_buf, h_buf = take(2)
    else:
        u_buf, h_buf = u_in, h_in
    if last:
        fresh, low, order = refs[-3:]
        del refs[-3:]
    else:
        fresh, low = take(2)
    if first:
        u_parts = refs.pop()
    m_buf, sems = refs

    pairs, depth = m_buf.shape[1], m_buf.shape[2]
    fsdp, grp, tp = (lax.axis_index(a) for a in AXES)
    z, core = fsdp // 2, lax.rem(fsdp, 2)
    place = grp * lay.depth + jnp.where(lax.rem(grp, 2) == 0, z, lay.depth - 1 - z)
    per_lane = lay.fsdp * lay.grp // lay.tp

    if first:
        for i, h in enumerate(hidden):
            h_buf[lax.rem(tp + i, lay.tp)] = h[...]
        for i, up in enumerate(ups):
            flip, rest = divmod(i, len(ups) // 2)
            shift, turn = divmod(rest, lay.grp)
            zz = lax.rem(lax.rem(z, lay.block) + shift, lay.block)
            cc = 1 - core if flip else core
            slot = (zz * 2 + cc) * lay.grp + lax.rem(grp + turn, lay.grp)
            u_parts[slot] = up[...]
        columns = u_parts.shape[2] // pairs
        for k in range(pairs):
            u_buf[k] = ADAPTER_SCALING * jnp.concatenate(
                [u_parts[i, :, k * columns : (k + 1) * columns] for i in range(len(ups))], axis=1
            )
        fresh[...] = jnp.zeros_like(fresh)
        low[...] = jnp.zeros_like(low)
    else:
        fresh[...] = fresh_in[...]
        low[...] = low_in[...]

    chunk = min(depth, 256)
    copies = []
    for j, (delta, flip, n_parts) in enumerate(plan):
        spot = lax.rem(place + (delta + lay.ring), lay.ring)
        g = spot // lay.depth
        along = lax.rem(spot, lay.depth)
        zz = jnp.where(lax.rem(g, 2) == 0, along, lay.depth - 1 - along)
        index = (zz * 2 + (1 - core if flip else core)) * lay.grp + g
        start = pl.multiple_of(index * depth, depth)
        column = pl.multiple_of(lax.rem(index, per_lane) * depth, depth)
        source = index // per_lane
        for k in range(pairs):
            d_ref = downs[j][0].at[k] if n_parts == 1 else downs[j][k].at[0]
            for begin in range(0, depth, chunk):
                rows = slice(begin, begin + chunk)
                d = d_ref[:, rows]
                w = weights[k][pl.ds(start + begin, chunk), :]
                h = h_buf[source, :, pl.ds(column + begin, chunk)]
                added = lax.dot_general(
                    d, u_buf[k], (((0,), (0,)), ((), ())), preferred_element_type=jnp.float32
                )
                m_buf[j, k, rows, :] = (w.astype(jnp.float32) + added).astype(jnp.bfloat16)
                fresh[k] += jnp.dot(h, w, preferred_element_type=jnp.float32)
                low[k] += lax.dot_general(
                    h, d, (((1,), (1,)), ((), ())), preferred_element_type=jnp.float32
                )
            copy = pltpu.make_async_copy(
                m_buf.at[j, k], m_hbm.at[k, pl.ds(start, depth), :], sems.at[j, k]
            )
            copy.start()
            copies.append(copy)

    if last:
        sort_rows(lengths, order)
        new = []
        for k in range(pairs):
            high = low[k].astype(jnp.bfloat16)
            rest = (low[k] - high.astype(jnp.float32)).astype(jnp.bfloat16)
            new.append(
                (
                    fresh[k]
                    + jnp.dot(high, u_buf[k], preferred_element_type=jnp.float32)
                    + jnp.dot(rest, u_buf[k], preferred_element_type=jnp.float32)
                ).astype(jnp.bfloat16)
            )
        add_new_tokens(q_ref, order, caches, new, out_ref, scale)
    for copy in copies:
        copy.wait()


def add_new_tokens(q_ref, order, caches, new, out_ref, scale):
    steps, rows, heads, size = q_ref.shape
    kv = new[0].shape[1] // size
    new = [
        jnp.concatenate([x[:, g * size : (g + 1) * size] for g in range(kv)], axis=0) for x in new
    ]
    n = kv * steps * rows
    lanes = steps * heads
    left = lax.broadcasted_iota(jnp.int32, (lanes, n), 0)
    right = lax.broadcasted_iota(jnp.int32, (lanes, n), 1)
    same_head = (left % heads) // (heads // kv) == right // (steps * rows)
    earlier = (right // rows) % steps <= left // heads
    right_row = jnp.where(same_head & earlier, right % rows, -1)
    spot = 0
    for o_ref, lse_ref in caches:
        for i in range(o_ref.shape[0]):
            row = order[spot]
            q = q_ref[:, row].reshape(lanes, size)
            s = lax.dot_general(
                q, new[0], (((1,), (1,)), ((), ())), preferred_element_type=jnp.float32
            )
            s = jnp.where(right_row == row, s * scale, -jnp.inf)
            lse = lse_ref[i][:, :1]
            highest = jnp.maximum(jnp.max(s, axis=1, keepdims=True), lse)
            p = jnp.exp2(s - highest)
            old = jnp.exp2(lse - highest)
            divisor = jnp.sum(p, axis=1, keepdims=True) + old
            o = old * o_ref[i] + jnp.dot(
                p.astype(jnp.bfloat16), new[1], preferred_element_type=jnp.float32
            )
            out_ref[:, row] = (o / divisor).reshape(steps, heads, size).astype(out_ref.dtype)
            spot += 1


def merge(lay, shape, entries, weights, inputs, state, final, after):
    pairs, total, width = shape
    rank, depth = entries[0][2][0].shape[1:]
    first, last = state is None, final is not None
    n = len(entries)
    operands = [pinned(w, pltpu.VMEM) for w in weights] + [d for e in entries for d in e[2]]
    specs = [VMEM] * len(operands)
    counts = (0, 0)
    aliases = {}
    if first:
        hidden, ups = inputs
        counts = (len(hidden), len(ups))
        operands += hidden + ups
        specs += [VMEM] * (len(hidden) + len(ups))
        tokens, features = hidden[0].shape
        up_shape = (pairs, rank, width)
        h_shape = (lay.tp, tokens, features)
    else:
        m_prev, u, h, fresh, low = state
        aliases = {len(operands) + 2: 0}
        operands += [u, h, pinned(m_prev), fresh, low]
        specs += [VMEM, VMEM, HBM, VMEM, VMEM]
        tokens = h.shape[1]
    out_shape = [pltpu.HBM(shape, jnp.bfloat16)]
    sums = [(pairs, tokens, width), (pairs, tokens, rank)]
    scratch = [
        pltpu.VMEM((n, pairs, depth, width), jnp.bfloat16),
        pltpu.SemaphoreType.DMA((n, 2)),
    ]
    scale = 0.0
    if first:
        out_shape += [jax.ShapeDtypeStruct(s, jnp.bfloat16) for s in (up_shape, h_shape)]
        scratch.append(pltpu.VMEM((len(ups),) + ups[0].shape, jnp.bfloat16))
    if last:
        lengths, queries, caches = final
        operands += [lengths, queries] + caches
        specs += [SMEM] + [VMEM] * (1 + len(caches))
        out_shape.append(jax.ShapeDtypeStruct(queries.shape, jnp.bfloat16))
        scale = LOG2E / math.sqrt(queries.shape[3])
        scratch += [pltpu.VMEM(s, jnp.float32) for s in sums]
        scratch.append(pltpu.SMEM((queries.shape[1],), jnp.int32))
    else:
        out_shape += [jax.ShapeDtypeStruct(s, jnp.float32) for s in sums]
    operands += after
    specs += [ANY] * len(after)
    out = pl.pallas_call(
        functools.partial(
            merge_blocks,
            lay,
            [(delta, flip, len(arrays)) for delta, flip, arrays in entries],
            counts,
            first,
            last,
            scale,
        ),
        out_shape=out_shape,
        in_specs=specs,
        out_specs=[HBM] + [VMEM] * (len(out_shape) - 1),
        input_output_aliases=aliases,
        scratch_shapes=scratch,
        compiler_params=pltpu.CompilerParams(vmem_limit_bytes=14 * MIB),
        cost_estimate=pl.CostEstimate(
            flops=2 * n * pairs * depth * width * (rank + tokens),
            bytes_accessed=2 * n * pairs * depth * width,
            transcendentals=0,
        ),
        name="merge_blocks",
    )(*operands)
    if last or first:
        return list(out)
    return [out[0], u, h, *out[1:]]


def shards(
    lay,
    hidden_states,
    queries,
    cache_keys,
    cache_values,
    cache_lengths,
    projection_weight_matrices,
    factor_down,
    factor_up,
):
    send = functools.partial(lax.ppermute, axis_name=AXES)
    steps, rows, features = hidden_states.shape
    slots, kv, size = cache_keys.shape[1:]
    shape = projection_weight_matrices.shape
    own = jnp.swapaxes(factor_down, 1, 2)
    own_up = jnp.concatenate([factor_up[k] for k in range(factor_up.shape[0])], axis=1)
    tokens = hidden_states.reshape(steps * rows, features)
    keys = cache_keys.reshape(rows, slots * kv, size)
    values = cache_values.reshape(rows, slots * kv, size)
    swap = lay.core_swap()
    ring = {1: lay.ring_step(1), -1: lay.ring_step(-1)}
    caches, weights = [], []

    def attention(part, after):
        o, lse, w = cache_attention(
            part,
            rows // 4,
            cache_lengths,
            queries,
            keys,
            values,
            projection_weight_matrices,
            slots,
            after,
        )
        caches.extend([o, lse])
        weights.append(w)
        return o

    ups = [
        send(own_up, perm=lay.column_step(shift, turn))
        for shift in range(lay.block)
        for turn in range(lay.grp)
    ]
    came = {d: send(own, perm=ring[d]) for d in ring}
    partner = send(own, perm=swap)
    hidden = [tokens] + [send(tokens, perm=lay.feature_step(i)) for i in range(1, lay.tp)]
    ups, token = gate(ups, attention(0, []))
    other_ups = [send(u, perm=swap) for u in ups]
    token = attention(1, [token])
    arrivals, token = gate([came[1], came[-1], partner] + hidden[1:] + other_ups, token)
    came = {1: arrivals[0], -1: arrivals[1]}
    partner = arrivals[2]
    hidden[1:] = list(arrivals[3 : 2 + lay.tp])
    other_ups = list(arrivals[2 + lay.tp :])

    entries = [(0, False, [own]), (0, True, [partner])]
    inputs = (hidden, list(ups) + other_ups)
    state = None
    last_step = lay.ring // 2
    for step in range(1, last_step):
        entries += [(-d * step, False, [came[d]]) for d in ring]
        if step + 1 < last_step:
            sent = {d: send(came[d], perm=ring[d]) for d in ring}
        else:
            sent = {1: send(came[1][:1], perm=ring[1]), -1: send(came[-1][1:], perm=ring[-1])}
        swapped = [send(came[d], perm=swap) for d in ring]
        state = merge(lay, shape, entries, weights, inputs, state, None, [token])
        arrivals, token = gate([sent[1], sent[-1]] + swapped, state[3])
        came = {1: arrivals[0], -1: arrivals[1]}
        entries = [(-d * step, True, [a]) for d, a in zip(ring, arrivals[2:])]
    halves = [came[1], came[-1]]
    swapped = [send(c, perm=swap) for c in halves]
    entries.append((last_step, False, halves))
    state = merge(lay, shape, entries, weights, inputs, state, None, [token])
    entries = [(last_step, True, swapped)]
    final = (cache_lengths, queries, caches)
    return tuple(merge(lay, shape, entries, weights, inputs, state, final, []))


def solution(mesh):
    return jax.shard_map(
        functools.partial(shards, Layout(mesh)),
        mesh=mesh,
        in_specs=(
            P(None, ("fsdp", "grp"), "tp"),
            P(None, ("fsdp", "grp"), "tp", None),
            P(("fsdp", "grp"), None, "tp", None),
            P(("fsdp", "grp"), None, "tp", None),
            P(("fsdp", "grp")),
            P(None, None, "tp"),
            P(None, ("fsdp", "grp"), None),
            P(None, None, ("fsdp", "grp")),
        ),
        out_specs=(P(None, None, "tp"), P(None, ("fsdp", "grp"), "tp", None)),
        check_vma=False,
    )
```

```python
import functools
import math

import jax
import jax.numpy as jnp
from jax import lax
from jax.experimental import pallas as pl
from jax.experimental.pallas import tpu as pltpu
from jax.sharding import PartitionSpec as P

AXES = ("fsdp", "grp", "tp")
ADAPTER_SCALING = 2.0
LOG2E = math.log2(math.e)
MIB = 1024 * 1024
ANY = pl.BlockSpec(memory_space=pl.ANY)
HBM = pl.BlockSpec(memory_space=pltpu.HBM)
VMEM = pl.BlockSpec(memory_space=pltpu.VMEM)
SMEM = pl.BlockSpec(memory_space=pltpu.SMEM)


class Layout:
    def __init__(self, mesh):
        self.fsdp, self.grp, self.tp = (mesh.shape[a] for a in AXES)
        self.depth = self.fsdp // 2
        self.ring = self.depth * self.grp
        self.block = self.depth // self.tp

    def flat(self, z, core, g, t):
        return ((z * 2 + core) * self.grp + g) * self.tp + t

    def devices(self):
        for z in range(self.depth):
            for core in range(2):
                for g in range(self.grp):
                    for t in range(self.tp):
                        yield z, core, g, t

    def place(self, z, g):
        return g * self.depth + (z if g % 2 == 0 else self.depth - 1 - z)

    def at(self, position):
        g, z = divmod(position, self.depth)
        return (z if g % 2 == 0 else self.depth - 1 - z), g

    def ring_step(self):
        pairs = []
        for z, core, g, t in self.devices():
            to_z, to_g = self.at((self.place(z, g) + (1 - 2 * core)) % self.ring)
            pairs.append((self.flat(z, core, g, t), self.flat(to_z, core, to_g, t)))
        return pairs

    def core_swap(self):
        return [
            (self.flat(z, c, g, t), self.flat(z, 1 - c, g, t)) for z, c, g, t in self.devices()
        ]

    def feature_step(self, step):
        return [
            (self.flat(z, c, g, (t + step) % self.tp), self.flat(z, c, g, t))
            for z, c, g, t in self.devices()
        ]

    def column_step(self, turn):
        pairs = []
        for z, c, g, t in self.devices():
            shift, turn_g = divmod(2 * turn + c, self.grp)
            source = t * self.block + (z % self.block + shift) % self.block
            pairs.append(
                (
                    self.flat(source, c, (g + turn_g) % self.grp, z // self.block),
                    self.flat(z, c, g, t),
                )
            )
        return pairs


def over(x, n):
    return x >> (n.bit_length() - 1) if n & (n - 1) == 0 else x // n


def within(x, n):
    return x & (n - 1) if n & (n - 1) == 0 else x % n


def after_all(arrays, token):
    return lax.optimization_barrier((arrays, token))


def pinned(x, space=pltpu.HBM):
    return pltpu.with_memory_space_constraint(x, space)


def sort_rows(lengths, order):
    rows = lengths.shape[0]
    held = [lengths[r] for r in range(rows)]
    for r in range(rows):
        rank = jnp.int32(0)
        for other in range(rows):
            if other != r:
                ahead = held[other] >= held[r] if other < r else held[other] > held[r]
                rank = rank + ahead.astype(jnp.int32)
        order[rank] = r


def by_length(length, sizes, act):
    below = 0
    for slots in sizes:

        @pl.when((length > below) & (length <= slots))
        def _():
            act(slots)

        below = slots


def cache_copies(first, slots, kv, order, hbms, bufs, sems):
    span = pl.ds(0, slots * kv)
    return [
        [
            pltpu.make_async_copy(
                hbm.at[order[first + i], span], buf.at[i, span], sems.at[i, which]
            )
            for which, (hbm, buf) in enumerate(zip(hbms, bufs))
        ]
        for i in range(2)
    ]


def begin_blocks(sizes, kv, len_hbm, q_hbm, k_hbm, v_hbm, *refs):
    len_ref, order, q_ref, k_ref, v_ref, sems, kv_sems = refs
    len_copy = pltpu.make_async_copy(len_hbm, len_ref, sems.at[0])
    q_copy = pltpu.make_async_copy(q_hbm, q_ref, sems.at[1])
    len_copy.start()
    q_copy.start()
    len_copy.wait()
    sort_rows(len_ref, order)

    def bring(slots):
        made = cache_copies(0, slots, kv, order, (k_hbm, v_hbm), (k_ref, v_ref), kv_sems)
        for copies in made:
            for copy in copies:
                copy.start()
        for copies in made:
            for copy in copies:
                copy.wait()

    by_length(len_ref[order[0]], sizes, bring)
    q_copy.wait()


def begin(lengths, queries, keys, values, sizes, kv):
    rows = lengths.shape[0]
    pair = pltpu.VMEM((2,) + keys.shape[1:], keys.dtype)
    return pl.pallas_call(
        functools.partial(begin_blocks, sizes, kv),
        out_shape=(
            pltpu.SMEM((rows,), jnp.int32),
            pltpu.SMEM((rows,), jnp.int32),
            pltpu.VMEM(queries.shape, queries.dtype),
            pair,
            pair,
        ),
        in_specs=[HBM] * 4,
        out_specs=(SMEM, SMEM, VMEM, VMEM, VMEM),
        scratch_shapes=[pltpu.SemaphoreType.DMA((2,)), pltpu.SemaphoreType.DMA((2, 2))],
        compiler_params=pltpu.CompilerParams(vmem_limit_bytes=8 * MIB),
        cost_estimate=pl.CostEstimate(
            flops=0, bytes_accessed=8 * keys[0].size, transcendentals=0
        ),
        name="begin",
    )(pinned(lengths), pinned(queries), pinned(keys), pinned(values))


def pack_pair(own_hbm, other, own_up, other_up, *refs):
    pair, up_pair, sems = refs[-3:]
    core = lax.rem(lax.axis_index("fsdp"), 2)
    copies = [
        pltpu.make_async_copy(own_hbm, pair.at[core], sems.at[0]),
        pltpu.make_async_copy(other, pair.at[1 - core], sems.at[1]),
    ]
    for copy in copies:
        copy.start()
    for ref, place in ((own_up, core), (other_up, 1 - core)):
        up_pair[place] = jnp.concatenate([ref[k] for k in range(ref.shape[0])], axis=1)
    for copy in copies:
        copy.wait()


def pack(own, other, own_up, other_up, after):
    count, rank, columns = own_up.shape
    return pl.pallas_call(
        pack_pair,
        out_shape=(
            pltpu.VMEM((2,) + own.shape, own.dtype),
            pltpu.VMEM((2, rank, count * columns), own.dtype),
        ),
        in_specs=[HBM, ANY, VMEM, VMEM] + [ANY] * len(after),
        out_specs=(VMEM, VMEM),
        scratch_shapes=[pltpu.SemaphoreType.DMA((2,))],
        compiler_params=pltpu.CompilerParams(vmem_limit_bytes=4 * MIB),
        name="pack_pair",
    )(pinned(own), other, own_up, other_up, *after)


def attend_cache(part, pairs, sizes, scale, brought, *refs):
    lengths, order, q_ref, k_hbm, v_hbm, w_hbm = refs[:6]
    k_pair, v_pair = refs[6:8] if brought else (None, None)
    k_buf, v_buf, sems, w_sems = refs[-4:]
    cuts = w_sems.shape[0]
    o_ref, lse_ref, *w_refs = refs[-6 - cuts : -4]
    steps, _, heads, size = q_ref.shape
    kv = k_hbm.shape[1] // sizes[-1]
    lanes = steps * heads
    cut = w_refs[0].shape[1]
    buffers = []
    for pair in range(pairs):
        if pair == 0 and brought:
            buffers.append((k_pair, v_pair))
        else:
            buffers.append((k_buf.at[pl.ds(2 * pair, 2)], v_buf.at[pl.ds(2 * pair, 2)]))

    def copies(pair, slots):
        first = 2 * (part * pairs + pair)
        return cache_copies(
            first, slots, kv, order, (k_hbm, v_hbm), buffers[pair], sems.at[pair]
        )

    for pair in range(pairs):
        if pair > 0 or not brought:

            def bring(slots):
                for made in copies(pair, slots):
                    for copy in made:
                        copy.start()

            by_length(lengths[order[2 * (part * pairs + pair)]], sizes, bring)
    w_copies = [
        pltpu.make_async_copy(
            w_hbm.at[part, :, pl.ds(i * cut, cut)], w, w_sems.at[i]
        )
        for i, w in enumerate(w_refs)
    ]
    for copy in w_copies:
        copy.start()

    row_head = over(within(lax.broadcasted_iota(jnp.int32, (lanes, size), 0), heads), heads // kv)
    slot_head = within(lax.broadcasted_iota(jnp.int32, (lanes, size), 1), kv)
    head_bias = jnp.where(row_head == slot_head, 0.0, -jnp.inf)

    for pair in range(pairs):
        first = 2 * (part * pairs + pair)

        def compute(slots):
            waits = None if pair == 0 and brought else copies(pair, slots)
            n = slots * kv
            bias = jnp.concatenate([head_bias[:, : min(n, size)]] * max(n // size, 1), axis=1)
            column = lax.broadcasted_iota(jnp.int32, (1, n), 1)
            k_rows, v_rows = buffers[pair]
            scores = []
            for i in range(2):
                row = order[first + i]
                q = q_ref[:, row].reshape(lanes, size)
                if waits is not None:
                    waits[i][0].wait()
                s = lax.dot_general(
                    q,
                    k_rows[i, :n],
                    (((1,), (1,)), ((), ())),
                    preferred_element_type=jnp.float32,
                )
                closed = jnp.where(column < lengths[row] * kv, 0.0, -jnp.inf)
                scores.append(s + (bias + closed))
            highest = [jnp.max(s, axis=1, keepdims=True) * scale for s in scores]
            weights = [jnp.exp2(s * scale - h) for s, h in zip(scores, highest)]
            totals = [jnp.sum(p, axis=1, keepdims=True) for p in weights]
            for i in range(2):
                spot = 2 * pair + i
                if waits is not None:
                    waits[i][1].wait()
                o = jnp.dot(
                    weights[i].astype(jnp.bfloat16),
                    v_rows[i, :n],
                    preferred_element_type=jnp.float32,
                )
                o_ref[spot] = o / totals[i]
                lse = highest[i] + jnp.log(totals[i]) * LOG2E
                lse_ref[spot] = jnp.broadcast_to(lse, (lanes, size))

        by_length(lengths[order[first]], sizes, compute)

    for copy in w_copies:
        copy.wait()


def cache_attention(part, pairs, lengths, order, queries, keys, values, weights, sizes, brought, after):
    steps, rows, heads, size = queries.shape
    slots = sizes[-1]
    kv = keys.shape[1] // slots
    scale = LOG2E / math.sqrt(size)
    piece = pltpu.VMEM((2 * pairs, steps * heads, size), jnp.float32)
    cuts = max(1, weights.shape[2] // 256)
    w_cut = pltpu.VMEM((weights.shape[1], weights.shape[2] // cuts), weights.dtype)
    operands = [pinned(lengths, pltpu.SMEM), pinned(order, pltpu.SMEM), pinned(queries, pltpu.VMEM)]
    operands += [pinned(keys), pinned(values), pinned(weights)]
    operands += [pinned(b, pltpu.VMEM) for b in brought]
    specs = [SMEM, SMEM, VMEM, HBM, HBM, HBM] + [VMEM] * len(brought) + [ANY] * len(after)
    return pl.pallas_call(
        functools.partial(attend_cache, part, pairs, sizes, scale, bool(brought)),
        out_shape=(piece, piece) + (w_cut,) * cuts,
        in_specs=specs,
        out_specs=(VMEM,) * (2 + cuts),
        scratch_shapes=[
            pltpu.VMEM((2 * pairs, slots * kv, size), jnp.bfloat16),
            pltpu.VMEM((2 * pairs, slots * kv, size), jnp.bfloat16),
            pltpu.SemaphoreType.DMA((pairs, 2, 2)),
            pltpu.SemaphoreType.DMA((cuts,)),
        ],
        compiler_params=pltpu.CompilerParams(vmem_limit_bytes=24 * MIB),
        cost_estimate=pl.CostEstimate(
            flops=8 * steps * heads * pairs * slots * kv * size,
            bytes_accessed=8 * pairs * slots * kv * size + 2 * weights[0].size,
            transcendentals=2 * steps * heads * pairs * slots * kv,
        ),
        name="cache_attention",
    )(*operands, *after)


def merge_blocks(lay, plan, counts, first, last, scale, *refs):
    refs = list(refs)

    def take(n):
        out = refs[:n]
        del refs[:n]
        return out

    weights = [take(n) for n in counts[2:]]
    downs = take(len(plan))
    if first:
        hidden, ups = take(counts[0]), take(counts[1])
    else:
        u_in, h_in, _, fresh_in, low_in = take(5)
    if last:
        order, q_ref = take(2)
        caches = [take(2) for _ in range(2)]
    take(len(refs) - (2 if last else 3) - (3 if first else 0) - 2 - (2 if last else 0))
    (m_hbm,) = take(1)
    (out_ref,) = take(1) if last else (None,)
    if first:
        u_buf, h_buf = take(2)
    else:
        u_buf, h_buf = u_in, h_in
    if last:
        fresh, low = refs[-2:]
        del refs[-2:]
    else:
        fresh, low = take(2)
    if first:
        u_parts = refs.pop()
    m_buf, sems = refs

    pairs, depth, width = m_buf.shape[1:]
    cut = weights[0][0].shape[1]
    fsdp, grp, tp = (lax.axis_index(a) for a in AXES)
    z, core = fsdp // 2, lax.rem(fsdp, 2)
    place = grp * lay.depth + jnp.where(lax.rem(grp, 2) == 0, z, lay.depth - 1 - z)
    per_lane = lay.fsdp * lay.grp // lay.tp

    if first:
        for i, h in enumerate(hidden):
            h_buf[lax.rem(tp + i, lay.tp)] = h[...]
        for i, up in enumerate(ups):
            flip, turn = divmod(i, len(ups) // 2)
            spot = 2 * turn + (1 - core if flip else core)
            shift, turn = spot // lay.grp, lax.rem(spot, lay.grp)
            zz = lax.rem(lax.rem(z, lay.block) + shift, lay.block)
            for c in range(2):
                u_parts[(zz * 2 + c) * lay.grp + lax.rem(grp + turn, lay.grp)] = up[c]
        columns = u_parts.shape[2] // pairs
        for k in range(pairs):
            u_buf[k] = ADAPTER_SCALING * jnp.concatenate(
                [u_parts[i, :, k * columns : (k + 1) * columns] for i in range(u_parts.shape[0])],
                axis=1,
            )
        fresh[...] = jnp.zeros_like(fresh)
        low[...] = jnp.zeros_like(low)
    else:
        fresh[...] = fresh_in[...]
        low[...] = low_in[...]

    chunk = min(depth, 256)
    copies = []
    j = 0
    for (step, flip, whole), down in zip(plan, downs):
        towards = 2 * core - 1
        spot = lax.rem(place + lay.ring + step * (-towards if flip else towards), lay.ring)
        g = spot // lay.depth
        along = lax.rem(spot, lay.depth)
        zz = jnp.where(lax.rem(g, 2) == 0, along, lay.depth - 1 - along)
        for c in range(down.shape[0]):
            cc = c if whole else (1 - core if flip else core)
            index = (zz * 2 + cc) * lay.grp + g
            start = pl.multiple_of(index * depth, depth)
            column = pl.multiple_of(lax.rem(index, per_lane) * depth, depth)
            source = index // per_lane
            for k in range(pairs):
                for begin in range(0, depth, chunk):
                    rows = slice(begin, begin + chunk)
                    d = down[c, k, :, rows]
                    h = h_buf[source, :, pl.ds(column + begin, chunk)]
                    for side in range(width // cut):
                        cols = slice(side * cut, (side + 1) * cut)
                        w = weights[k][side][pl.ds(start + begin, chunk), :]
                        added = lax.dot_general(
                            d,
                            u_buf[k, :, cols],
                            (((0,), (0,)), ((), ())),
                            preferred_element_type=jnp.float32,
                        )
                        m_buf[j, k, rows, cols] = (w.astype(jnp.float32) + added).astype(
                            jnp.bfloat16
                        )
                        fresh[k, :, cols] += jnp.dot(h, w, preferred_element_type=jnp.float32)
                    low[k] += lax.dot_general(
                        h, d, (((1,), (1,)), ((), ())), preferred_element_type=jnp.float32
                    )
                copy = pltpu.make_async_copy(
                    m_buf.at[j, k], m_hbm.at[k, pl.ds(start, depth), :], sems.at[j, k]
                )
                copy.start()
                copies.append(copy)
            j += 1

    if last:
        new = []
        for k in range(pairs):
            high = low[k].astype(jnp.bfloat16)
            rest = (low[k] - high.astype(jnp.float32)).astype(jnp.bfloat16)
            new.append(
                (
                    fresh[k]
                    + jnp.dot(high, u_buf[k], preferred_element_type=jnp.float32)
                    + jnp.dot(rest, u_buf[k], preferred_element_type=jnp.float32)
                ).astype(jnp.bfloat16)
            )
        add_new_tokens(q_ref, order, caches, new, out_ref, scale)
    for copy in copies:
        copy.wait()


def add_new_tokens(q_ref, order, caches, new, out_ref, scale):
    steps, rows, heads, size = q_ref.shape
    kv = new[0].shape[1] // size
    new = [
        jnp.concatenate([x[:, g * size : (g + 1) * size] for g in range(kv)], axis=0) for x in new
    ]
    n = kv * steps * rows
    lanes = steps * heads
    left = lax.broadcasted_iota(jnp.int32, (lanes, n), 0)
    right = lax.broadcasted_iota(jnp.int32, (lanes, n), 1)
    same_head = over(within(left, heads), heads // kv) == over(right, steps * rows)
    earlier = within(over(right, rows), steps) <= over(left, heads)
    right_row = jnp.where(same_head & earlier, within(right, rows), -1)
    spots = [(o, lse, i) for o, lse in caches for i in range(o.shape[0])]
    for spot, (o_ref, lse_ref, i) in enumerate(spots):
        row = order[spot]
        q = q_ref[:, row].reshape(lanes, size)
        s = lax.dot_general(
            q, new[0], (((1,), (1,)), ((), ())), preferred_element_type=jnp.float32
        )
        s = jnp.where(right_row == row, s * scale, -jnp.inf)
        lse = lse_ref[i]
        highest = jnp.maximum(jnp.max(s, axis=1, keepdims=True), lse)
        p = jnp.exp2(s - highest[:, :n])
        old = jnp.exp2(lse - highest)
        divisor = jnp.sum(p, axis=1, keepdims=True) + old
        o = old * o_ref[i] + jnp.dot(
            p.astype(jnp.bfloat16), new[1], preferred_element_type=jnp.float32
        )
        out_ref[:, row] = (o / divisor).reshape(steps, heads, size).astype(out_ref.dtype)


def merge(lay, shape, entries, weights, inputs, state, final, after):
    pairs, total, width = shape
    rank, depth = entries[0][3].shape[2:]
    first, last = state is None, final is not None
    n = sum(e[3].shape[0] for e in entries)
    operands = [pinned(w, pltpu.VMEM) for part in weights for w in part]
    operands += [e[3] for e in entries]
    specs = [VMEM] * len(operands)
    counts = (0, 0)
    cuts = tuple(len(part) for part in weights)
    aliases = {}
    if first:
        hidden, ups = inputs
        counts = (len(hidden), len(ups))
        operands += hidden + ups
        specs += [VMEM] * (len(hidden) + len(ups))
        tokens, features = hidden[0].shape
    else:
        m_prev, u, h, fresh, low = state
        aliases = {len(operands) + 2: 0}
        operands += [u, h, pinned(m_prev), fresh, low]
        specs += [VMEM, VMEM, HBM, VMEM, VMEM]
        tokens = h.shape[1]
    out_shape = [pltpu.HBM(shape, jnp.bfloat16)]
    sums = [(pairs, tokens, width), (pairs, tokens, rank)]
    scratch = [
        pltpu.VMEM((n, pairs, depth, width), jnp.bfloat16),
        pltpu.SemaphoreType.DMA((n, 2)),
    ]
    scale = 0.0
    if first:
        out_shape += [
            pltpu.VMEM(s, jnp.bfloat16)
            for s in ((pairs, rank, width), (lay.tp, tokens, features))
        ]
        parts = len(ups) * 2
        scratch.append(pltpu.VMEM((parts,) + ups[0].shape[1:], jnp.bfloat16))
    if last:
        order, queries, caches = final
        operands += [pinned(order, pltpu.SMEM), pinned(queries, pltpu.VMEM)] + caches
        specs += [SMEM] + [VMEM] * (1 + len(caches))
        out_shape.append(jax.ShapeDtypeStruct(queries.shape, jnp.bfloat16))
        scale = LOG2E / math.sqrt(queries.shape[3])
        scratch += [pltpu.VMEM(s, jnp.float32) for s in sums]
    else:
        out_shape += [pltpu.VMEM(s, jnp.float32) for s in sums]
    operands += after
    specs += [ANY] * len(after)
    out = pl.pallas_call(
        functools.partial(
            merge_blocks, lay, [e[:3] for e in entries], counts + cuts, first, last, scale
        ),
        out_shape=out_shape,
        in_specs=specs,
        out_specs=[HBM] + [VMEM] * (len(out_shape) - 1),
        input_output_aliases=aliases,
        scratch_shapes=scratch,
        compiler_params=pltpu.CompilerParams(vmem_limit_bytes=14 * MIB),
        cost_estimate=pl.CostEstimate(
            flops=2 * n * pairs * depth * width * (rank + tokens),
            bytes_accessed=2 * n * pairs * depth * width,
            transcendentals=0,
        ),
        name="merge_blocks",
    )(*operands)
    if last or first:
        return list(out)
    return [out[0], u, h, *out[1:]]


def shards(
    lay,
    hidden_states,
    queries,
    cache_keys,
    cache_values,
    cache_lengths,
    projection_weight_matrices,
    factor_down,
    factor_up,
):
    send = functools.partial(lax.ppermute, axis_name=AXES)
    steps, rows, features = hidden_states.shape
    slots, kv, size = cache_keys.shape[1:]
    shape = projection_weight_matrices.shape
    sizes = tuple(slots * i // 24 for i in (1, 4, 8, 12, 16, 20, 24))
    own = jnp.swapaxes(factor_down, 1, 2)
    tokens = hidden_states.reshape(steps * rows, features)
    keys = cache_keys.reshape(rows, slots * kv, size)
    values = cache_values.reshape(rows, slots * kv, size)
    swap, ring = lay.core_swap(), lay.ring_step()
    caches, weights = [], []

    other, other_up = send(own, perm=swap), send(factor_up, perm=swap)
    lengths, order, q, *longest = begin(cache_lengths, queries, keys, values, sizes, kv)
    pair, up_pair = pack(own, other, factor_up, other_up, [q])

    def attention(part, brought, after):
        o, lse, *brought_weights = cache_attention(
            part,
            rows // 4,
            lengths,
            order,
            q,
            keys,
            values,
            projection_weight_matrices,
            sizes,
            brought,
            after,
        )
        caches.extend([o, lse])
        weights.append(brought_weights)
        return o

    came = send(pair, perm=ring)
    ups = [
        send(up_pair, perm=lay.column_step(turn)) for turn in range(lay.block * lay.grp // 2)
    ]
    (came, ups), token = after_all((came, ups), attention(0, longest, [pair]))

    swapped = send(came, perm=swap)
    other_ups = [send(u, perm=swap) for u in ups]
    hidden = [send(tokens, perm=lay.feature_step(i)) for i in range(1, lay.tp)]
    sent = send(came, perm=ring)
    token = attention(1, [], [token])
    (sent, swapped, other_ups, hidden), token = after_all(
        (sent, swapped, other_ups, hidden), token
    )
    entries = [(0, False, True, pair), (1, False, True, came), (1, True, True, swapped)]
    came = sent

    inputs = ([tokens] + hidden, ups + other_ups)
    state = None
    last_step = lay.ring // 2
    for step in range(2, last_step):
        if step + 1 < last_step:
            sent = send(came, perm=ring)
        else:
            core = lax.rem(lax.axis_index("fsdp"), 2)
            sent = send(lax.dynamic_slice_in_dim(came, core, 1, 0), perm=ring)
        swapped = send(came, perm=swap)
        state = merge(lay, shape, entries, weights, inputs, state, None, [token])
        (sent, swapped), token = after_all((sent, swapped), state[3])
        entries = [(step, False, True, came), (step, True, True, swapped)]
        came = sent
    swapped = send(came, perm=swap)
    entries.append((last_step, False, False, came))
    state = merge(lay, shape, entries, weights, inputs, state, None, [token])
    entries = [(last_step, True, False, swapped)]
    return tuple(merge(lay, shape, entries, weights, inputs, state, (order, q, caches), []))


def solution(mesh):
    return jax.shard_map(
        functools.partial(shards, Layout(mesh)),
        mesh=mesh,
        in_specs=(
            P(None, ("fsdp", "grp"), "tp"),
            P(None, ("fsdp", "grp"), "tp", None),
            P(("fsdp", "grp"), None, "tp", None),
            P(("fsdp", "grp"), None, "tp", None),
            P(("fsdp", "grp")),
            P(None, None, "tp"),
            P(None, ("fsdp", "grp"), None),
            P(None, None, ("fsdp", "grp")),
        ),
        out_specs=(P(None, None, "tp"), P(None, ("fsdp", "grp"), "tp", None)),
        check_vma=False,
    )
```

```python
import functools
import math

import jax
import jax.numpy as jnp
from jax import lax
from jax.experimental import pallas as pl
from jax.experimental.pallas import tpu as pltpu
from jax.sharding import PartitionSpec as P

AXES = ("fsdp", "grp", "tp")
ADAPTER_SCALING = 2.0
LOG2E = math.log2(math.e)
MIB = 1024 * 1024
ANY = pl.BlockSpec(memory_space=pl.ANY)
HBM = pl.BlockSpec(memory_space=pltpu.HBM)
VMEM = pl.BlockSpec(memory_space=pltpu.VMEM)
SMEM = pl.BlockSpec(memory_space=pltpu.SMEM)


class Layout:
    def __init__(self, mesh):
        self.fsdp, self.grp, self.tp = (mesh.shape[a] for a in AXES)
        self.depth = self.fsdp // 2
        self.ring = self.depth * self.grp
        self.block = self.depth // self.tp

    def flat(self, z, core, g, t):
        return ((z * 2 + core) * self.grp + g) * self.tp + t

    def devices(self):
        for z in range(self.depth):
            for core in range(2):
                for g in range(self.grp):
                    for t in range(self.tp):
                        yield z, core, g, t

    def place(self, z, g):
        return g * self.depth + (z if g % 2 == 0 else self.depth - 1 - z)

    def at(self, position):
        g, z = divmod(position, self.depth)
        return (z if g % 2 == 0 else self.depth - 1 - z), g

    def ring_step(self):
        pairs = []
        for z, core, g, t in self.devices():
            to_z, to_g = self.at((self.place(z, g) + (1 - 2 * core)) % self.ring)
            pairs.append((self.flat(z, core, g, t), self.flat(to_z, core, to_g, t)))
        return pairs

    def core_swap(self):
        return [
            (self.flat(z, c, g, t), self.flat(z, 1 - c, g, t)) for z, c, g, t in self.devices()
        ]

    def feature_step(self, step):
        return [
            (self.flat(z, c, g, (t + step) % self.tp), self.flat(z, c, g, t))
            for z, c, g, t in self.devices()
        ]

    def column_step(self, turn):
        pairs = []
        for z, c, g, t in self.devices():
            shift, turn_g = divmod(2 * turn + c, self.grp)
            source = t * self.block + (z % self.block + shift) % self.block
            pairs.append(
                (
                    self.flat(source, c, (g + turn_g) % self.grp, z // self.block),
                    self.flat(z, c, g, t),
                )
            )
        return pairs


def over(x, n):
    return x >> (n.bit_length() - 1) if n & (n - 1) == 0 else x // n


def within(x, n):
    return x & (n - 1) if n & (n - 1) == 0 else x % n


def after_all(arrays, token):
    return lax.optimization_barrier((arrays, token))


def pinned(x, space=pltpu.HBM):
    return pltpu.with_memory_space_constraint(x, space)


def sort_rows(lengths, order):
    rows = lengths.shape[0]
    held = [lengths[r] for r in range(rows)]
    for r in range(rows):
        rank = jnp.int32(0)
        for other in range(rows):
            if other != r:
                ahead = held[other] >= held[r] if other < r else held[other] > held[r]
                rank = rank + ahead.astype(jnp.int32)
        order[rank] = r


def by_length(length, sizes, act):
    below = 0
    for slots in sizes:

        @pl.when((length > below) & (length <= slots))
        def _():
            act(slots)

        below = slots


def cache_copies(first, spot, slots, kv, order, hbms, bufs, sems):
    span = pl.ds(0, slots * kv)
    return [
        [
            pltpu.make_async_copy(
                hbm.at[order[first + i], span], buf.at[spot + i, span], sems.at[i, which]
            )
            for which, (hbm, buf) in enumerate(zip(hbms, bufs))
        ]
        for i in range(2)
    ]


def begin_blocks(sizes, kv, len_hbm, q_hbm, k_hbm, v_hbm, *refs):
    len_ref, order, q_ref, k_ref, v_ref, sems, kv_sems = refs
    len_copy = pltpu.make_async_copy(len_hbm, len_ref, sems.at[0])
    q_copy = pltpu.make_async_copy(q_hbm, q_ref, sems.at[1])
    len_copy.start()
    q_copy.start()
    len_copy.wait()
    sort_rows(len_ref, order)

    def bring(slots):
        made = cache_copies(0, 0, slots, kv, order, (k_hbm, v_hbm), (k_ref, v_ref), kv_sems)
        for copies in made:
            for copy in copies:
                copy.start()
        for copies in made:
            for copy in copies:
                copy.wait()

    by_length(len_ref[order[0]], sizes, bring)
    q_copy.wait()


def begin(lengths, queries, keys, values, sizes, kv):
    rows = lengths.shape[0]
    buffer = pltpu.VMEM((rows // 2,) + keys.shape[1:], keys.dtype)
    return pl.pallas_call(
        functools.partial(begin_blocks, sizes, kv),
        out_shape=(
            pltpu.SMEM((rows,), jnp.int32),
            pltpu.SMEM((rows,), jnp.int32),
            pltpu.VMEM(queries.shape, queries.dtype),
            buffer,
            buffer,
        ),
        in_specs=[HBM] * 4,
        out_specs=(SMEM, SMEM, VMEM, VMEM, VMEM),
        scratch_shapes=[pltpu.SemaphoreType.DMA((2,)), pltpu.SemaphoreType.DMA((2, 2))],
        compiler_params=pltpu.CompilerParams(vmem_limit_bytes=8 * MIB),
        cost_estimate=pl.CostEstimate(
            flops=0, bytes_accessed=8 * keys[0].size, transcendentals=0
        ),
        name="begin",
    )(pinned(lengths), pinned(queries), pinned(keys), pinned(values))


def pack_pair(own_hbm, other, own_up, other_up, *refs):
    pair, up_pair, sems = refs[-3:]
    core = lax.rem(lax.axis_index("fsdp"), 2)
    copies = [
        pltpu.make_async_copy(own_hbm, pair.at[core], sems.at[0]),
        pltpu.make_async_copy(other, pair.at[1 - core], sems.at[1]),
    ]
    for copy in copies:
        copy.start()
    for ref, place in ((own_up, core), (other_up, 1 - core)):
        up_pair[place] = jnp.concatenate([ref[k] for k in range(ref.shape[0])], axis=1)
    for copy in copies:
        copy.wait()


def pack(own, other, own_up, other_up, after):
    count, rank, columns = own_up.shape
    return pl.pallas_call(
        pack_pair,
        out_shape=(
            pltpu.VMEM((2,) + own.shape, own.dtype),
            pltpu.VMEM((2, rank, count * columns), own.dtype),
        ),
        in_specs=[HBM, ANY, VMEM, VMEM] + [ANY] * len(after),
        out_specs=(VMEM, VMEM),
        scratch_shapes=[pltpu.SemaphoreType.DMA((2,))],
        compiler_params=pltpu.CompilerParams(vmem_limit_bytes=4 * MIB),
        name="pack_pair",
    )(pinned(own), other, own_up, other_up, *after)


def attend_cache(part, pairs, sizes, scale, n_kept, *refs):
    lengths, order, q_ref, k_hbm, v_hbm, w_hbm = refs[:6]
    sems, w_sem = refs[-2:]
    k_buf, v_buf, w_ref, o_ref, lse_ref = refs[-7 - n_kept : -2 - n_kept]
    steps, _, heads, size = q_ref.shape
    kv = k_hbm.shape[1] // sizes[-1]
    lanes = steps * heads
    brought = 1 if part == 0 else 0

    def copies(pair, slots):
        first = 2 * (part * pairs + pair)
        return cache_copies(
            first, 2 * pair, slots, kv, order, (k_hbm, v_hbm), (k_buf, v_buf), sems.at[pair]
        )

    def start(pair, slots):
        for made in copies(pair, slots):
            for copy in made:
                copy.start()

    for pair in range(brought, pairs):
        length = lengths[order[2 * (part * pairs + pair)]]
        by_length(length, sizes, functools.partial(start, pair))
    w_copy = pltpu.make_async_copy(w_hbm.at[part], w_ref, w_sem)
    w_copy.start()

    row_head = over(within(lax.broadcasted_iota(jnp.int32, (lanes, size), 0), heads), heads // kv)
    slot_head = within(lax.broadcasted_iota(jnp.int32, (lanes, size), 1), kv)
    head_bias = jnp.where(row_head == slot_head, 0.0, -jnp.inf)

    @pl.loop(0, pairs)
    def _(pair):
        first = 2 * (part * pairs + pair)

        def compute(slots):
            waits = copies(pair, slots)

            def wait(which):
                @pl.when(pair >= brought)
                def _():
                    for made in waits:
                        made[which].wait()

            n = slots * kv
            bias = jnp.concatenate([head_bias[:, : min(n, size)]] * max(n // size, 1), axis=1)
            column = lax.broadcasted_iota(jnp.int32, (1, n), 1)
            wait(0)
            wait(1)
            scores = []
            for i in range(2):
                row = order[first + i]
                q = q_ref[:, row].reshape(lanes, size)
                s = lax.dot_general(
                    q,
                    k_buf[2 * pair + i, :n],
                    (((1,), (1,)), ((), ())),
                    preferred_element_type=jnp.float32,
                )
                closed = jnp.where(column < lengths[row] * kv, 0.0, -jnp.inf)
                scores.append(s + (bias + closed))
            highest = [jnp.max(s, axis=1, keepdims=True) * scale for s in scores]
            weights = [jnp.exp2(s * scale - h) for s, h in zip(scores, highest)]
            totals = [jnp.sum(p, axis=1, keepdims=True) for p in weights]
            for i in range(2):
                spot = 2 * pair + i
                o = jnp.dot(
                    weights[i].astype(jnp.bfloat16),
                    v_buf[spot, :n],
                    preferred_element_type=jnp.float32,
                )
                o_ref[spot] = o / totals[i]
                lse = highest[i] + jnp.log(totals[i]) * LOG2E
                lse_ref[spot] = jnp.broadcast_to(lse, (lanes, size))

        by_length(lengths[order[first]], sizes, compute)

    w_copy.wait()


def cache_attention(part, lengths, order, queries, keys, values, weights, buffers, kept, sizes, after):
    steps, rows, heads, size = queries.shape
    pairs = rows // 4
    slots = sizes[-1]
    kv = keys.shape[1] // slots
    scale = LOG2E / math.sqrt(size)
    piece = pltpu.VMEM((2 * pairs, steps * heads, size), jnp.float32)
    operands = [pinned(lengths, pltpu.SMEM), pinned(order, pltpu.SMEM), pinned(queries, pltpu.VMEM)]
    operands += [pinned(keys), pinned(values), pinned(weights)]
    specs = [SMEM, SMEM, VMEM, HBM, HBM, HBM]
    at = len(operands)
    aliases = {at: 0, at + 1: 1} | {at + 2 + i: 5 + i for i in range(len(kept))}
    operands += [pinned(b, pltpu.VMEM) for b in buffers + kept] + after
    specs += [VMEM] * (len(buffers) + len(kept)) + [ANY] * len(after)

    def like(x):
        return pltpu.VMEM(x.shape, x.dtype)

    return pl.pallas_call(
        functools.partial(attend_cache, part, pairs, sizes, scale, len(kept)),
        out_shape=(
            *(like(b) for b in buffers),
            pltpu.VMEM(weights.shape[1:], weights.dtype),
            piece,
            piece,
            *(like(x) for x in kept),
        ),
        in_specs=specs,
        out_specs=(VMEM,) * (5 + len(kept)),
        input_output_aliases=aliases,
        scratch_shapes=[
            pltpu.SemaphoreType.DMA((pairs, 2, 2)),
            pltpu.SemaphoreType.DMA,
        ],
        compiler_params=pltpu.CompilerParams(vmem_limit_bytes=16 * MIB),
        cost_estimate=pl.CostEstimate(
            flops=8 * steps * heads * pairs * slots * kv * size,
            bytes_accessed=8 * pairs * slots * kv * size + 2 * weights[0].size,
            transcendentals=2 * steps * heads * pairs * slots * kv,
        ),
        name="cache_attention",
    )(*operands)


def merge_blocks(lay, plan, counts, first, last, scale, *refs):
    refs = list(refs)

    def take(n):
        out = refs[:n]
        del refs[:n]
        return out

    take(2)
    downs = take(len(plan))
    if first:
        hidden, ups = take(counts[0]), take(counts[1])
    else:
        u_in, h_in, _, fresh_in, low_in = take(5)
    if last:
        order, q_ref = take(2)
        caches = [take(2) for _ in range(2)]
    take(len(refs) - (4 if last else 5) - (3 if first else 0) - 2 - (2 if last else 0))
    m_hbm, *weights = take(3)
    (out_ref,) = take(1) if last else (None,)
    if first:
        u_buf, h_buf = take(2)
    else:
        u_buf, h_buf = u_in, h_in
    if last:
        fresh, low = refs[-2:]
        del refs[-2:]
    else:
        fresh, low = take(2)
    if first:
        u_parts = refs.pop()
    m_buf, sems = refs

    pairs, depth, width = m_buf.shape[1:]
    cut = min(width, 256)
    fsdp, grp, tp = (lax.axis_index(a) for a in AXES)
    z, core = fsdp // 2, lax.rem(fsdp, 2)
    place = grp * lay.depth + jnp.where(lax.rem(grp, 2) == 0, z, lay.depth - 1 - z)
    per_lane = lay.fsdp * lay.grp // lay.tp

    if first:
        for i, h in enumerate(hidden):
            h_buf[lax.rem(tp + i, lay.tp)] = h[...]
        for i, up in enumerate(ups):
            flip, turn = divmod(i, len(ups) // 2)
            spot = 2 * turn + (1 - core if flip else core)
            shift, turn = spot // lay.grp, lax.rem(spot, lay.grp)
            zz = lax.rem(lax.rem(z, lay.block) + shift, lay.block)
            for c in range(2):
                u_parts[(zz * 2 + c) * lay.grp + lax.rem(grp + turn, lay.grp)] = up[c]
        columns = u_parts.shape[2] // pairs
        for k in range(pairs):
            u_buf[k] = ADAPTER_SCALING * jnp.concatenate(
                [u_parts[i, :, k * columns : (k + 1) * columns] for i in range(u_parts.shape[0])],
                axis=1,
            )
        fresh[...] = jnp.zeros_like(fresh)
        low[...] = jnp.zeros_like(low)
    else:
        fresh[...] = fresh_in[...]
        low[...] = low_in[...]

    chunk = min(depth, 256)
    j = 0
    for (step, flip, whole), down in zip(plan, downs):
        towards = 2 * core - 1
        spot = lax.rem(place + lay.ring + step * (-towards if flip else towards), lay.ring)
        g = spot // lay.depth
        along = lax.rem(spot, lay.depth)
        zz = jnp.where(lax.rem(g, 2) == 0, along, lay.depth - 1 - along)
        def block(c, j=j, down=down, flip=flip, whole=whole, zz=zz):
            cc = c if whole else (1 - core if flip else core)
            index = (zz * 2 + cc) * lay.grp + g
            start = pl.multiple_of(index * depth, depth)
            column = pl.multiple_of(lax.rem(index, per_lane) * depth, depth)
            source = index // per_lane
            for k in range(pairs):
                for begin in range(0, depth, chunk):
                    rows = slice(begin, begin + chunk)
                    d = down[c, k, :, rows]
                    h = h_buf[source, :, pl.ds(column + begin, chunk)]
                    for side in range(width // cut):
                        cols = slice(side * cut, (side + 1) * cut)
                        w = weights[k][pl.ds(start + begin, chunk), cols]
                        added = lax.dot_general(
                            d,
                            u_buf[k, :, cols],
                            (((0,), (0,)), ((), ())),
                            preferred_element_type=jnp.float32,
                        )
                        m_buf[j + c, k, rows, cols] = (w.astype(jnp.float32) + added).astype(
                            jnp.bfloat16
                        )
                        fresh[k, :, cols] += jnp.dot(h, w, preferred_element_type=jnp.float32)
                    low[k] += lax.dot_general(
                        h, d, (((1,), (1,)), ((), ())), preferred_element_type=jnp.float32
                    )
                pltpu.make_async_copy(
                    m_buf.at[j + c, k], m_hbm.at[k, pl.ds(start, depth), :], sems.at[j + c, k]
                ).start()

        if down.shape[0] == 1:
            block(0)
        else:
            pl.loop(0, down.shape[0])(block)
        j += down.shape[0]

    if last:
        new = []
        for k in range(pairs):
            high = low[k].astype(jnp.bfloat16)
            rest = (low[k] - high.astype(jnp.float32)).astype(jnp.bfloat16)
            new.append(
                (
                    fresh[k]
                    + jnp.dot(high, u_buf[k], preferred_element_type=jnp.float32)
                    + jnp.dot(rest, u_buf[k], preferred_element_type=jnp.float32)
                ).astype(jnp.bfloat16)
            )
        add_new_tokens(q_ref, order, caches, new, out_ref, scale)
    for i in range(j):
        for k in range(pairs):
            pltpu.make_async_copy(
                m_buf.at[i, k], m_hbm.at[k, pl.ds(0, depth), :], sems.at[i, k]
            ).wait()


def add_new_tokens(q_ref, order, caches, new, out_ref, scale):
    steps, rows, heads, size = q_ref.shape
    kv = new[0].shape[1] // size
    new = [
        jnp.concatenate([x[:, g * size : (g + 1) * size] for g in range(kv)], axis=0) for x in new
    ]
    n = kv * steps * rows
    lanes = steps * heads
    left = lax.broadcasted_iota(jnp.int32, (lanes, n), 0)
    right = lax.broadcasted_iota(jnp.int32, (lanes, n), 1)
    same_head = over(within(left, heads), heads // kv) == over(right, steps * rows)
    earlier = within(over(right, rows), steps) <= over(left, heads)
    right_row = jnp.where(same_head & earlier, within(right, rows), -1)
    spots = [(o, lse, i) for o, lse in caches for i in range(o.shape[0])]
    for spot, (o_ref, lse_ref, i) in enumerate(spots):
        row = order[spot]
        q = q_ref[:, row].reshape(lanes, size)
        s = lax.dot_general(
            q, new[0], (((1,), (1,)), ((), ())), preferred_element_type=jnp.float32
        )
        s = jnp.where(right_row == row, s * scale, -jnp.inf)
        lse = lse_ref[i]
        highest = jnp.maximum(jnp.max(s, axis=1, keepdims=True), lse)
        p = jnp.exp2(s - highest[:, :n])
        old = jnp.exp2(lse - highest)
        divisor = jnp.sum(p, axis=1, keepdims=True) + old
        o = old * o_ref[i] + jnp.dot(
            p.astype(jnp.bfloat16), new[1], preferred_element_type=jnp.float32
        )
        out_ref[:, row] = (o / divisor).reshape(steps, heads, size).astype(out_ref.dtype)


def merge(lay, shape, entries, weights, inputs, state, final, after):
    pairs, total, width = shape
    rank, depth = entries[0][3].shape[2:]
    first, last = state is None, final is not None
    n = sum(e[3].shape[0] for e in entries)
    operands = [pinned(w, pltpu.VMEM) for w in weights] + [e[3] for e in entries]
    specs = [VMEM] * len(operands)
    counts = (0, 0)
    aliases = {0: 1, 1: 2}
    if first:
        hidden, ups = inputs
        counts = (len(hidden), len(ups))
        operands += hidden + ups
        specs += [VMEM] * (len(hidden) + len(ups))
        tokens, features = hidden[0].shape
    else:
        m_prev, u, h, fresh, low = state
        aliases[len(operands) + 2] = 0
        operands += [u, h, pinned(m_prev), fresh, low]
        specs += [VMEM, VMEM, HBM, VMEM, VMEM]
        tokens = h.shape[1]
    out_shape = [pltpu.HBM(shape, jnp.bfloat16)]
    out_shape += [pltpu.VMEM(w.shape, w.dtype) for w in weights]
    sums = [(pairs, tokens, width), (pairs, tokens, rank)]
    scratch = [
        pltpu.VMEM((n, pairs, depth, width), jnp.bfloat16),
        pltpu.SemaphoreType.DMA((n, 2)),
    ]
    scale = 0.0
    if first:
        out_shape += [
            pltpu.VMEM(s, jnp.bfloat16)
            for s in ((pairs, rank, width), (lay.tp, tokens, features))
        ]
        parts = len(ups) * 2
        scratch.append(pltpu.VMEM((parts,) + ups[0].shape[1:], jnp.bfloat16))
    if last:
        order, queries, caches = final
        operands += [pinned(order, pltpu.SMEM), pinned(queries, pltpu.VMEM)] + caches
        specs += [SMEM] + [VMEM] * (1 + len(caches))
        out_shape.append(jax.ShapeDtypeStruct(queries.shape, jnp.bfloat16))
        scale = LOG2E / math.sqrt(queries.shape[3])
        scratch += [pltpu.VMEM(s, jnp.float32) for s in sums]
    else:
        out_shape += [pltpu.VMEM(s, jnp.float32) for s in sums]
    operands += after
    specs += [ANY] * len(after)
    out = pl.pallas_call(
        functools.partial(
            merge_blocks, lay, [e[:3] for e in entries], counts, first, last, scale
        ),
        out_shape=out_shape,
        in_specs=specs,
        out_specs=[HBM] + [VMEM] * (len(out_shape) - 1),
        input_output_aliases=aliases,
        scratch_shapes=scratch,
        compiler_params=pltpu.CompilerParams(vmem_limit_bytes=14 * MIB),
        cost_estimate=pl.CostEstimate(
            flops=2 * n * pairs * depth * width * (rank + tokens),
            bytes_accessed=2 * n * pairs * depth * width,
            transcendentals=0,
        ),
        name="merge_blocks",
    )(*operands)
    out, weights = [out[0], *out[3:]], out[1:3]
    if not last and not first:
        out = [out[0], u, h, *out[1:]]
    return out, weights


def shards(
    lay,
    hidden_states,
    queries,
    cache_keys,
    cache_values,
    cache_lengths,
    projection_weight_matrices,
    factor_down,
    factor_up,
):
    send = functools.partial(lax.ppermute, axis_name=AXES)
    steps, rows, features = hidden_states.shape
    slots, kv, size = cache_keys.shape[1:]
    shape = projection_weight_matrices.shape
    sizes = tuple(slots * i // 24 for i in (1, 4, 8, 16, 24))
    own = jnp.swapaxes(factor_down, 1, 2)
    tokens = hidden_states.reshape(steps * rows, features)
    keys = cache_keys.reshape(rows, slots * kv, size)
    values = cache_values.reshape(rows, slots * kv, size)
    swap, ring = lay.core_swap(), lay.ring_step()
    caches = []

    other, other_up = send(own, perm=swap), send(factor_up, perm=swap)
    lengths, order, q, *buffers = begin(cache_lengths, queries, keys, values, sizes, kv)
    pair, up_pair = pack(own, other, factor_up, other_up, [q])

    def attention(part, buffers, kept, after):
        out = cache_attention(
            part,
            lengths,
            order,
            q,
            keys,
            values,
            projection_weight_matrices,
            list(buffers),
            list(kept),
            sizes,
            after,
        )
        caches.extend(out[3:5])
        return out[:2], [*out[5:], out[2]]

    ups = [
        send(up_pair, perm=lay.column_step(turn)) for turn in range(lay.block * lay.grp // 2)
    ]
    came = send(pair, perm=ring)
    buffers, weights = attention(0, buffers, [], [pair])
    (came, ups, tokens), token = after_all((came, ups, tokens), caches[0])

    sent = send(came, perm=ring)
    swapped = send(came, perm=swap)
    other_ups = [send(u, perm=swap) for u in ups]
    hidden = [send(tokens, perm=lay.feature_step(i)) for i in range(1, lay.tp)]
    buffers, weights = attention(1, buffers, weights, [token])
    (sent, swapped, other_ups, hidden), token = after_all(
        (sent, swapped, other_ups, hidden), caches[2]
    )
    entries = [(0, False, True, pair), (1, False, True, came), (1, True, True, swapped)]
    came = sent

    inputs = ([tokens] + hidden, ups + other_ups)
    state = None
    last_step = lay.ring // 2
    for step in range(2, last_step):
        if step + 1 < last_step:
            sent = send(came, perm=ring)
        else:
            core = lax.rem(lax.axis_index("fsdp"), 2)
            sent = send(lax.dynamic_slice_in_dim(came, core, 1, 0), perm=ring)
        swapped = send(came, perm=swap)
        state, weights = merge(lay, shape, entries, weights, inputs, state, None, [token])
        (sent, swapped), token = after_all((sent, swapped), state[3])
        entries = [(step, False, True, came), (step, True, True, swapped)]
        came = sent
    swapped = send(came, perm=swap)
    entries.append((last_step, False, False, came))
    state, weights = merge(lay, shape, entries, weights, inputs, state, None, [token])
    entries = [(last_step, True, False, swapped)]
    out, _ = merge(lay, shape, entries, weights, inputs, state, (order, q, caches), [])
    return tuple(out)


def solution(mesh):
    return jax.shard_map(
        functools.partial(shards, Layout(mesh)),
        mesh=mesh,
        in_specs=(
            P(None, ("fsdp", "grp"), "tp"),
            P(None, ("fsdp", "grp"), "tp", None),
            P(("fsdp", "grp"), None, "tp", None),
            P(("fsdp", "grp"), None, "tp", None),
            P(("fsdp", "grp")),
            P(None, None, "tp"),
            P(None, ("fsdp", "grp"), None),
            P(None, None, ("fsdp", "grp")),
        ),
        out_specs=(P(None, None, "tp"), P(None, ("fsdp", "grp"), "tp", None)),
        check_vma=False,
    )
```

```python
import functools
import math

import jax
import jax.numpy as jnp
from jax import lax
from jax.experimental import pallas as pl
from jax.experimental.pallas import tpu as pltpu
from jax.sharding import PartitionSpec as P

AXES = ("fsdp", "grp", "tp")
ADAPTER_SCALING = 2.0
LOG2E = math.log2(math.e)
MIB = 1024 * 1024
ANY = pl.BlockSpec(memory_space=pl.ANY)
HBM = pl.BlockSpec(memory_space=pltpu.HBM)
VMEM = pl.BlockSpec(memory_space=pltpu.VMEM)
SMEM = pl.BlockSpec(memory_space=pltpu.SMEM)


class Layout:
    def __init__(self, mesh):
        self.fsdp, self.grp, self.tp = (mesh.shape[a] for a in AXES)
        self.depth = self.fsdp // 2
        self.ring = self.depth * self.grp
        self.block = self.depth // self.tp

    def flat(self, z, core, g, t):
        return ((z * 2 + core) * self.grp + g) * self.tp + t

    def devices(self):
        for z in range(self.depth):
            for core in range(2):
                for g in range(self.grp):
                    for t in range(self.tp):
                        yield z, core, g, t

    def place(self, z, g):
        return g * self.depth + (z if g % 2 == 0 else self.depth - 1 - z)

    def at(self, position):
        g, z = divmod(position, self.depth)
        return (z if g % 2 == 0 else self.depth - 1 - z), g

    def ring_step(self):
        pairs = []
        for z, core, g, t in self.devices():
            to_z, to_g = self.at((self.place(z, g) + (1 - 2 * core)) % self.ring)
            pairs.append((self.flat(z, core, g, t), self.flat(to_z, core, to_g, t)))
        return pairs

    def core_swap(self):
        return [
            (self.flat(z, c, g, t), self.flat(z, 1 - c, g, t)) for z, c, g, t in self.devices()
        ]

    def feature_step(self, step):
        return [
            (self.flat(z, c, g, (t + step) % self.tp), self.flat(z, c, g, t))
            for z, c, g, t in self.devices()
        ]

    def sources(self, t):
        count = self.block * self.grp
        places = sorted(
            self.place(z, g)
            for z in range(t * self.block, (t + 1) * self.block)
            for g in range(self.grp)
        )
        assert sorted(p % count for p in places) == list(range(count)) and count <= 4
        return sorted(places, key=lambda p: p % count)

    def column_step(self, flip):
        count = self.block * self.grp
        pairs = []
        for t in range(self.tp):
            for s, source in enumerate(self.sources(t)):
                places = list(range(s, self.ring, count))
                places.remove(source)
                others = [x for x in range(self.tp) if x != t]
                for to, lane in [(source, t)] + list(zip(places, others)):
                    for c in range(2):
                        from_z, from_g = self.at(source)
                        to_z, to_g = self.at(to)
                        pairs.append(
                            (
                                self.flat(from_z, c ^ flip, from_g, lane),
                                self.flat(to_z, c, to_g, t),
                            )
                        )
        return pairs


def over(x, n):
    return x >> (n.bit_length() - 1) if n & (n - 1) == 0 else x // n


def within(x, n):
    return x & (n - 1) if n & (n - 1) == 0 else x % n


def after_all(arrays, token):
    return lax.optimization_barrier((arrays, token))


def pinned(x, space=pltpu.HBM):
    return pltpu.with_memory_space_constraint(x, space)


def sort_rows(lengths, order):
    rows = lengths.shape[0]
    held = [lengths[r] for r in range(rows)]
    for r in range(rows):
        rank = jnp.int32(0)
        for other in range(rows):
            if other != r:
                ahead = held[other] >= held[r] if other < r else held[other] > held[r]
                rank = rank + ahead.astype(jnp.int32)
        order[rank] = r


def by_length(length, sizes, act):
    below = 0
    for slots in sizes:

        @pl.when((length > below) & (length <= slots))
        def _():
            act(slots)

        below = slots


def cache_copies(first, spot, slots, kv, order, hbms, bufs, sems):
    span = pl.ds(0, slots * kv)
    return [
        [
            pltpu.make_async_copy(
                hbm.at[order[first + i], span], buf.at[spot + i, span], sems.at[i, which]
            )
            for which, (hbm, buf) in enumerate(zip(hbms, bufs))
        ]
        for i in range(2)
    ]


def begin_blocks(sizes, kv, len_hbm, q_hbm, k_hbm, v_hbm, *refs):
    len_ref, order, q_ref, k_ref, v_ref, sems, kv_sems = refs
    len_copy = pltpu.make_async_copy(len_hbm, len_ref, sems.at[0])
    q_copy = pltpu.make_async_copy(q_hbm, q_ref, sems.at[1])
    len_copy.start()
    q_copy.start()
    len_copy.wait()
    sort_rows(len_ref, order)

    def bring(slots):
        made = cache_copies(0, 0, slots, kv, order, (k_hbm, v_hbm), (k_ref, v_ref), kv_sems)
        for copies in made:
            for copy in copies:
                copy.start()
        for copies in made:
            for copy in copies:
                copy.wait()

    by_length(len_ref[order[0]], sizes, bring)
    q_copy.wait()


def begin(lengths, queries, keys, values, sizes, kv):
    rows = lengths.shape[0]
    buffer = pltpu.VMEM((rows // 2,) + keys.shape[1:], keys.dtype)
    return pl.pallas_call(
        functools.partial(begin_blocks, sizes, kv),
        out_shape=(
            pltpu.SMEM((rows,), jnp.int32),
            pltpu.SMEM((rows,), jnp.int32),
            pltpu.VMEM(queries.shape, queries.dtype),
            buffer,
            buffer,
        ),
        in_specs=[HBM] * 4,
        out_specs=(SMEM, SMEM, VMEM, VMEM, VMEM),
        scratch_shapes=[pltpu.SemaphoreType.DMA((2,)), pltpu.SemaphoreType.DMA((2, 2))],
        compiler_params=pltpu.CompilerParams(vmem_limit_bytes=8 * MIB),
        cost_estimate=pl.CostEstimate(
            flops=0, bytes_accessed=8 * keys[0].size, transcendentals=0
        ),
        name="begin",
    )(pinned(lengths), pinned(queries), pinned(keys), pinned(values))


def pack_pair(own, other, own_up, other_up, *refs):
    pair = refs[-1]
    lanes = pair.shape[3]
    for place, (down, up) in enumerate(((own, own_up), (other, other_up))):
        count, _, depth = down.shape
        tiles = depth // lanes
        for k in range(count):
            for i in range(tiles):
                pair[place, k * tiles + i] = down[k, :, i * lanes : (i + 1) * lanes]
        columns = jnp.concatenate([up[k] for k in range(count)], axis=1)
        pair[place, count * tiles, :, : columns.shape[1]] = columns


def pack(own, other, own_up, other_up, after):
    count, rank, depth = own.shape
    tiles = count * depth // 128 + 1
    return pl.pallas_call(
        pack_pair,
        out_shape=pltpu.VMEM((2, tiles, rank, 128), own.dtype),
        in_specs=[VMEM] * 4 + [ANY] * len(after),
        out_specs=VMEM,
        compiler_params=pltpu.CompilerParams(vmem_limit_bytes=4 * MIB),
        name="pack_pair",
    )(own, other, own_up, other_up, *after)


def attend_cache(part, pairs, sizes, scale, n_kept, *refs):
    lengths, order, q_ref, k_hbm, v_hbm, w_hbm = refs[:6]
    sems, w_sem = refs[-2:]
    k_buf, v_buf, w_ref, o_ref, lse_ref = refs[-7 - n_kept : -2 - n_kept]
    steps, _, heads, size = q_ref.shape
    kv = k_hbm.shape[1] // sizes[-1]
    lanes = steps * heads
    brought = 1 if part == 0 else 0

    def copies(pair, slots):
        first = 2 * (part * pairs + pair)
        return cache_copies(
            first, 2 * pair, slots, kv, order, (k_hbm, v_hbm), (k_buf, v_buf), sems.at[pair]
        )

    def start(pair, slots):
        for made in copies(pair, slots):
            for copy in made:
                copy.start()

    for pair in range(brought, pairs):
        length = lengths[order[2 * (part * pairs + pair)]]
        by_length(length, sizes, functools.partial(start, pair))
    w_copy = pltpu.make_async_copy(w_hbm.at[part], w_ref, w_sem)
    w_copy.start()

    row_head = over(within(lax.broadcasted_iota(jnp.int32, (lanes, size), 0), heads), heads // kv)
    slot_head = within(lax.broadcasted_iota(jnp.int32, (lanes, size), 1), kv)
    head_bias = jnp.where(row_head == slot_head, 0.0, -jnp.inf)

    @pl.loop(0, pairs)
    def _(pair):
        first = 2 * (part * pairs + pair)

        def compute(slots):
            waits = copies(pair, slots)

            def wait(which):
                @pl.when(pair >= brought)
                def _():
                    for made in waits:
                        made[which].wait()

            n = slots * kv
            bias = jnp.concatenate([head_bias[:, : min(n, size)]] * max(n // size, 1), axis=1)
            column = lax.broadcasted_iota(jnp.int32, (1, n), 1)
            wait(0)
            wait(1)
            scores = []
            for i in range(2):
                row = order[first + i]
                q = q_ref[:, row].reshape(lanes, size)
                s = lax.dot_general(
                    q,
                    k_buf[2 * pair + i, :n],
                    (((1,), (1,)), ((), ())),
                    preferred_element_type=jnp.float32,
                )
                closed = jnp.where(column < lengths[row] * kv, 0.0, -jnp.inf)
                scores.append(s + (bias + closed))
            highest = [jnp.max(s, axis=1, keepdims=True) * scale for s in scores]
            weights = [jnp.exp2(s * scale - h) for s, h in zip(scores, highest)]
            totals = [jnp.sum(p, axis=1, keepdims=True) for p in weights]
            for i in range(2):
                spot = 2 * pair + i
                o = jnp.dot(
                    weights[i].astype(jnp.bfloat16),
                    v_buf[spot, :n],
                    preferred_element_type=jnp.float32,
                )
                o_ref[spot] = o / totals[i]
                lse = highest[i] + jnp.log(totals[i]) * LOG2E
                lse_ref[spot] = jnp.broadcast_to(lse, (lanes, size))

        by_length(lengths[order[first]], sizes, compute)

    w_copy.wait()


def cache_attention(part, lengths, order, queries, keys, values, weights, buffers, kept, sizes, after):
    steps, rows, heads, size = queries.shape
    pairs = rows // 4
    slots = sizes[-1]
    kv = keys.shape[1] // slots
    scale = LOG2E / math.sqrt(size)
    piece = pltpu.VMEM((2 * pairs, steps * heads, size), jnp.float32)
    operands = [pinned(lengths, pltpu.SMEM), pinned(order, pltpu.SMEM), pinned(queries, pltpu.VMEM)]
    operands += [pinned(keys), pinned(values), pinned(weights)]
    specs = [SMEM, SMEM, VMEM, HBM, HBM, HBM]
    at = len(operands)
    aliases = {at: 0, at + 1: 1} | {at + 2 + i: 5 + i for i in range(len(kept))}
    operands += [pinned(b, pltpu.VMEM) for b in buffers + kept] + after
    specs += [VMEM] * (len(buffers) + len(kept)) + [ANY] * len(after)

    def like(x):
        return pltpu.VMEM(x.shape, x.dtype)

    return pl.pallas_call(
        functools.partial(attend_cache, part, pairs, sizes, scale, len(kept)),
        out_shape=(
            *(like(b) for b in buffers),
            pltpu.VMEM(weights.shape[1:], weights.dtype),
            piece,
            piece,
            *(like(x) for x in kept),
        ),
        in_specs=specs,
        out_specs=(VMEM,) * (5 + len(kept)),
        input_output_aliases=aliases,
        scratch_shapes=[
            pltpu.SemaphoreType.DMA((pairs, 2, 2)),
            pltpu.SemaphoreType.DMA,
        ],
        compiler_params=pltpu.CompilerParams(vmem_limit_bytes=16 * MIB),
        cost_estimate=pl.CostEstimate(
            flops=8 * steps * heads * pairs * slots * kv * size,
            bytes_accessed=8 * pairs * slots * kv * size + 2 * weights[0].size,
            transcendentals=2 * steps * heads * pairs * slots * kv,
        ),
        name="cache_attention",
    )(*operands)


def merge_blocks(lay, plan, counts, first, last, scale, *refs):
    refs = list(refs)

    def take(n):
        out = refs[:n]
        del refs[:n]
        return out

    take(2)
    downs = take(len(plan))
    if first:
        hidden, ups = take(counts[0]), take(counts[1])
    else:
        u_in, h_in, _, fresh_in, low_in = take(5)
    if last:
        order, q_ref = take(2)
        caches = [take(2) for _ in range(2)]
    take(len(refs) - (4 if last else 5) - (3 if first else 0) - 2 - (2 if last else 0))
    m_hbm, *weights = take(3)
    (out_ref,) = take(1) if last else (None,)
    if first:
        u_buf, h_buf = take(2)
    else:
        u_buf, h_buf = u_in, h_in
    if last:
        fresh, low = refs[-2:]
        del refs[-2:]
    else:
        fresh, low = take(2)
    if first:
        u_parts = refs.pop()
    m_buf, sems = refs

    pairs, depth, width = m_buf.shape[1:]
    cut = min(width, 256)
    lanes = downs[0].shape[3]
    tiles = depth // lanes
    fsdp, grp, tp = (lax.axis_index(a) for a in AXES)
    z, core = fsdp // 2, lax.rem(fsdp, 2)
    place = grp * lay.depth + jnp.where(lax.rem(grp, 2) == 0, z, lay.depth - 1 - z)
    per_lane = lay.fsdp * lay.grp // lay.tp

    def position(step, flip):
        towards = 2 * core - 1
        return lax.rem(place + lay.ring + step * (-towards if flip else towards), lay.ring)

    if first:
        for i, h in enumerate(hidden):
            h_buf[lax.rem(tp + i, lay.tp)] = h[...]
        columns = width // u_parts.shape[0]
        tables = [lay.sources(t) for t in range(lay.tp)]
        for (step, flip), up in zip([e[:2] for e in plan] + [(2, False)], downs + ups):
            remainder = lax.rem(position(step, flip), len(tables[0]))
            source = jnp.int32(0)
            for t, table in enumerate(tables):
                for i, spot in enumerate(table):
                    source = jnp.where((tp == t) & (remainder == i), spot, source)
            g = source // lay.depth
            along = lax.rem(source, lay.depth)
            zz = jnp.where(lax.rem(g, 2) == 0, along, lay.depth - 1 - along) - tp * lay.block
            for c in range(2):
                cc = lax.rem(core + c + (1 if flip else 0), 2)
                u_parts[(zz * 2 + cc) * lay.grp + g] = up[c, pairs * tiles, :, : pairs * columns]
        for k in range(pairs):
            u_buf[k] = ADAPTER_SCALING * jnp.concatenate(
                [u_parts[i, :, k * columns : (k + 1) * columns] for i in range(u_parts.shape[0])],
                axis=1,
            )
        fresh[...] = jnp.zeros_like(fresh)
        low[...] = jnp.zeros_like(low)
    else:
        fresh[...] = fresh_in[...]
        low[...] = low_in[...]

    chunk = min(depth, 256)
    j = 0
    for (step, flip), down in zip(plan, downs):
        spot = position(step, flip)
        g = spot // lay.depth
        along = lax.rem(spot, lay.depth)
        zz = jnp.where(lax.rem(g, 2) == 0, along, lay.depth - 1 - along)

        def block(c, j=j, down=down, flip=flip, zz=zz, g=g):
            cc = lax.rem(core + c + (1 if flip else 0), 2)
            index = (zz * 2 + cc) * lay.grp + g
            start = pl.multiple_of(index * depth, depth)
            column = pl.multiple_of(lax.rem(index, per_lane) * depth, depth)
            source = index // per_lane
            for k in range(pairs):
                for begin in range(0, depth, chunk):
                    rows = slice(begin, begin + chunk)
                    tile = k * tiles + begin // lanes
                    d = jnp.concatenate(
                        [down[c, tile + i] for i in range(chunk // lanes)], axis=1
                    )
                    h = h_buf[source, :, pl.ds(column + begin, chunk)]
                    for side in range(width // cut):
                        cols = slice(side * cut, (side + 1) * cut)
                        w = weights[k][pl.ds(start + begin, chunk), cols]
                        added = lax.dot_general(
                            d,
                            u_buf[k, :, cols],
                            (((0,), (0,)), ((), ())),
                            preferred_element_type=jnp.float32,
                        )
                        m_buf[j + c, k, rows, cols] = (w.astype(jnp.float32) + added).astype(
                            jnp.bfloat16
                        )
                        fresh[k, :, cols] += jnp.dot(h, w, preferred_element_type=jnp.float32)
                    low[k] += lax.dot_general(
                        h, d, (((1,), (1,)), ((), ())), preferred_element_type=jnp.float32
                    )
                pltpu.make_async_copy(
                    m_buf.at[j + c, k], m_hbm.at[k, pl.ds(start, depth), :], sems.at[j + c, k]
                ).start()

        pl.loop(0, 2)(block)
        j += 2

    if last:
        new = []
        for k in range(pairs):
            high = low[k].astype(jnp.bfloat16)
            rest = (low[k] - high.astype(jnp.float32)).astype(jnp.bfloat16)
            new.append(
                (
                    fresh[k]
                    + jnp.dot(high, u_buf[k], preferred_element_type=jnp.float32)
                    + jnp.dot(rest, u_buf[k], preferred_element_type=jnp.float32)
                ).astype(jnp.bfloat16)
            )
        add_new_tokens(q_ref, order, caches, new, out_ref, scale)
    for i in range(j):
        for k in range(pairs):
            pltpu.make_async_copy(
                m_buf.at[i, k], m_hbm.at[k, pl.ds(0, depth), :], sems.at[i, k]
            ).wait()


def add_new_tokens(q_ref, order, caches, new, out_ref, scale):
    steps, rows, heads, size = q_ref.shape
    kv = new[0].shape[1] // size
    new = [
        jnp.concatenate([x[:, g * size : (g + 1) * size] for g in range(kv)], axis=0) for x in new
    ]
    n = kv * steps * rows
    lanes = steps * heads
    left = lax.broadcasted_iota(jnp.int32, (lanes, n), 0)
    right = lax.broadcasted_iota(jnp.int32, (lanes, n), 1)
    same_head = over(within(left, heads), heads // kv) == over(right, steps * rows)
    earlier = within(over(right, rows), steps) <= over(left, heads)
    right_row = jnp.where(same_head & earlier, within(right, rows), -1)
    spots = [(o, lse, i) for o, lse in caches for i in range(o.shape[0])]
    for spot, (o_ref, lse_ref, i) in enumerate(spots):
        row = order[spot]
        q = q_ref[:, row].reshape(lanes, size)
        s = lax.dot_general(
            q, new[0], (((1,), (1,)), ((), ())), preferred_element_type=jnp.float32
        )
        s = jnp.where(right_row == row, s * scale, -jnp.inf)
        lse = lse_ref[i]
        highest = jnp.maximum(jnp.max(s, axis=1, keepdims=True), lse)
        p = jnp.exp2(s - highest[:, :n])
        old = jnp.exp2(lse - highest)
        divisor = jnp.sum(p, axis=1, keepdims=True) + old
        o = old * o_ref[i] + jnp.dot(
            p.astype(jnp.bfloat16), new[1], preferred_element_type=jnp.float32
        )
        out_ref[:, row] = (o / divisor).reshape(steps, heads, size).astype(out_ref.dtype)


def merge(lay, shape, entries, weights, inputs, state, final, after):
    pairs, total, width = shape
    rank = entries[0][2].shape[2]
    depth = total // (lay.fsdp * lay.grp)
    first, last = state is None, final is not None
    n = 2 * len(entries)
    operands = [pinned(w, pltpu.VMEM) for w in weights] + [e[2] for e in entries]
    specs = [VMEM] * len(operands)
    counts = (0, 0)
    aliases = {0: 1, 1: 2}
    if first:
        hidden, ups = inputs
        counts = (len(hidden), len(ups))
        operands += hidden + ups
        specs += [VMEM] * (len(hidden) + len(ups))
        tokens, features = hidden[0].shape
    else:
        m_prev, u, h, fresh, low = state
        aliases[len(operands) + 2] = 0
        operands += [u, h, pinned(m_prev), fresh, low]
        specs += [VMEM, VMEM, HBM, VMEM, VMEM]
        tokens = h.shape[1]
    out_shape = [pltpu.HBM(shape, jnp.bfloat16)]
    out_shape += [pltpu.VMEM(w.shape, w.dtype) for w in weights]
    sums = [(pairs, tokens, width), (pairs, tokens, rank)]
    scratch = [
        pltpu.VMEM((n, pairs, depth, width), jnp.bfloat16),
        pltpu.SemaphoreType.DMA((n, 2)),
    ]
    scale = 0.0
    if first:
        out_shape += [
            pltpu.VMEM(s, jnp.bfloat16)
            for s in ((pairs, rank, width), (lay.tp, tokens, features))
        ]
        parts = 2 * lay.block * lay.grp
        scratch.append(pltpu.VMEM((parts, rank, pairs * width // parts), jnp.bfloat16))
    if last:
        order, queries, caches = final
        operands += [pinned(order, pltpu.SMEM), pinned(queries, pltpu.VMEM)] + caches
        specs += [SMEM] + [VMEM] * (1 + len(caches))
        out_shape.append(jax.ShapeDtypeStruct(queries.shape, jnp.bfloat16))
        scale = LOG2E / math.sqrt(queries.shape[3])
        scratch += [pltpu.VMEM(s, jnp.float32) for s in sums]
    else:
        out_shape += [pltpu.VMEM(s, jnp.float32) for s in sums]
    operands += after
    specs += [ANY] * len(after)
    out = pl.pallas_call(
        functools.partial(
            merge_blocks, lay, [e[:2] for e in entries], counts, first, last, scale
        ),
        out_shape=out_shape,
        in_specs=specs,
        out_specs=[HBM] + [VMEM] * (len(out_shape) - 1),
        input_output_aliases=aliases,
        scratch_shapes=scratch,
        compiler_params=pltpu.CompilerParams(vmem_limit_bytes=14 * MIB),
        cost_estimate=pl.CostEstimate(
            flops=2 * n * pairs * depth * width * (rank + tokens),
            bytes_accessed=2 * n * pairs * depth * width,
            transcendentals=0,
        ),
        name="merge_blocks",
    )(*operands)
    out, weights = [out[0], *out[3:]], out[1:3]
    if not last and not first:
        out = [out[0], u, h, *out[1:]]
    return out, weights


def shards(
    lay,
    hidden_states,
    queries,
    cache_keys,
    cache_values,
    cache_lengths,
    projection_weight_matrices,
    factor_down,
    factor_up,
):
    send = functools.partial(lax.ppermute, axis_name=AXES)
    steps, rows, features = hidden_states.shape
    slots, kv, size = cache_keys.shape[1:]
    shape = projection_weight_matrices.shape
    sizes = tuple(slots * i // 24 for i in (1, 4, 8, 16, 24))
    own = jnp.swapaxes(factor_down, 1, 2)
    tokens = hidden_states.reshape(steps * rows, features)
    keys = cache_keys.reshape(rows, slots * kv, size)
    values = cache_values.reshape(rows, slots * kv, size)
    swap, ring = lay.core_swap(), lay.ring_step()
    caches = []

    other = send(own, perm=swap)
    own_up, other_up = (send(factor_up, perm=lay.column_step(flip)) for flip in range(2))
    lengths, order, q, *buffers = begin(cache_lengths, queries, keys, values, sizes, kv)
    pair = pack(own, other, own_up, other_up, [q])

    def attention(part, buffers, kept, after):
        out = cache_attention(
            part,
            lengths,
            order,
            q,
            keys,
            values,
            projection_weight_matrices,
            list(buffers),
            list(kept),
            sizes,
            after,
        )
        caches.extend(out[3:5])
        return out[:2], [*out[5:], out[2]]

    came = send(pair, perm=ring)
    buffers, weights = attention(0, buffers, [], [pair])
    (came, tokens), token = after_all((came, tokens), caches[0])

    sent = send(came, perm=ring)
    swapped = send(came, perm=swap)
    hidden = [send(tokens, perm=lay.feature_step(i)) for i in range(1, lay.tp)]
    buffers, weights = attention(1, buffers, weights, [token])
    (sent, swapped, hidden), token = after_all((sent, swapped, hidden), caches[2])
    entries = [(0, False, pair), (1, False, came), (1, True, swapped)]
    came = sent

    inputs = ([tokens] + hidden, [came])
    state = None
    last_step = lay.ring // 2
    for step in range(2, last_step):
        sent = send(came, perm=ring)
        swapped = send(came, perm=swap)
        state, weights = merge(lay, shape, entries, weights, inputs, state, None, [token])
        (sent, swapped), token = after_all((sent, swapped), state[3])
        entries = [(step, False, came), (step, True, swapped)]
        came = sent
    entries.append((last_step, False, came))
    out, _ = merge(lay, shape, entries, weights, inputs, state, (order, q, caches), [])
    return tuple(out)


def solution(mesh):
    return jax.shard_map(
        functools.partial(shards, Layout(mesh)),
        mesh=mesh,
        in_specs=(
            P(None, ("fsdp", "grp"), "tp"),
            P(None, ("fsdp", "grp"), "tp", None),
            P(("fsdp", "grp"), None, "tp", None),
            P(("fsdp", "grp"), None, "tp", None),
            P(("fsdp", "grp")),
            P(None, None, "tp"),
            P(None, ("fsdp", "grp"), None),
            P(None, None, ("fsdp", "grp")),
        ),
        out_specs=(P(None, None, "tp"), P(None, ("fsdp", "grp"), "tp", None)),
        check_vma=False,
    )
```

```python
import functools
import math

import jax
import jax.numpy as jnp
from jax import lax
from jax.experimental import pallas as pl
from jax.experimental.pallas import tpu as pltpu
from jax.sharding import PartitionSpec as P

AXES = ("fsdp", "grp", "tp")
ADAPTER_SCALING = 2.0
LOG2E = math.log2(math.e)
MIB = 1024 * 1024
ANY = pl.BlockSpec(memory_space=pl.ANY)
HBM = pl.BlockSpec(memory_space=pltpu.HBM)
VMEM = pl.BlockSpec(memory_space=pltpu.VMEM)
SMEM = pl.BlockSpec(memory_space=pltpu.SMEM)


class Layout:
    def __init__(self, mesh):
        self.fsdp, self.grp, self.tp = (mesh.shape[a] for a in AXES)
        self.depth = self.fsdp // 2
        self.ring = self.depth * self.grp
        self.block = self.depth // self.tp

    def flat(self, z, core, g, t):
        return ((z * 2 + core) * self.grp + g) * self.tp + t

    def devices(self):
        for z in range(self.depth):
            for core in range(2):
                for g in range(self.grp):
                    for t in range(self.tp):
                        yield z, core, g, t

    def place(self, z, g):
        return g * self.depth + (z if g % 2 == 0 else self.depth - 1 - z)

    def at(self, position):
        g, z = divmod(position, self.depth)
        return (z if g % 2 == 0 else self.depth - 1 - z), g

    def ring_step(self):
        pairs = []
        for z, core, g, t in self.devices():
            to_z, to_g = self.at((self.place(z, g) + (1 - 2 * core)) % self.ring)
            pairs.append((self.flat(z, core, g, t), self.flat(to_z, core, to_g, t)))
        return pairs

    def core_swap(self):
        return [
            (self.flat(z, c, g, t), self.flat(z, 1 - c, g, t)) for z, c, g, t in self.devices()
        ]

    def feature_step(self, step):
        return [
            (self.flat(z, c, g, (t + step) % self.tp), self.flat(z, c, g, t))
            for z, c, g, t in self.devices()
        ]


def over(x, n):
    return x >> (n.bit_length() - 1) if n & (n - 1) == 0 else x // n


def within(x, n):
    return x & (n - 1) if n & (n - 1) == 0 else x % n


def after_all(arrays, token):
    return lax.optimization_barrier((arrays, token))


def pinned(x, space=pltpu.HBM):
    return pltpu.with_memory_space_constraint(x, space)


def sort_rows(lengths, order):
    rows = lengths.shape[0]
    held = [lengths[r] for r in range(rows)]
    for r in range(rows):
        rank = jnp.int32(0)
        for other in range(rows):
            if other != r:
                ahead = held[other] >= held[r] if other < r else held[other] > held[r]
                rank = rank + ahead.astype(jnp.int32)
        order[rank] = r


def by_length(length, sizes, act):
    below = 0
    for slots in sizes:

        @pl.when((length > below) & (length <= slots))
        def _():
            act(slots)

        below = slots


def cache_copies(first, spot, slots, kv, order, hbms, bufs, sems):
    span = pl.ds(0, slots * kv)
    return [
        [
            pltpu.make_async_copy(
                hbm.at[order[first + i], span], buf.at[spot + i, span], sems.at[i, which]
            )
            for which, (hbm, buf) in enumerate(zip(hbms, bufs))
        ]
        for i in range(2)
    ]


def pack_own(down, up, pair, up_buf, sems, up_sem):
    lanes = pair.shape[3]
    count, _, depth = down.shape
    tiles = depth // lanes
    copies = [
        pltpu.make_async_copy(
            down.at[k, :, pl.ds(i * lanes, lanes)], pair.at[0, k * tiles + i], sems.at[k, i]
        )
        for k in range(count)
        for i in range(tiles)
    ]
    up_copy = pltpu.make_async_copy(up, up_buf, up_sem)
    up_copy.start()
    for copy in copies:
        copy.start()
    up_copy.wait()
    columns = jnp.concatenate([up_buf[k] for k in range(count)], axis=1)
    pair[0, count * tiles, :, : columns.shape[1]] = columns
    for copy in copies:
        copy.wait()


def pack_other(down, up, _, pair):
    lanes = pair.shape[3]
    count, _, depth = down.shape
    tiles = depth // lanes
    for k in range(count):
        for i in range(tiles):
            pair[1, k * tiles + i] = down[k, :, i * lanes : (i + 1) * lanes]
    columns = jnp.concatenate([up[k] for k in range(count)], axis=1)
    pair[1, count * tiles, :, : columns.shape[1]] = columns


def pack(own, other, own_up, other_up):
    count, rank, depth = own.shape
    tiles = depth // 128
    pair = pltpu.VMEM((2, count * tiles + 1, rank, 128), own.dtype)
    params = pltpu.CompilerParams(vmem_limit_bytes=2 * MIB)
    half = pl.pallas_call(
        pack_own,
        out_shape=pair,
        in_specs=[HBM, HBM],
        out_specs=VMEM,
        scratch_shapes=[
            pltpu.VMEM(own_up.shape, own.dtype),
            pltpu.SemaphoreType.DMA((count, tiles)),
            pltpu.SemaphoreType.DMA,
        ],
        compiler_params=params,
        name="pack_own",
    )(pinned(own), pinned(own_up))
    return pl.pallas_call(
        pack_other,
        out_shape=pair,
        in_specs=[VMEM, VMEM, VMEM],
        out_specs=VMEM,
        input_output_aliases={2: 0},
        compiler_params=params,
        name="pack_other",
    )(other, other_up, pinned(half, pltpu.VMEM))


def attend_cache(pairs, done, ready, sizes, scale, has_w, n_kept, *refs):
    refs = list(refs)
    sems, w_sem = refs[-2:]
    first = done == 0
    if first:
        len_hbm, q_hbm, k_hbm, v_hbm, w_hbm = refs[:5]
        lengths, order, q_ref, k_buf, v_buf, *outs = refs[-2 - 7 - has_w : -2]
        len_copy = pltpu.make_async_copy(len_hbm, lengths, sems.at[0, 0, 0])
        q_copy = pltpu.make_async_copy(q_hbm, q_ref, w_sem)
        len_copy.start()
        q_copy.start()
        len_copy.wait()
        sort_rows(lengths, order)
    else:
        lengths, order, q_ref, k_hbm, v_hbm, w_hbm = refs[:6]
        k_buf, v_buf, *outs = refs[-2 - 4 - has_w - n_kept : -2 - n_kept]
    o_ref, lse_ref = outs[:2]
    steps, _, heads, size = q_ref.shape
    kv = k_hbm.shape[1] // sizes[-1]
    lanes = steps * heads

    def copies(pair, slots):
        span = pl.ds(0, slots * kv)
        return [
            [
                pltpu.make_async_copy(
                    hbm.at[order[2 * pair + i], span],
                    buf.at[2 * pair + i, span],
                    sems.at[pair, i, which],
                )
                for which, (hbm, buf) in enumerate(((k_hbm, k_buf), (v_hbm, v_buf)))
            ]
            for i in range(2)
        ]

    def start(pair, slots):
        for made in copies(pair, slots):
            for copy in made:
                copy.start()

    def finish(pair, slots):
        for made in copies(pair, slots):
            for copy in made:
                copy.wait()

    for pair in range(*ready):
        by_length(lengths[order[2 * pair]], sizes, functools.partial(start, pair))
    if has_w:
        w_copy = pltpu.make_async_copy(w_hbm.at[0], outs[2], w_sem)
        w_copy.start()
    if first:
        q_copy.wait()

    row_head = over(within(lax.broadcasted_iota(jnp.int32, (lanes, size), 0), heads), heads // kv)
    slot_head = within(lax.broadcasted_iota(jnp.int32, (lanes, size), 1), kv)
    head_bias = jnp.where(row_head == slot_head, 0.0, -jnp.inf)

    def attend(pair):
        def compute(slots):
            @pl.when(pair >= ready[0])
            def _():
                finish(pair, slots)

            n = slots * kv
            bias = jnp.concatenate([head_bias[:, : min(n, size)]] * max(n // size, 1), axis=1)
            column = lax.broadcasted_iota(jnp.int32, (1, n), 1)
            scores = []
            for i in range(2):
                row = order[2 * pair + i]
                q = q_ref[:, row].reshape(lanes, size)
                s = lax.dot_general(
                    q,
                    k_buf[2 * pair + i, :n],
                    (((1,), (1,)), ((), ())),
                    preferred_element_type=jnp.float32,
                )
                closed = jnp.where(column < lengths[row] * kv, 0.0, -jnp.inf)
                scores.append(s + (bias + closed))
            highest = [jnp.max(s, axis=1, keepdims=True) * scale for s in scores]
            weights = [jnp.exp2(s * scale - h) for s, h in zip(scores, highest)]
            totals = [jnp.sum(p, axis=1, keepdims=True) for p in weights]
            for i in range(2):
                o = jnp.dot(
                    weights[i].astype(jnp.bfloat16),
                    v_buf[2 * pair + i, :n],
                    preferred_element_type=jnp.float32,
                )
                spot = 2 * (pair - done) + i
                o_ref[spot] = o / totals[i]
                lse = highest[i] + jnp.log(totals[i]) * LOG2E
                lse_ref[spot] = jnp.broadcast_to(lse, (lanes, size))

        by_length(lengths[order[2 * pair]], sizes, compute)

    if pairs[1] - pairs[0] == 1:
        attend(pairs[0])
    else:
        pl.loop(*pairs)(attend)
    for pair in range(max(pairs[1], ready[0]), ready[1]):
        by_length(lengths[order[2 * pair]], sizes, functools.partial(finish, pair))
    if has_w:
        w_copy.wait()


def like(x):
    return pltpu.VMEM(x.shape, x.dtype)


def cache_attention(pairs, ready, lengths, order, queries, keys, values, weights, buffers, has_w, sizes, after):
    rows, steps, _, heads, size = (keys.shape[0], *queries.shape)
    slots = sizes[-1]
    scale = LOG2E / math.sqrt(size)
    count = 2 * (pairs[1] - pairs[0])
    piece = pltpu.VMEM((count, steps * heads, size), jnp.float32)
    outs = [piece, piece] + ([pltpu.VMEM(weights.shape[1:], weights.dtype)] if has_w else [])
    aliases = {}
    if not buffers:
        operands = [pinned(x) for x in (lengths, queries, keys, values, weights)]
        specs = [HBM] * 5
        scalars = pltpu.SMEM((rows,), jnp.int32)
        buffer = pltpu.VMEM(keys.shape, keys.dtype)
        out_shape = [scalars, scalars, like(queries), buffer, buffer]
        out_specs = [SMEM, SMEM, VMEM, VMEM, VMEM]
    else:
        operands = [pinned(x, pltpu.SMEM) for x in (lengths, order)]
        operands += [pinned(queries, pltpu.VMEM)]
        operands += [pinned(x) for x in (keys, values, weights)]
        aliases = {len(operands) + i: i for i in range(len(buffers))}
        operands += [pinned(b, pltpu.VMEM) for b in buffers]
        specs = [SMEM, SMEM, VMEM, HBM, HBM, HBM] + [VMEM] * len(buffers)
        out_shape = [like(b) for b in buffers]
        out_specs = [VMEM] * len(buffers)
    out_shape += outs
    out_specs += [VMEM] * len(outs)
    return pl.pallas_call(
        functools.partial(attend_cache, pairs, pairs[0], ready, sizes, scale, int(has_w), 0),
        out_shape=out_shape,
        in_specs=specs + [ANY] * len(after),
        out_specs=out_specs,
        input_output_aliases=aliases,
        scratch_shapes=[
            pltpu.SemaphoreType.DMA((rows // 2, 2, 2)),
            pltpu.SemaphoreType.DMA,
        ],
        compiler_params=pltpu.CompilerParams(vmem_limit_bytes=8 * MIB),
        cost_estimate=pl.CostEstimate(
            flops=4 * steps * heads * count * keys.shape[1] * size,
            bytes_accessed=4 * count * keys.shape[1] * size + 2 * has_w * weights[0].size,
            transcendentals=steps * heads * count * keys.shape[1],
        ),
        name="cache_attention",
    )(*operands, *after)


def project_old(part, lay, n_hidden, *refs):
    refs = list(refs)
    tp = lax.axis_index("tp")
    if part == 0:
        hidden = refs[1 : 1 + n_hidden]
        w_hbm = refs[1 + n_hidden]
        w_ref, next_ref, h_ref, out_ref, sem = refs[-5:]
        copy = pltpu.make_async_copy(w_hbm.at[1], next_ref, sem)
        copy.start()
        for i, h in enumerate(hidden):
            h_ref[lax.rem(tp + i, lay.tp)] = h[...]
    else:
        h_ref = refs[2]
        w_ref, out_ref = refs[-2:]
    features = h_ref.shape[2]
    chunk = min(features, 1024)
    total = jnp.zeros(out_ref.shape, jnp.float32)
    for t in range(lay.tp):
        for low in range(0, features, chunk):
            start = t * features + low
            total += jnp.dot(
                h_ref[t, :, low : low + chunk],
                w_ref[start : start + chunk, :],
                preferred_element_type=jnp.float32,
            )
    out_ref[...] = total
    if part == 0:
        copy.wait()


def project(part, lay, w, hidden, weights, after):
    tokens, features = hidden[0].shape[-2:]
    out = pltpu.VMEM((tokens, w.shape[1]), jnp.float32)
    operands = [pinned(w, pltpu.VMEM)] + hidden
    specs = [VMEM] * len(operands)
    if part == 0:
        states = pltpu.VMEM((lay.tp, tokens, features), jnp.bfloat16)
        operands.append(pinned(weights))
        specs.append(HBM)
        out_shape = [like(w), like(w), states, out]
        aliases = {0: 0}
        scratch = [pltpu.SemaphoreType.DMA]
    else:
        operands = [pinned(weights, pltpu.VMEM)] + operands
        specs.append(VMEM)
        operands[2] = pinned(operands[2], pltpu.VMEM)
        out_shape = [like(w), like(w), out]
        aliases = {0: 0, 1: 1}
        scratch = []
    return pl.pallas_call(
        functools.partial(project_old, part, lay, len(hidden)),
        out_shape=out_shape,
        in_specs=specs + [ANY] * len(after),
        out_specs=[VMEM] * len(out_shape),
        input_output_aliases=aliases,
        scratch_shapes=scratch,
        compiler_params=pltpu.CompilerParams(vmem_limit_bytes=8 * MIB),
        cost_estimate=pl.CostEstimate(
            flops=2 * tokens * w.size, bytes_accessed=2 * w.size, transcendentals=0
        ),
        name="project",
    )(*operands, *after)


def merge_all(lay, plan, n_caches, scale, *refs):
    refs = list(refs)

    def take(n):
        out = refs[:n]
        del refs[:n]
        return out

    weights, downs = take(2), take(len(plan))
    h_buf, *olds = take(3)
    order, q_ref = take(2)
    caches = [take(2) for _ in range(n_caches)]
    m_hbm, out_ref, m_buf, u_parts, u_buf, low, sems = refs

    pairs, depth, width = m_buf.shape[1:]
    cut = min(width, 256)
    lanes = downs[0].shape[3]
    tiles = depth // lanes
    fsdp, grp, tp = (lax.axis_index(a) for a in AXES)
    z, core = fsdp // 2, lax.rem(fsdp, 2)
    place = grp * lay.depth + jnp.where(lax.rem(grp, 2) == 0, z, lay.depth - 1 - z)
    per_lane = lay.fsdp * lay.grp // lay.tp

    shards = []
    for (step, flip), down in zip(plan, downs):
        towards = 2 * core - 1
        spot = lax.rem(place + lay.ring + step * (-towards if flip else towards), lay.ring)
        g = spot // lay.depth
        along = lax.rem(spot, lay.depth)
        zz = jnp.where(lax.rem(g, 2) == 0, along, lay.depth - 1 - along)
        for c in range(2):
            cc = lax.rem(core + c + (1 if flip else 0), 2)
            shards.append((down, c, (zz * 2 + cc) * lay.grp + g))

    columns = width // per_lane
    for down, c, index in shards:
        @pl.when(index // per_lane == tp)
        def _():
            u_parts[lax.rem(index, per_lane)] = down[c, pairs * tiles, :, : pairs * columns]

    for k in range(pairs):
        u_buf[k] = ADAPTER_SCALING * jnp.concatenate(
            [u_parts[i, :, k * columns : (k + 1) * columns] for i in range(per_lane)], axis=1
        )
    low[...] = jnp.zeros_like(low)

    chunk = min(depth, 256)
    copies = []
    for j, (down, c, index) in enumerate(shards):
        start = pl.multiple_of(index * depth, depth)
        column = pl.multiple_of(lax.rem(index, per_lane) * depth, depth)
        source = index // per_lane
        for k in range(pairs):
            for begin in range(0, depth, chunk):
                rows = slice(begin, begin + chunk)
                tile = k * tiles + begin // lanes
                d = jnp.concatenate([down[c, tile + i] for i in range(chunk // lanes)], axis=1)
                for side in range(width // cut):
                    cols = slice(side * cut, (side + 1) * cut)
                    added = lax.dot_general(
                        d,
                        u_buf[k, :, cols],
                        (((0,), (0,)), ((), ())),
                        preferred_element_type=jnp.float32,
                    )
                    w = weights[k][pl.ds(start + begin, chunk), cols]
                    m_buf[j, k, rows, cols] = (w.astype(jnp.float32) + added).astype(jnp.bfloat16)
                low[k] += lax.dot_general(
                    h_buf[source, :, pl.ds(column + begin, chunk)],
                    d,
                    (((1,), (1,)), ((), ())),
                    preferred_element_type=jnp.float32,
                )
            copy = pltpu.make_async_copy(
                m_buf.at[j, k], m_hbm.at[k, pl.ds(start, depth), :], sems.at[j, k]
            )
            copy.start()
            copies.append(copy)

    new = []
    for k in range(pairs):
        high = low[k].astype(jnp.bfloat16)
        rest = (low[k] - high.astype(jnp.float32)).astype(jnp.bfloat16)
        new.append(
            (
                olds[k][...]
                + jnp.dot(high, u_buf[k], preferred_element_type=jnp.float32)
                + jnp.dot(rest, u_buf[k], preferred_element_type=jnp.float32)
            ).astype(jnp.bfloat16)
        )
    add_new_tokens(q_ref, order, caches, new, out_ref, scale)
    for copy in copies:
        copy.wait()


def add_new_tokens(q_ref, order, caches, new, out_ref, scale):
    steps, rows, heads, size = q_ref.shape
    kv = new[0].shape[1] // size
    new = [
        jnp.concatenate([x[:, g * size : (g + 1) * size] for g in range(kv)], axis=0) for x in new
    ]
    n = kv * steps * rows
    lanes = steps * heads
    left = lax.broadcasted_iota(jnp.int32, (lanes, n), 0)
    right = lax.broadcasted_iota(jnp.int32, (lanes, n), 1)
    same_head = over(within(left, heads), heads // kv) == over(right, steps * rows)
    earlier = within(over(right, rows), steps) <= over(left, heads)
    right_row = jnp.where(same_head & earlier, within(right, rows), -1)
    spots = [(o, lse, i) for o, lse in caches for i in range(o.shape[0])]
    for spot, (o_ref, lse_ref, i) in enumerate(spots):
        row = order[spot]
        q = q_ref[:, row].reshape(lanes, size)
        s = lax.dot_general(
            q, new[0], (((1,), (1,)), ((), ())), preferred_element_type=jnp.float32
        )
        s = jnp.where(right_row == row, s * scale, -jnp.inf)
        lse = lse_ref[i]
        highest = jnp.maximum(jnp.max(s, axis=1, keepdims=True), lse)
        p = jnp.exp2(s - highest[:, :n])
        old = jnp.exp2(lse - highest)
        divisor = jnp.sum(p, axis=1, keepdims=True) + old
        o = old * o_ref[i] + jnp.dot(
            p.astype(jnp.bfloat16), new[1], preferred_element_type=jnp.float32
        )
        out_ref[:, row] = (o / divisor).reshape(steps, heads, size).astype(out_ref.dtype)


def merge(lay, shape, entries, weights, states, olds, order, queries, caches):
    pairs, total, width = shape
    rank = entries[0][2].shape[2]
    tokens = states.shape[1]
    depth = total // (lay.fsdp * lay.grp)
    per_lane = lay.fsdp * lay.grp // lay.tp
    n = 2 * len(entries)
    operands = [pinned(w, pltpu.VMEM) for w in weights] + [e[2] for e in entries]
    operands += [states, *olds, pinned(order, pltpu.SMEM), pinned(queries, pltpu.VMEM), *caches]
    specs = [VMEM] * len(operands)
    specs[-2 - len(caches)] = SMEM
    return pl.pallas_call(
        functools.partial(
            merge_all,
            lay,
            [e[:2] for e in entries],
            len(caches) // 2,
            LOG2E / math.sqrt(queries.shape[3]),
        ),
        out_shape=(pltpu.HBM(shape, jnp.bfloat16), jax.ShapeDtypeStruct(queries.shape, jnp.bfloat16)),
        in_specs=specs,
        out_specs=(HBM, VMEM),
        scratch_shapes=[
            pltpu.VMEM((n, pairs, depth, width), jnp.bfloat16),
            pltpu.VMEM((per_lane, rank, pairs * width // per_lane), jnp.bfloat16),
            pltpu.VMEM((pairs, rank, width), jnp.bfloat16),
            pltpu.VMEM((pairs, tokens, rank), jnp.float32),
            pltpu.SemaphoreType.DMA((n, pairs)),
        ],
        compiler_params=pltpu.CompilerParams(vmem_limit_bytes=24 * MIB),
        cost_estimate=pl.CostEstimate(
            flops=2 * pairs * total * width * rank,
            bytes_accessed=2 * pairs * total * width,
            transcendentals=0,
        ),
        name="merge",
    )(*operands)


def shards(
    lay,
    hidden_states,
    queries,
    cache_keys,
    cache_values,
    cache_lengths,
    projection_weight_matrices,
    factor_down,
    factor_up,
):
    send = functools.partial(lax.ppermute, axis_name=AXES)
    steps, rows, features = hidden_states.shape
    slots, kv, size = cache_keys.shape[1:]
    shape = projection_weight_matrices.shape
    sizes = tuple(slots * i // 24 for i in (1, 4, 8, 16, 24))
    own = jnp.swapaxes(factor_down, 1, 2)
    tokens = hidden_states.reshape(steps * rows, features)
    keys = cache_keys.reshape(rows, slots * kv, size)
    values = cache_values.reshape(rows, slots * kv, size)
    swap, ring = lay.core_swap(), lay.ring_step()

    other, other_up = send(own, perm=swap), send(factor_up, perm=swap)
    pair = pack(own, other, factor_up, other_up)
    entries = [(0, False, pair)]

    projections = projection_weight_matrices
    came = send(pair, perm=ring)
    hidden = [tokens] + [send(tokens, perm=lay.feature_step(i)) for i in range(1, lay.tp)]
    lengths, order, q, *buffers, o, lse = cache_attention(
        (0, 1), (0, 2), cache_lengths, None, queries, keys, values, projections, [], False, sizes, [pair]
    )
    caches = [o, lse]
    (came, hidden), token = after_all((came, hidden), o)

    sent, swapped = send(came, perm=ring), send(came, perm=swap)
    *_, o, lse, w_keys = cache_attention(
        (1, rows // 2), (2, rows // 2), lengths, order, q, keys, values, projections, buffers, True, sizes, [token]
    )
    caches += [o, lse]
    entries += [(1, False, came), (1, True, swapped)]
    (came, swapped), token = after_all((sent, swapped), o)
    entries[-1] = (1, True, swapped)

    last_step = lay.ring // 2
    for step in range(2, last_step):
        sent, swapped = send(came, perm=ring), send(came, perm=swap)
        if step == 2:
            w_keys, w_values, states, old_keys = project(0, lay, w_keys, hidden, projections, [token])
            token = old_keys
        elif step == 3:
            w_keys, w_values, old_values = project(1, lay, w_values, [states], w_keys, [token])
            token = old_values
        entries += [(step, False, came), (step, True, swapped)]
        (came, swapped), token = after_all((sent, swapped), token)
        entries[-1] = (step, True, swapped)
    entries.append((last_step, False, came))
    return tuple(
        merge(
            lay,
            shape,
            entries,
            [w_keys, w_values],
            states,
            [old_keys, old_values],
            order,
            q,
            caches,
        )
    )


def solution(mesh):
    return jax.shard_map(
        functools.partial(shards, Layout(mesh)),
        mesh=mesh,
        in_specs=(
            P(None, ("fsdp", "grp"), "tp"),
            P(None, ("fsdp", "grp"), "tp", None),
            P(("fsdp", "grp"), None, "tp", None),
            P(("fsdp", "grp"), None, "tp", None),
            P(("fsdp", "grp")),
            P(None, None, "tp"),
            P(None, ("fsdp", "grp"), None),
            P(None, None, ("fsdp", "grp")),
        ),
        out_specs=(P(None, None, "tp"), P(None, ("fsdp", "grp"), "tp", None)),
        check_vma=False,
    )
```

```python
import functools
import math

import jax
import jax.numpy as jnp
from jax import lax
from jax.experimental import pallas as pl
from jax.experimental.pallas import tpu as pltpu
from jax.sharding import PartitionSpec as P

AXES = ("fsdp", "grp", "tp")
ADAPTER_SCALING = 2.0
LOG2E = math.log2(math.e)
MIB = 1024 * 1024
ANY = pl.BlockSpec(memory_space=pl.ANY)
HBM = pl.BlockSpec(memory_space=pltpu.HBM)
VMEM = pl.BlockSpec(memory_space=pltpu.VMEM)
SMEM = pl.BlockSpec(memory_space=pltpu.SMEM)


class Layout:
    def __init__(self, mesh):
        self.fsdp, self.grp, self.tp = (mesh.shape[a] for a in AXES)
        self.depth = self.fsdp // 2
        self.ring = self.depth * self.grp
        self.block = self.depth // self.tp

    def flat(self, z, core, g, t):
        return ((z * 2 + core) * self.grp + g) * self.tp + t

    def devices(self):
        for z in range(self.depth):
            for core in range(2):
                for g in range(self.grp):
                    for t in range(self.tp):
                        yield z, core, g, t

    def place(self, z, g):
        return g * self.depth + (z if g % 2 == 0 else self.depth - 1 - z)

    def at(self, position):
        g, z = divmod(position, self.depth)
        return (z if g % 2 == 0 else self.depth - 1 - z), g

    def ring_step(self, step, flip=0):
        pairs = []
        for z, core, g, t in self.devices():
            to_z, to_g = self.at((self.place(z, g) + step) % self.ring)
            pairs.append((self.flat(z, core, g, t), self.flat(to_z, core ^ flip, to_g, t)))
        return pairs

    def core_swap(self):
        return [
            (self.flat(z, c, g, t), self.flat(z, 1 - c, g, t)) for z, c, g, t in self.devices()
        ]

    def feature_step(self, step):
        return [
            (self.flat(z, c, g, (t + step) % self.tp), self.flat(z, c, g, t))
            for z, c, g, t in self.devices()
        ]


def over(x, n):
    return x >> (n.bit_length() - 1) if n & (n - 1) == 0 else x // n


def within(x, n):
    return x & (n - 1) if n & (n - 1) == 0 else x % n


def after_all(arrays, token):
    return lax.optimization_barrier((arrays, token))


def pinned(x, space=pltpu.HBM):
    return pltpu.with_memory_space_constraint(x, space)


def sort_rows(lengths, order):
    rows = lengths.shape[0]
    held = [lengths[r] for r in range(rows)]
    for r in range(rows):
        rank = jnp.int32(0)
        for other in range(rows):
            if other != r:
                ahead = held[other] >= held[r] if other < r else held[other] > held[r]
                rank = rank + ahead.astype(jnp.int32)
        order[rank] = r


def by_length(length, sizes, act):
    below = 0
    for slots in sizes:

        @pl.when((length > below) & (length <= slots))
        def _():
            act(slots)

        below = slots


def cache_copies(first, spot, slots, kv, order, hbms, bufs, sems):
    span = pl.ds(0, slots * kv)
    return [
        [
            pltpu.make_async_copy(
                hbm.at[order[first + i], span], buf.at[spot + i, span], sems.at[i, which]
            )
            for which, (hbm, buf) in enumerate(zip(hbms, bufs))
        ]
        for i in range(2)
    ]


def copy_pieces(src, dst, sems):
    rows = dst.shape[0] // sems.shape[0]
    return [
        pltpu.make_async_copy(
            src.at[pl.ds(i * rows, rows)], dst.at[pl.ds(i * rows, rows)], sems.at[i]
        )
        for i in range(sems.shape[0])
    ]


def begin_all(down, up, len_hbm, q_hbm, shard, lengths, order, q_ref, up_buf, sems, more):
    lanes = shard.shape[2]
    count, _, depth = down.shape
    tiles = depth // lanes
    copies = [
        pltpu.make_async_copy(
            down.at[k, :, pl.ds(i * lanes, lanes)], shard.at[k * tiles + i], sems.at[k, i]
        )
        for k in range(count)
        for i in range(tiles)
    ]
    up_copy = pltpu.make_async_copy(up, up_buf, more.at[0])
    len_copy = pltpu.make_async_copy(len_hbm, lengths, more.at[1])
    q_copy = pltpu.make_async_copy(q_hbm, q_ref, more.at[2])
    for copy in [up_copy, len_copy] + copies + [q_copy]:
        copy.start()
    up_copy.wait()
    columns = jnp.concatenate([up_buf[k] for k in range(count)], axis=1)
    shard[count * tiles, :, : columns.shape[1]] = columns
    len_copy.wait()
    sort_rows(lengths, order)
    for copy in copies + [q_copy]:
        copy.wait()


def begin(down, up, lengths, queries):
    count, rank, depth = down.shape
    tiles = depth // 128
    scalars = pltpu.SMEM(lengths.shape, jnp.int32)
    return pl.pallas_call(
        begin_all,
        out_shape=(
            pltpu.VMEM((count * tiles + 1, rank, 128), down.dtype),
            scalars,
            scalars,
            pltpu.VMEM(queries.shape, queries.dtype),
        ),
        in_specs=[HBM] * 4,
        out_specs=(VMEM, SMEM, SMEM, VMEM),
        scratch_shapes=[
            pltpu.VMEM(up.shape, up.dtype),
            pltpu.SemaphoreType.DMA((count, tiles)),
            pltpu.SemaphoreType.DMA((3,)),
        ],
        compiler_params=pltpu.CompilerParams(vmem_limit_bytes=2 * MIB),
        name="begin",
    )(pinned(down), pinned(up), pinned(lengths), pinned(queries))


def attend_cache(pairs, ready, sizes, scale, has_w, *refs):
    lengths, order, q_ref, k_hbm, v_hbm, w_hbm = refs[:6]
    sems, w_sems = refs[-2:]
    k_buf, v_buf, *outs = refs[-6 - has_w : -2]
    done = pairs[0]
    o_ref, lse_ref = outs[:2]
    steps, _, heads, size = q_ref.shape
    kv = k_hbm.shape[1] // sizes[-1]
    lanes = steps * heads

    def copies(pair, slots):
        span = pl.ds(0, slots * kv)
        return [
            [
                pltpu.make_async_copy(
                    hbm.at[order[2 * pair + i], span],
                    buf.at[2 * pair + i, span],
                    sems.at[pair, i, which],
                )
                for which, (hbm, buf) in enumerate(((k_hbm, k_buf), (v_hbm, v_buf)))
            ]
            for i in range(2)
        ]

    def start(pair, slots):
        for made in copies(pair, slots):
            for copy in made:
                copy.start()

    def finish(pair, slots):
        for made in copies(pair, slots):
            for copy in made:
                copy.wait()

    for pair in range(*ready):
        by_length(lengths[order[2 * pair]], sizes, functools.partial(start, pair))
    if has_w:
        w_copies = copy_pieces(w_hbm.at[0], outs[2], w_sems)
        for copy in w_copies:
            copy.start()

    row_head = over(within(lax.broadcasted_iota(jnp.int32, (lanes, size), 0), heads), heads // kv)
    slot_head = within(lax.broadcasted_iota(jnp.int32, (lanes, size), 1), kv)
    head_bias = jnp.where(row_head == slot_head, 0.0, -jnp.inf)

    def attend(pair):
        def compute(slots):
            @pl.when(pair >= ready[0])
            def _():
                finish(pair, slots)

            n = slots * kv
            bias = jnp.concatenate([head_bias[:, : min(n, size)]] * max(n // size, 1), axis=1)
            column = lax.broadcasted_iota(jnp.int32, (1, n), 1)
            scores = []
            for i in range(2):
                row = order[2 * pair + i]
                q = q_ref[:, row].reshape(lanes, size)
                s = lax.dot_general(
                    q,
                    k_buf[2 * pair + i, :n],
                    (((1,), (1,)), ((), ())),
                    preferred_element_type=jnp.float32,
                )
                closed = jnp.where(column < lengths[row] * kv, 0.0, -jnp.inf)
                scores.append(s + (bias + closed))
            highest = [jnp.max(s, axis=1, keepdims=True) * scale for s in scores]
            weights = [jnp.exp2(s * scale - h) for s, h in zip(scores, highest)]
            totals = [jnp.sum(p, axis=1, keepdims=True) for p in weights]
            for i in range(2):
                o = jnp.dot(
                    weights[i].astype(jnp.bfloat16),
                    v_buf[2 * pair + i, :n],
                    preferred_element_type=jnp.float32,
                )
                spot = 2 * (pair - done) + i
                o_ref[spot] = o / totals[i]
                lse = highest[i] + jnp.log(totals[i]) * LOG2E
                lse_ref[spot] = jnp.broadcast_to(lse, (lanes, size))

        by_length(lengths[order[2 * pair]], sizes, compute)

    if pairs[1] - pairs[0] == 1:
        attend(pairs[0])
    else:
        pl.loop(*pairs)(attend)
    for pair in range(max(pairs[1], ready[0]), ready[1]):
        by_length(lengths[order[2 * pair]], sizes, functools.partial(finish, pair))
    if has_w:
        for copy in w_copies:
            copy.wait()


def like(x):
    return pltpu.VMEM(x.shape, x.dtype)


def cache_attention(pairs, ready, lengths, order, queries, keys, values, weights, buffers, has_w, sizes, after):
    rows, steps, _, heads, size = (keys.shape[0], *queries.shape)
    slots = sizes[-1]
    scale = LOG2E / math.sqrt(size)
    count = 2 * (pairs[1] - pairs[0])
    piece = pltpu.VMEM((count, steps * heads, size), jnp.float32)
    outs = [piece, piece] + ([pltpu.VMEM(weights.shape[1:], weights.dtype)] if has_w else [])
    operands = [pinned(x, pltpu.SMEM) for x in (lengths, order)]
    operands += [pinned(queries, pltpu.VMEM)]
    operands += [pinned(x) for x in (keys, values, weights)]
    aliases = {len(operands) + i: i for i in range(len(buffers))}
    operands += [pinned(b, pltpu.VMEM) for b in buffers]
    specs = [SMEM, SMEM, VMEM, HBM, HBM, HBM] + [VMEM] * len(buffers)
    out_shape = [pltpu.VMEM(keys.shape, keys.dtype)] * 2
    out_specs = [VMEM] * 2
    out_shape += outs
    out_specs += [VMEM] * len(outs)
    return pl.pallas_call(
        functools.partial(attend_cache, pairs, ready, sizes, scale, int(has_w)),
        out_shape=out_shape,
        in_specs=specs + [ANY] * len(after),
        out_specs=out_specs,
        input_output_aliases=aliases,
        scratch_shapes=[
            pltpu.SemaphoreType.DMA((rows // 2, 2, 2)),
            pltpu.SemaphoreType.DMA((8,)),
        ],
        compiler_params=pltpu.CompilerParams(vmem_limit_bytes=8 * MIB),
        cost_estimate=pl.CostEstimate(
            flops=4 * steps * heads * count * keys.shape[1] * size,
            bytes_accessed=4 * count * keys.shape[1] * size + 2 * has_w * weights[0].size,
            transcendentals=steps * heads * count * keys.shape[1],
        ),
        name="cache_attention",
    )(*operands, *after)


def project_old(part, lay, n_hidden, *refs):
    refs = list(refs)
    tp = lax.axis_index("tp")
    if part == 0:
        hidden = refs[1 : 1 + n_hidden]
        w_hbm = refs[1 + n_hidden]
        w_ref, next_ref, h_ref, out_ref, sems = refs[-5:]
        copies = copy_pieces(w_hbm.at[1], next_ref, sems)
        for copy in copies:
            copy.start()
        for i, h in enumerate(hidden):
            h_ref[lax.rem(tp + i, lay.tp)] = h[...]
    else:
        h_ref = refs[2]
        w_ref, out_ref = refs[-2:]
    features = h_ref.shape[2]
    chunk = min(features, 1024)
    total = jnp.zeros(out_ref.shape, jnp.float32)
    for t in range(lay.tp):
        for low in range(0, features, chunk):
            start = t * features + low
            total += jnp.dot(
                h_ref[t, :, low : low + chunk],
                w_ref[start : start + chunk, :],
                preferred_element_type=jnp.float32,
            )
    out_ref[...] = total
    if part == 0:
        for copy in copies:
            copy.wait()


def project(part, lay, w, hidden, weights, after):
    tokens, features = hidden[0].shape[-2:]
    out = pltpu.VMEM((tokens, w.shape[1]), jnp.float32)
    operands = [pinned(w, pltpu.VMEM)] + hidden
    specs = [VMEM] * len(operands)
    if part == 0:
        states = pltpu.VMEM((lay.tp, tokens, features), jnp.bfloat16)
        operands.append(pinned(weights))
        specs.append(HBM)
        out_shape = [like(w), like(w), states, out]
        aliases = {0: 0}
        scratch = [pltpu.SemaphoreType.DMA((8,))]
    else:
        operands = [pinned(weights, pltpu.VMEM)] + operands
        specs.append(VMEM)
        operands[2] = pinned(operands[2], pltpu.VMEM)
        out_shape = [like(w), like(w), out]
        aliases = {0: 0, 1: 1}
        scratch = []
    return pl.pallas_call(
        functools.partial(project_old, part, lay, len(hidden)),
        out_shape=out_shape,
        in_specs=specs + [ANY] * len(after),
        out_specs=[VMEM] * len(out_shape),
        input_output_aliases=aliases,
        scratch_shapes=scratch,
        compiler_params=pltpu.CompilerParams(vmem_limit_bytes=8 * MIB),
        cost_estimate=pl.CostEstimate(
            flops=2 * tokens * w.size, bytes_accessed=2 * w.size, transcendentals=0
        ),
        name="project",
    )(*operands, *after)


def merge_all(lay, plan, n_caches, scale, *refs):
    refs = list(refs)

    def take(n):
        out = refs[:n]
        del refs[:n]
        return out

    weights, downs = take(2), take(len(plan))
    h_buf, *olds = take(3)
    order, q_ref = take(2)
    caches = [take(2) for _ in range(n_caches)]
    m_hbm, out_ref, m_buf, u_parts, u_buf, low, sems = refs

    pairs, depth, width = m_buf.shape[1:]
    cut = min(width, 256)
    lanes = downs[0].shape[2]
    tiles = depth // lanes
    fsdp, grp, tp = (lax.axis_index(a) for a in AXES)
    z, core = fsdp // 2, lax.rem(fsdp, 2)
    place = grp * lay.depth + jnp.where(lax.rem(grp, 2) == 0, z, lay.depth - 1 - z)
    per_lane = lay.fsdp * lay.grp // lay.tp

    shards = []
    for (step, flip), down in zip(plan, downs):
        spot = lax.rem(place + (lay.ring + step), lay.ring)
        g = spot // lay.depth
        along = lax.rem(spot, lay.depth)
        zz = jnp.where(lax.rem(g, 2) == 0, along, lay.depth - 1 - along)
        shards.append((down, (zz * 2 + (1 - core if flip else core)) * lay.grp + g))

    columns = width // per_lane
    for down, index in shards:

        @pl.when(index // per_lane == tp)
        def _():
            u_parts[lax.rem(index, per_lane)] = down[pairs * tiles, :, : pairs * columns]

    for k in range(pairs):
        u_buf[k] = ADAPTER_SCALING * jnp.concatenate(
            [u_parts[i, :, k * columns : (k + 1) * columns] for i in range(per_lane)], axis=1
        )
    low[...] = jnp.zeros_like(low)

    chunk = min(depth, 256)
    copies = []
    for j, (down, index) in enumerate(shards):
        start = pl.multiple_of(index * depth, depth)
        column = pl.multiple_of(lax.rem(index, per_lane) * depth, depth)
        source = index // per_lane
        for k in range(pairs):
            for begin in range(0, depth, chunk):
                rows = slice(begin, begin + chunk)
                tile = k * tiles + begin // lanes
                d = jnp.concatenate([down[tile + i] for i in range(chunk // lanes)], axis=1)
                for side in range(width // cut):
                    cols = slice(side * cut, (side + 1) * cut)
                    added = lax.dot_general(
                        d,
                        u_buf[k, :, cols],
                        (((0,), (0,)), ((), ())),
                        preferred_element_type=jnp.float32,
                    )
                    w = weights[k][pl.ds(start + begin, chunk), cols]
                    m_buf[j, k, rows, cols] = (w.astype(jnp.float32) + added).astype(jnp.bfloat16)
                low[k] += lax.dot_general(
                    h_buf[source, :, pl.ds(column + begin, chunk)],
                    d,
                    (((1,), (1,)), ((), ())),
                    preferred_element_type=jnp.float32,
                )
            copy = pltpu.make_async_copy(
                m_buf.at[j, k], m_hbm.at[k, pl.ds(start, depth), :], sems.at[j, k]
            )
            copy.start()
            copies.append(copy)

    new = []
    for k in range(pairs):
        high = low[k].astype(jnp.bfloat16)
        rest = (low[k] - high.astype(jnp.float32)).astype(jnp.bfloat16)
        new.append(
            (
                olds[k][...]
                + jnp.dot(high, u_buf[k], preferred_element_type=jnp.float32)
                + jnp.dot(rest, u_buf[k], preferred_element_type=jnp.float32)
            ).astype(jnp.bfloat16)
        )
    add_new_tokens(q_ref, order, caches, new, out_ref, scale)
    for copy in copies:
        copy.wait()


def add_new_tokens(q_ref, order, caches, new, out_ref, scale):
    steps, rows, heads, size = q_ref.shape
    kv = new[0].shape[1] // size
    new = [
        jnp.concatenate([x[:, g * size : (g + 1) * size] for g in range(kv)], axis=0) for x in new
    ]
    n = kv * steps * rows
    lanes = steps * heads
    left = lax.broadcasted_iota(jnp.int32, (lanes, n), 0)
    right = lax.broadcasted_iota(jnp.int32, (lanes, n), 1)
    same_head = over(within(left, heads), heads // kv) == over(right, steps * rows)
    earlier = within(over(right, rows), steps) <= over(left, heads)
    right_row = jnp.where(same_head & earlier, within(right, rows), -1)
    spots = [(o, lse, i) for o, lse in caches for i in range(o.shape[0])]
    for spot, (o_ref, lse_ref, i) in enumerate(spots):
        row = order[spot]
        q = q_ref[:, row].reshape(lanes, size)
        s = lax.dot_general(
            q, new[0], (((1,), (1,)), ((), ())), preferred_element_type=jnp.float32
        )
        s = jnp.where(right_row == row, s * scale, -jnp.inf)
        lse = lse_ref[i]
        highest = jnp.maximum(jnp.max(s, axis=1, keepdims=True), lse)
        p = jnp.exp2(s - highest[:, :n])
        old = jnp.exp2(lse - highest)
        divisor = jnp.sum(p, axis=1, keepdims=True) + old
        o = old * o_ref[i] + jnp.dot(
            p.astype(jnp.bfloat16), new[1], preferred_element_type=jnp.float32
        )
        out_ref[:, row] = (o / divisor).reshape(steps, heads, size).astype(out_ref.dtype)


def merge(lay, shape, entries, weights, states, olds, order, queries, caches):
    pairs, total, width = shape
    rank = entries[0][2].shape[1]
    tokens = states.shape[1]
    depth = total // (lay.fsdp * lay.grp)
    per_lane = lay.fsdp * lay.grp // lay.tp
    n = len(entries)
    operands = [pinned(w, pltpu.VMEM) for w in weights] + [e[2] for e in entries]
    operands += [states, *olds, pinned(order, pltpu.SMEM), pinned(queries, pltpu.VMEM), *caches]
    specs = [VMEM] * len(operands)
    specs[-2 - len(caches)] = SMEM
    return pl.pallas_call(
        functools.partial(
            merge_all,
            lay,
            [e[:2] for e in entries],
            len(caches) // 2,
            LOG2E / math.sqrt(queries.shape[3]),
        ),
        out_shape=(pltpu.HBM(shape, jnp.bfloat16), jax.ShapeDtypeStruct(queries.shape, jnp.bfloat16)),
        in_specs=specs,
        out_specs=(HBM, VMEM),
        scratch_shapes=[
            pltpu.VMEM((n, pairs, depth, width), jnp.bfloat16),
            pltpu.VMEM((per_lane, rank, pairs * width // per_lane), jnp.bfloat16),
            pltpu.VMEM((pairs, rank, width), jnp.bfloat16),
            pltpu.VMEM((pairs, tokens, rank), jnp.float32),
            pltpu.SemaphoreType.DMA((n, pairs)),
        ],
        compiler_params=pltpu.CompilerParams(vmem_limit_bytes=24 * MIB),
        cost_estimate=pl.CostEstimate(
            flops=2 * pairs * total * width * rank,
            bytes_accessed=2 * pairs * total * width,
            transcendentals=0,
        ),
        name="merge",
    )(*operands)


def shards(
    lay,
    hidden_states,
    queries,
    cache_keys,
    cache_values,
    cache_lengths,
    projection_weight_matrices,
    factor_down,
    factor_up,
):
    send = functools.partial(lax.ppermute, axis_name=AXES)
    steps, rows, features = hidden_states.shape
    slots, kv, size = cache_keys.shape[1:]
    shape = projection_weight_matrices.shape
    sizes = tuple(slots * i // 24 for i in (1, 4, 8, 16, 24))
    own = jnp.swapaxes(factor_down, 1, 2)
    tokens = hidden_states.reshape(steps * rows, features)
    keys = cache_keys.reshape(rows, slots * kv, size)
    values = cache_values.reshape(rows, slots * kv, size)
    swap, ring = lay.core_swap(), {d: lay.ring_step(d) for d in (1, -1)}
    shard, lengths, order, q = begin(own, factor_up, cache_lengths, queries)
    entries = [(0, False, shard)]

    projections = projection_weight_matrices
    came = {d: send(shard, perm=ring[d]) for d in ring}
    partner = send(shard, perm=swap)
    hidden = [tokens] + [send(tokens, perm=lay.feature_step(i)) for i in range(1, lay.tp)]
    *buffers, o, lse = cache_attention(
        (0, 1), (0, 2), lengths, order, q, keys, values, projections, [], False, sizes, [shard]
    )
    caches = [o, lse]
    (came, partner), token = after_all((came, partner), o)
    entries.append((0, True, partner))

    last_step = lay.ring // 2
    for step in range(1, last_step):
        last = step + 1 == last_step
        sent = {
            1: send(came[1], perm=ring[1]),
            -1: send(came[-1], perm=lay.ring_step(-1, 1) if last else ring[-1]),
        }
        swapped = {d: send(came[d], perm=swap) for d in ring}
        if step == 1:
            *_, o, lse, w_keys = cache_attention(
                (1, rows // 4 * 2),
                (2, rows // 4 * 2),
                lengths,
                order,
                q,
                keys,
                values,
                projections,
                buffers,
                True,
                sizes,
                [token],
            )
            caches += [o, lse]
            token = o
        elif step == 2:
            w_keys, w_values, states, old_keys = project(0, lay, w_keys, hidden, projections, [token])
            token = old_keys
        elif step == 3:
            w_keys, w_values, old_values = project(1, lay, w_values, [states], w_keys, [token])
            token = old_values
        entries += [(-d * step, False, came[d]) for d in ring]
        if step == 1:
            (came, swapped, hidden), token = after_all((sent, swapped, hidden), token)
        else:
            (came, swapped), token = after_all((sent, swapped), token)
        entries += [(-d * step, True, swapped[d]) for d in ring]
    entries += [(-last_step, False, came[1]), (last_step, True, came[-1])]
    return tuple(
        merge(
            lay,
            shape,
            entries,
            [w_keys, w_values],
            states,
            [old_keys, old_values],
            order,
            q,
            caches,
        )
    )


def solution(mesh):
    return jax.shard_map(
        functools.partial(shards, Layout(mesh)),
        mesh=mesh,
        in_specs=(
            P(None, ("fsdp", "grp"), "tp"),
            P(None, ("fsdp", "grp"), "tp", None),
            P(("fsdp", "grp"), None, "tp", None),
            P(("fsdp", "grp"), None, "tp", None),
            P(("fsdp", "grp")),
            P(None, None, "tp"),
            P(None, ("fsdp", "grp"), None),
            P(None, None, ("fsdp", "grp")),
        ),
        out_specs=(P(None, None, "tp"), P(None, ("fsdp", "grp"), "tp", None)),
        check_vma=False,
    )
```

```python
import functools
import math

import jax
import jax.numpy as jnp
from jax import lax
from jax.experimental import pallas as pl
from jax.experimental.pallas import tpu as pltpu
from jax.sharding import PartitionSpec as P

AXES = ("fsdp", "grp", "tp")
ADAPTER_SCALING = 2.0
LOG2E = math.log2(math.e)
MIB = 1024 * 1024
ANY = pl.BlockSpec(memory_space=pl.ANY)
HBM = pl.BlockSpec(memory_space=pltpu.HBM)
VMEM = pl.BlockSpec(memory_space=pltpu.VMEM)
SMEM = pl.BlockSpec(memory_space=pltpu.SMEM)


class Layout:
    def __init__(self, mesh):
        self.fsdp, self.grp, self.tp = (mesh.shape[a] for a in AXES)
        self.depth = self.fsdp // 2
        self.ring = self.depth * self.grp
        self.block = self.depth // self.tp

    def flat(self, z, core, g, t):
        return ((z * 2 + core) * self.grp + g) * self.tp + t

    def devices(self):
        for z in range(self.depth):
            for core in range(2):
                for g in range(self.grp):
                    for t in range(self.tp):
                        yield z, core, g, t

    def place(self, z, g):
        return g * self.depth + (z if g % 2 == 0 else self.depth - 1 - z)

    def at(self, position):
        g, z = divmod(position, self.depth)
        return (z if g % 2 == 0 else self.depth - 1 - z), g

    def ring_step(self, step, flip=0):
        pairs = []
        for z, core, g, t in self.devices():
            to_z, to_g = self.at((self.place(z, g) + step) % self.ring)
            pairs.append((self.flat(z, core, g, t), self.flat(to_z, core ^ flip, to_g, t)))
        return pairs

    def core_swap(self):
        return [
            (self.flat(z, c, g, t), self.flat(z, 1 - c, g, t)) for z, c, g, t in self.devices()
        ]

    def feature_step(self, step):
        return [
            (self.flat(z, c, g, (t + step) % self.tp), self.flat(z, c, g, t))
            for z, c, g, t in self.devices()
        ]


def over(x, n):
    return x >> (n.bit_length() - 1) if n & (n - 1) == 0 else x // n


def within(x, n):
    return x & (n - 1) if n & (n - 1) == 0 else x % n


def after_all(arrays, token):
    return lax.optimization_barrier((arrays, token))


def pinned(x, space=pltpu.HBM):
    return pltpu.with_memory_space_constraint(x, space)


def sort_rows(lengths, order):
    rows = lengths.shape[0]
    held = [lengths[r] for r in range(rows)]
    for r in range(rows):
        rank = jnp.int32(0)
        for other in range(rows):
            if other != r:
                ahead = held[other] >= held[r] if other < r else held[other] > held[r]
                rank = rank + ahead.astype(jnp.int32)
        order[rank] = r


def by_length(length, sizes, act):
    below = 0
    for slots in sizes:

        @pl.when((length > below) & (length <= slots))
        def _():
            act(slots)

        below = slots


def cache_copies(first, spot, slots, kv, order, hbms, bufs, sems):
    span = pl.ds(0, slots * kv)
    return [
        [
            pltpu.make_async_copy(
                hbm.at[order[first + i], span], buf.at[spot + i, span], sems.at[i, which]
            )
            for which, (hbm, buf) in enumerate(zip(hbms, bufs))
        ]
        for i in range(2)
    ]


def quarter_copies(quarter, src, dst, sems):
    k, half = divmod(quarter, 2)
    rows = dst.shape[1] // (2 * sems.shape[0])
    spans = [
        pl.ds((half * sems.shape[0] + i) * rows, rows) for i in range(sems.shape[0])
    ]
    return [
        pltpu.make_async_copy(src.at[k, span], dst.at[k, span], sems.at[i])
        for i, span in enumerate(spans)
    ]


def begin_all(down, up, len_hbm, q_hbm, shard, lengths, order, q_ref, up_buf, sems, more):
    lanes = shard.shape[2]
    count, _, depth = down.shape
    tiles = depth // lanes
    copies = [
        pltpu.make_async_copy(
            down.at[k, :, pl.ds(i * lanes, lanes)], shard.at[k * tiles + i], sems.at[k, i]
        )
        for k in range(count)
        for i in range(tiles)
    ]
    up_copy = pltpu.make_async_copy(up, up_buf, more.at[0])
    len_copy = pltpu.make_async_copy(len_hbm, lengths, more.at[1])
    q_copy = pltpu.make_async_copy(q_hbm, q_ref, more.at[2])
    for copy in [up_copy, len_copy] + copies + [q_copy]:
        copy.start()
    up_copy.wait()
    columns = jnp.concatenate([up_buf[k] for k in range(count)], axis=1)
    shard[count * tiles, :, : columns.shape[1]] = columns
    len_copy.wait()
    sort_rows(lengths, order)
    for copy in copies + [q_copy]:
        copy.wait()


def begin(down, up, lengths, queries):
    count, rank, depth = down.shape
    tiles = depth // 128
    scalars = pltpu.SMEM(lengths.shape, jnp.int32)
    return pl.pallas_call(
        begin_all,
        out_shape=(
            pltpu.VMEM((count * tiles + 1, rank, 128), down.dtype),
            scalars,
            scalars,
            pltpu.VMEM(queries.shape, queries.dtype),
        ),
        in_specs=[HBM] * 4,
        out_specs=(VMEM, SMEM, SMEM, VMEM),
        scratch_shapes=[
            pltpu.VMEM(up.shape, up.dtype),
            pltpu.SemaphoreType.DMA((count, tiles)),
            pltpu.SemaphoreType.DMA((3,)),
        ],
        compiler_params=pltpu.CompilerParams(vmem_limit_bytes=2 * MIB),
        name="begin",
    )(pinned(down), pinned(up), pinned(lengths), pinned(queries))


def attend_cache(pairs, ready, sizes, scale, quarter, n_packed, *refs):
    lengths, order, q_ref, k_hbm, v_hbm, w_hbm = refs[:6]
    sems, w_sems = refs[-2:]
    n_out = 6 if n_packed else 5
    k_buf, v_buf, w_buf, *outs = refs[-2 - n_out : -2]
    done = pairs[0]
    o_ref, lse_ref = outs[:2]
    steps, _, heads, size = q_ref.shape
    kv = k_hbm.shape[1] // sizes[-1]
    lanes = steps * heads

    def copies(which, pair, slots):
        span = pl.ds(0, slots * kv)
        hbm, buf = ((k_hbm, k_buf), (v_hbm, v_buf))[which]
        return [
            pltpu.make_async_copy(
                hbm.at[order[2 * pair + i], span],
                buf.at[2 * pair + i, span],
                sems.at[pair, i, which],
            )
            for i in range(2)
        ]

    def start(pair, slots):
        for copy in copies(0, pair, slots) + copies(1, pair, slots):
            copy.start()

    def finish(which, pair, slots):
        for i in which:
            for copy in copies(i, pair, slots):
                copy.wait()

    for pair in range(*ready):
        by_length(lengths[order[2 * pair]], sizes, functools.partial(start, pair))
    w_copies = quarter_copies(quarter, w_hbm, w_buf, w_sems)
    for copy in w_copies:
        copy.start()
    if n_packed:
        packed = refs[-2 - n_out - n_packed : -2 - n_out]
        for i, ref in enumerate(packed):
            outs[2][i] = ref[...]

    row_head = over(within(lax.broadcasted_iota(jnp.int32, (lanes, size), 0), heads), heads // kv)
    slot_head = within(lax.broadcasted_iota(jnp.int32, (lanes, size), 1), kv)
    head_bias = jnp.where(row_head == slot_head, 0.0, -jnp.inf)

    def attend(pair):
        def compute(slots):
            def wait(which):
                @pl.when(pair >= ready[0])
                def _():
                    finish((which,), pair, slots)

            n = slots * kv
            bias = jnp.concatenate([head_bias[:, : min(n, size)]] * max(n // size, 1), axis=1)
            column = lax.broadcasted_iota(jnp.int32, (1, n), 1)
            wait(0)
            scores = []
            for i in range(2):
                row = order[2 * pair + i]
                q = q_ref[:, row].reshape(lanes, size)
                s = lax.dot_general(
                    q,
                    k_buf[2 * pair + i, :n],
                    (((1,), (1,)), ((), ())),
                    preferred_element_type=jnp.float32,
                )
                closed = jnp.where(column < lengths[row] * kv, 0.0, -jnp.inf)
                scores.append(s + (bias + closed))
            highest = [jnp.max(s, axis=1, keepdims=True) * scale for s in scores]
            weights = [jnp.exp2(s * scale - h) for s, h in zip(scores, highest)]
            totals = [jnp.sum(p, axis=1, keepdims=True) for p in weights]
            wait(1)
            for i in range(2):
                o = jnp.dot(
                    weights[i].astype(jnp.bfloat16),
                    v_buf[2 * pair + i, :n],
                    preferred_element_type=jnp.float32,
                )
                spot = 2 * (pair - done) + i
                o_ref[spot] = o / totals[i]
                lse = highest[i] + jnp.log(totals[i]) * LOG2E
                lse_ref[spot] = jnp.broadcast_to(lse, (lanes, size))

        by_length(lengths[order[2 * pair]], sizes, compute)

    if pairs[1] - pairs[0] == 1:
        attend(pairs[0])
    else:
        pl.loop(*pairs)(attend)
    for pair in range(max(pairs[1], ready[0]), ready[1]):
        by_length(lengths[order[2 * pair]], sizes, functools.partial(finish, (0, 1), pair))
    for copy in w_copies:
        copy.wait()


def like(x):
    return pltpu.VMEM(x.shape, x.dtype)


def cache_attention(pairs, ready, rows_args, caches, weights, quarter, buffers, packed, sizes, after):
    lengths, order, queries = rows_args
    keys, values = caches
    rows, steps, _, heads, size = (keys.shape[0], *queries.shape)
    slots = sizes[-1]
    scale = LOG2E / math.sqrt(size)
    count = 2 * (pairs[1] - pairs[0])
    piece = pltpu.VMEM((count, steps * heads, size), jnp.float32)
    operands = [pinned(x, pltpu.SMEM) for x in (lengths, order)]
    operands += [pinned(queries, pltpu.VMEM)]
    operands += [pinned(x) for x in (keys, values, weights)]
    aliases = {len(operands) + i: i for i in range(len(buffers))}
    specs = [SMEM, SMEM, VMEM, HBM, HBM, HBM] + [VMEM] * len(buffers) + [ANY] * len(after)
    specs += [VMEM] * len(packed)
    operands += [pinned(b, pltpu.VMEM) for b in buffers] + after + packed
    out_shape = [pltpu.VMEM(x.shape, x.dtype) for x in (keys, values, weights)] + [piece] * 2
    if packed:
        out_shape.append(pltpu.VMEM((len(packed),) + packed[0].shape, packed[0].dtype))
    return pl.pallas_call(
        functools.partial(attend_cache, pairs, ready, sizes, scale, quarter, len(packed)),
        out_shape=out_shape,
        in_specs=specs,
        out_specs=[VMEM] * len(out_shape),
        input_output_aliases=aliases,
        scratch_shapes=[
            pltpu.SemaphoreType.DMA((rows // 2, 2, 2)),
            pltpu.SemaphoreType.DMA((4,)),
        ],
        compiler_params=pltpu.CompilerParams(vmem_limit_bytes=8 * MIB),
        cost_estimate=pl.CostEstimate(
            flops=4 * steps * heads * count * keys.shape[1] * size,
            bytes_accessed=4 * count * keys.shape[1] * size + weights[0].size,
            transcendentals=steps * heads * count * keys.shape[1],
        ),
        name="cache_attention",
    )(*operands)


def project_old(part, lay, n_hidden, n_packed, *refs):
    refs = list(refs)
    tp = lax.axis_index("tp")
    w_hbm = refs[1]
    sems = refs.pop()
    if part == 0:
        hidden = refs[2 : 2 + n_hidden]
        packed = refs[2 + n_hidden : 2 + n_hidden + n_packed]
        w_buf, out_ref, h_ref, pack_ref = refs[-4:]
    else:
        h_ref = refs[2]
        w_buf, out_ref = refs[-2:]
    copies = quarter_copies(2 + part, w_hbm, w_buf, sems)
    for copy in copies:
        copy.start()
    if part == 0:
        for i, h in enumerate(hidden):
            h_ref[lax.rem(tp + i, lay.tp)] = h[...]
        for i, ref in enumerate(packed):
            pack_ref[i] = ref[...]
    features = h_ref.shape[2]
    chunk = min(features, 1024)
    total = jnp.zeros(out_ref.shape, jnp.float32)
    for t in range(lay.tp):
        if part == 1 and 2 * t == lay.tp:
            for copy in copies:
                copy.wait()
        for low in range(0, features, chunk):
            start = t * features + low
            total += jnp.dot(
                h_ref[t, :, low : low + chunk],
                w_buf[part, start : start + chunk, :],
                preferred_element_type=jnp.float32,
            )
    out_ref[...] = total
    if part == 0:
        for copy in copies:
            copy.wait()


def project(part, lay, w_buf, weights, hidden, packed, after):
    tokens, features = hidden[0].shape[-2:]
    operands = [pinned(w_buf, pltpu.VMEM), pinned(weights)]
    specs = [VMEM, HBM] + [VMEM] * (len(hidden) + len(packed)) + [ANY] * len(after)
    out_shape = [like(w_buf), pltpu.VMEM((tokens, weights.shape[2]), jnp.float32)]
    if part == 0:
        operands += hidden + packed + after
        out_shape.append(pltpu.VMEM((lay.tp, tokens, features), jnp.bfloat16))
        out_shape.append(pltpu.VMEM((len(packed),) + packed[0].shape, packed[0].dtype))
    else:
        operands += [pinned(h, pltpu.VMEM) for h in hidden] + after
    return pl.pallas_call(
        functools.partial(project_old, part, lay, len(hidden), len(packed)),
        out_shape=out_shape,
        in_specs=specs,
        out_specs=[VMEM] * len(out_shape),
        input_output_aliases={0: 0},
        scratch_shapes=[pltpu.SemaphoreType.DMA((4,))],
        compiler_params=pltpu.CompilerParams(vmem_limit_bytes=8 * MIB),
        cost_estimate=pl.CostEstimate(
            flops=2 * tokens * weights[0].size, bytes_accessed=weights.size, transcendentals=0
        ),
        name="project",
    )(*operands)


def merge_all(lay, plan, n_caches, scale, *refs):
    refs = list(refs)

    def take(n):
        out = refs[:n]
        del refs[:n]
        return out

    (weights,) = take(1)
    downs = take(len(plan))
    h_buf, *olds = take(3)
    order, q_ref = take(2)
    caches = [take(2) for _ in range(n_caches)]
    m_hbm, out_hbm, m_buf, u_parts, u_buf, out_buf, sems, out_sems = refs

    pairs, depth, width = m_buf.shape[1:]
    cut = min(width, 256)
    lanes = downs[0].shape[-1]
    tiles = depth // lanes
    fsdp, grp, tp = (lax.axis_index(a) for a in AXES)
    z, core = fsdp // 2, lax.rem(fsdp, 2)
    place = grp * lay.depth + jnp.where(lax.rem(grp, 2) == 0, z, lay.depth - 1 - z)
    per_lane = lay.fsdp * lay.grp // lay.tp

    shards = []
    for (steps, flip), down in zip(plan, downs):
        for i, step in enumerate(steps):
            spot = lax.rem(place + (lay.ring + step), lay.ring)
            g = spot // lay.depth
            along = lax.rem(spot, lay.depth)
            zz = jnp.where(lax.rem(g, 2) == 0, along, lay.depth - 1 - along)
            shards.append(
                (
                    down.at[i] if len(steps) > 1 else down,
                    (zz * 2 + (1 - core if flip else core)) * lay.grp + g,
                )
            )

    columns = width // per_lane
    for down, index in shards:

        @pl.when(index // per_lane == tp)
        def _():
            u_parts[lax.rem(index, per_lane)] = down[pairs * tiles, :, : pairs * columns]

    for k in range(pairs):
        u_buf[k] = ADAPTER_SCALING * jnp.concatenate(
            [u_parts[i, :, k * columns : (k + 1) * columns] for i in range(per_lane)], axis=1
        )

    new = []
    for k in range(pairs):
        low = jnp.zeros((h_buf.shape[1], u_buf.shape[1]), jnp.float32)
        for down, index in shards:
            column = pl.multiple_of(lax.rem(index, per_lane) * depth, depth)
            low += lax.dot_general(
                h_buf[index // per_lane, :, pl.ds(column, depth)],
                jnp.concatenate([down[k * tiles + i] for i in range(tiles)], axis=1),
                (((1,), (1,)), ((), ())),
                preferred_element_type=jnp.float32,
            )
        high = low.astype(jnp.bfloat16)
        rest = (low - high.astype(jnp.float32)).astype(jnp.bfloat16)
        new.append(
            (
                olds[k][...]
                + jnp.dot(high, u_buf[k], preferred_element_type=jnp.float32)
                + jnp.dot(rest, u_buf[k], preferred_element_type=jnp.float32)
            ).astype(jnp.bfloat16)
        )
    finish_row = new_token_attention(q_ref, order, caches, new, out_buf, scale)
    spots = q_ref.shape[1]

    def out_copy(spot):
        return pltpu.make_async_copy(
            out_buf.at[:, spot], out_hbm.at[:, order[spot]], out_sems.at[spot]
        )

    chunk = min(depth, 256)
    copies = []
    rows_done = 0
    for j, (down, index) in enumerate(shards):
        start = pl.multiple_of(index * depth, depth)
        for k in range(pairs):
            for begin in range(0, depth, chunk):
                rows = slice(begin, begin + chunk)
                tile = k * tiles + begin // lanes
                d = jnp.concatenate([down[tile + i] for i in range(chunk // lanes)], axis=1)
                for side in range(width // cut):
                    cols = slice(side * cut, (side + 1) * cut)
                    added = lax.dot_general(
                        d,
                        u_buf[k, :, cols],
                        (((0,), (0,)), ((), ())),
                        preferred_element_type=jnp.float32,
                    )
                    w = weights[k, pl.ds(start + begin, chunk), cols]
                    m_buf[j, k, rows, cols] = (w.astype(jnp.float32) + added).astype(jnp.bfloat16)
            copy = pltpu.make_async_copy(
                m_buf.at[j, k], m_hbm.at[k, pl.ds(start, depth), :], sems.at[j, k]
            )
            copy.start()
            copies.append(copy)
        while rows_done < min(spots, (j + 1) * spots // (len(shards) - 2)):
            finish_row(rows_done)
            out_copy(rows_done).start()
            rows_done += 1
    for copy in copies + [out_copy(spot) for spot in range(spots)]:
        copy.wait()


def new_token_attention(q_ref, order, caches, new, out_buf, scale):
    steps, rows, heads, size = q_ref.shape
    kv = new[0].shape[1] // size
    new = [
        jnp.concatenate([x[:, g * size : (g + 1) * size] for g in range(kv)], axis=0) for x in new
    ]
    n = kv * steps * rows
    lanes = steps * heads
    left = lax.broadcasted_iota(jnp.int32, (lanes, n), 0)
    right = lax.broadcasted_iota(jnp.int32, (lanes, n), 1)
    same_head = over(within(left, heads), heads // kv) == over(right, steps * rows)
    earlier = within(over(right, rows), steps) <= over(left, heads)
    right_row = jnp.where(same_head & earlier, within(right, rows), -1)
    spots = [(o, lse, i) for o, lse in caches for i in range(o.shape[0])]

    def finish_row(spot):
        o_ref, lse_ref, i = spots[spot]
        row = order[spot]
        q = q_ref[:, row].reshape(lanes, size)
        s = lax.dot_general(
            q, new[0], (((1,), (1,)), ((), ())), preferred_element_type=jnp.float32
        )
        s = jnp.where(right_row == row, s * scale, -jnp.inf)
        lse = lse_ref[i]
        highest = jnp.maximum(jnp.max(s, axis=1, keepdims=True), lse)
        p = jnp.exp2(s - highest[:, :n])
        old = jnp.exp2(lse - highest)
        divisor = jnp.sum(p, axis=1, keepdims=True) + old
        o = old * o_ref[i] + jnp.dot(
            p.astype(jnp.bfloat16), new[1], preferred_element_type=jnp.float32
        )
        out_buf[:, spot] = (o / divisor).reshape(steps, heads, size).astype(out_buf.dtype)

    return finish_row


def merge(lay, shape, entries, weights, states, olds, order, queries, caches):
    pairs, total, width = shape
    rank = entries[0][2].shape[-2]
    depth = total // (lay.fsdp * lay.grp)
    per_lane = lay.fsdp * lay.grp // lay.tp
    n = sum(len(e[0]) for e in entries)
    operands = [pinned(weights, pltpu.VMEM)] + [e[2] for e in entries]
    operands += [states, *olds, pinned(order, pltpu.SMEM), pinned(queries, pltpu.VMEM), *caches]
    specs = [VMEM] * len(operands)
    specs[-2 - len(caches)] = SMEM
    return pl.pallas_call(
        functools.partial(
            merge_all,
            lay,
            [e[:2] for e in entries],
            len(caches) // 2,
            LOG2E / math.sqrt(queries.shape[3]),
        ),
        out_shape=(pltpu.HBM(shape, jnp.bfloat16), pltpu.HBM(queries.shape, jnp.bfloat16)),
        in_specs=specs,
        out_specs=(HBM, HBM),
        scratch_shapes=[
            pltpu.VMEM((n, pairs, depth, width), jnp.bfloat16),
            pltpu.VMEM((per_lane, rank, pairs * width // per_lane), jnp.bfloat16),
            pltpu.VMEM((pairs, rank, width), jnp.bfloat16),
            pltpu.VMEM(queries.shape, jnp.bfloat16),
            pltpu.SemaphoreType.DMA((n, pairs)),
            pltpu.SemaphoreType.DMA((queries.shape[1],)),
        ],
        compiler_params=pltpu.CompilerParams(vmem_limit_bytes=24 * MIB),
        cost_estimate=pl.CostEstimate(
            flops=2 * pairs * total * width * rank,
            bytes_accessed=2 * pairs * total * width,
            transcendentals=0,
        ),
        name="merge",
    )(*operands)


def shards(
    lay,
    hidden_states,
    queries,
    cache_keys,
    cache_values,
    cache_lengths,
    projection_weight_matrices,
    factor_down,
    factor_up,
):
    send = functools.partial(lax.ppermute, axis_name=AXES)
    steps, rows, features = hidden_states.shape
    slots, kv, size = cache_keys.shape[1:]
    shape = projection_weight_matrices.shape
    sizes = tuple(slots * i // 24 for i in (1, 4, 8, 16, 24))
    own = jnp.swapaxes(factor_down, 1, 2)
    tokens = hidden_states.reshape(steps * rows, features)
    keys = cache_keys.reshape(rows, slots * kv, size)
    values = cache_values.reshape(rows, slots * kv, size)
    swap, ring = lay.core_swap(), {d: lay.ring_step(d) for d in (1, -1)}
    shard, *rows_args = begin(own, factor_up, cache_lengths, queries)
    lengths, order, q = rows_args
    projections = projection_weight_matrices
    entries = [((0,), False, shard)]
    caches, olds = [], []
    last_step = lay.ring // 2

    def ring_sends(came, step):
        back = lay.ring_step(-1, 1) if step == last_step else ring[-1]
        return {-1: send(came[-1], perm=back), 1: send(came[1], perm=ring[1])}

    hidden = [tokens] + [send(tokens, perm=lay.feature_step(i)) for i in range(1, lay.tp)]
    came = ring_sends({1: shard, -1: shard}, 1)
    *buffers, o, lse = cache_attention(
        (0, 1), (0, 2), rows_args, (keys, values), projections, 0, [], [], sizes, [shard]
    )
    caches += [o, lse]
    came, token = after_all(came, o)

    packed = [shard, came[1], came[-1]]
    entries += [((-d,), False, came[d]) for d in ring]
    came = ring_sends(came, 2)
    *buffers, o, lse, packed = cache_attention(
        (1, rows // 4 * 2),
        (2, rows // 4 * 2),
        rows_args,
        (keys, values),
        projections,
        1,
        buffers,
        packed,
        sizes,
        [token],
    )
    caches += [o, lse]
    (came, hidden, packed), token = after_all((came, hidden, packed), o)

    w_buf, packed = buffers[2], [packed]
    for step in range(3, last_step + 1):
        entries += [((-d * (step - 1),), False, came[d]) for d in ring]
        arrived, came = came, ring_sends(came, step)
        swapped = [send(x, perm=swap) for x in packed]
        if step == 3:
            w_buf, old, states, packed = project(
                0, lay, w_buf, projections, hidden, [arrived[1], arrived[-1]], [token]
            )
            places, packed = [(0, -1, 1)], [packed]
        elif step == 4:
            w_buf, old = project(1, lay, w_buf, projections, [states], [], [token])
            places, packed = [(-2, 2), (-3,), (3,)], []
        else:
            places, packed = [(1 - step,), (step - 1,)], []
        if step < 5:
            olds.append(old)
            token = old
        (came, swapped, packed), token = after_all((came, swapped, packed), token)
        entries += [(p, True, x) for p, x in zip(places, swapped)]
        packed += [came[1], came[-1]]
    entries += [((-last_step,), False, came[1]), ((last_step,), True, came[-1])]
    return tuple(merge(lay, shape, entries, w_buf, states, olds, order, q, caches))


def solution(mesh):
    return jax.shard_map(
        functools.partial(shards, Layout(mesh)),
        mesh=mesh,
        in_specs=(
            P(None, ("fsdp", "grp"), "tp"),
            P(None, ("fsdp", "grp"), "tp", None),
            P(("fsdp", "grp"), None, "tp", None),
            P(("fsdp", "grp"), None, "tp", None),
            P(("fsdp", "grp")),
            P(None, None, "tp"),
            P(None, ("fsdp", "grp"), None),
            P(None, None, ("fsdp", "grp")),
        ),
        out_specs=(P(None, None, "tp"), P(None, ("fsdp", "grp"), "tp", None)),
        check_vma=False,
    )
```

```python
import functools
import math

import jax
import jax.numpy as jnp
from jax import lax
from jax.experimental import pallas as pl
from jax.experimental.pallas import tpu as pltpu
from jax.sharding import PartitionSpec as P

AXES = ("fsdp", "grp", "tp")
ADAPTER_SCALING = 2.0
LOG2E = math.log2(math.e)
MIB = 1024 * 1024
ANY = pl.BlockSpec(memory_space=pl.ANY)
HBM = pl.BlockSpec(memory_space=pltpu.HBM)
VMEM = pl.BlockSpec(memory_space=pltpu.VMEM)
SMEM = pl.BlockSpec(memory_space=pltpu.SMEM)


class Layout:
    def __init__(self, mesh):
        self.fsdp, self.grp, self.tp = (mesh.shape[a] for a in AXES)
        self.depth = self.fsdp // 2
        self.ring = self.depth * self.grp
        self.block = self.depth // self.tp

    def flat(self, z, core, g, t):
        return ((z * 2 + core) * self.grp + g) * self.tp + t

    def devices(self):
        for z in range(self.depth):
            for core in range(2):
                for g in range(self.grp):
                    for t in range(self.tp):
                        yield z, core, g, t

    def place(self, z, g):
        return g * self.depth + (z if g % 2 == 0 else self.depth - 1 - z)

    def at(self, position):
        g, z = divmod(position, self.depth)
        return (z if g % 2 == 0 else self.depth - 1 - z), g

    def ring_step(self, step, flip=0):
        pairs = []
        for z, core, g, t in self.devices():
            to_z, to_g = self.at((self.place(z, g) + step) % self.ring)
            pairs.append((self.flat(z, core, g, t), self.flat(to_z, core ^ flip, to_g, t)))
        return pairs

    def core_swap(self):
        return [
            (self.flat(z, c, g, t), self.flat(z, 1 - c, g, t)) for z, c, g, t in self.devices()
        ]

    def feature_step(self, step):
        return [
            (self.flat(z, c, g, (t + step) % self.tp), self.flat(z, c, g, t))
            for z, c, g, t in self.devices()
        ]


BRIEF = pl.CostEstimate(flops=1000, bytes_accessed=1000, transcendentals=0)


def over(x, n):
    return x >> (n.bit_length() - 1) if n & (n - 1) == 0 else x // n


def within(x, n):
    return x & (n - 1) if n & (n - 1) == 0 else x % n


def after_all(arrays, token):
    return lax.optimization_barrier((arrays, token))


def pinned(x, space=pltpu.HBM):
    return pltpu.with_memory_space_constraint(x, space)


def sort_rows(lengths, order):
    rows = lengths.shape[0]
    held = [lengths[r] for r in range(rows)]
    for r in range(rows):
        rank = jnp.int32(0)
        for other in range(rows):
            if other != r:
                ahead = held[other] >= held[r] if other < r else held[other] > held[r]
                rank = rank + ahead.astype(jnp.int32)
        order[rank] = r


def by_length(length, sizes, act):
    below = 0
    for slots in sizes:

        @pl.when((length > below) & (length <= slots))
        def _():
            act(slots)

        below = slots


def quarter_copies(quarter, src, dst, sems):
    k, half = divmod(quarter, 2)
    rows = dst.shape[1] // (2 * sems.shape[0])
    spans = [
        pl.ds((half * sems.shape[0] + i) * rows, rows) for i in range(sems.shape[0])
    ]
    return [
        pltpu.make_async_copy(src.at[k, span], dst.at[k, span], sems.at[i])
        for i, span in enumerate(spans)
    ]


def begin_all(down, up, len_hbm, q_hbm, shard, lengths, order, q_ref, up_buf, sems, more):
    lanes = shard.shape[2]
    count, _, depth = down.shape
    tiles = depth // lanes
    copies = [
        pltpu.make_async_copy(
            down.at[k, :, pl.ds(i * lanes, lanes)], shard.at[k * tiles + i], sems.at[k, i]
        )
        for k in range(count)
        for i in range(tiles)
    ]
    up_copy = pltpu.make_async_copy(up, up_buf, more.at[0])
    len_copy = pltpu.make_async_copy(len_hbm, lengths, more.at[1])
    q_copy = pltpu.make_async_copy(q_hbm, q_ref, more.at[2])
    for copy in [up_copy, len_copy] + copies + [q_copy]:
        copy.start()
    up_copy.wait()
    columns = jnp.concatenate([up_buf[k] for k in range(count)], axis=1)
    shard[count * tiles, :, : columns.shape[1]] = columns
    len_copy.wait()
    sort_rows(lengths, order)
    for copy in copies + [q_copy]:
        copy.wait()


def begin(down, up, lengths, queries):
    count, rank, depth = down.shape
    tiles = depth // 128
    scalars = pltpu.SMEM(lengths.shape, jnp.int32)
    return pl.pallas_call(
        begin_all,
        out_shape=(
            pltpu.VMEM((count * tiles + 1, rank, 128), down.dtype),
            scalars,
            scalars,
            pltpu.VMEM(queries.shape, queries.dtype),
        ),
        in_specs=[HBM] * 4,
        out_specs=(VMEM, SMEM, SMEM, VMEM),
        scratch_shapes=[
            pltpu.VMEM(up.shape, up.dtype),
            pltpu.SemaphoreType.DMA((count, tiles)),
            pltpu.SemaphoreType.DMA((3,)),
        ],
        compiler_params=pltpu.CompilerParams(vmem_limit_bytes=2 * MIB),
        cost_estimate=BRIEF,
        name="begin",
    )(pinned(down), pinned(up), pinned(lengths), pinned(queries))


def attend_cache(pairs, ready, sizes, scale, quarter, *refs):
    lengths, order, q_ref, k_hbm, v_hbm, w_hbm = refs[:6]
    sems, w_sems = refs[-2:]
    k_buf, v_buf, w_buf, *outs = refs[-7:-2]
    done = pairs[0]
    o_ref, lse_ref = outs[:2]
    steps, _, heads, size = q_ref.shape
    kv = k_hbm.shape[1] // sizes[-1]
    lanes = steps * heads

    def copies(which, pair, slots):
        span = pl.ds(0, slots * kv)
        hbm, buf = ((k_hbm, k_buf), (v_hbm, v_buf))[which]
        return [
            pltpu.make_async_copy(
                hbm.at[order[2 * pair + i], span],
                buf.at[2 * pair + i, span],
                sems.at[pair, i, which],
            )
            for i in range(2)
        ]

    def start(pair, slots):
        for copy in copies(0, pair, slots) + copies(1, pair, slots):
            copy.start()

    def finish(which, pair, slots):
        for i in which:
            for copy in copies(i, pair, slots):
                copy.wait()

    for pair in range(*ready):
        by_length(lengths[order[2 * pair]], sizes, functools.partial(start, pair))
    w_copies = quarter_copies(quarter, w_hbm, w_buf, w_sems)
    for copy in w_copies:
        copy.start()

    row_head = over(within(lax.broadcasted_iota(jnp.int32, (lanes, size), 0), heads), heads // kv)
    slot_head = within(lax.broadcasted_iota(jnp.int32, (lanes, size), 1), kv)
    head_bias = jnp.where(row_head == slot_head, 0.0, -jnp.inf)

    def attend(pair):
        def compute(slots):
            def wait(which):
                @pl.when(pair >= ready[0])
                def _():
                    finish((which,), pair, slots)

            n = slots * kv
            bias = jnp.concatenate([head_bias[:, : min(n, size)]] * max(n // size, 1), axis=1)
            column = lax.broadcasted_iota(jnp.int32, (1, n), 1)
            wait(0)
            scores = []
            for i in range(2):
                row = order[2 * pair + i]
                q = q_ref[:, row].reshape(lanes, size)
                s = lax.dot_general(
                    q,
                    k_buf[2 * pair + i, :n],
                    (((1,), (1,)), ((), ())),
                    preferred_element_type=jnp.float32,
                )
                closed = jnp.where(column < lengths[row] * kv, 0.0, -jnp.inf)
                scores.append(s + (bias + closed))
            highest = [jnp.max(s, axis=1, keepdims=True) * scale for s in scores]
            weights = [jnp.exp2(s * scale - h) for s, h in zip(scores, highest)]
            totals = [jnp.sum(p, axis=1, keepdims=True) for p in weights]
            wait(1)
            for i in range(2):
                o = jnp.dot(
                    weights[i].astype(jnp.bfloat16),
                    v_buf[2 * pair + i, :n],
                    preferred_element_type=jnp.float32,
                )
                spot = 2 * (pair - done) + i
                o_ref[spot] = o / totals[i]
                lse = highest[i] + jnp.log(totals[i]) * LOG2E
                lse_ref[spot] = jnp.broadcast_to(lse, (lanes, size))

        by_length(lengths[order[2 * pair]], sizes, compute)

    if pairs[1] - pairs[0] == 1:
        attend(pairs[0])
    else:
        pl.loop(*pairs)(attend)
    for pair in range(max(pairs[1], ready[0]), ready[1]):
        by_length(lengths[order[2 * pair]], sizes, functools.partial(finish, (0, 1), pair))
    for copy in w_copies:
        copy.wait()


def like(x):
    return pltpu.VMEM(x.shape, x.dtype)


def cache_attention(pairs, ready, rows_args, caches, weights, quarter, buffers, sizes, after):
    lengths, order, queries = rows_args
    keys, values = caches
    rows, steps, _, heads, size = (keys.shape[0], *queries.shape)
    slots = sizes[-1]
    scale = LOG2E / math.sqrt(size)
    count = 2 * (pairs[1] - pairs[0])
    piece = pltpu.VMEM((count, steps * heads, size), jnp.float32)
    operands = [pinned(x, pltpu.SMEM) for x in (lengths, order)]
    operands += [pinned(queries, pltpu.VMEM)]
    operands += [pinned(x) for x in (keys, values, weights)]
    aliases = {len(operands) + i: i for i in range(len(buffers))}
    specs = [SMEM, SMEM, VMEM, HBM, HBM, HBM] + [VMEM] * len(buffers) + [ANY] * len(after)
    operands += [pinned(b, pltpu.VMEM) for b in buffers] + after
    out_shape = [pltpu.VMEM(x.shape, x.dtype) for x in (keys, values, weights)] + [piece] * 2
    return pl.pallas_call(
        functools.partial(attend_cache, pairs, ready, sizes, scale, quarter),
        out_shape=out_shape,
        in_specs=specs,
        out_specs=[VMEM] * len(out_shape),
        input_output_aliases=aliases,
        scratch_shapes=[
            pltpu.SemaphoreType.DMA((rows // 2, 2, 2)),
            pltpu.SemaphoreType.DMA((4,)),
        ],
        compiler_params=pltpu.CompilerParams(vmem_limit_bytes=8 * MIB),
        cost_estimate=BRIEF,
        name="cache_attention",
    )(*operands)


def project_old(part, lay, n_hidden, *refs):
    refs = list(refs)
    tp = lax.axis_index("tp")
    if part == 0:
        sems = refs.pop()
        w_hbm, *hidden = refs[1 : 2 + n_hidden]
        w_buf, out_ref, h_ref = refs[-3:]
        copies = quarter_copies(3, w_hbm, w_buf, sems)
        for copy in copies:
            copy.start()
        for i, h in enumerate(hidden):
            h_ref[lax.rem(tp + i, lay.tp)] = h[...]
    else:
        h_ref = refs[1]
        w_buf, out_ref = refs[-2:]
    features = h_ref.shape[2]
    chunk = min(features, 1024)
    total = jnp.zeros(out_ref.shape, jnp.float32)
    for t in range(lay.tp):
        for low in range(0, features, chunk):
            start = t * features + low
            total += jnp.dot(
                h_ref[t, :, low : low + chunk],
                w_buf[part, start : start + chunk, :],
                preferred_element_type=jnp.float32,
            )
    out_ref[...] = total
    if part == 0:
        for copy in copies:
            copy.wait()


def project(part, lay, w_buf, weights, hidden, after):
    tokens, features = hidden[0].shape[-2:]
    out_shape = [like(w_buf), pltpu.VMEM((tokens, weights.shape[2]), jnp.float32)]
    scratch = []
    if part == 0:
        operands = [pinned(weights)] + hidden
        specs = [HBM] + [VMEM] * len(hidden)
        out_shape.append(pltpu.VMEM((lay.tp, tokens, features), jnp.bfloat16))
        scratch = [pltpu.SemaphoreType.DMA((4,))]
    else:
        operands = [pinned(hidden[0], pltpu.VMEM)]
        specs = [VMEM]
    return pl.pallas_call(
        functools.partial(project_old, part, lay, len(hidden)),
        out_shape=out_shape,
        in_specs=[VMEM] + specs + [ANY] * len(after),
        out_specs=[VMEM] * len(out_shape),
        input_output_aliases={0: 0},
        scratch_shapes=scratch,
        compiler_params=pltpu.CompilerParams(vmem_limit_bytes=8 * MIB),
        cost_estimate=BRIEF,
        name="project",
    )(pinned(w_buf, pltpu.VMEM), *operands, *after)


class Place:
    def __init__(self, lay):
        fsdp, grp, self.tp = (lax.axis_index(a) for a in AXES)
        z, self.core = fsdp // 2, lax.rem(fsdp, 2)
        self.lay = lay
        self.own = grp * lay.depth + jnp.where(lax.rem(grp, 2) == 0, z, lay.depth - 1 - z)
        self.per_lane = lay.fsdp * lay.grp // lay.tp

    def find(self, plan, downs):
        lay, found = self.lay, []
        for (steps, flip), down in zip(plan, downs):
            for i, step in enumerate(steps):
                spot = lax.rem(self.own + (lay.ring + step), lay.ring)
                g = spot // lay.depth
                along = lax.rem(spot, lay.depth)
                zz = jnp.where(lax.rem(g, 2) == 0, along, lay.depth - 1 - along)
                core = 1 - self.core if flip else self.core
                found.append(
                    (down.at[i] if len(steps) > 1 else down, (zz * 2 + core) * lay.grp + g)
                )
        return found

    def add_low(self, total, k, shards, h_ref, depth):
        for down, index in shards:
            tiles = depth // down.shape[-1]
            column = pl.multiple_of(lax.rem(index, self.per_lane) * depth, depth)
            total += lax.dot_general(
                h_ref[index // self.per_lane, :, pl.ds(column, depth)],
                jnp.concatenate([down[k * tiles + i] for i in range(tiles)], axis=1),
                (((1,), (1,)), ((), ())),
                preferred_element_type=jnp.float32,
            )
        return total


def low_part(lay, plan, depth, *refs):
    downs, h_ref, out_ref = refs[: len(plan)], refs[len(plan)], refs[-1]
    place = Place(lay)
    shards = place.find(plan, downs)
    for k in range(out_ref.shape[0]):
        old = refs[len(plan) + 1][k]
        out_ref[k] = place.add_low(old, k, shards, h_ref, depth)


def low_start(lay, plan, depth, *refs):
    downs, h_ref, out_ref = refs[: len(plan)], refs[len(plan)], refs[-1]
    place = Place(lay)
    shards = place.find(plan, downs)
    for k in range(out_ref.shape[0]):
        out_ref[k] = place.add_low(jnp.zeros(out_ref.shape[1:], jnp.float32), k, shards, h_ref, depth)


def project_low(lay, entries, states, pairs, depth, old, after):
    operands = [e[2] for e in entries] + [pinned(states, pltpu.VMEM)]
    body = low_start
    if old is not None:
        body = low_part
        operands.append(pinned(old, pltpu.VMEM))
    rank = entries[0][2].shape[-2]
    return pl.pallas_call(
        functools.partial(body, lay, [e[:2] for e in entries], depth),
        out_shape=pltpu.VMEM((pairs, states.shape[1], rank), jnp.float32),
        in_specs=[VMEM] * len(operands) + [ANY] * len(after),
        out_specs=VMEM,
        compiler_params=pltpu.CompilerParams(vmem_limit_bytes=2 * MIB),
        cost_estimate=BRIEF,
        name="project_low",
    )(*operands, *after)


def merge_all(lay, plan, n_low, n_caches, scale, *refs):
    refs = list(refs)

    def take(n):
        out = refs[:n]
        del refs[:n]
        return out

    (weights,) = take(1)
    downs = take(len(plan))
    h_buf, low_ref, *olds = take(4)
    order, q_ref = take(2)
    caches = [take(2) for _ in range(n_caches)]
    m_hbm, out_ref, m_buf, u_parts, u_buf, sems = refs

    pairs, depth, width = m_buf.shape[1:]
    cut = min(width, 256)
    lanes = downs[0].shape[-1]
    tiles = depth // lanes
    place = Place(lay)
    per_lane = place.per_lane
    shards = place.find(plan, downs)

    columns = width // per_lane
    for down, index in shards:

        @pl.when(index // per_lane == place.tp)
        def _():
            u_parts[lax.rem(index, per_lane)] = down[pairs * tiles, :, : pairs * columns]

    for k in range(pairs):
        u_buf[k] = ADAPTER_SCALING * jnp.concatenate(
            [u_parts[i, :, k * columns : (k + 1) * columns] for i in range(per_lane)], axis=1
        )

    chunk = min(depth, 256)
    copies = []
    for j, (down, index) in enumerate(shards):
        start = pl.multiple_of(index * depth, depth)
        for k in range(pairs):
            for begin in range(0, depth, chunk):
                rows = slice(begin, begin + chunk)
                tile = k * tiles + begin // lanes
                d = jnp.concatenate([down[tile + i] for i in range(chunk // lanes)], axis=1)
                for side in range(width // cut):
                    cols = slice(side * cut, (side + 1) * cut)
                    added = lax.dot_general(
                        d,
                        u_buf[k, :, cols],
                        (((0,), (0,)), ((), ())),
                        preferred_element_type=jnp.float32,
                    )
                    w = weights[k, pl.ds(start + begin, chunk), cols]
                    m_buf[j, k, rows, cols] = (w.astype(jnp.float32) + added).astype(jnp.bfloat16)
            copy = pltpu.make_async_copy(
                m_buf.at[j, k], m_hbm.at[k, pl.ds(start, depth), :], sems.at[j, k]
            )
            copy.start()
            copies.append(copy)

    new = []
    for k in range(pairs):
        low = place.add_low(low_ref[k], k, shards[n_low:], h_buf, depth)
        high = low.astype(jnp.bfloat16)
        rest = (low - high.astype(jnp.float32)).astype(jnp.bfloat16)
        new.append(
            (
                olds[k][...]
                + jnp.dot(high, u_buf[k], preferred_element_type=jnp.float32)
                + jnp.dot(rest, u_buf[k], preferred_element_type=jnp.float32)
            ).astype(jnp.bfloat16)
        )
    add_new_tokens(q_ref, order, caches, new, out_ref, scale)
    for copy in copies:
        copy.wait()


def add_new_tokens(q_ref, order, caches, new, out_ref, scale):
    steps, rows, heads, size = q_ref.shape
    kv = new[0].shape[1] // size
    new = [
        jnp.concatenate([x[:, g * size : (g + 1) * size] for g in range(kv)], axis=0) for x in new
    ]
    n = kv * steps * rows
    lanes = steps * heads
    left = lax.broadcasted_iota(jnp.int32, (lanes, n), 0)
    right = lax.broadcasted_iota(jnp.int32, (lanes, n), 1)
    same_head = over(within(left, heads), heads // kv) == over(right, steps * rows)
    earlier = within(over(right, rows), steps) <= over(left, heads)
    right_row = jnp.where(same_head & earlier, within(right, rows), -1)
    spots = [(o, lse, i) for o, lse in caches for i in range(o.shape[0])]
    for spot, (o_ref, lse_ref, i) in enumerate(spots):
        row = order[spot]
        q = q_ref[:, row].reshape(lanes, size)
        s = lax.dot_general(
            q, new[0], (((1,), (1,)), ((), ())), preferred_element_type=jnp.float32
        )
        s = jnp.where(right_row == row, s * scale, -jnp.inf)
        lse = lse_ref[i]
        highest = jnp.maximum(jnp.max(s, axis=1, keepdims=True), lse)
        p = jnp.exp2(s - highest[:, :n])
        old = jnp.exp2(lse - highest)
        divisor = jnp.sum(p, axis=1, keepdims=True) + old
        o = old * o_ref[i] + jnp.dot(
            p.astype(jnp.bfloat16), new[1], preferred_element_type=jnp.float32
        )
        out_ref[:, row] = (o / divisor).reshape(steps, heads, size).astype(out_ref.dtype)


def merge(lay, shape, entries, n_low, weights, states, low, olds, order, queries, caches):
    pairs, total, width = shape
    rank = entries[0][2].shape[-2]
    depth = total // (lay.fsdp * lay.grp)
    per_lane = lay.fsdp * lay.grp // lay.tp
    n = sum(len(e[0]) for e in entries)
    operands = [pinned(weights, pltpu.VMEM)] + [e[2] for e in entries]
    operands += [states, low, *olds, pinned(order, pltpu.SMEM), pinned(queries, pltpu.VMEM)]
    operands += caches
    specs = [VMEM] * len(operands)
    specs[-2 - len(caches)] = SMEM
    return pl.pallas_call(
        functools.partial(
            merge_all,
            lay,
            [e[:2] for e in entries],
            sum(len(e[0]) for e in entries[:n_low]),
            len(caches) // 2,
            LOG2E / math.sqrt(queries.shape[3]),
        ),
        out_shape=(
            pltpu.HBM(shape, jnp.bfloat16),
            jax.ShapeDtypeStruct(queries.shape, jnp.bfloat16),
        ),
        in_specs=specs,
        out_specs=(HBM, VMEM),
        scratch_shapes=[
            pltpu.VMEM((n, pairs, depth, width), jnp.bfloat16),
            pltpu.VMEM((per_lane, rank, pairs * width // per_lane), jnp.bfloat16),
            pltpu.VMEM((pairs, rank, width), jnp.bfloat16),
            pltpu.SemaphoreType.DMA((n, pairs)),
        ],
        compiler_params=pltpu.CompilerParams(vmem_limit_bytes=24 * MIB),
        cost_estimate=BRIEF,
        name="merge",
    )(*operands)


def shards(
    lay,
    hidden_states,
    queries,
    cache_keys,
    cache_values,
    cache_lengths,
    projection_weight_matrices,
    factor_down,
    factor_up,
):
    send = functools.partial(lax.ppermute, axis_name=AXES)
    steps, rows, features = hidden_states.shape
    slots, kv, size = cache_keys.shape[1:]
    shape = projection_weight_matrices.shape
    sizes = tuple(slots * i // 24 for i in (1, 4, 8, 16, 24))
    own = jnp.swapaxes(factor_down, 1, 2)
    tokens = hidden_states.reshape(steps * rows, features)
    keys = cache_keys.reshape(rows, slots * kv, size)
    values = cache_values.reshape(rows, slots * kv, size)
    swap, ring = lay.core_swap(), {d: lay.ring_step(d) for d in (1, -1)}
    shard, *rows_args = begin(own, factor_up, cache_lengths, queries)
    lengths, order, q = rows_args
    projections = projection_weight_matrices
    pair_count = rows // 2
    depth = own.shape[2]
    last_step = lay.ring // 2
    back = lay.ring_step(-1, 1)
    caches, olds = [], []
    buffers = []

    def attention(pairs, ready, quarter, after):
        nonlocal buffers
        out = cache_attention(
            pairs, ready, rows_args, (keys, values), projections, quarter, buffers, sizes, after
        )
        buffers = list(out[:3])
        caches.extend(out[3:])
        return out[3]

    def project_one(part, arrays, after):
        out = project(part, lay, buffers[2], projections, arrays, after)
        buffers[2] = out[0]
        olds.append(out[1])
        return out[1], out[2:]

    sent = {d: send(shard, perm=ring[d]) for d in ring}
    hidden = [tokens] + [send(tokens, perm=lay.feature_step(i)) for i in range(1, lay.tp)]
    token = attention((0, 1), (0, 2), 0, [shard])
    entries = [((0,), False, shard)]
    came, swapped = {}, []
    states = low = None
    slot = n_low = 0
    for step in range(1, last_step):
        for d in ring:
            slot += 1
            held = [x for _, x in swapped] + (hidden if slot == 2 else [])
            (came[d], held), token = after_all((sent[d], held), token)
            entries.append(((-d * step,), False, came[d]))
            entries += [(places, True, x) for (places, _), x in zip(swapped, held)]
            sent[d] = send(came[d], perm=back if d < 0 and step + 1 == last_step else ring[d])
            swapped = [((-d * step,), send(came[d], perm=swap))]
            if slot == 1:
                token = attention((1, 2), (2, pair_count), 1, [token])
            elif slot == 2:
                hidden = held[-lay.tp :]
                token = attention((2, pair_count), (pair_count, pair_count), 2, [token])
            elif slot == 3:
                token, (states,) = project_one(0, hidden, [token])
            elif slot == 4:
                swapped.append(((0,), send(shard, perm=swap)))
                token, _ = project_one(1, [states], [token])
            elif slot == 5:
                n_low = len(entries)
                low = project_low(lay, entries, states, shape[0], depth, None, [token])
                token = low
    low = project_low(lay, entries[n_low:], states, shape[0], depth, low, [token])
    forward, low = after_all(sent[1], low)
    entries.append(((-last_step,), False, forward))
    low = project_low(lay, entries[-1:], states, shape[0], depth, low, [])
    n_low = len(entries)
    (last, held), low = after_all((sent[-1], [x for _, x in swapped]), low)
    entries += [(places, True, x) for (places, _), x in zip(swapped, held)]
    entries.append(((last_step,), True, last))
    return tuple(
        merge(lay, shape, entries, n_low, buffers[2], states, low, olds, order, q, caches)
    )


def solution(mesh):
    return jax.shard_map(
        functools.partial(shards, Layout(mesh)),
        mesh=mesh,
        in_specs=(
            P(None, ("fsdp", "grp"), "tp"),
            P(None, ("fsdp", "grp"), "tp", None),
            P(("fsdp", "grp"), None, "tp", None),
            P(("fsdp", "grp"), None, "tp", None),
            P(("fsdp", "grp")),
            P(None, None, "tp"),
            P(None, ("fsdp", "grp"), None),
            P(None, None, ("fsdp", "grp")),
        ),
        out_specs=(P(None, None, "tp"), P(None, ("fsdp", "grp"), "tp", None)),
        check_vma=False,
    )
```

```python
import functools
import math

import jax
import jax.numpy as jnp
from jax import lax
from jax.experimental import pallas as pl
from jax.experimental.pallas import tpu as pltpu
from jax.sharding import PartitionSpec as P

AXES = ("fsdp", "grp", "tp")
ADAPTER_SCALING = 2.0
LOG2E = math.log2(math.e)
MIB = 1024 * 1024
ANY = pl.BlockSpec(memory_space=pl.ANY)
HBM = pl.BlockSpec(memory_space=pltpu.HBM)
VMEM = pl.BlockSpec(memory_space=pltpu.VMEM)
SMEM = pl.BlockSpec(memory_space=pltpu.SMEM)


class Layout:
    def __init__(self, mesh):
        self.fsdp, self.grp, self.tp = (mesh.shape[a] for a in AXES)
        self.depth = self.fsdp // 2
        self.ring = self.depth * self.grp
        self.block = self.depth // self.tp

    def flat(self, z, core, g, t):
        return ((z * 2 + core) * self.grp + g) * self.tp + t

    def devices(self):
        for z in range(self.depth):
            for core in range(2):
                for g in range(self.grp):
                    for t in range(self.tp):
                        yield z, core, g, t

    def place(self, z, g):
        return g * self.depth + (z if g % 2 == 0 else self.depth - 1 - z)

    def at(self, position):
        g, z = divmod(position, self.depth)
        return (z if g % 2 == 0 else self.depth - 1 - z), g

    def ring_step(self):
        pairs = []
        for z, core, g, t in self.devices():
            to_z, to_g = self.at((self.place(z, g) + (1 - 2 * core)) % self.ring)
            pairs.append((self.flat(z, core, g, t), self.flat(to_z, core, to_g, t)))
        return pairs

    def plane_step(self):
        return [
            (
                self.flat(t * self.block + z % self.block, c, g, z // self.block),
                self.flat(z, c, g, t),
            )
            for z, c, g, t in self.devices()
        ]

    def near_step(self, turn, shift):
        pairs = []
        for z, c, g, t in self.devices():
            source = z - z % self.block + (z % self.block + shift) % self.block
            pairs.append(
                (self.flat(source, c, (g + turn) % self.grp, t), self.flat(z, c, g, t))
            )
        return pairs

    def core_swap(self):
        return [
            (self.flat(z, c, g, t), self.flat(z, 1 - c, g, t)) for z, c, g, t in self.devices()
        ]

    def feature_step(self, step):
        return [
            (self.flat(z, c, g, (t + step) % self.tp), self.flat(z, c, g, t))
            for z, c, g, t in self.devices()
        ]


BRIEF = pl.CostEstimate(flops=1000, bytes_accessed=1000, transcendentals=0)


def over(x, n):
    return x >> (n.bit_length() - 1) if n & (n - 1) == 0 else x // n


def within(x, n):
    return x & (n - 1) if n & (n - 1) == 0 else x % n


def after_all(arrays, token):
    return lax.optimization_barrier((arrays, token))


def pinned(x, space=pltpu.HBM):
    return pltpu.with_memory_space_constraint(x, space)


def sort_rows(lengths, order):
    rows = lengths.shape[0]
    held = [lengths[r] for r in range(rows)]
    for r in range(rows):
        rank = jnp.int32(0)
        for other in range(rows):
            if other != r:
                ahead = held[other] >= held[r] if other < r else held[other] > held[r]
                rank = rank + ahead.astype(jnp.int32)
        order[rank] = r


def by_length(length, sizes, act):
    below = 0
    for slots in sizes:

        @pl.when((length > below) & (length <= slots))
        def _():
            act(slots)

        below = slots


def quarter_copies(quarter, src, dst, sems):
    k, half = divmod(quarter, 2)
    rows = dst.shape[1] // (2 * sems.shape[0])
    spans = [
        pl.ds((half * sems.shape[0] + i) * rows, rows) for i in range(sems.shape[0])
    ]
    return [
        pltpu.make_async_copy(src.at[k, span], dst.at[k, span], sems.at[i])
        for i, span in enumerate(spans)
    ]


def up_columns(up):
    return jnp.concatenate([up[k] for k in range(up.shape[0])], axis=1)


def begin_all(down, up, len_hbm, q_hbm, pair, up_pair, lengths, order, q_ref, up_buf, sems, more):
    lanes = pair.shape[3]
    count, _, depth = down.shape
    tiles = depth // lanes
    copies = [
        pltpu.make_async_copy(
            down.at[k, :, pl.ds(i * lanes, lanes)], pair.at[0, k * tiles + i], sems.at[k, i]
        )
        for k in range(count)
        for i in range(tiles)
    ]
    up_copy = pltpu.make_async_copy(up, up_buf, more.at[0])
    len_copy = pltpu.make_async_copy(len_hbm, lengths, more.at[1])
    q_copy = pltpu.make_async_copy(q_hbm, q_ref, more.at[2])
    for copy in [len_copy, up_copy] + copies + [q_copy]:
        copy.start()
    len_copy.wait()
    sort_rows(lengths, order)
    up_copy.wait()
    up_pair[lax.rem(lax.axis_index("fsdp"), 2)] = up_columns(up_buf)
    for copy in copies + [q_copy]:
        copy.wait()


def begin(down, up, lengths, queries):
    count, rank, depth = down.shape
    scalars = pltpu.SMEM(lengths.shape, jnp.int32)
    return pl.pallas_call(
        begin_all,
        out_shape=(
            pltpu.VMEM((2, count * depth // 128, rank, 128), down.dtype),
            pltpu.VMEM((2, rank, count * up.shape[2]), up.dtype),
            scalars,
            scalars,
            pltpu.VMEM(queries.shape, queries.dtype),
        ),
        in_specs=[HBM] * 4,
        out_specs=(VMEM, VMEM, SMEM, SMEM, VMEM),
        scratch_shapes=[
            pltpu.VMEM(up.shape, up.dtype),
            pltpu.SemaphoreType.DMA((count, depth // 128)),
            pltpu.SemaphoreType.DMA((3,)),
        ],
        compiler_params=pltpu.CompilerParams(vmem_limit_bytes=2 * MIB),
        cost_estimate=BRIEF,
        name="begin",
    )(pinned(down), pinned(up), pinned(lengths), pinned(queries))


def pack_other(down, up, _, __, pair, up_pair):
    lanes = pair.shape[3]
    count, _, depth = down.shape
    tiles = depth // lanes
    for k in range(count):
        for i in range(tiles):
            pair[1, k * tiles + i] = down[k, :, i * lanes : (i + 1) * lanes]
    up_pair[1 - lax.rem(lax.axis_index("fsdp"), 2)] = up_columns(up)


def pack(down, up, pair, up_pair):
    return pl.pallas_call(
        pack_other,
        out_shape=(like(pair), like(up_pair)),
        in_specs=[VMEM] * 4,
        out_specs=(VMEM, VMEM),
        input_output_aliases={2: 0, 3: 1},
        compiler_params=pltpu.CompilerParams(vmem_limit_bytes=2 * MIB),
        cost_estimate=BRIEF,
        name="pack_other",
    )(down, up, pinned(pair, pltpu.VMEM), pinned(up_pair, pltpu.VMEM))


def attend_cache(pairs, ready, sizes, scale, quarter, *refs):
    lengths, order, q_ref, k_hbm, v_hbm, w_hbm = refs[:6]
    sems, w_sems = refs[-2:]
    k_buf, v_buf, w_buf, *outs = refs[-7:-2]
    done = pairs[0]
    o_ref, lse_ref = outs[:2]
    steps, _, heads, size = q_ref.shape
    kv = k_hbm.shape[1] // sizes[-1]
    lanes = steps * heads

    def copies(which, pair, slots):
        span = pl.ds(0, slots * kv)
        hbm, buf = ((k_hbm, k_buf), (v_hbm, v_buf))[which]
        return [
            pltpu.make_async_copy(
                hbm.at[order[2 * pair + i], span],
                buf.at[2 * pair + i, span],
                sems.at[pair, i, which],
            )
            for i in range(2)
        ]

    def start(pair, slots):
        for copy in copies(0, pair, slots) + copies(1, pair, slots):
            copy.start()

    def finish(which, pair, slots):
        for i in which:
            for copy in copies(i, pair, slots):
                copy.wait()

    for pair in range(*ready):
        by_length(lengths[order[2 * pair]], sizes, functools.partial(start, pair))
    w_copies = quarter_copies(quarter, w_hbm, w_buf, w_sems)
    for copy in w_copies:
        copy.start()

    row_head = over(within(lax.broadcasted_iota(jnp.int32, (lanes, size), 0), heads), heads // kv)
    slot_head = within(lax.broadcasted_iota(jnp.int32, (lanes, size), 1), kv)
    head_bias = jnp.where(row_head == slot_head, 0.0, -jnp.inf)

    def attend(pair):
        def compute(slots):
            def wait(which):
                @pl.when(pair >= ready[0])
                def _():
                    finish((which,), pair, slots)

            n = slots * kv
            bias = jnp.concatenate([head_bias[:, : min(n, size)]] * max(n // size, 1), axis=1)
            column = lax.broadcasted_iota(jnp.int32, (1, n), 1)
            wait(0)
            scores = []
            for i in range(2):
                row = order[2 * pair + i]
                q = q_ref[:, row].reshape(lanes, size)
                s = lax.dot_general(
                    q,
                    k_buf[2 * pair + i, :n],
                    (((1,), (1,)), ((), ())),
                    preferred_element_type=jnp.float32,
                )
                closed = jnp.where(column < lengths[row] * kv, 0.0, -jnp.inf)
                scores.append(s + (bias + closed))
            highest = [jnp.max(s, axis=1, keepdims=True) * scale for s in scores]
            weights = [jnp.exp2(s * scale - h) for s, h in zip(scores, highest)]
            totals = [jnp.sum(p, axis=1, keepdims=True) for p in weights]
            wait(1)
            for i in range(2):
                o = jnp.dot(
                    weights[i].astype(jnp.bfloat16),
                    v_buf[2 * pair + i, :n],
                    preferred_element_type=jnp.float32,
                )
                spot = 2 * (pair - done) + i
                o_ref[spot] = o / totals[i]
                lse = highest[i] + jnp.log(totals[i]) * LOG2E
                lse_ref[spot] = jnp.broadcast_to(lse, (lanes, size))

        by_length(lengths[order[2 * pair]], sizes, compute)

    if pairs[1] - pairs[0] == 1:
        attend(pairs[0])
    else:
        pl.loop(*pairs)(attend)
    for pair in range(max(pairs[1], ready[0]), ready[1]):
        by_length(lengths[order[2 * pair]], sizes, functools.partial(finish, (0, 1), pair))
    for copy in w_copies:
        copy.wait()


def like(x):
    return pltpu.VMEM(x.shape, x.dtype)


def cache_attention(pairs, ready, rows_args, caches, weights, quarter, buffers, sizes, after):
    lengths, order, queries = rows_args
    keys, values = caches
    rows, steps, _, heads, size = (keys.shape[0], *queries.shape)
    slots = sizes[-1]
    scale = LOG2E / math.sqrt(size)
    count = 2 * (pairs[1] - pairs[0])
    piece = pltpu.VMEM((count, steps * heads, size), jnp.float32)
    operands = [pinned(x, pltpu.SMEM) for x in (lengths, order)]
    operands += [pinned(queries, pltpu.VMEM)]
    operands += [pinned(x) for x in (keys, values, weights)]
    aliases = {len(operands) + i: i for i in range(len(buffers))}
    specs = [SMEM, SMEM, VMEM, HBM, HBM, HBM] + [VMEM] * len(buffers) + [ANY] * len(after)
    operands += [pinned(b, pltpu.VMEM) for b in buffers] + after
    out_shape = [pltpu.VMEM(x.shape, x.dtype) for x in (keys, values, weights)] + [piece] * 2
    return pl.pallas_call(
        functools.partial(attend_cache, pairs, ready, sizes, scale, quarter),
        out_shape=out_shape,
        in_specs=specs,
        out_specs=[VMEM] * len(out_shape),
        input_output_aliases=aliases,
        scratch_shapes=[
            pltpu.SemaphoreType.DMA((rows // 2, 2, 2)),
            pltpu.SemaphoreType.DMA((4,)),
        ],
        compiler_params=pltpu.CompilerParams(vmem_limit_bytes=8 * MIB),
        cost_estimate=BRIEF,
        name="cache_attention",
    )(*operands)


def project_old(lay, n_hidden, *refs):
    w_hbm, *hidden = refs[1 : 2 + n_hidden]
    w_buf, out_ref, h_ref, sems = refs[-4:]
    tp = lax.axis_index("tp")
    copies = [quarter_copies(2 + i, w_hbm, w_buf, sems.at[i]) for i in range(2)]
    for copy in copies[0] + copies[1]:
        copy.start()
    for i, h in enumerate(hidden):
        h_ref[lax.rem(tp + i, lay.tp)] = h[...]
    features = h_ref.shape[2]
    chunk = min(features, 1024)
    for k in range(2):
        total = jnp.zeros(out_ref.shape[1:], jnp.float32)
        for t in range(lay.tp):
            if k == 1 and t % (lay.tp // 2) == 0:
                for copy in copies[t // (lay.tp // 2)]:
                    copy.wait()
            for low in range(0, features, chunk):
                start = t * features + low
                total += jnp.dot(
                    h_ref[t, :, low : low + chunk],
                    w_buf[k, start : start + chunk, :],
                    preferred_element_type=jnp.float32,
                )
        out_ref[k] = total


def project(lay, w_buf, weights, hidden, after):
    tokens, features = hidden[0].shape
    return pl.pallas_call(
        functools.partial(project_old, lay, len(hidden)),
        out_shape=(
            like(w_buf),
            pltpu.VMEM((2, tokens, weights.shape[2]), jnp.float32),
            pltpu.VMEM((lay.tp, tokens, features), jnp.bfloat16),
        ),
        in_specs=[VMEM, HBM] + [VMEM] * len(hidden) + [ANY] * len(after),
        out_specs=(VMEM, VMEM, VMEM),
        input_output_aliases={0: 0},
        scratch_shapes=[pltpu.SemaphoreType.DMA((2, 4))],
        compiler_params=pltpu.CompilerParams(vmem_limit_bytes=4 * MIB),
        cost_estimate=BRIEF,
        name="project",
    )(pinned(w_buf, pltpu.VMEM), pinned(weights), *hidden, *after)


class Place:
    def __init__(self, lay):
        fsdp, self.grp, self.tp = (lax.axis_index(a) for a in AXES)
        self.z, self.core = fsdp // 2, lax.rem(fsdp, 2)
        self.lay = lay
        there = jnp.where(lax.rem(self.grp, 2) == 0, self.z, lay.depth - 1 - self.z)
        self.own = self.grp * lay.depth + there
        self.per_lane = lay.fsdp * lay.grp // lay.tp

    def find(self, plan, downs):
        lay, found = self.lay, []
        for (step, flip), down in zip(plan, downs):
            towards = (1 - 2 * self.core if flip else 2 * self.core - 1) * step
            spot = lax.rem(self.own + (lay.ring + towards), lay.ring)
            g = spot // lay.depth
            along = lax.rem(spot, lay.depth)
            zz = jnp.where(lax.rem(g, 2) == 0, along, lay.depth - 1 - along)
            for i in range(2):
                core = lax.rem(self.core + (i + flip), 2)
                found.append((down.at[i], (zz * 2 + core) * lay.grp + g))
        return found

    def add_low(self, total, k, shards, h_ref, depth):
        for down, index in shards:
            tiles = depth // down.shape[-1]
            column = pl.multiple_of(lax.rem(index, self.per_lane) * depth, depth)
            total += lax.dot_general(
                h_ref[index // self.per_lane, :, pl.ds(column, depth)],
                jnp.concatenate([down[k * tiles + i] for i in range(tiles)], axis=1),
                (((1,), (1,)), ((), ())),
                preferred_element_type=jnp.float32,
            )
        return total


def merge_some(lay, plan, ups, n_caches, scale, *refs):
    refs = list(refs)

    def take(n):
        out = refs[:n]
        del refs[:n]
        return out

    first, last = ups is not None, n_caches > 0
    downs = take(len(plan))
    (h_buf,) = take(1)
    if first:
        up_refs = take(len(ups))
        weights = refs[1]
        m_hbm, weights, u_buf, low_out, m_buf, sems, u_parts = refs[-7:]
    else:
        old, order, q_ref = take(3)
        caches = [take(2) for _ in range(n_caches)]
        u_buf, low_in = take(2)
        m_hbm, weights, out_ref, m_buf, sems = refs[-5:]
    pairs, depth, width = m_buf.shape[1:]
    cut = min(width, 256)
    lanes = downs[0].shape[-1]
    tiles = depth // lanes
    place = Place(lay)
    shards = place.find(plan, downs)

    if first:
        columns = width // place.per_lane
        for (turn, shift), up in zip(ups, up_refs):
            zz = lax.rem(lax.rem(place.z, lay.block) + shift, lay.block)
            g = lax.rem(place.grp + turn, lay.grp)
            for c in range(2):
                u_parts[(zz * 2 + c) * lay.grp + g] = up[c]
        for k in range(pairs):
            u_buf[k] = ADAPTER_SCALING * jnp.concatenate(
                [
                    u_parts[i, :, k * columns : (k + 1) * columns]
                    for i in range(place.per_lane)
                ],
                axis=1,
            )

    chunk = min(depth, 256)
    copies = []
    for j, (down, index) in enumerate(shards):
        start = pl.multiple_of(index * depth, depth)
        for k in range(pairs):
            for begin in range(0, depth, chunk):
                rows = slice(begin, begin + chunk)
                tile = k * tiles + begin // lanes
                d = jnp.concatenate([down[tile + i] for i in range(chunk // lanes)], axis=1)
                for side in range(width // cut):
                    cols = slice(side * cut, (side + 1) * cut)
                    added = lax.dot_general(
                        d,
                        u_buf[k, :, cols],
                        (((0,), (0,)), ((), ())),
                        preferred_element_type=jnp.float32,
                    )
                    w = weights[k, pl.ds(start + begin, chunk), cols]
                    m_buf[j, k, rows, cols] = (w.astype(jnp.float32) + added).astype(jnp.bfloat16)
            copy = pltpu.make_async_copy(
                m_buf.at[j, k], m_hbm.at[k, pl.ds(start, depth), :], sems.at[j, k]
            )
            copy.start()
            copies.append(copy)

    if first:
        for k in range(pairs):
            low_out[k] = place.add_low(
                jnp.zeros(low_out.shape[1:], jnp.float32), k, shards, h_buf, depth
            )
    if last:
        new = []
        for k in range(pairs):
            low = place.add_low(low_in[k], k, shards, h_buf, depth)
            high = low.astype(jnp.bfloat16)
            rest = (low - high.astype(jnp.float32)).astype(jnp.bfloat16)
            new.append(
                (
                    old[k]
                    + jnp.dot(high, u_buf[k], preferred_element_type=jnp.float32)
                    + jnp.dot(rest, u_buf[k], preferred_element_type=jnp.float32)
                ).astype(jnp.bfloat16)
            )
        add_new_tokens(q_ref, order, caches, new, out_ref, scale)
    for copy in copies:
        copy.wait()


def add_new_tokens(q_ref, order, caches, new, out_ref, scale):
    steps, rows, heads, size = q_ref.shape
    kv = new[0].shape[1] // size
    new = [
        jnp.concatenate([x[:, g * size : (g + 1) * size] for g in range(kv)], axis=0) for x in new
    ]
    n = kv * steps * rows
    lanes = steps * heads
    left = lax.broadcasted_iota(jnp.int32, (lanes, n), 0)
    right = lax.broadcasted_iota(jnp.int32, (lanes, n), 1)
    same_head = over(within(left, heads), heads // kv) == over(right, steps * rows)
    earlier = within(over(right, rows), steps) <= over(left, heads)
    right_row = jnp.where(same_head & earlier, within(right, rows), -1)
    spots = [(o, lse, i) for o, lse in caches for i in range(o.shape[0])]
    for spot, (o_ref, lse_ref, i) in enumerate(spots):
        row = order[spot]
        q = q_ref[:, row].reshape(lanes, size)
        s = lax.dot_general(
            q, new[0], (((1,), (1,)), ((), ())), preferred_element_type=jnp.float32
        )
        s = jnp.where(right_row == row, s * scale, -jnp.inf)
        lse = lse_ref[i]
        highest = jnp.maximum(jnp.max(s, axis=1, keepdims=True), lse)
        p = jnp.exp2(s - highest[:, :n])
        old = jnp.exp2(lse - highest)
        divisor = jnp.sum(p, axis=1, keepdims=True) + old
        o = old * o_ref[i] + jnp.dot(
            p.astype(jnp.bfloat16), new[1], preferred_element_type=jnp.float32
        )
        out_ref[:, row] = (o / divisor).reshape(steps, heads, size).astype(out_ref.dtype)


def merge(lay, shape, entries, states, w_buf, ups, state, final, after):
    pairs, total, width = shape
    tokens, rank = states.shape[1], entries[0][2].shape[-2]
    depth = total // (lay.fsdp * lay.grp)
    per_lane = lay.fsdp * lay.grp // lay.tp
    n = 2 * len(entries)
    merged = pltpu.HBM(shape, jnp.bfloat16)
    u_shape, low_shape = (pairs, rank, width), (pairs, tokens, rank)
    operands = [e[2] for e in entries] + [pinned(states, pltpu.VMEM)]
    scratch = [
        pltpu.VMEM((n, pairs, depth, width), jnp.bfloat16),
        pltpu.SemaphoreType.DMA((n, pairs)),
    ]
    specs = [VMEM] * len(operands)
    if state is None:
        operands += [x for _, _, x in ups] + [pinned(w_buf, pltpu.VMEM)]
        specs += [VMEM] * (len(ups) + 1)
        aliases = {len(operands) - 1: 1}
        out_shape = [
            merged,
            like(w_buf),
            pltpu.VMEM(u_shape, jnp.bfloat16),
            pltpu.VMEM(low_shape, jnp.float32),
        ]
        out_specs = [HBM, VMEM, VMEM, VMEM]
        scratch.append(pltpu.VMEM((per_lane, rank, pairs * width // per_lane), jnp.bfloat16))
        n_caches, scale = 0, 0.0
        plan_ups = [(turn, shift) for turn, shift, _ in ups]
    else:
        olds, order, queries, caches = final
        m_prev, u_buf, low = state
        operands += [olds, pinned(order, pltpu.SMEM), pinned(queries, pltpu.VMEM), *caches]
        specs += [VMEM, SMEM, VMEM] + [VMEM] * len(caches)
        operands += [pinned(u_buf, pltpu.VMEM), pinned(low, pltpu.VMEM)]
        operands += [pinned(m_prev), pinned(w_buf, pltpu.VMEM)]
        specs += [VMEM, VMEM, HBM, VMEM]
        aliases = {len(operands) - 2: 0, len(operands) - 1: 1}
        out_shape = [merged, like(w_buf), jax.ShapeDtypeStruct(queries.shape, jnp.bfloat16)]
        out_specs = [HBM, VMEM, VMEM]
        n_caches, scale = len(caches) // 2, LOG2E / math.sqrt(queries.shape[3])
        plan_ups = None
    return pl.pallas_call(
        functools.partial(merge_some, lay, [e[:2] for e in entries], plan_ups, n_caches, scale),
        out_shape=out_shape,
        in_specs=specs + [ANY] * len(after),
        out_specs=out_specs,
        input_output_aliases=aliases,
        scratch_shapes=scratch,
        compiler_params=pltpu.CompilerParams(vmem_limit_bytes=18 * MIB),
        cost_estimate=BRIEF,
        name="merge",
    )(*operands, *after)


def shards(
    lay,
    hidden_states,
    queries,
    cache_keys,
    cache_values,
    cache_lengths,
    projection_weight_matrices,
    factor_down,
    factor_up,
):
    send = functools.partial(lax.ppermute, axis_name=AXES)
    steps, rows, features = hidden_states.shape
    slots, kv, size = cache_keys.shape[1:]
    shape = projection_weight_matrices.shape
    sizes = tuple(slots * i // 24 for i in (1, 4, 8, 16, 24))
    own = jnp.swapaxes(factor_down, 1, 2)
    tokens = hidden_states.reshape(steps * rows, features)
    keys = cache_keys.reshape(rows, slots * kv, size)
    values = cache_values.reshape(rows, slots * kv, size)
    swap, ring = lay.core_swap(), lay.ring_step()
    projections = projection_weight_matrices
    pair_count = rows // 2
    last_step = lay.ring // 2
    buffers, caches = [], []

    other, other_up = send(own, perm=swap), send(factor_up, perm=swap)
    pair, up_pair, *rows_args = begin(own, factor_up, cache_lengths, queries)
    pair, up_pair = pack(other, other_up, pair, up_pair)

    def attention(pairs, ready, quarter, after):
        nonlocal buffers
        out = cache_attention(
            pairs, ready, rows_args, (keys, values), projections, quarter, buffers, sizes, after
        )
        buffers = list(out[:3])
        caches.extend(out[3:])
        return out[3]

    came = send(pair, perm=ring)
    up = send(up_pair, perm=lay.plane_step())
    token = attention((0, 1), (0, 2), 0, [pair])
    (came, up, tokens), token = after_all((came, up, tokens), token)
    entries = [(0, 0, pair), (1, 0, came)]

    sent, swapped = send(came, perm=ring), send(came, perm=swap)
    up_y = [send(up, perm=lay.near_step(turn, 0)) for turn in range(1, lay.grp)]
    up_z = [send(up, perm=lay.near_step(0, shift)) for shift in range(1, lay.block)]
    hidden = [tokens] + [send(tokens, perm=lay.feature_step(i)) for i in range(1, lay.tp)]
    token = attention((1, pair_count), (2, pair_count), 1, [token])
    (came, swapped, up_y, up_z), token = after_all((sent, swapped, up_y, up_z), token)
    entries += [(1, 1, swapped), (2, 0, came)]
    ups = [(0, 0, up)] + [(turn + 1, 0, x) for turn, x in enumerate(up_y)]
    ups += [(0, shift + 1, x) for shift, x in enumerate(up_z)]

    sent, swapped = send(came, perm=ring), send(came, perm=swap)
    up_yz = [
        (turn + 1, shift, send(x, perm=lay.near_step(0, shift)))
        for turn, x in enumerate(up_y)
        for shift in range(1, lay.block)
    ]
    w_buf, olds, states = project(lay, buffers[2], projections, hidden, [token])
    (came, swapped, diagonal), token = after_all(
        (sent, swapped, [x for _, _, x in up_yz]), olds
    )
    entries += [(2, 1, swapped), (3, 0, came)]
    ups += [(turn, shift, x) for (turn, shift, _), x in zip(up_yz, diagonal)]

    for step in range(3, last_step - 1):
        sent, swapped = send(came, perm=ring), send(came, perm=swap)
        came, swapped = lax.optimization_barrier((sent, swapped))
        entries += [(step, 1, swapped), (step + 1, 0, came)]
    sent, swapped = send(came, perm=ring), send(came, perm=swap)
    m, w_buf, *state = merge(lay, shape, entries, states, w_buf, ups, None, None, [token])
    (came, swapped), low = after_all((sent, swapped), state[1])
    entries = [(last_step - 1, 1, swapped), (last_step, 0, came)]
    _, order, q = rows_args
    m, _, attended = merge(
        lay, shape, entries, states, w_buf, None, [m, state[0], low], (olds, order, q, caches), []
    )
    return m, attended


def solution(mesh):
    return jax.shard_map(
        functools.partial(shards, Layout(mesh)),
        mesh=mesh,
        in_specs=(
            P(None, ("fsdp", "grp"), "tp"),
            P(None, ("fsdp", "grp"), "tp", None),
            P(("fsdp", "grp"), None, "tp", None),
            P(("fsdp", "grp"), None, "tp", None),
            P(("fsdp", "grp")),
            P(None, None, "tp"),
            P(None, ("fsdp", "grp"), None),
            P(None, None, ("fsdp", "grp")),
        ),
        out_specs=(P(None, None, "tp"), P(None, ("fsdp", "grp"), "tp", None)),
        check_vma=False,
    )
```

```python
import functools
import math

import jax
import jax.numpy as jnp
from jax import lax
from jax.experimental import pallas as pl
from jax.experimental.pallas import tpu as pltpu
from jax.sharding import PartitionSpec as P

AXES = ("fsdp", "grp", "tp")
ADAPTER_SCALING = 2.0
LOG2E = math.log2(math.e)
MIB = 1024 * 1024
ANY = pl.BlockSpec(memory_space=pl.ANY)
HBM = pl.BlockSpec(memory_space=pltpu.HBM)
VMEM = pl.BlockSpec(memory_space=pltpu.VMEM)
SMEM = pl.BlockSpec(memory_space=pltpu.SMEM)


class Layout:
    def __init__(self, mesh):
        self.fsdp, self.grp, self.tp = (mesh.shape[a] for a in AXES)
        self.depth = self.fsdp // 2
        self.ring = self.depth * self.grp
        self.block = self.depth // self.tp

    def flat(self, z, core, g, t):
        return ((z * 2 + core) * self.grp + g) * self.tp + t

    def devices(self):
        for z in range(self.depth):
            for core in range(2):
                for g in range(self.grp):
                    for t in range(self.tp):
                        yield z, core, g, t

    def place(self, z, g):
        return g * self.depth + (z if g % 2 == 0 else self.depth - 1 - z)

    def at(self, position):
        g, z = divmod(position, self.depth)
        return (z if g % 2 == 0 else self.depth - 1 - z), g

    def ring_step(self):
        pairs = []
        for z, core, g, t in self.devices():
            to_z, to_g = self.at((self.place(z, g) + (1 - 2 * core)) % self.ring)
            pairs.append((self.flat(z, core, g, t), self.flat(to_z, core, to_g, t)))
        return pairs

    def plane_step(self):
        return [
            (
                self.flat(t * self.block + z % self.block, c, g, z // self.block),
                self.flat(z, c, g, t),
            )
            for z, c, g, t in self.devices()
        ]

    def near_step(self, turn, shift):
        pairs = []
        for z, c, g, t in self.devices():
            source = z - z % self.block + (z % self.block + shift) % self.block
            pairs.append(
                (self.flat(source, c, (g + turn) % self.grp, t), self.flat(z, c, g, t))
            )
        return pairs

    def core_swap(self):
        return [
            (self.flat(z, c, g, t), self.flat(z, 1 - c, g, t)) for z, c, g, t in self.devices()
        ]

    def feature_step(self, step):
        return [
            (self.flat(z, c, g, (t + step) % self.tp), self.flat(z, c, g, t))
            for z, c, g, t in self.devices()
        ]


TYPICAL = pl.CostEstimate(flops=3 * 10**9, bytes_accessed=10**7, transcendentals=0)


def over(x, n):
    return x >> (n.bit_length() - 1) if n & (n - 1) == 0 else x // n


def within(x, n):
    return x & (n - 1) if n & (n - 1) == 0 else x % n


def after_all(arrays, token):
    return lax.optimization_barrier((arrays, token))


def pinned(x, space=pltpu.HBM):
    return pltpu.with_memory_space_constraint(x, space)


def sort_rows(lengths, order):
    rows = lengths.shape[0]
    held = [lengths[r] for r in range(rows)]
    for r in range(rows):
        rank = jnp.int32(0)
        for other in range(rows):
            if other != r:
                ahead = held[other] >= held[r] if other < r else held[other] > held[r]
                rank = rank + ahead.astype(jnp.int32)
        order[rank] = r


def by_length(length, sizes, act):
    below = 0
    for slots in sizes:

        @pl.when((length > below) & (length <= slots))
        def _():
            act(slots)

        below = slots


def up_columns(up):
    return jnp.concatenate([up[k] for k in range(up.shape[0])], axis=1)


def begin_all(down, up, len_hbm, q_hbm, pair, up_pair, lengths, order, q_ref, up_buf, sems, more):
    lanes = pair.shape[3]
    count, _, depth = down.shape
    tiles = depth // lanes
    copies = [
        pltpu.make_async_copy(
            down.at[k, :, pl.ds(i * lanes, lanes)], pair.at[0, k * tiles + i], sems.at[k, i]
        )
        for k in range(count)
        for i in range(tiles)
    ]
    up_copy = pltpu.make_async_copy(up, up_buf, more.at[0])
    len_copy = pltpu.make_async_copy(len_hbm, lengths, more.at[1])
    q_copy = pltpu.make_async_copy(q_hbm, q_ref, more.at[2])
    for copy in [len_copy, up_copy] + copies + [q_copy]:
        copy.start()
    len_copy.wait()
    sort_rows(lengths, order)
    up_copy.wait()
    up_pair[lax.rem(lax.axis_index("fsdp"), 2)] = up_columns(up_buf)
    for copy in copies + [q_copy]:
        copy.wait()


def begin(down, up, lengths, queries):
    count, rank, depth = down.shape
    scalars = pltpu.SMEM(lengths.shape, jnp.int32)
    return pl.pallas_call(
        begin_all,
        out_shape=(
            pltpu.VMEM((2, count * depth // 128, rank, 128), down.dtype),
            pltpu.VMEM((2, rank, count * up.shape[2]), up.dtype),
            scalars,
            scalars,
            pltpu.VMEM(queries.shape, queries.dtype),
        ),
        in_specs=[HBM] * 4,
        out_specs=(VMEM, VMEM, SMEM, SMEM, VMEM),
        scratch_shapes=[
            pltpu.VMEM(up.shape, up.dtype),
            pltpu.SemaphoreType.DMA((count, depth // 128)),
            pltpu.SemaphoreType.DMA((3,)),
        ],
        compiler_params=pltpu.CompilerParams(vmem_limit_bytes=2 * MIB),
        cost_estimate=TYPICAL,
        name="begin",
    )(pinned(down), pinned(up), pinned(lengths), pinned(queries))


def pack_other(down, up, _, __, pair, up_pair):
    lanes = pair.shape[3]
    count, _, depth = down.shape
    tiles = depth // lanes
    for k in range(count):
        for i in range(tiles):
            pair[1, k * tiles + i] = down[k, :, i * lanes : (i + 1) * lanes]
    up_pair[1 - lax.rem(lax.axis_index("fsdp"), 2)] = up_columns(up)


def pack(down, up, pair, up_pair):
    return pl.pallas_call(
        pack_other,
        out_shape=(like(pair), like(up_pair)),
        in_specs=[VMEM] * 4,
        out_specs=(VMEM, VMEM),
        input_output_aliases={2: 0, 3: 1},
        compiler_params=pltpu.CompilerParams(vmem_limit_bytes=2 * MIB),
        cost_estimate=TYPICAL,
        name="pack_other",
    )(down, up, pinned(pair, pltpu.VMEM), pinned(up_pair, pltpu.VMEM))


def attend_cache(pairs, ready, sizes, scale, *refs):
    lengths, order, q_ref, k_hbm, v_hbm = refs[:5]
    k_buf, v_buf, *outs, sems = refs[-5:]
    done = pairs[0]
    o_ref, lse_ref = outs[:2]
    steps, _, heads, size = q_ref.shape
    kv = k_hbm.shape[1] // sizes[-1]
    lanes = steps * heads

    def copies(which, pair, slots):
        span = pl.ds(0, slots * kv)
        hbm, buf = ((k_hbm, k_buf), (v_hbm, v_buf))[which]
        return [
            pltpu.make_async_copy(
                hbm.at[order[2 * pair + i], span],
                buf.at[2 * pair + i, span],
                sems.at[pair, i, which],
            )
            for i in range(2)
        ]

    def start(pair, slots):
        for copy in copies(0, pair, slots) + copies(1, pair, slots):
            copy.start()

    def finish(which, pair, slots):
        for i in which:
            for copy in copies(i, pair, slots):
                copy.wait()

    for pair in range(*ready):
        by_length(lengths[order[2 * pair]], sizes, functools.partial(start, pair))

    row_head = over(within(lax.broadcasted_iota(jnp.int32, (lanes, size), 0), heads), heads // kv)
    slot_head = within(lax.broadcasted_iota(jnp.int32, (lanes, size), 1), kv)
    head_bias = jnp.where(row_head == slot_head, 0.0, -jnp.inf)

    def attend(pair):
        def compute(slots):
            def wait(which):
                @pl.when(pair >= ready[0])
                def _():
                    finish((which,), pair, slots)

            n = slots * kv
            bias = jnp.concatenate([head_bias[:, : min(n, size)]] * max(n // size, 1), axis=1)
            column = lax.broadcasted_iota(jnp.int32, (1, n), 1)
            wait(0)
            scores = []
            for i in range(2):
                row = order[2 * pair + i]
                q = q_ref[:, row].reshape(lanes, size)
                s = lax.dot_general(
                    q,
                    k_buf[2 * pair + i, :n],
                    (((1,), (1,)), ((), ())),
                    preferred_element_type=jnp.float32,
                )
                closed = jnp.where(column < lengths[row] * kv, 0.0, -jnp.inf)
                scores.append(s + (bias + closed))
            highest = [jnp.max(s, axis=1, keepdims=True) * scale for s in scores]
            weights = [jnp.exp2(s * scale - h) for s, h in zip(scores, highest)]
            totals = [jnp.sum(p, axis=1, keepdims=True) for p in weights]
            wait(1)
            for i in range(2):
                o = jnp.dot(
                    weights[i].astype(jnp.bfloat16),
                    v_buf[2 * pair + i, :n],
                    preferred_element_type=jnp.float32,
                )
                spot = 2 * (pair - done) + i
                o_ref[spot] = o / totals[i]
                lse = highest[i] + jnp.log(totals[i]) * LOG2E
                lse_ref[spot] = jnp.broadcast_to(lse, (lanes, size))

        by_length(lengths[order[2 * pair]], sizes, compute)

    if pairs[1] - pairs[0] == 1:
        attend(pairs[0])
    else:
        pl.loop(*pairs)(attend)
    for pair in range(max(pairs[1], ready[0]), ready[1]):
        by_length(lengths[order[2 * pair]], sizes, functools.partial(finish, (0, 1), pair))


def like(x):
    return pltpu.VMEM(x.shape, x.dtype)


def cache_attention(pairs, ready, rows_args, caches, buffers, sizes, after):
    lengths, order, queries = rows_args
    keys, values = caches
    rows, steps, _, heads, size = (keys.shape[0], *queries.shape)
    slots = sizes[-1]
    scale = LOG2E / math.sqrt(size)
    count = 2 * (pairs[1] - pairs[0])
    piece = pltpu.VMEM((count, steps * heads, size), jnp.float32)
    operands = [pinned(x, pltpu.SMEM) for x in (lengths, order)]
    operands += [pinned(queries, pltpu.VMEM)]
    operands += [pinned(keys), pinned(values)]
    aliases = {len(operands) + i: i for i in range(len(buffers))}
    specs = [SMEM, SMEM, VMEM, HBM, HBM] + [VMEM] * len(buffers) + [ANY] * len(after)
    operands += [pinned(b, pltpu.VMEM) for b in buffers] + after
    out_shape = [like(keys), like(values), piece, piece]
    return pl.pallas_call(
        functools.partial(attend_cache, pairs, ready, sizes, scale),
        out_shape=out_shape,
        in_specs=specs,
        out_specs=[VMEM] * len(out_shape),
        input_output_aliases=aliases,
        scratch_shapes=[
            pltpu.SemaphoreType.DMA((rows // 2, 2, 2)),
        ],
        compiler_params=pltpu.CompilerParams(vmem_limit_bytes=8 * MIB),
        cost_estimate=TYPICAL,
        name="cache_attention",
    )(*operands)


def project_old(lay, n_hidden, *refs):
    w_buf, *hidden = refs[: 1 + n_hidden]
    out_ref, h_ref = refs[-2:]
    tp = lax.axis_index("tp")
    for i, h in enumerate(hidden):
        h_ref[lax.rem(tp + i, lay.tp)] = h[...]
    features = h_ref.shape[2]
    chunk = min(features, 1024)
    for k in range(2):
        total = jnp.zeros(out_ref.shape[1:], jnp.float32)
        for t in range(lay.tp):
            for low in range(0, features, chunk):
                start = t * features + low
                total += jnp.dot(
                    h_ref[t, :, low : low + chunk],
                    w_buf[k, start : start + chunk, :],
                    preferred_element_type=jnp.float32,
                )
        out_ref[k] = total


def project(lay, w_buf, hidden, after):
    tokens, features = hidden[0].shape
    return pl.pallas_call(
        functools.partial(project_old, lay, len(hidden)),
        out_shape=(
            pltpu.VMEM((2, tokens, w_buf.shape[2]), jnp.float32),
            pltpu.VMEM((lay.tp, tokens, features), jnp.bfloat16),
        ),
        in_specs=[VMEM] * (1 + len(hidden)) + [ANY] * len(after),
        out_specs=(VMEM, VMEM),
        compiler_params=pltpu.CompilerParams(vmem_limit_bytes=4 * MIB),
        cost_estimate=TYPICAL,
        name="project",
    )(pinned(w_buf, pltpu.VMEM), *hidden, *after)


class Place:
    def __init__(self, lay):
        fsdp, self.grp, self.tp = (lax.axis_index(a) for a in AXES)
        self.z, self.core = fsdp // 2, lax.rem(fsdp, 2)
        self.lay = lay
        there = jnp.where(lax.rem(self.grp, 2) == 0, self.z, lay.depth - 1 - self.z)
        self.own = self.grp * lay.depth + there
        self.per_lane = lay.fsdp * lay.grp // lay.tp

    def find(self, plan, downs):
        lay, found = self.lay, []
        for (step, flip), down in zip(plan, downs):
            towards = (1 - 2 * self.core if flip else 2 * self.core - 1) * step
            spot = lax.rem(self.own + (lay.ring + towards), lay.ring)
            g = spot // lay.depth
            along = lax.rem(spot, lay.depth)
            zz = jnp.where(lax.rem(g, 2) == 0, along, lay.depth - 1 - along)
            for i in range(2):
                core = lax.rem(self.core + (i + flip), 2)
                found.append((down.at[i], (zz * 2 + core) * lay.grp + g))
        return found

    def add_low(self, total, k, shards, h_ref, depth):
        for down, index in shards:
            tiles = depth // down.shape[-1]
            column = pl.multiple_of(lax.rem(index, self.per_lane) * depth, depth)
            total += lax.dot_general(
                h_ref[index // self.per_lane, :, pl.ds(column, depth)],
                jnp.concatenate([down[k * tiles + i] for i in range(tiles)], axis=1),
                (((1,), (1,)), ((), ())),
                preferred_element_type=jnp.float32,
            )
        return total


def merge_some(lay, plan, ups, n_caches, scale, *refs):
    refs = list(refs)

    def take(n):
        out = refs[:n]
        del refs[:n]
        return out

    first, last = ups is not None, n_caches > 0
    downs = take(len(plan))
    (h_buf,) = take(1)
    if first:
        up_refs = refs[: len(ups)]
        weights = refs[len(ups)]
        m_hbm, u_buf, low_out, m_buf, sems, u_parts = refs[-6:]
    else:
        old, order, q_ref = take(3)
        caches = [take(2) for _ in range(n_caches)]
        u_buf, low_in, _, weights = take(4)
        m_hbm, out_hbm, m_buf, sems, out_buf, out_sem = refs[-6:]
    pairs, depth, width = m_buf.shape[1:]
    cut = min(width, 256)
    lanes = downs[0].shape[-1]
    tiles = depth // lanes
    place = Place(lay)
    shards = place.find(plan, downs)

    if first:
        columns = width // place.per_lane
        for (turn, shift), up in zip(ups, up_refs):
            zz = lax.rem(lax.rem(place.z, lay.block) + shift, lay.block)
            g = lax.rem(place.grp + turn, lay.grp)
            for c in range(2):
                u_parts[(zz * 2 + c) * lay.grp + g] = up[c]
        for k in range(pairs):
            u_buf[k] = ADAPTER_SCALING * jnp.concatenate(
                [
                    u_parts[i, :, k * columns : (k + 1) * columns]
                    for i in range(place.per_lane)
                ],
                axis=1,
            )

    if last:
        new = []
        for k in range(pairs):
            low = place.add_low(low_in[k], k, shards, h_buf, depth)
            high = low.astype(jnp.bfloat16)
            rest = (low - high.astype(jnp.float32)).astype(jnp.bfloat16)
            new.append(
                (
                    old[k]
                    + jnp.dot(high, u_buf[k], preferred_element_type=jnp.float32)
                    + jnp.dot(rest, u_buf[k], preferred_element_type=jnp.float32)
                ).astype(jnp.bfloat16)
            )
        add_new_tokens(q_ref, order, caches, new, out_buf, scale)
        out_copy = pltpu.make_async_copy(out_buf, out_hbm, out_sem)
        out_copy.start()

    chunk = min(depth, 256)
    copies = []
    for j, (down, index) in enumerate(shards):
        start = pl.multiple_of(index * depth, depth)
        for k in range(pairs):
            for begin in range(0, depth, chunk):
                rows = slice(begin, begin + chunk)
                tile = k * tiles + begin // lanes
                d = jnp.concatenate([down[tile + i] for i in range(chunk // lanes)], axis=1)
                for side in range(width // cut):
                    cols = slice(side * cut, (side + 1) * cut)
                    added = lax.dot_general(
                        d,
                        u_buf[k, :, cols],
                        (((0,), (0,)), ((), ())),
                        preferred_element_type=jnp.float32,
                    )
                    w = weights[k, pl.ds(start + begin, chunk), cols]
                    m_buf[j, k, rows, cols] = (w.astype(jnp.float32) + added).astype(jnp.bfloat16)
            copy = pltpu.make_async_copy(
                m_buf.at[j, k], m_hbm.at[k, pl.ds(start, depth), :], sems.at[j, k]
            )
            copy.start()
            copies.append(copy)

    if first:
        for k in range(pairs):
            low_out[k] = place.add_low(
                jnp.zeros(low_out.shape[1:], jnp.float32), k, shards, h_buf, depth
            )
    for copy in copies + ([out_copy] if last else []):
        copy.wait()


def add_new_tokens(q_ref, order, caches, new, out_buf, scale):
    steps, rows, heads, size = q_ref.shape
    kv = new[0].shape[1] // size
    new = [
        jnp.concatenate([x[:, g * size : (g + 1) * size] for g in range(kv)], axis=0) for x in new
    ]
    n = kv * steps * rows
    lanes = steps * heads
    left = lax.broadcasted_iota(jnp.int32, (lanes, n), 0)
    right = lax.broadcasted_iota(jnp.int32, (lanes, n), 1)
    same_head = over(within(left, heads), heads // kv) == over(right, steps * rows)
    earlier = within(over(right, rows), steps) <= over(left, heads)
    right_row = jnp.where(same_head & earlier, within(right, rows), -1)

    def all_rows(pieces):
        return jnp.concatenate(list(pieces), axis=0)

    q = all_rows(q_ref[:, order[spot]].reshape(lanes, size) for spot in range(rows))
    s = lax.dot_general(q, new[0], (((1,), (1,)), ((), ())), preferred_element_type=jnp.float32)
    bias = all_rows(
        jnp.where(right_row == order[spot], 0.0, -jnp.inf) for spot in range(rows)
    )
    s = s * scale + bias
    lse = all_rows(ref[i] for _, ref in caches for i in range(ref.shape[0]))
    highest = jnp.maximum(jnp.max(s, axis=1, keepdims=True), lse)
    p = jnp.exp2(s - highest[:, :n])
    old = jnp.exp2(lse - highest)
    divisor = jnp.sum(p, axis=1, keepdims=True) + old
    o = old * all_rows(ref[i] for ref, _ in caches for i in range(ref.shape[0]))
    o = (o + jnp.dot(p.astype(jnp.bfloat16), new[1], preferred_element_type=jnp.float32)) / divisor
    for spot in range(rows):
        piece = o[spot * lanes : (spot + 1) * lanes].astype(out_buf.dtype)
        out_buf[:, order[spot]] = piece.reshape(steps, heads, size)


def merge(lay, shape, entries, states, w_buf, ups, state, final, after):
    pairs, total, width = shape
    tokens, rank = states.shape[1], entries[0][2].shape[-2]
    depth = total // (lay.fsdp * lay.grp)
    per_lane = lay.fsdp * lay.grp // lay.tp
    n = 2 * len(entries)
    merged = pltpu.HBM(shape, jnp.bfloat16)
    u_shape, low_shape = (pairs, rank, width), (pairs, tokens, rank)
    operands = [e[2] for e in entries] + [pinned(states, pltpu.VMEM)]
    scratch = [
        pltpu.VMEM((n, pairs, depth, width), jnp.bfloat16),
        pltpu.SemaphoreType.DMA((n, pairs)),
    ]
    specs = [VMEM] * len(operands)
    if state is None:
        operands += [x for _, _, x in ups] + [pinned(w_buf, pltpu.VMEM)]
        specs += [VMEM] * (len(ups) + 1)
        aliases = {}
        out_shape = [
            merged,
            pltpu.VMEM(u_shape, jnp.bfloat16),
            pltpu.VMEM(low_shape, jnp.float32),
        ]
        out_specs = [HBM, VMEM, VMEM]
        scratch.append(pltpu.VMEM((per_lane, rank, pairs * width // per_lane), jnp.bfloat16))
        n_caches, scale = 0, 0.0
        plan_ups = [(turn, shift) for turn, shift, _ in ups]
    else:
        olds, order, queries, caches = final
        m_prev, u_buf, low = state
        operands += [olds, pinned(order, pltpu.SMEM), pinned(queries, pltpu.VMEM), *caches]
        specs += [VMEM, SMEM, VMEM] + [VMEM] * len(caches)
        operands += [pinned(u_buf, pltpu.VMEM), pinned(low, pltpu.VMEM)]
        operands += [pinned(m_prev), pinned(w_buf, pltpu.VMEM)]
        specs += [VMEM, VMEM, HBM, VMEM]
        aliases = {len(operands) - 2: 0}
        out_shape = [merged, pltpu.HBM(queries.shape, jnp.bfloat16)]
        out_specs = [HBM, HBM]
        scratch += [pltpu.VMEM(queries.shape, jnp.bfloat16), pltpu.SemaphoreType.DMA]
        n_caches, scale = len(caches) // 2, LOG2E / math.sqrt(queries.shape[3])
        plan_ups = None
    return pl.pallas_call(
        functools.partial(merge_some, lay, [e[:2] for e in entries], plan_ups, n_caches, scale),
        out_shape=out_shape,
        in_specs=specs + [ANY] * len(after),
        out_specs=out_specs,
        input_output_aliases=aliases,
        scratch_shapes=scratch,
        compiler_params=pltpu.CompilerParams(vmem_limit_bytes=18 * MIB),
        cost_estimate=TYPICAL,
        name="merge",
    )(*operands, *after)


def shards(
    lay,
    hidden_states,
    queries,
    cache_keys,
    cache_values,
    cache_lengths,
    projection_weight_matrices,
    factor_down,
    factor_up,
):
    send = functools.partial(lax.ppermute, axis_name=AXES)
    steps, rows, features = hidden_states.shape
    slots, kv, size = cache_keys.shape[1:]
    shape = projection_weight_matrices.shape
    sizes = tuple(slots * i // 24 for i in (1, 4, 8, 16, 24))
    own = jnp.swapaxes(factor_down, 1, 2)
    tokens = hidden_states.reshape(steps * rows, features)
    keys = cache_keys.reshape(rows, slots * kv, size)
    values = cache_values.reshape(rows, slots * kv, size)
    swap, ring = lay.core_swap(), lay.ring_step()
    pair_count = rows // 2
    last_step = lay.ring // 2
    buffers, caches = [], []

    other, other_up = send(own, perm=swap), send(factor_up, perm=swap)
    pair, up_pair, *rows_args = begin(own, factor_up, cache_lengths, queries)
    pair, up_pair = pack(other, other_up, pair, up_pair)

    def attention(pairs, ready, after):
        nonlocal buffers
        out = cache_attention(pairs, ready, rows_args, (keys, values), buffers, sizes, after)
        buffers = list(out[:2])
        caches.extend(out[2:])
        return out[2]

    came = send(pair, perm=ring)
    up = send(up_pair, perm=lay.plane_step())
    token = attention((0, 1), (0, 2), [pair])
    (came, up, tokens), token = after_all((came, up, tokens), token)
    entries = [(0, 0, pair), (1, 0, came)]

    sent, swapped = send(came, perm=ring), send(came, perm=swap)
    up_y = [send(up, perm=lay.near_step(turn, 0)) for turn in range(1, lay.grp)]
    up_z = [send(up, perm=lay.near_step(0, shift)) for shift in range(1, lay.block)]
    hidden = [tokens] + [send(tokens, perm=lay.feature_step(i)) for i in range(1, lay.tp)]
    token = attention((1, pair_count), (2, pair_count), [token])
    (came, swapped, up_y, up_z), token = after_all((sent, swapped, up_y, up_z), token)
    entries += [(1, 1, swapped), (2, 0, came)]
    ups = [(0, 0, up)] + [(turn + 1, 0, x) for turn, x in enumerate(up_y)]
    ups += [(0, shift + 1, x) for shift, x in enumerate(up_z)]

    up_yz = [
        (turn + 1, shift, send(x, perm=lay.near_step(0, shift)))
        for turn, x in enumerate(up_y)
        for shift in range(1, lay.block)
    ]
    sent, swapped = send(came, perm=ring), send(came, perm=swap)
    w_buf = projection_weight_matrices
    olds, states = project(lay, w_buf, hidden, [token])
    (came, swapped, diagonal), token = after_all(
        (sent, swapped, [x for _, _, x in up_yz]), olds
    )
    entries += [(2, 1, swapped), (3, 0, came)]
    ups += [(turn, shift, x) for (turn, shift, _), x in zip(up_yz, diagonal)]

    for step in range(3, last_step - 1):
        sent, swapped = send(came, perm=ring), send(came, perm=swap)
        came, swapped = lax.optimization_barrier((sent, swapped))
        entries += [(step, 1, swapped), (step + 1, 0, came)]
    sent, swapped = send(came, perm=ring), send(came, perm=swap)
    m, *state = merge(lay, shape, entries, states, w_buf, ups, None, None, [token])
    (came, swapped), low = after_all((sent, swapped), state[1])
    entries = [(last_step - 1, 1, swapped), (last_step, 0, came)]
    _, order, q = rows_args
    m, attended = merge(
        lay, shape, entries, states, w_buf, None, [m, state[0], low], (olds, order, q, caches), []
    )
    return m, attended


def solution(mesh):
    return jax.shard_map(
        functools.partial(shards, Layout(mesh)),
        mesh=mesh,
        in_specs=(
            P(None, ("fsdp", "grp"), "tp"),
            P(None, ("fsdp", "grp"), "tp", None),
            P(("fsdp", "grp"), None, "tp", None),
            P(("fsdp", "grp"), None, "tp", None),
            P(("fsdp", "grp")),
            P(None, None, "tp"),
            P(None, ("fsdp", "grp"), None),
            P(None, None, ("fsdp", "grp")),
        ),
        out_specs=(P(None, None, "tp"), P(None, ("fsdp", "grp"), "tp", None)),
        check_vma=False,
    )
```

```python
import functools
import math

import jax
import jax.numpy as jnp
from jax import lax
from jax.experimental import pallas as pl
from jax.experimental.pallas import tpu as pltpu
from jax.sharding import PartitionSpec as P

AXES = ("fsdp", "grp", "tp")
ADAPTER_SCALING = 2.0
LOG2E = math.log2(math.e)
MIB = 1024 * 1024
ANY = pl.BlockSpec(memory_space=pl.ANY)
HBM = pl.BlockSpec(memory_space=pltpu.HBM)
VMEM = pl.BlockSpec(memory_space=pltpu.VMEM)
SMEM = pl.BlockSpec(memory_space=pltpu.SMEM)


class Layout:
    def __init__(self, mesh):
        self.fsdp, self.grp, self.tp = (mesh.shape[a] for a in AXES)
        self.depth = self.fsdp // 2
        self.ring = self.depth * self.grp
        self.block = self.depth // self.tp

    def flat(self, z, core, g, t):
        return ((z * 2 + core) * self.grp + g) * self.tp + t

    def devices(self):
        for z in range(self.depth):
            for core in range(2):
                for g in range(self.grp):
                    for t in range(self.tp):
                        yield z, core, g, t

    def place(self, z, g):
        return g * self.depth + (z if g % 2 == 0 else self.depth - 1 - z)

    def at(self, position):
        g, z = divmod(position, self.depth)
        return (z if g % 2 == 0 else self.depth - 1 - z), g

    def ring_step(self):
        pairs = []
        for z, core, g, t in self.devices():
            to_z, to_g = self.at((self.place(z, g) + (1 - 2 * core)) % self.ring)
            pairs.append((self.flat(z, core, g, t), self.flat(to_z, core, to_g, t)))
        return pairs

    def plane_swap(self):
        return [(self.flat(z, c, g, t), self.flat(z, c, g, t ^ 1)) for z, c, g, t in self.devices()]

    def core_swap(self):
        return [
            (self.flat(z, c, g, t), self.flat(z, 1 - c, g, t)) for z, c, g, t in self.devices()
        ]

    def feature_step(self, step):
        return [
            (self.flat(z, c, g, (t + step) % self.tp), self.flat(z, c, g, t))
            for z, c, g, t in self.devices()
        ]


TYPICAL = pl.CostEstimate(flops=3 * 10**9, bytes_accessed=10**7, transcendentals=0)


def over(x, n):
    return x >> (n.bit_length() - 1) if n & (n - 1) == 0 else x // n


def within(x, n):
    return x & (n - 1) if n & (n - 1) == 0 else x % n


def after_all(arrays, token):
    return lax.optimization_barrier((arrays, token))


def pinned(x, space=pltpu.HBM):
    return pltpu.with_memory_space_constraint(x, space)


def sort_rows(lengths, order):
    rows = lengths.shape[0]
    held = [lengths[r] for r in range(rows)]
    for r in range(rows):
        rank = jnp.int32(0)
        for other in range(rows):
            if other != r:
                ahead = held[other] >= held[r] if other < r else held[other] > held[r]
                rank = rank + ahead.astype(jnp.int32)
        order[rank] = r


def by_length(length, sizes, act):
    below = 0
    for slots in sizes:

        @pl.when((length > below) & (length <= slots))
        def _():
            act(slots)

        below = slots


def up_columns(up):
    return jnp.concatenate([up[k] for k in range(up.shape[0])], axis=1)


def plane_part():
    return lax.rem(lax.axis_index("tp"), 2)


def begin_all(down, up, len_hbm, q_hbm, pair, rest, lengths, order, q_ref, up_buf, sems, more):
    lanes = pair.shape[3]
    depth = down.shape[2]
    tiles = depth // lanes
    part = plane_part()
    copies = [
        pltpu.make_async_copy(
            down.at[k, :, pl.ds(i * lanes, lanes)], array.at[0, i], sems.at[which, i]
        )
        for which, (k, array) in enumerate(((part, pair), (1 - part, rest)))
        for i in range(tiles)
    ]
    up_copy = pltpu.make_async_copy(up, up_buf, more.at[0])
    len_copy = pltpu.make_async_copy(len_hbm, lengths, more.at[1])
    q_copy = pltpu.make_async_copy(q_hbm, q_ref, more.at[2])
    for copy in [len_copy, up_copy] + copies + [q_copy]:
        copy.start()
    len_copy.wait()
    sort_rows(lengths, order)
    up_copy.wait()
    columns = up_columns(up_buf)
    pair[0, tiles, :, : columns.shape[1]] = columns
    for copy in copies + [q_copy]:
        copy.wait()


def begin(down, up, lengths, queries):
    count, rank, depth = down.shape
    tiles = depth // 128
    scalars = pltpu.SMEM(lengths.shape, jnp.int32)
    return pl.pallas_call(
        begin_all,
        out_shape=(
            pltpu.VMEM((2, tiles + 1, rank, 128), down.dtype),
            pltpu.VMEM((2, tiles, rank, 128), down.dtype),
            scalars,
            scalars,
            pltpu.VMEM(queries.shape, queries.dtype),
        ),
        in_specs=[HBM] * 4,
        out_specs=(VMEM, VMEM, SMEM, SMEM, VMEM),
        scratch_shapes=[
            pltpu.VMEM(up.shape, up.dtype),
            pltpu.SemaphoreType.DMA((count, tiles)),
            pltpu.SemaphoreType.DMA((3,)),
        ],
        compiler_params=pltpu.CompilerParams(vmem_limit_bytes=2 * MIB),
        cost_estimate=TYPICAL,
        name="begin",
    )(pinned(down), pinned(up), pinned(lengths), pinned(queries))


def pack_other(down, up, _, __, pair, rest):
    lanes = pair.shape[3]
    tiles = down.shape[2] // lanes
    part = plane_part()
    for i in range(tiles):
        cols = slice(i * lanes, (i + 1) * lanes)
        pair[1, i] = down[part, :, cols]
        rest[1, i] = down[1 - part, :, cols]
    columns = up_columns(up)
    pair[1, tiles, :, : columns.shape[1]] = columns


def pack(down, up, pair, rest):
    return pl.pallas_call(
        pack_other,
        out_shape=(like(pair), like(rest)),
        in_specs=[VMEM] * 4,
        out_specs=(VMEM, VMEM),
        input_output_aliases={2: 0, 3: 1},
        compiler_params=pltpu.CompilerParams(vmem_limit_bytes=2 * MIB),
        cost_estimate=TYPICAL,
        name="pack_other",
    )(down, up, pinned(pair, pltpu.VMEM), pinned(rest, pltpu.VMEM))


def attend_cache(pairs, ready, sizes, scale, *refs):
    lengths, order, q_ref, k_hbm, v_hbm = refs[:5]
    k_buf, v_buf, *outs, sems = refs[-5:]
    done = pairs[0]
    o_ref, lse_ref = outs[:2]
    steps, _, heads, size = q_ref.shape
    kv = k_hbm.shape[1] // sizes[-1]
    lanes = steps * heads

    def copies(which, pair, slots):
        span = pl.ds(0, slots * kv)
        hbm, buf = ((k_hbm, k_buf), (v_hbm, v_buf))[which]
        return [
            pltpu.make_async_copy(
                hbm.at[order[2 * pair + i], span],
                buf.at[2 * pair + i, span],
                sems.at[pair, i, which],
            )
            for i in range(2)
        ]

    def start(pair, slots):
        for copy in copies(0, pair, slots) + copies(1, pair, slots):
            copy.start()

    def finish(which, pair, slots):
        for i in which:
            for copy in copies(i, pair, slots):
                copy.wait()

    for pair in range(*ready):
        by_length(lengths[order[2 * pair]], sizes, functools.partial(start, pair))

    row_head = over(within(lax.broadcasted_iota(jnp.int32, (lanes, size), 0), heads), heads // kv)
    slot_head = within(lax.broadcasted_iota(jnp.int32, (lanes, size), 1), kv)
    head_bias = jnp.where(row_head == slot_head, 0.0, -jnp.inf)

    def attend(pair):
        def compute(slots):
            def wait(which):
                @pl.when(pair >= ready[0])
                def _():
                    finish((which,), pair, slots)

            n = slots * kv
            bias = jnp.concatenate([head_bias[:, : min(n, size)]] * max(n // size, 1), axis=1)
            column = lax.broadcasted_iota(jnp.int32, (1, n), 1)
            wait(0)
            scores = []
            for i in range(2):
                row = order[2 * pair + i]
                q = q_ref[:, row].reshape(lanes, size)
                s = lax.dot_general(
                    q,
                    k_buf[2 * pair + i, :n],
                    (((1,), (1,)), ((), ())),
                    preferred_element_type=jnp.float32,
                )
                closed = jnp.where(column < lengths[row] * kv, 0.0, -jnp.inf)
                scores.append(s + (bias + closed))
            highest = [jnp.max(s, axis=1, keepdims=True) * scale for s in scores]
            weights = [jnp.exp2(s * scale - h) for s, h in zip(scores, highest)]
            totals = [jnp.sum(p, axis=1, keepdims=True) for p in weights]
            wait(1)
            for i in range(2):
                o = jnp.dot(
                    weights[i].astype(jnp.bfloat16),
                    v_buf[2 * pair + i, :n],
                    preferred_element_type=jnp.float32,
                )
                spot = 2 * (pair - done) + i
                o_ref[spot] = o / totals[i]
                lse = highest[i] + jnp.log(totals[i]) * LOG2E
                lse_ref[spot] = jnp.broadcast_to(lse, (lanes, size))

        by_length(lengths[order[2 * pair]], sizes, compute)

    if pairs[1] - pairs[0] == 1:
        attend(pairs[0])
    else:
        pl.loop(*pairs)(attend)
    for pair in range(max(pairs[1], ready[0]), ready[1]):
        by_length(lengths[order[2 * pair]], sizes, functools.partial(finish, (0, 1), pair))


def like(x):
    return pltpu.VMEM(x.shape, x.dtype)


def cache_attention(pairs, ready, rows_args, caches, buffers, sizes, after):
    lengths, order, queries = rows_args
    keys, values = caches
    rows, steps, _, heads, size = (keys.shape[0], *queries.shape)
    slots = sizes[-1]
    scale = LOG2E / math.sqrt(size)
    count = 2 * (pairs[1] - pairs[0])
    piece = pltpu.VMEM((count, steps * heads, size), jnp.float32)
    operands = [pinned(x, pltpu.SMEM) for x in (lengths, order)]
    operands += [pinned(queries, pltpu.VMEM)]
    operands += [pinned(keys), pinned(values)]
    aliases = {len(operands) + i: i for i in range(len(buffers))}
    specs = [SMEM, SMEM, VMEM, HBM, HBM] + [VMEM] * len(buffers) + [ANY] * len(after)
    operands += [pinned(b, pltpu.VMEM) for b in buffers] + after
    out_shape = [like(keys), like(values), piece, piece]
    return pl.pallas_call(
        functools.partial(attend_cache, pairs, ready, sizes, scale),
        out_shape=out_shape,
        in_specs=specs,
        out_specs=[VMEM] * len(out_shape),
        input_output_aliases=aliases,
        scratch_shapes=[
            pltpu.SemaphoreType.DMA((rows // 2, 2, 2)),
        ],
        compiler_params=pltpu.CompilerParams(vmem_limit_bytes=8 * MIB),
        cost_estimate=TYPICAL,
        name="cache_attention",
    )(*operands)


def project_old(lay, n_hidden, *refs):
    w_buf, *hidden = refs[: 1 + n_hidden]
    out_ref, h_ref = refs[-2:]
    tp = lax.axis_index("tp")
    for i, h in enumerate(hidden):
        h_ref[lax.rem(tp + i, lay.tp)] = h[...]
    features = h_ref.shape[2]
    chunk = min(features, 1024)
    for k in range(2):
        total = jnp.zeros(out_ref.shape[1:], jnp.float32)
        for t in range(lay.tp):
            for low in range(0, features, chunk):
                start = t * features + low
                total += jnp.dot(
                    h_ref[t, :, low : low + chunk],
                    w_buf[k, start : start + chunk, :],
                    preferred_element_type=jnp.float32,
                )
        out_ref[k] = total


def project(lay, w_buf, hidden, after):
    tokens, features = hidden[0].shape
    return pl.pallas_call(
        functools.partial(project_old, lay, len(hidden)),
        out_shape=(
            pltpu.VMEM((2, tokens, w_buf.shape[2]), jnp.float32),
            pltpu.VMEM((lay.tp, tokens, features), jnp.bfloat16),
        ),
        in_specs=[VMEM] * (1 + len(hidden)) + [ANY] * len(after),
        out_specs=(VMEM, VMEM),
        compiler_params=pltpu.CompilerParams(vmem_limit_bytes=4 * MIB),
        cost_estimate=TYPICAL,
        name="project",
    )(pinned(w_buf, pltpu.VMEM), *hidden, *after)


class Place:
    def __init__(self, lay):
        fsdp, self.grp, self.tp = (lax.axis_index(a) for a in AXES)
        self.z, self.core = fsdp // 2, lax.rem(fsdp, 2)
        self.lay = lay
        there = jnp.where(lax.rem(self.grp, 2) == 0, self.z, lay.depth - 1 - self.z)
        self.own = self.grp * lay.depth + there
        self.per_lane = lay.fsdp * lay.grp // lay.tp
        self.part = plane_part()

    def find(self, plan, downs):
        lay, found = self.lay, []
        for (step, flip, other), down in zip(plan, downs):
            towards = (1 - 2 * self.core if flip else 2 * self.core - 1) * step
            spot = lax.rem(self.own + (lay.ring + towards), lay.ring)
            g = spot // lay.depth
            along = lax.rem(spot, lay.depth)
            zz = jnp.where(lax.rem(g, 2) == 0, along, lay.depth - 1 - along)
            for i in range(2):
                core = lax.rem(self.core + (i + flip), 2)
                index = (zz * 2 + core) * lay.grp + g
                found.append((down.at[i], index, 1 - self.part if other else self.part))
        return found

    def low(self, shards, h_ref, tiles):
        total = None
        for down, index, _ in shards:
            depth = tiles * down.shape[-1]
            column = pl.multiple_of(lax.rem(index, self.per_lane) * depth, depth)
            term = lax.dot_general(
                h_ref[index // self.per_lane, :, pl.ds(column, depth)],
                jnp.concatenate([down[i] for i in range(tiles)], axis=1),
                (((1,), (1,)), ((), ())),
                preferred_element_type=jnp.float32,
            )
            total = term if total is None else total + term
        return total


def merge_some(lay, plan, n_caches, scale, *refs):
    refs = list(refs)

    def take(n):
        out = refs[:n]
        del refs[:n]
        return out

    last = n_caches > 0
    downs = take(len(plan))
    h_buf, weights = take(2)
    if last:
        old, order, q_ref = take(3)
        caches = [take(2) for _ in range(n_caches)]
        u_buf, low_in, _ = take(3)
        m_hbm, out_hbm, m_buf, sems, low, out_buf, out_sem = refs[-7:]
    else:
        m_hbm, u_buf, low, m_buf, sems, u_parts = refs[-6:]
    depth, width = m_buf.shape[1:]
    pairs = weights.shape[0]
    cut = min(width, 256)
    lanes = downs[0].shape[-1]
    tiles = depth // lanes
    place = Place(lay)
    shards = place.find(plan, downs)
    groups = [
        (place.part, [s for s, e in zip(shards, [e for e in plan for _ in range(2)]) if not e[2]]),
        (1 - place.part, [s for s, e in zip(shards, [e for e in plan for _ in range(2)]) if e[2]]),
    ]

    if last:
        low[...] = low_in[...]
        for part, group in groups:
            if group:
                low[part] += place.low(group, h_buf, tiles)
        new = []
        for k in range(pairs):
            high = low[k].astype(jnp.bfloat16)
            rest = (low[k] - high.astype(jnp.float32)).astype(jnp.bfloat16)
            new.append(
                (
                    old[k]
                    + jnp.dot(high, u_buf[k], preferred_element_type=jnp.float32)
                    + jnp.dot(rest, u_buf[k], preferred_element_type=jnp.float32)
                ).astype(jnp.bfloat16)
            )
        add_new_tokens(q_ref, order, caches, new, out_buf, scale)
        out_copy = pltpu.make_async_copy(out_buf, out_hbm, out_sem)
        out_copy.start()
    else:
        columns = width // place.per_lane
        for down, index, _ in groups[0][1]:

            @pl.when(index // place.per_lane == place.tp)
            def _():
                u_parts[lax.rem(index, place.per_lane)] = down[tiles, :, : pairs * columns]

        for k in range(pairs):
            u_buf[k] = ADAPTER_SCALING * jnp.concatenate(
                [
                    u_parts[i, :, k * columns : (k + 1) * columns]
                    for i in range(place.per_lane)
                ],
                axis=1,
            )

    chunk = min(depth, 256)
    copies = []
    for j, (down, index, k) in enumerate(shards):
        start = pl.multiple_of(index * depth, depth)
        for begin in range(0, depth, chunk):
            rows = slice(begin, begin + chunk)
            tile = begin // lanes
            d = jnp.concatenate([down[tile + i] for i in range(chunk // lanes)], axis=1)
            for side in range(width // cut):
                cols = slice(side * cut, (side + 1) * cut)
                added = lax.dot_general(
                    d,
                    u_buf[k, :, cols],
                    (((0,), (0,)), ((), ())),
                    preferred_element_type=jnp.float32,
                )
                w = weights[k, pl.ds(start + begin, chunk), cols]
                m_buf[j, rows, cols] = (w.astype(jnp.float32) + added).astype(jnp.bfloat16)
        copy = pltpu.make_async_copy(m_buf.at[j], m_hbm.at[k, pl.ds(start, depth), :], sems.at[j])
        copy.start()
        copies.append(copy)

    if not last:
        for part, group in groups:
            low[part] = place.low(group, h_buf, tiles)
    for copy in copies + ([out_copy] if last else []):
        copy.wait()


def add_new_tokens(q_ref, order, caches, new, out_buf, scale):
    steps, rows, heads, size = q_ref.shape
    kv = new[0].shape[1] // size
    new = [
        jnp.concatenate([x[:, g * size : (g + 1) * size] for g in range(kv)], axis=0) for x in new
    ]
    n = kv * steps * rows
    lanes = steps * heads
    left = lax.broadcasted_iota(jnp.int32, (lanes, n), 0)
    right = lax.broadcasted_iota(jnp.int32, (lanes, n), 1)
    same_head = over(within(left, heads), heads // kv) == over(right, steps * rows)
    earlier = within(over(right, rows), steps) <= over(left, heads)
    right_row = jnp.where(same_head & earlier, within(right, rows), -1)

    def all_rows(pieces):
        return jnp.concatenate(list(pieces), axis=0)

    q = all_rows(q_ref[:, order[spot]].reshape(lanes, size) for spot in range(rows))
    s = lax.dot_general(q, new[0], (((1,), (1,)), ((), ())), preferred_element_type=jnp.float32)
    bias = all_rows(
        jnp.where(right_row == order[spot], 0.0, -jnp.inf) for spot in range(rows)
    )
    s = s * scale + bias
    lse = all_rows(ref[i] for _, ref in caches for i in range(ref.shape[0]))
    highest = jnp.maximum(jnp.max(s, axis=1, keepdims=True), lse)
    p = jnp.exp2(s - highest[:, :n])
    old = jnp.exp2(lse - highest)
    divisor = jnp.sum(p, axis=1, keepdims=True) + old
    o = old * all_rows(ref[i] for ref, _ in caches for i in range(ref.shape[0]))
    o = (o + jnp.dot(p.astype(jnp.bfloat16), new[1], preferred_element_type=jnp.float32)) / divisor
    for spot in range(rows):
        piece = o[spot * lanes : (spot + 1) * lanes].astype(out_buf.dtype)
        out_buf[:, order[spot]] = piece.reshape(steps, heads, size)


def merge(lay, shape, entries, states, weights, state, final, after):
    pairs, total, width = shape
    tokens, rank = states.shape[1], entries[0][3].shape[-2]
    depth = total // (lay.fsdp * lay.grp)
    per_lane = lay.fsdp * lay.grp // lay.tp
    n = 2 * len(entries)
    merged = pltpu.HBM(shape, jnp.bfloat16)
    low_shape = (pairs, tokens, rank)
    operands = [e[3] for e in entries] + [pinned(states, pltpu.VMEM), pinned(weights, pltpu.VMEM)]
    specs = [VMEM] * len(operands)
    scratch = [pltpu.VMEM((n, depth, width), jnp.bfloat16), pltpu.SemaphoreType.DMA((n,))]
    aliases = {}
    if state is None:
        out_shape = [
            merged,
            pltpu.VMEM((pairs, rank, width), jnp.bfloat16),
            pltpu.VMEM(low_shape, jnp.float32),
        ]
        out_specs = [HBM, VMEM, VMEM]
        scratch.append(pltpu.VMEM((per_lane, rank, pairs * width // per_lane), jnp.bfloat16))
        n_caches, scale = 0, 0.0
    else:
        olds, order, queries, caches = final
        m_prev, u_buf, low = state
        operands += [olds, pinned(order, pltpu.SMEM), pinned(queries, pltpu.VMEM), *caches]
        specs += [VMEM, SMEM, VMEM] + [VMEM] * len(caches)
        operands += [pinned(u_buf, pltpu.VMEM), pinned(low, pltpu.VMEM), pinned(m_prev)]
        specs += [VMEM, VMEM, HBM]
        aliases = {len(operands) - 1: 0}
        out_shape = [merged, pltpu.HBM(queries.shape, jnp.bfloat16)]
        out_specs = [HBM, HBM]
        scratch += [
            pltpu.VMEM(low_shape, jnp.float32),
            pltpu.VMEM(queries.shape, jnp.bfloat16),
            pltpu.SemaphoreType.DMA,
        ]
        n_caches, scale = len(caches) // 2, LOG2E / math.sqrt(queries.shape[3])
    return pl.pallas_call(
        functools.partial(merge_some, lay, [e[:3] for e in entries], n_caches, scale),
        out_shape=out_shape,
        in_specs=specs + [ANY] * len(after),
        out_specs=out_specs,
        input_output_aliases=aliases,
        scratch_shapes=scratch,
        compiler_params=pltpu.CompilerParams(vmem_limit_bytes=20 * MIB),
        cost_estimate=TYPICAL,
        name="merge",
    )(*operands, *after)


def shards(
    lay,
    hidden_states,
    queries,
    cache_keys,
    cache_values,
    cache_lengths,
    projection_weight_matrices,
    factor_down,
    factor_up,
):
    send = functools.partial(lax.ppermute, axis_name=AXES)
    steps, rows, features = hidden_states.shape
    slots, kv, size = cache_keys.shape[1:]
    shape = projection_weight_matrices.shape
    sizes = tuple(slots * i // 24 for i in (1, 4, 8, 16, 24))
    own = jnp.swapaxes(factor_down, 1, 2)
    tokens = hidden_states.reshape(steps * rows, features)
    keys = cache_keys.reshape(rows, slots * kv, size)
    values = cache_values.reshape(rows, slots * kv, size)
    swap, ring, planes = lay.core_swap(), lay.ring_step(), lay.plane_swap()
    pair_count = rows // 2
    last_step = lay.ring // 2
    buffers, caches = [], []

    other, other_up = send(own, perm=swap), send(factor_up, perm=swap)
    pair, rest, *rows_args = begin(own, factor_up, cache_lengths, queries)
    pair, rest = pack(other, other_up, pair, rest)

    def attention(pairs, ready, after):
        nonlocal buffers
        out = cache_attention(pairs, ready, rows_args, (keys, values), buffers, sizes, after)
        buffers = list(out[:2])
        caches.extend(out[2:])
        return out[2]

    entries = [(0, 0, 0, pair), (0, 0, 1, rest)]
    sent = send(pair, perm=ring)
    hidden = [tokens] + [send(tokens, perm=lay.feature_step(i)) for i in range(1, lay.tp)]
    token = attention((0, 1), (0, 2), [pair])
    came, token = after_all(sent, token)
    crossed = []
    for step in range(1, last_step):
        entries.append((step, 0, 0, came))
        crossed_on = [send(x, perm=swap) for x in crossed]
        here = [send(came, perm=planes), send(came, perm=swap)]
        sent = send(came, perm=ring)
        waited = []
        if step == 1:
            waited = hidden
            token = attention((1, pair_count), (2, pair_count), [token])
        elif step == 2:
            olds, states = project(lay, projection_weight_matrices, hidden, [token])
            token = olds
        (came, here, crossed_on, waited), token = after_all((sent, here, crossed_on, waited), token)
        if step == 1:
            hidden = waited
        entries += [(step, 0, 1, here[0]), (step, 1, 0, here[1])]
        entries += [(step - 1, 1, 1, x) for x in crossed_on]
        crossed = here[:1]
    entries.append((last_step, 0, 0, came))
    late = [send(came, perm=planes), send(crossed[0], perm=swap)]
    m, *state = merge(
        lay, shape, entries, states, projection_weight_matrices, None, None, [token]
    )
    late, state[1] = after_all(late, state[1])
    entries = [(last_step, 0, 1, late[0]), (last_step - 1, 1, 1, late[1])]
    _, order, q = rows_args
    final = (olds, order, q, caches)
    return tuple(
        merge(
            lay, shape, entries, states, projection_weight_matrices, [m, *state], final, []
        )
    )


def solution(mesh):
    return jax.shard_map(
        functools.partial(shards, Layout(mesh)),
        mesh=mesh,
        in_specs=(
            P(None, ("fsdp", "grp"), "tp"),
            P(None, ("fsdp", "grp"), "tp", None),
            P(("fsdp", "grp"), None, "tp", None),
            P(("fsdp", "grp"), None, "tp", None),
            P(("fsdp", "grp")),
            P(None, None, "tp"),
            P(None, ("fsdp", "grp"), None),
            P(None, None, ("fsdp", "grp")),
        ),
        out_specs=(P(None, None, "tp"), P(None, ("fsdp", "grp"), "tp", None)),
        check_vma=False,
    )
```

```python
import functools
import math

import jax
import jax.numpy as jnp
from jax import lax
from jax.experimental import pallas as pl
from jax.experimental.pallas import tpu as pltpu
from jax.sharding import PartitionSpec as P

AXES = ("fsdp", "grp", "tp")
ADAPTER_SCALING = 2.0
LOG2E = math.log2(math.e)
MIB = 1024 * 1024
ANY = pl.BlockSpec(memory_space=pl.ANY)
HBM = pl.BlockSpec(memory_space=pltpu.HBM)
VMEM = pl.BlockSpec(memory_space=pltpu.VMEM)
SMEM = pl.BlockSpec(memory_space=pltpu.SMEM)


class Layout:
    def __init__(self, mesh):
        self.fsdp, self.grp, self.tp = (mesh.shape[a] for a in AXES)
        self.depth = self.fsdp // 2
        self.ring = self.depth * self.grp
        self.block = self.depth // self.tp

    def flat(self, z, core, g, t):
        return ((z * 2 + core) * self.grp + g) * self.tp + t

    def devices(self):
        for z in range(self.depth):
            for core in range(2):
                for g in range(self.grp):
                    for t in range(self.tp):
                        yield z, core, g, t

    def place(self, z, g):
        return g * self.depth + (z if g % 2 == 0 else self.depth - 1 - z)

    def at(self, position):
        g, z = divmod(position, self.depth)
        return (z if g % 2 == 0 else self.depth - 1 - z), g

    def ring_step(self):
        pairs = []
        for z, core, g, t in self.devices():
            to_z, to_g = self.at((self.place(z, g) + (1 - 2 * core)) % self.ring)
            pairs.append((self.flat(z, core, g, t), self.flat(to_z, core, to_g, t)))
        return pairs

    def plane_swap(self):
        return [(self.flat(z, c, g, t), self.flat(z, c, g, t ^ 1)) for z, c, g, t in self.devices()]

    def core_swap(self):
        return [
            (self.flat(z, c, g, t), self.flat(z, 1 - c, g, t)) for z, c, g, t in self.devices()
        ]

    def feature_step(self, step):
        return [
            (self.flat(z, c, g, (t + step) % self.tp), self.flat(z, c, g, t))
            for z, c, g, t in self.devices()
        ]


TYPICAL = pl.CostEstimate(flops=6 * 10**8, bytes_accessed=10**7, transcendentals=0)


def over(x, n):
    return x >> (n.bit_length() - 1) if n & (n - 1) == 0 else x // n


def within(x, n):
    return x & (n - 1) if n & (n - 1) == 0 else x % n


def after_all(arrays, token):
    return lax.optimization_barrier((arrays, token))


def pinned(x, space=pltpu.HBM):
    return pltpu.with_memory_space_constraint(x, space)


def sort_rows(lengths, order):
    rows = lengths.shape[0]
    held = [lengths[r] for r in range(rows)]
    for r in range(rows):
        rank = jnp.int32(0)
        for other in range(rows):
            if other != r:
                ahead = held[other] >= held[r] if other < r else held[other] > held[r]
                rank = rank + ahead.astype(jnp.int32)
        order[rank] = r


def by_length(length, sizes, act):
    below = 0
    for slots in sizes:

        @pl.when((length > below) & (length <= slots))
        def _():
            act(slots)

        below = slots


def up_columns(up):
    return jnp.concatenate([up[k] for k in range(up.shape[0])], axis=1)


def plane_part():
    return lax.rem(lax.axis_index("tp"), 2)


def begin_all(down, up, len_hbm, q_hbm, pair, rest, lengths, order, q_ref, up_buf, sems, more):
    lanes = pair.shape[3]
    depth = down.shape[2]
    tiles = depth // lanes
    part = plane_part()
    copies = [
        pltpu.make_async_copy(
            down.at[k, :, pl.ds(i * lanes, lanes)], array.at[0, i], sems.at[which, i]
        )
        for which, (k, array) in enumerate(((part, pair), (1 - part, rest)))
        for i in range(tiles)
    ]
    up_copy = pltpu.make_async_copy(up, up_buf, more.at[0])
    len_copy = pltpu.make_async_copy(len_hbm, lengths, more.at[1])
    q_copy = pltpu.make_async_copy(q_hbm, q_ref, more.at[2])
    for copy in [len_copy, up_copy] + copies + [q_copy]:
        copy.start()
    len_copy.wait()
    sort_rows(lengths, order)
    up_copy.wait()
    columns = up_columns(up_buf)
    pair[0, tiles, :, : columns.shape[1]] = columns
    for copy in copies + [q_copy]:
        copy.wait()


def begin(down, up, lengths, queries):
    count, rank, depth = down.shape
    tiles = depth // 128
    scalars = pltpu.SMEM(lengths.shape, jnp.int32)
    return pl.pallas_call(
        begin_all,
        out_shape=(
            pltpu.VMEM((2, tiles + 1, rank, 128), down.dtype),
            pltpu.VMEM((2, tiles, rank, 128), down.dtype),
            scalars,
            scalars,
            pltpu.VMEM(queries.shape, queries.dtype),
        ),
        in_specs=[HBM] * 4,
        out_specs=(VMEM, VMEM, SMEM, SMEM, VMEM),
        scratch_shapes=[
            pltpu.VMEM(up.shape, up.dtype),
            pltpu.SemaphoreType.DMA((count, tiles)),
            pltpu.SemaphoreType.DMA((3,)),
        ],
        compiler_params=pltpu.CompilerParams(vmem_limit_bytes=2 * MIB),
        cost_estimate=TYPICAL,
        name="begin",
    )(pinned(down), pinned(up), pinned(lengths), pinned(queries))


def pack_other(down, up, _, __, pair, rest):
    lanes = pair.shape[3]
    tiles = down.shape[2] // lanes
    part = plane_part()
    for i in range(tiles):
        cols = slice(i * lanes, (i + 1) * lanes)
        pair[1, i] = down[part, :, cols]
        rest[1, i] = down[1 - part, :, cols]
    columns = up_columns(up)
    pair[1, tiles, :, : columns.shape[1]] = columns


def pack(down, up, pair, rest):
    return pl.pallas_call(
        pack_other,
        out_shape=(like(pair), like(rest)),
        in_specs=[VMEM] * 4,
        out_specs=(VMEM, VMEM),
        input_output_aliases={2: 0, 3: 1},
        compiler_params=pltpu.CompilerParams(vmem_limit_bytes=2 * MIB),
        cost_estimate=TYPICAL,
        name="pack_other",
    )(down, up, pinned(pair, pltpu.VMEM), pinned(rest, pltpu.VMEM))


def attend_cache(pairs, ready, sizes, scale, *refs):
    lengths, order, q_ref, k_hbm, v_hbm = refs[:5]
    k_buf, v_buf, *outs, sems = refs[-5:]
    done = pairs[0]
    o_ref, lse_ref = outs[:2]
    steps, _, heads, size = q_ref.shape
    kv = k_hbm.shape[1] // sizes[-1]
    lanes = steps * heads

    def copies(which, pair, slots):
        span = pl.ds(0, slots * kv)
        hbm, buf = ((k_hbm, k_buf), (v_hbm, v_buf))[which]
        return [
            pltpu.make_async_copy(
                hbm.at[order[2 * pair + i], span],
                buf.at[2 * pair + i, span],
                sems.at[pair, i, which],
            )
            for i in range(2)
        ]

    def start(pair, slots):
        for copy in copies(0, pair, slots) + copies(1, pair, slots):
            copy.start()

    def finish(which, pair, slots):
        for i in which:
            for copy in copies(i, pair, slots):
                copy.wait()

    for pair in range(*ready):
        by_length(lengths[order[2 * pair]], sizes, functools.partial(start, pair))

    row_head = over(within(lax.broadcasted_iota(jnp.int32, (lanes, size), 0), heads), heads // kv)
    slot_head = within(lax.broadcasted_iota(jnp.int32, (lanes, size), 1), kv)
    head_bias = jnp.where(row_head == slot_head, 0.0, -jnp.inf)

    def attend(pair):
        def compute(slots):
            def wait(which):
                @pl.when(pair >= ready[0])
                def _():
                    finish((which,), pair, slots)

            n = slots * kv
            bias = jnp.concatenate([head_bias[:, : min(n, size)]] * max(n // size, 1), axis=1)
            column = lax.broadcasted_iota(jnp.int32, (1, n), 1)
            wait(0)
            scores = []
            for i in range(2):
                row = order[2 * pair + i]
                q = q_ref[:, row].reshape(lanes, size)
                s = lax.dot_general(
                    q,
                    k_buf[2 * pair + i, :n],
                    (((1,), (1,)), ((), ())),
                    preferred_element_type=jnp.float32,
                )
                closed = jnp.where(column < lengths[row] * kv, 0.0, -jnp.inf)
                scores.append(s + (bias + closed))
            highest = [jnp.max(s, axis=1, keepdims=True) * scale for s in scores]
            weights = [jnp.exp2(s * scale - h) for s, h in zip(scores, highest)]
            totals = [jnp.sum(p, axis=1, keepdims=True) for p in weights]
            wait(1)
            for i in range(2):
                o = jnp.dot(
                    weights[i].astype(jnp.bfloat16),
                    v_buf[2 * pair + i, :n],
                    preferred_element_type=jnp.float32,
                )
                spot = 2 * (pair - done) + i
                o_ref[spot] = o / totals[i]
                lse = highest[i] + jnp.log(totals[i]) * LOG2E
                lse_ref[spot] = jnp.broadcast_to(lse, (lanes, size))

        by_length(lengths[order[2 * pair]], sizes, compute)

    if pairs[1] - pairs[0] == 1:
        attend(pairs[0])
    else:
        pl.loop(*pairs)(attend)
    for pair in range(max(pairs[1], ready[0]), ready[1]):
        by_length(lengths[order[2 * pair]], sizes, functools.partial(finish, (0, 1), pair))


def like(x):
    return pltpu.VMEM(x.shape, x.dtype)


def cache_attention(pairs, ready, rows_args, caches, buffers, sizes, after):
    lengths, order, queries = rows_args
    keys, values = caches
    rows, steps, _, heads, size = (keys.shape[0], *queries.shape)
    slots = sizes[-1]
    scale = LOG2E / math.sqrt(size)
    count = 2 * (pairs[1] - pairs[0])
    piece = pltpu.VMEM((count, steps * heads, size), jnp.float32)
    operands = [pinned(x, pltpu.SMEM) for x in (lengths, order)]
    operands += [pinned(queries, pltpu.VMEM)]
    operands += [pinned(keys), pinned(values)]
    aliases = {len(operands) + i: i for i in range(len(buffers))}
    specs = [SMEM, SMEM, VMEM, HBM, HBM] + [VMEM] * len(buffers) + [ANY] * len(after)
    operands += [pinned(b, pltpu.VMEM) for b in buffers] + after
    out_shape = [like(keys), like(values), piece, piece]
    return pl.pallas_call(
        functools.partial(attend_cache, pairs, ready, sizes, scale),
        out_shape=out_shape,
        in_specs=specs,
        out_specs=[VMEM] * len(out_shape),
        input_output_aliases=aliases,
        scratch_shapes=[
            pltpu.SemaphoreType.DMA((rows // 2, 2, 2)),
        ],
        compiler_params=pltpu.CompilerParams(vmem_limit_bytes=8 * MIB),
        cost_estimate=TYPICAL,
        name="cache_attention",
    )(*operands)


def project_old(lay, n_hidden, *refs):
    w_buf, *hidden = refs[: 1 + n_hidden]
    out_ref, h_ref = refs[-2:]
    tp = lax.axis_index("tp")
    for i, h in enumerate(hidden):
        h_ref[lax.rem(tp + i, lay.tp)] = h[...]
    features = h_ref.shape[2]
    chunk = min(features, 1024)
    for k in range(2):
        total = jnp.zeros(out_ref.shape[1:], jnp.float32)
        for t in range(lay.tp):
            for low in range(0, features, chunk):
                start = t * features + low
                total += jnp.dot(
                    h_ref[t, :, low : low + chunk],
                    w_buf[k, start : start + chunk, :],
                    preferred_element_type=jnp.float32,
                )
        out_ref[k] = total


def project(lay, w_buf, hidden, after):
    tokens, features = hidden[0].shape
    return pl.pallas_call(
        functools.partial(project_old, lay, len(hidden)),
        out_shape=(
            pltpu.VMEM((2, tokens, w_buf.shape[2]), jnp.float32),
            pltpu.VMEM((lay.tp, tokens, features), jnp.bfloat16),
        ),
        in_specs=[VMEM] * (1 + len(hidden)) + [ANY] * len(after),
        out_specs=(VMEM, VMEM),
        compiler_params=pltpu.CompilerParams(vmem_limit_bytes=4 * MIB),
        cost_estimate=TYPICAL,
        name="project",
    )(pinned(w_buf, pltpu.VMEM), *hidden, *after)


class Place:
    def __init__(self, lay):
        fsdp, self.grp, self.tp = (lax.axis_index(a) for a in AXES)
        self.z, self.core = fsdp // 2, lax.rem(fsdp, 2)
        self.lay = lay
        there = jnp.where(lax.rem(self.grp, 2) == 0, self.z, lay.depth - 1 - self.z)
        self.own = self.grp * lay.depth + there
        self.per_lane = lay.fsdp * lay.grp // lay.tp
        self.part = plane_part()

    def find(self, plan, downs):
        lay, found = self.lay, []
        for (step, flip, other), down in zip(plan, downs):
            towards = (1 - 2 * self.core if flip else 2 * self.core - 1) * step
            spot = lax.rem(self.own + (lay.ring + towards), lay.ring)
            g = spot // lay.depth
            along = lax.rem(spot, lay.depth)
            zz = jnp.where(lax.rem(g, 2) == 0, along, lay.depth - 1 - along)
            for i in range(2):
                core = lax.rem(self.core + (i + flip), 2)
                index = (zz * 2 + core) * lay.grp + g
                found.append((down.at[i], index, 1 - self.part if other else self.part))
        return found

    def low(self, shards, h_ref, tiles):
        total = jnp.zeros((h_ref.shape[1], shards[0][0].shape[1]), jnp.float32) if shards else 0.0
        for down, index, _ in shards:
            depth = tiles * down.shape[-1]
            column = pl.multiple_of(lax.rem(index, self.per_lane) * depth, depth)
            term = lax.dot_general(
                h_ref[index // self.per_lane, :, pl.ds(column, depth)],
                jnp.concatenate([down[i] for i in range(tiles)], axis=1),
                (((1,), (1,)), ((), ())),
                preferred_element_type=jnp.float32,
            )
            total += term
        return total


def by_projection(place, plan, shards):
    crossed = [other for _, _, other in plan for _ in range(2)]
    return [
        (place.part, [s for s, other in zip(shards, crossed) if not other]),
        (1 - place.part, [s for s, other in zip(shards, crossed) if other]),
    ]


def low_some(lay, plan, tiles, *refs):
    downs, h_ref, out_ref = refs[: len(plan)], refs[len(plan)], refs[-1]
    place = Place(lay)
    for part, group in by_projection(place, plan, place.find(plan, downs)):
        out_ref[part] = place.low(group, h_ref, tiles)


def project_low(lay, entries, states, pairs, tiles, after):
    return pl.pallas_call(
        functools.partial(low_some, lay, [e[:3] for e in entries], tiles),
        out_shape=pltpu.VMEM((pairs, states.shape[1], entries[0][3].shape[-2]), jnp.float32),
        in_specs=[VMEM] * (len(entries) + 1) + [ANY] * len(after),
        out_specs=VMEM,
        compiler_params=pltpu.CompilerParams(vmem_limit_bytes=2 * MIB),
        cost_estimate=TYPICAL,
        name="project_low",
    )(*[e[3] for e in entries], pinned(states, pltpu.VMEM), *after)


def merge_some(lay, plan, n_low, n_caches, scale, *refs):
    refs = list(refs)

    def take(n):
        out = refs[:n]
        del refs[:n]
        return out

    last = n_caches > 0
    downs = take(len(plan))
    h_buf, weights = take(2)
    if last:
        old, order, q_ref = take(3)
        caches = [take(2) for _ in range(n_caches)]
        u_buf, low_in, _ = take(3)
        m_hbm, out_hbm, m_buf, sems, low, out_buf, out_sem = refs[-7:]
    else:
        (low_in,) = take(1)
        m_hbm, u_buf, low, m_buf, sems, u_parts = refs[-6:]
    depth, width = m_buf.shape[1:]
    pairs = weights.shape[0]
    cut = min(width, 256)
    lanes = downs[0].shape[-1]
    tiles = depth // lanes
    place = Place(lay)
    shards = place.find(plan, downs)
    groups = by_projection(place, plan, shards)
    low_groups = by_projection(place, plan[n_low:], shards[2 * n_low :])

    if last:
        low[...] = low_in[...]
        for part, group in low_groups:
            low[part] += place.low(group, h_buf, tiles)
        new = []
        for k in range(pairs):
            high = low[k].astype(jnp.bfloat16)
            rest = (low[k] - high.astype(jnp.float32)).astype(jnp.bfloat16)
            new.append(
                (
                    old[k]
                    + jnp.dot(high, u_buf[k], preferred_element_type=jnp.float32)
                    + jnp.dot(rest, u_buf[k], preferred_element_type=jnp.float32)
                ).astype(jnp.bfloat16)
            )
        add_new_tokens(q_ref, order, caches, new, out_buf, scale)
        out_copy = pltpu.make_async_copy(out_buf, out_hbm, out_sem)
        out_copy.start()
    else:
        columns = width // place.per_lane
        for down, index, _ in groups[0][1]:

            @pl.when(index // place.per_lane == place.tp)
            def _():
                u_parts[lax.rem(index, place.per_lane)] = down[tiles, :, : pairs * columns]

        for k in range(pairs):
            u_buf[k] = ADAPTER_SCALING * jnp.concatenate(
                [
                    u_parts[i, :, k * columns : (k + 1) * columns]
                    for i in range(place.per_lane)
                ],
                axis=1,
            )

    chunk = min(depth, 256)
    copies = []
    for j, (down, index, k) in enumerate(shards):
        start = pl.multiple_of(index * depth, depth)
        for begin in range(0, depth, chunk):
            rows = slice(begin, begin + chunk)
            tile = begin // lanes
            d = jnp.concatenate([down[tile + i] for i in range(chunk // lanes)], axis=1)
            for side in range(width // cut):
                cols = slice(side * cut, (side + 1) * cut)
                added = lax.dot_general(
                    d,
                    u_buf[k, :, cols],
                    (((0,), (0,)), ((), ())),
                    preferred_element_type=jnp.float32,
                )
                w = weights[k, pl.ds(start + begin, chunk), cols]
                m_buf[j, rows, cols] = (w.astype(jnp.float32) + added).astype(jnp.bfloat16)
        copy = pltpu.make_async_copy(m_buf.at[j], m_hbm.at[k, pl.ds(start, depth), :], sems.at[j])
        copy.start()
        copies.append(copy)

    if not last:
        low[...] = low_in[...]
        for part, group in low_groups:
            low[part] += place.low(group, h_buf, tiles)
    for copy in copies + ([out_copy] if last else []):
        copy.wait()


def add_new_tokens(q_ref, order, caches, new, out_buf, scale):
    steps, rows, heads, size = q_ref.shape
    kv = new[0].shape[1] // size
    new = [
        jnp.concatenate([x[:, g * size : (g + 1) * size] for g in range(kv)], axis=0) for x in new
    ]
    n = kv * steps * rows
    lanes = steps * heads
    left = lax.broadcasted_iota(jnp.int32, (lanes, n), 0)
    right = lax.broadcasted_iota(jnp.int32, (lanes, n), 1)
    same_head = over(within(left, heads), heads // kv) == over(right, steps * rows)
    earlier = within(over(right, rows), steps) <= over(left, heads)
    right_row = jnp.where(same_head & earlier, within(right, rows), -1)

    def all_rows(pieces):
        return jnp.concatenate(list(pieces), axis=0)

    q = all_rows(q_ref[:, order[spot]].reshape(lanes, size) for spot in range(rows))
    s = lax.dot_general(q, new[0], (((1,), (1,)), ((), ())), preferred_element_type=jnp.float32)
    bias = all_rows(
        jnp.where(right_row == order[spot], 0.0, -jnp.inf) for spot in range(rows)
    )
    s = s * scale + bias
    lse = all_rows(ref[i] for _, ref in caches for i in range(ref.shape[0]))
    highest = jnp.maximum(jnp.max(s, axis=1, keepdims=True), lse)
    p = jnp.exp2(s - highest[:, :n])
    old = jnp.exp2(lse - highest)
    divisor = jnp.sum(p, axis=1, keepdims=True) + old
    o = old * all_rows(ref[i] for ref, _ in caches for i in range(ref.shape[0]))
    o = (o + jnp.dot(p.astype(jnp.bfloat16), new[1], preferred_element_type=jnp.float32)) / divisor
    for spot in range(rows):
        piece = o[spot * lanes : (spot + 1) * lanes].astype(out_buf.dtype)
        out_buf[:, order[spot]] = piece.reshape(steps, heads, size)


def merge(lay, shape, entries, n_low, states, weights, state, final, after):
    pairs, total, width = shape
    tokens, rank = states.shape[1], entries[0][3].shape[-2]
    depth = total // (lay.fsdp * lay.grp)
    per_lane = lay.fsdp * lay.grp // lay.tp
    n = 2 * len(entries)
    merged = pltpu.HBM(shape, jnp.bfloat16)
    low_shape = (pairs, tokens, rank)
    operands = [e[3] for e in entries] + [pinned(states, pltpu.VMEM), pinned(weights, pltpu.VMEM)]
    specs = [VMEM] * len(operands)
    scratch = [pltpu.VMEM((n, depth, width), jnp.bfloat16), pltpu.SemaphoreType.DMA((n,))]
    aliases = {}
    if final is None:
        operands.append(pinned(state, pltpu.VMEM))
        specs.append(VMEM)
        out_shape = [
            merged,
            pltpu.VMEM((pairs, rank, width), jnp.bfloat16),
            pltpu.VMEM(low_shape, jnp.float32),
        ]
        out_specs = [HBM, VMEM, VMEM]
        scratch.append(pltpu.VMEM((per_lane, rank, pairs * width // per_lane), jnp.bfloat16))
        n_caches, scale = 0, 0.0
    else:
        olds, order, queries, caches = final
        m_prev, u_buf, low = state
        operands += [olds, pinned(order, pltpu.SMEM), pinned(queries, pltpu.VMEM), *caches]
        specs += [VMEM, SMEM, VMEM] + [VMEM] * len(caches)
        operands += [pinned(u_buf, pltpu.VMEM), pinned(low, pltpu.VMEM), pinned(m_prev)]
        specs += [VMEM, VMEM, HBM]
        aliases = {len(operands) - 1: 0}
        out_shape = [merged, pltpu.HBM(queries.shape, jnp.bfloat16)]
        out_specs = [HBM, HBM]
        scratch += [
            pltpu.VMEM(low_shape, jnp.float32),
            pltpu.VMEM(queries.shape, jnp.bfloat16),
            pltpu.SemaphoreType.DMA,
        ]
        n_caches, scale = len(caches) // 2, LOG2E / math.sqrt(queries.shape[3])
    return pl.pallas_call(
        functools.partial(merge_some, lay, [e[:3] for e in entries], n_low, n_caches, scale),
        out_shape=out_shape,
        in_specs=specs + [ANY] * len(after),
        out_specs=out_specs,
        input_output_aliases=aliases,
        scratch_shapes=scratch,
        compiler_params=pltpu.CompilerParams(vmem_limit_bytes=20 * MIB),
        cost_estimate=TYPICAL,
        name="merge",
    )(*operands, *after)


def shards(
    lay,
    hidden_states,
    queries,
    cache_keys,
    cache_values,
    cache_lengths,
    projection_weight_matrices,
    factor_down,
    factor_up,
):
    send = functools.partial(lax.ppermute, axis_name=AXES)
    steps, rows, features = hidden_states.shape
    slots, kv, size = cache_keys.shape[1:]
    shape = projection_weight_matrices.shape
    sizes = tuple(slots * i // 24 for i in (1, 4, 8, 16, 24))
    own = jnp.swapaxes(factor_down, 1, 2)
    tokens = hidden_states.reshape(steps * rows, features)
    keys = cache_keys.reshape(rows, slots * kv, size)
    values = cache_values.reshape(rows, slots * kv, size)
    swap, ring, planes = lay.core_swap(), lay.ring_step(), lay.plane_swap()
    pair_count = rows // 2
    last_step = lay.ring // 2
    buffers, caches = [], []

    other, other_up = send(own, perm=swap), send(factor_up, perm=swap)
    pair, rest, *rows_args = begin(own, factor_up, cache_lengths, queries)
    pair, rest = pack(other, other_up, pair, rest)

    def attention(pairs, ready, after):
        nonlocal buffers
        out = cache_attention(pairs, ready, rows_args, (keys, values), buffers, sizes, after)
        buffers = list(out[:2])
        caches.extend(out[2:])
        return out[2]

    entries = [(0, 0, 0, pair), (0, 0, 1, rest)]
    sent = send(pair, perm=ring)
    hidden = [tokens] + [send(tokens, perm=lay.feature_step(i)) for i in range(1, lay.tp)]
    token = attention((0, 1), (0, 2), [pair])
    came, token = after_all(sent, token)
    crossing, crossed = [], []
    for step in range(1, last_step):
        entries.append((step, 0, 0, came))
        over_there = [(s, send(x, perm=swap)) for s, x in crossed]
        across = [(step, send(came, perm=planes))]
        swapped = send(came, perm=swap)
        sent = send(came, perm=ring)
        if step == 1:
            token = attention((1, pair_count), (2, pair_count), [token])
        elif step == 2:
            olds, states = project(lay, projection_weight_matrices, hidden, [token])
            token = olds
        elif step == 3:
            n_low = len(entries)
            tiles = own.shape[2] // 128
            token = low = project_low(lay, entries, states, shape[0], tiles, [token])
        late = crossing + (across if step + 1 == last_step else [])
        (held, swapped, hidden, arrived, came), token = after_all(
            ([x for _, x in over_there], swapped, hidden, [x for _, x in late], sent), token
        )
        entries.append((step, 1, 0, swapped))
        entries += [(s, 1, 1, x) for (s, _), x in zip(over_there, held)]
        crossed = [(s, x) for (s, _), x in zip(late, arrived)]
        entries += [(s, 0, 1, x) for s, x in crossed]
        crossing = across
    entries.append((last_step, 0, 0, came))
    late = [(last_step, 0, 1, send(came, perm=planes))]
    late += [(s, 1, 1, send(x, perm=swap)) for s, x in crossed]
    m, *state = merge(
        lay, shape, entries, n_low, states, projection_weight_matrices, low, None, [token]
    )
    arrived, state[1] = after_all([x for _, _, _, x in late], state[1])
    entries = [(*e[:3], x) for e, x in zip(late, arrived)]
    _, order, q = rows_args
    final = (olds, order, q, caches)
    return tuple(
        merge(
            lay, shape, entries, 0, states, projection_weight_matrices, [m, *state], final, []
        )
    )


def solution(mesh):
    return jax.shard_map(
        functools.partial(shards, Layout(mesh)),
        mesh=mesh,
        in_specs=(
            P(None, ("fsdp", "grp"), "tp"),
            P(None, ("fsdp", "grp"), "tp", None),
            P(("fsdp", "grp"), None, "tp", None),
            P(("fsdp", "grp"), None, "tp", None),
            P(("fsdp", "grp")),
            P(None, None, "tp"),
            P(None, ("fsdp", "grp"), None),
            P(None, None, ("fsdp", "grp")),
        ),
        out_specs=(P(None, None, "tp"), P(None, ("fsdp", "grp"), "tp", None)),
        check_vma=False,
    )
```

```python
import functools
import math

import jax
import jax.numpy as jnp
from jax import lax
from jax.experimental import pallas as pl
from jax.experimental.pallas import tpu as pltpu
from jax.sharding import PartitionSpec as P

AXES = ("fsdp", "grp", "tp")
ADAPTER_SCALING = 2.0
LOG2E = math.log2(math.e)
MIB = 1024 * 1024
ANY = pl.BlockSpec(memory_space=pl.ANY)
HBM = pl.BlockSpec(memory_space=pltpu.HBM)
VMEM = pl.BlockSpec(memory_space=pltpu.VMEM)
SMEM = pl.BlockSpec(memory_space=pltpu.SMEM)


class Layout:
    def __init__(self, mesh):
        self.fsdp, self.grp, self.tp = (mesh.shape[a] for a in AXES)
        self.depth = self.fsdp // 2
        self.ring = self.depth * self.grp
        self.block = self.depth // self.tp

    def flat(self, z, core, g, t):
        return ((z * 2 + core) * self.grp + g) * self.tp + t

    def devices(self):
        for z in range(self.depth):
            for core in range(2):
                for g in range(self.grp):
                    for t in range(self.tp):
                        yield z, core, g, t

    def place(self, z, g):
        return g * self.depth + (z if g % 2 == 0 else self.depth - 1 - z)

    def at(self, position):
        g, z = divmod(position, self.depth)
        return (z if g % 2 == 0 else self.depth - 1 - z), g

    def ring_step(self):
        pairs = []
        for z, core, g, t in self.devices():
            to_z, to_g = self.at((self.place(z, g) + (1 - 2 * core)) % self.ring)
            pairs.append((self.flat(z, core, g, t), self.flat(to_z, core, to_g, t)))
        return pairs

    def plane_swap(self):
        return [(self.flat(z, c, g, t), self.flat(z, c, g, t ^ 1)) for z, c, g, t in self.devices()]

    def core_swap(self):
        return [
            (self.flat(z, c, g, t), self.flat(z, 1 - c, g, t)) for z, c, g, t in self.devices()
        ]

    def feature_step(self, step):
        return [
            (self.flat(z, c, g, (t + step) % self.tp), self.flat(z, c, g, t))
            for z, c, g, t in self.devices()
        ]


TYPICAL = pl.CostEstimate(flops=6 * 10**8, bytes_accessed=10**7, transcendentals=0)


def over(x, n):
    return x >> (n.bit_length() - 1) if n & (n - 1) == 0 else x // n


def within(x, n):
    return x & (n - 1) if n & (n - 1) == 0 else x % n


def after_all(arrays, token):
    return lax.optimization_barrier((arrays, token))


def pinned(x, space=pltpu.HBM):
    return pltpu.with_memory_space_constraint(x, space)


def sort_rows(lengths, order):
    rows = lengths.shape[0]
    held = [lengths[r] for r in range(rows)]
    for r in range(rows):
        rank = jnp.int32(0)
        for other in range(rows):
            if other != r:
                ahead = held[other] >= held[r] if other < r else held[other] > held[r]
                rank = rank + ahead.astype(jnp.int32)
        order[rank] = r


def by_length(length, sizes, act):
    below = 0
    for slots in sizes:

        @pl.when((length > below) & (length <= slots))
        def _():
            act(slots)

        below = slots


def up_columns(up):
    return jnp.concatenate([up[k] for k in range(up.shape[0])], axis=1)


def plane_part():
    return lax.rem(lax.axis_index("tp"), 2)


def begin_all(down, up, len_hbm, q_hbm, pair, rest, lengths, order, q_ref, up_buf, sems, more):
    lanes = pair.shape[3]
    depth = down.shape[2]
    tiles = depth // lanes
    part = plane_part()
    copies = [
        pltpu.make_async_copy(
            down.at[k, :, pl.ds(i * lanes, lanes)], array.at[0, i], sems.at[which, i]
        )
        for which, (k, array) in enumerate(((part, pair), (1 - part, rest)))
        for i in range(tiles)
    ]
    up_copy = pltpu.make_async_copy(up, up_buf, more.at[0])
    len_copy = pltpu.make_async_copy(len_hbm, lengths, more.at[1])
    q_copy = pltpu.make_async_copy(q_hbm, q_ref, more.at[2])
    for copy in [len_copy, up_copy] + copies + [q_copy]:
        copy.start()
    len_copy.wait()
    sort_rows(lengths, order)
    up_copy.wait()
    columns = up_columns(up_buf)
    pair[0, tiles, :, : columns.shape[1]] = columns
    for copy in copies + [q_copy]:
        copy.wait()


def begin(down, up, lengths, queries):
    count, rank, depth = down.shape
    tiles = depth // 128
    scalars = pltpu.SMEM(lengths.shape, jnp.int32)
    return pl.pallas_call(
        begin_all,
        out_shape=(
            pltpu.VMEM((2, tiles + 1, rank, 128), down.dtype),
            pltpu.VMEM((2, tiles, rank, 128), down.dtype),
            scalars,
            scalars,
            pltpu.VMEM(queries.shape, queries.dtype),
        ),
        in_specs=[HBM] * 4,
        out_specs=(VMEM, VMEM, SMEM, SMEM, VMEM),
        scratch_shapes=[
            pltpu.VMEM(up.shape, up.dtype),
            pltpu.SemaphoreType.DMA((count, tiles)),
            pltpu.SemaphoreType.DMA((3,)),
        ],
        compiler_params=pltpu.CompilerParams(vmem_limit_bytes=2 * MIB),
        cost_estimate=TYPICAL,
        name="begin",
    )(pinned(down), pinned(up), pinned(lengths), pinned(queries))


def pack_other(down, up, _, __, pair, rest):
    lanes = pair.shape[3]
    tiles = down.shape[2] // lanes
    part = plane_part()
    for i in range(tiles):
        cols = slice(i * lanes, (i + 1) * lanes)
        pair[1, i] = down[part, :, cols]
        rest[1, i] = down[1 - part, :, cols]
    columns = up_columns(up)
    pair[1, tiles, :, : columns.shape[1]] = columns


def pack(down, up, pair, rest):
    return pl.pallas_call(
        pack_other,
        out_shape=(like(pair), like(rest)),
        in_specs=[VMEM] * 4,
        out_specs=(VMEM, VMEM),
        input_output_aliases={2: 0, 3: 1},
        compiler_params=pltpu.CompilerParams(vmem_limit_bytes=2 * MIB),
        cost_estimate=TYPICAL,
        name="pack_other",
    )(down, up, pinned(pair, pltpu.VMEM), pinned(rest, pltpu.VMEM))


def attend_cache(pairs, ready, sizes, scale, *refs):
    lengths, order, q_ref, k_hbm, v_hbm = refs[:5]
    k_buf, v_buf, *outs, sems = refs[-5:]
    done = pairs[0]
    o_ref, lse_ref = outs[:2]
    steps, _, heads, size = q_ref.shape
    kv = k_hbm.shape[1] // sizes[-1]
    lanes = steps * heads

    def copies(which, pair, slots):
        span = pl.ds(0, slots * kv)
        hbm, buf = ((k_hbm, k_buf), (v_hbm, v_buf))[which]
        return [
            pltpu.make_async_copy(
                hbm.at[order[2 * pair + i], span],
                buf.at[2 * pair + i, span],
                sems.at[pair, i, which],
            )
            for i in range(2)
        ]

    def start(pair, slots):
        for copy in copies(0, pair, slots) + copies(1, pair, slots):
            copy.start()

    def finish(which, pair, slots):
        for i in which:
            for copy in copies(i, pair, slots):
                copy.wait()

    for pair in range(*ready):
        by_length(lengths[order[2 * pair]], sizes, functools.partial(start, pair))

    row_head = over(within(lax.broadcasted_iota(jnp.int32, (lanes, size), 0), heads), heads // kv)
    slot_head = within(lax.broadcasted_iota(jnp.int32, (lanes, size), 1), kv)
    head_bias = jnp.where(row_head == slot_head, 0.0, -jnp.inf)

    def attend(pair):
        def compute(slots):
            def wait(which):
                @pl.when(pair >= ready[0])
                def _():
                    finish((which,), pair, slots)

            n = slots * kv
            bias = jnp.concatenate([head_bias[:, : min(n, size)]] * max(n // size, 1), axis=1)
            column = lax.broadcasted_iota(jnp.int32, (1, n), 1)
            wait(0)
            scores = []
            for i in range(2):
                row = order[2 * pair + i]
                q = q_ref[:, row].reshape(lanes, size)
                s = lax.dot_general(
                    q,
                    k_buf[2 * pair + i, :n],
                    (((1,), (1,)), ((), ())),
                    preferred_element_type=jnp.float32,
                )
                closed = jnp.where(column < lengths[row] * kv, 0.0, -jnp.inf)
                scores.append(s + (bias + closed))
            highest = [jnp.max(s, axis=1, keepdims=True) * scale for s in scores]
            weights = [jnp.exp2(s * scale - h) for s, h in zip(scores, highest)]
            totals = [jnp.sum(p, axis=1, keepdims=True) for p in weights]
            wait(1)
            for i in range(2):
                o = jnp.dot(
                    weights[i].astype(jnp.bfloat16),
                    v_buf[2 * pair + i, :n],
                    preferred_element_type=jnp.float32,
                )
                spot = 2 * (pair - done) + i
                o_ref[spot] = o / totals[i]
                lse = highest[i] + jnp.log(totals[i]) * LOG2E
                lse_ref[spot] = jnp.broadcast_to(lse, (lanes, size))

        by_length(lengths[order[2 * pair]], sizes, compute)

    if pairs[1] - pairs[0] == 1:
        attend(pairs[0])
    else:
        pl.loop(*pairs)(attend)
    for pair in range(max(pairs[1], ready[0]), ready[1]):
        by_length(lengths[order[2 * pair]], sizes, functools.partial(finish, (0, 1), pair))


def like(x):
    return pltpu.VMEM(x.shape, x.dtype)


def cache_attention(pairs, ready, rows_args, caches, buffers, sizes, after):
    lengths, order, queries = rows_args
    keys, values = caches
    rows, steps, _, heads, size = (keys.shape[0], *queries.shape)
    slots = sizes[-1]
    scale = LOG2E / math.sqrt(size)
    count = 2 * (pairs[1] - pairs[0])
    piece = pltpu.VMEM((count, steps * heads, size), jnp.float32)
    operands = [pinned(x, pltpu.SMEM) for x in (lengths, order)]
    operands += [pinned(queries, pltpu.VMEM)]
    operands += [pinned(keys), pinned(values)]
    aliases = {len(operands) + i: i for i in range(len(buffers))}
    specs = [SMEM, SMEM, VMEM, HBM, HBM] + [VMEM] * len(buffers) + [ANY] * len(after)
    operands += [pinned(b, pltpu.VMEM) for b in buffers] + after
    out_shape = [like(keys), like(values), piece, piece]
    return pl.pallas_call(
        functools.partial(attend_cache, pairs, ready, sizes, scale),
        out_shape=out_shape,
        in_specs=specs,
        out_specs=[VMEM] * len(out_shape),
        input_output_aliases=aliases,
        scratch_shapes=[
            pltpu.SemaphoreType.DMA((rows // 2, 2, 2)),
        ],
        compiler_params=pltpu.CompilerParams(vmem_limit_bytes=8 * MIB),
        cost_estimate=TYPICAL,
        name="cache_attention",
    )(*operands)


def project_old(lay, n_hidden, *refs):
    w_buf, *hidden = refs[: 1 + n_hidden]
    out_ref, h_ref = refs[-2:]
    tp = lax.axis_index("tp")
    for i, h in enumerate(hidden):
        h_ref[lax.rem(tp + i, lay.tp)] = h[...]
    features = h_ref.shape[2]
    chunk = min(features, 1024)
    for k in range(2):
        total = jnp.zeros(out_ref.shape[1:], jnp.float32)
        for t in range(lay.tp):
            for low in range(0, features, chunk):
                start = t * features + low
                total += jnp.dot(
                    h_ref[t, :, low : low + chunk],
                    w_buf[k, start : start + chunk, :],
                    preferred_element_type=jnp.float32,
                )
        out_ref[k] = total


def project(lay, w_buf, hidden, after):
    tokens, features = hidden[0].shape
    return pl.pallas_call(
        functools.partial(project_old, lay, len(hidden)),
        out_shape=(
            pltpu.VMEM((2, tokens, w_buf.shape[2]), jnp.float32),
            pltpu.VMEM((lay.tp, tokens, features), jnp.bfloat16),
        ),
        in_specs=[VMEM] * (1 + len(hidden)) + [ANY] * len(after),
        out_specs=(VMEM, VMEM),
        compiler_params=pltpu.CompilerParams(vmem_limit_bytes=4 * MIB),
        cost_estimate=TYPICAL,
        name="project",
    )(pinned(w_buf, pltpu.VMEM), *hidden, *after)


class Place:
    def __init__(self, lay):
        fsdp, self.grp, self.tp = (lax.axis_index(a) for a in AXES)
        self.z, self.core = fsdp // 2, lax.rem(fsdp, 2)
        self.lay = lay
        there = jnp.where(lax.rem(self.grp, 2) == 0, self.z, lay.depth - 1 - self.z)
        self.own = self.grp * lay.depth + there
        self.per_lane = lay.fsdp * lay.grp // lay.tp
        self.part = plane_part()

    def find(self, plan, downs):
        lay, found = self.lay, []
        for (step, flip, other), down in zip(plan, downs):
            towards = (1 - 2 * self.core if flip else 2 * self.core - 1) * step
            spot = lax.rem(self.own + (lay.ring + towards), lay.ring)
            g = spot // lay.depth
            along = lax.rem(spot, lay.depth)
            zz = jnp.where(lax.rem(g, 2) == 0, along, lay.depth - 1 - along)
            for i in range(2):
                core = lax.rem(self.core + (i + flip), 2)
                index = (zz * 2 + core) * lay.grp + g
                found.append((down.at[i], index, 1 - self.part if other else self.part))
        return found

    def low(self, shards, h_ref, tiles):
        total = jnp.zeros((h_ref.shape[1], shards[0][0].shape[1]), jnp.float32) if shards else 0.0
        for down, index, _ in shards:
            depth = tiles * down.shape[-1]
            column = pl.multiple_of(lax.rem(index, self.per_lane) * depth, depth)
            term = lax.dot_general(
                h_ref[index // self.per_lane, :, pl.ds(column, depth)],
                jnp.concatenate([down[i] for i in range(tiles)], axis=1),
                (((1,), (1,)), ((), ())),
                preferred_element_type=jnp.float32,
            )
            total += term
        return total


def by_projection(place, plan, shards):
    crossed = [other for _, _, other in plan for _ in range(2)]
    return [
        (place.part, [s for s, other in zip(shards, crossed) if not other]),
        (1 - place.part, [s for s, other in zip(shards, crossed) if other]),
    ]


def merge_some(lay, plan, first, n_caches, scale, *refs):
    refs = list(refs)

    def take(n):
        out = refs[:n]
        del refs[:n]
        return out

    last = n_caches > 0
    downs = take(len(plan))
    h_buf, weights = take(2)
    if last:
        old, order, q_ref = take(3)
        caches = [take(2) for _ in range(n_caches)]
        u_buf, low_in, _ = take(3)
        m_hbm, out_hbm, m_buf, sems, low, out_buf, out_sem = refs[-7:]
    elif first:
        m_hbm, u_buf, low, m_buf, sems, u_parts = refs[-6:]
    else:
        u_buf, low_in, _ = take(3)
        m_hbm, low, m_buf, sems = refs[-4:]
    depth, width = m_buf.shape[1:]
    pairs = weights.shape[0]
    cut = min(width, 256)
    lanes = downs[0].shape[-1]
    tiles = depth // lanes
    place = Place(lay)
    shards = place.find(plan, downs)
    groups = by_projection(place, plan, shards)

    if last:
        low[...] = low_in[...]
        for part, group in groups:
            low[part] += place.low(group, h_buf, tiles)
        new = []
        for k in range(pairs):
            high = low[k].astype(jnp.bfloat16)
            rest = (low[k] - high.astype(jnp.float32)).astype(jnp.bfloat16)
            new.append(
                (
                    old[k]
                    + jnp.dot(high, u_buf[k], preferred_element_type=jnp.float32)
                    + jnp.dot(rest, u_buf[k], preferred_element_type=jnp.float32)
                ).astype(jnp.bfloat16)
            )
        add_new_tokens(q_ref, order, caches, new, out_buf, scale)
        out_copy = pltpu.make_async_copy(out_buf, out_hbm, out_sem)
        out_copy.start()
    elif first:
        columns = width // place.per_lane
        for down, index, _ in groups[0][1]:

            @pl.when(index // place.per_lane == place.tp)
            def _():
                u_parts[lax.rem(index, place.per_lane)] = down[tiles, :, : pairs * columns]

        for k in range(pairs):
            u_buf[k] = ADAPTER_SCALING * jnp.concatenate(
                [
                    u_parts[i, :, k * columns : (k + 1) * columns]
                    for i in range(place.per_lane)
                ],
                axis=1,
            )

    chunk = min(depth, 256)
    copies = []
    for j, (down, index, k) in enumerate(shards):
        start = pl.multiple_of(index * depth, depth)
        for begin in range(0, depth, chunk):
            rows = slice(begin, begin + chunk)
            tile = begin // lanes
            d = jnp.concatenate([down[tile + i] for i in range(chunk // lanes)], axis=1)
            for side in range(width // cut):
                cols = slice(side * cut, (side + 1) * cut)
                added = lax.dot_general(
                    d,
                    u_buf[k, :, cols],
                    (((0,), (0,)), ((), ())),
                    preferred_element_type=jnp.float32,
                )
                w = weights[k, pl.ds(start + begin, chunk), cols]
                m_buf[j, rows, cols] = (w.astype(jnp.float32) + added).astype(jnp.bfloat16)
        copy = pltpu.make_async_copy(m_buf.at[j], m_hbm.at[k, pl.ds(start, depth), :], sems.at[j])
        copy.start()
        copies.append(copy)

    if not last:
        low[...] = jnp.zeros_like(low) if first else low_in[...]
        for part, group in groups:
            low[part] += place.low(group, h_buf, tiles)
    for copy in copies + ([out_copy] if last else []):
        copy.wait()


def add_new_tokens(q_ref, order, caches, new, out_buf, scale):
    steps, rows, heads, size = q_ref.shape
    kv = new[0].shape[1] // size
    new = [
        jnp.concatenate([x[:, g * size : (g + 1) * size] for g in range(kv)], axis=0) for x in new
    ]
    n = kv * steps * rows
    lanes = steps * heads
    left = lax.broadcasted_iota(jnp.int32, (lanes, n), 0)
    right = lax.broadcasted_iota(jnp.int32, (lanes, n), 1)
    same_head = over(within(left, heads), heads // kv) == over(right, steps * rows)
    earlier = within(over(right, rows), steps) <= over(left, heads)
    right_row = jnp.where(same_head & earlier, within(right, rows), -1)

    def all_rows(pieces):
        return jnp.concatenate(list(pieces), axis=0)

    q = all_rows(q_ref[:, order[spot]].reshape(lanes, size) for spot in range(rows))
    s = lax.dot_general(q, new[0], (((1,), (1,)), ((), ())), preferred_element_type=jnp.float32)
    bias = all_rows(
        jnp.where(right_row == order[spot], 0.0, -jnp.inf) for spot in range(rows)
    )
    s = s * scale + bias
    lse = all_rows(ref[i] for _, ref in caches for i in range(ref.shape[0]))
    highest = jnp.maximum(jnp.max(s, axis=1, keepdims=True), lse)
    p = jnp.exp2(s - highest[:, :n])
    old = jnp.exp2(lse - highest)
    divisor = jnp.sum(p, axis=1, keepdims=True) + old
    o = old * all_rows(ref[i] for ref, _ in caches for i in range(ref.shape[0]))
    o = (o + jnp.dot(p.astype(jnp.bfloat16), new[1], preferred_element_type=jnp.float32)) / divisor
    for spot in range(rows):
        piece = o[spot * lanes : (spot + 1) * lanes].astype(out_buf.dtype)
        out_buf[:, order[spot]] = piece.reshape(steps, heads, size)


def merge(lay, shape, entries, states, weights, state, final, after):
    pairs, total, width = shape
    tokens, rank = states.shape[1], entries[0][3].shape[-2]
    depth = total // (lay.fsdp * lay.grp)
    per_lane = lay.fsdp * lay.grp // lay.tp
    n = 2 * len(entries)
    merged = pltpu.HBM(shape, jnp.bfloat16)
    low_shape = (pairs, tokens, rank)
    operands = [e[3] for e in entries] + [pinned(states, pltpu.VMEM), pinned(weights, pltpu.VMEM)]
    specs = [VMEM] * len(operands)
    scratch = [pltpu.VMEM((n, depth, width), jnp.bfloat16), pltpu.SemaphoreType.DMA((n,))]
    aliases = {}
    n_caches, scale = 0, 0.0
    if state is not None and final is None:
        m_prev, u_buf, low = state
        operands += [pinned(u_buf, pltpu.VMEM), pinned(low, pltpu.VMEM), pinned(m_prev)]
        specs += [VMEM, VMEM, HBM]
        aliases = {len(operands) - 1: 0}
        out_shape = [merged, pltpu.VMEM(low_shape, jnp.float32)]
        out_specs = [HBM, VMEM]
    elif final is None:
        out_shape = [
            merged,
            pltpu.VMEM((pairs, rank, width), jnp.bfloat16),
            pltpu.VMEM(low_shape, jnp.float32),
        ]
        out_specs = [HBM, VMEM, VMEM]
        scratch.append(pltpu.VMEM((per_lane, rank, pairs * width // per_lane), jnp.bfloat16))
    else:
        olds, order, queries, caches = final
        m_prev, u_buf, low = state
        operands += [olds, pinned(order, pltpu.SMEM), pinned(queries, pltpu.VMEM), *caches]
        specs += [VMEM, SMEM, VMEM] + [VMEM] * len(caches)
        operands += [pinned(u_buf, pltpu.VMEM), pinned(low, pltpu.VMEM), pinned(m_prev)]
        specs += [VMEM, VMEM, HBM]
        aliases = {len(operands) - 1: 0}
        out_shape = [merged, pltpu.HBM(queries.shape, jnp.bfloat16)]
        out_specs = [HBM, HBM]
        scratch += [
            pltpu.VMEM(low_shape, jnp.float32),
            pltpu.VMEM(queries.shape, jnp.bfloat16),
            pltpu.SemaphoreType.DMA,
        ]
        n_caches, scale = len(caches) // 2, LOG2E / math.sqrt(queries.shape[3])
    return pl.pallas_call(
        functools.partial(merge_some, lay, [e[:3] for e in entries], state is None, n_caches, scale),
        out_shape=out_shape,
        in_specs=specs + [ANY] * len(after),
        out_specs=out_specs,
        input_output_aliases=aliases,
        scratch_shapes=scratch,
        compiler_params=pltpu.CompilerParams(vmem_limit_bytes=20 * MIB),
        cost_estimate=TYPICAL,
        name="merge",
    )(*operands, *after)


def shards(
    lay,
    hidden_states,
    queries,
    cache_keys,
    cache_values,
    cache_lengths,
    projection_weight_matrices,
    factor_down,
    factor_up,
):
    send = functools.partial(lax.ppermute, axis_name=AXES)
    steps, rows, features = hidden_states.shape
    slots, kv, size = cache_keys.shape[1:]
    shape = projection_weight_matrices.shape
    sizes = tuple(slots * i // 24 for i in (1, 4, 8, 16, 24))
    own = jnp.swapaxes(factor_down, 1, 2)
    tokens = hidden_states.reshape(steps * rows, features)
    keys = cache_keys.reshape(rows, slots * kv, size)
    values = cache_values.reshape(rows, slots * kv, size)
    swap, ring, planes = lay.core_swap(), lay.ring_step(), lay.plane_swap()
    pair_count = rows // 2
    last_step = lay.ring // 2
    buffers, caches = [], []

    other, other_up = send(own, perm=swap), send(factor_up, perm=swap)
    pair, rest, *rows_args = begin(own, factor_up, cache_lengths, queries)
    pair, rest = pack(other, other_up, pair, rest)

    def attention(pairs, ready, after):
        nonlocal buffers
        out = cache_attention(pairs, ready, rows_args, (keys, values), buffers, sizes, after)
        buffers = list(out[:2])
        caches.extend(out[2:])
        return out[2]

    entries = [(0, 0, 0, pair), (0, 0, 1, rest)]
    sent = send(pair, perm=ring)
    hidden = [tokens] + [send(tokens, perm=lay.feature_step(i)) for i in range(1, lay.tp)]
    token = attention((0, 1), (0, 2), [pair])
    came, token = after_all(sent, token)
    crossing, crossed = [], []
    for step in range(1, last_step):
        entries.append((step, 0, 0, came))
        over_there = [(s, send(x, perm=swap)) for s, x in crossed]
        across = [(step, send(came, perm=planes))]
        swapped = send(came, perm=swap)
        sent = send(came, perm=ring)
        if step == 1:
            token = attention((1, 2), (2, pair_count), [token])
        elif step == 2:
            token = attention((2, pair_count), (pair_count, pair_count), [token])
        elif step == 3:
            olds, states = project(lay, projection_weight_matrices, hidden, [token])
            token = olds
        (came, hidden, arrived, swapped, held), token = after_all(
            (sent, hidden, [x for _, x in crossing], swapped, [x for _, x in over_there]), token
        )
        entries.append((step, 1, 0, swapped))
        entries += [(s, 1, 1, x) for (s, _), x in zip(over_there, held)]
        crossed = [(s, x) for (s, _), x in zip(crossing, arrived)]
        entries += [(s, 0, 1, x) for s, x in crossed]
        crossing = across
    weights = projection_weight_matrices
    entries.append((last_step, 0, 0, came))
    own_plane = [e for e in entries if not e[2]]
    others = [e for e in entries if e[2]]
    late = [(last_step, 0, 1, send(came, perm=planes))]
    late += [(s, 1, 1, send(x, perm=swap)) for s, x in crossed]
    m, u, low = merge(lay, shape, own_plane, states, weights, None, None, [token])
    (step, x), = crossing
    x, low = after_all(x, low)
    late.append((step, 1, 1, send(x, perm=swap)))
    others.append((step, 0, 1, x))
    m, low = merge(lay, shape, others, states, weights, [m, u, low], None, [])
    arrived, low = after_all([x for _, _, _, x in late], low)
    late = [(*e[:3], x) for e, x in zip(late, arrived)]
    _, order, q = rows_args
    final = (olds, order, q, caches)
    return tuple(merge(lay, shape, late, states, weights, [m, u, low], final, []))


def solution(mesh):
    return jax.shard_map(
        functools.partial(shards, Layout(mesh)),
        mesh=mesh,
        in_specs=(
            P(None, ("fsdp", "grp"), "tp"),
            P(None, ("fsdp", "grp"), "tp", None),
            P(("fsdp", "grp"), None, "tp", None),
            P(("fsdp", "grp"), None, "tp", None),
            P(("fsdp", "grp")),
            P(None, None, "tp"),
            P(None, ("fsdp", "grp"), None),
            P(None, None, ("fsdp", "grp")),
        ),
        out_specs=(P(None, None, "tp"), P(None, ("fsdp", "grp"), "tp", None)),
        check_vma=False,
    )
```

```python
import functools
import math

import jax
import jax.numpy as jnp
from jax import lax
from jax.experimental import pallas as pl
from jax.experimental.pallas import tpu as pltpu
from jax.sharding import PartitionSpec as P

AXES = ("fsdp", "grp", "tp")
ADAPTER_SCALING = 2.0
LOG2E = math.log2(math.e)
MIB = 1024 * 1024
ANY = pl.BlockSpec(memory_space=pl.ANY)
HBM = pl.BlockSpec(memory_space=pltpu.HBM)
VMEM = pl.BlockSpec(memory_space=pltpu.VMEM)
SMEM = pl.BlockSpec(memory_space=pltpu.SMEM)


class Layout:
    def __init__(self, mesh):
        self.fsdp, self.grp, self.tp = (mesh.shape[a] for a in AXES)
        self.depth = self.fsdp // 2
        self.ring = self.depth * self.grp
        self.block = self.depth // self.tp

    def flat(self, z, core, g, t):
        return ((z * 2 + core) * self.grp + g) * self.tp + t

    def devices(self):
        for z in range(self.depth):
            for core in range(2):
                for g in range(self.grp):
                    for t in range(self.tp):
                        yield z, core, g, t

    def place(self, z, g):
        return g * self.depth + (z if g % 2 == 0 else self.depth - 1 - z)

    def at(self, position):
        g, z = divmod(position, self.depth)
        return (z if g % 2 == 0 else self.depth - 1 - z), g

    def ring_step(self):
        pairs = []
        for z, core, g, t in self.devices():
            to_z, to_g = self.at((self.place(z, g) + (1 - 2 * core)) % self.ring)
            pairs.append((self.flat(z, core, g, t), self.flat(to_z, core, to_g, t)))
        return pairs

    def plane_swap(self):
        return [(self.flat(z, c, g, t), self.flat(z, c, g, t ^ 1)) for z, c, g, t in self.devices()]

    def core_swap(self):
        return [
            (self.flat(z, c, g, t), self.flat(z, 1 - c, g, t)) for z, c, g, t in self.devices()
        ]

    def feature_step(self, step):
        return [
            (self.flat(z, c, g, (t + step) % self.tp), self.flat(z, c, g, t))
            for z, c, g, t in self.devices()
        ]


TYPICAL = pl.CostEstimate(flops=6 * 10**8, bytes_accessed=10**7, transcendentals=0)


def over(x, n):
    return x >> (n.bit_length() - 1) if n & (n - 1) == 0 else x // n


def within(x, n):
    return x & (n - 1) if n & (n - 1) == 0 else x % n


def after_all(arrays, token):
    return lax.optimization_barrier((arrays, token))


def pinned(x, space=pltpu.HBM):
    return pltpu.with_memory_space_constraint(x, space)


def sort_rows(lengths, order):
    rows = lengths.shape[0]
    held = [lengths[r] for r in range(rows)]
    for r in range(rows):
        rank = jnp.int32(0)
        for other in range(rows):
            if other != r:
                ahead = held[other] >= held[r] if other < r else held[other] > held[r]
                rank = rank + ahead.astype(jnp.int32)
        order[rank] = r


def by_length(length, sizes, act):
    below = 0
    for slots in sizes:

        @pl.when((length > below) & (length <= slots))
        def _():
            act(slots)

        below = slots


def up_columns(up):
    return jnp.concatenate([up[k] for k in range(up.shape[0])], axis=1)


def plane_part():
    return lax.rem(lax.axis_index("tp"), 2)


def begin_all(down, up, len_hbm, q_hbm, pair, rest, lengths, order, q_ref, up_buf, sems, more):
    lanes = pair.shape[3]
    depth = down.shape[2]
    tiles = depth // lanes
    part = plane_part()
    copies = [
        pltpu.make_async_copy(
            down.at[k, :, pl.ds(i * lanes, lanes)], array.at[0, i], sems.at[which, i]
        )
        for which, (k, array) in enumerate(((part, pair), (1 - part, rest)))
        for i in range(tiles)
    ]
    up_copy = pltpu.make_async_copy(up, up_buf, more.at[0])
    len_copy = pltpu.make_async_copy(len_hbm, lengths, more.at[1])
    q_copy = pltpu.make_async_copy(q_hbm, q_ref, more.at[2])
    for copy in [len_copy, up_copy] + copies + [q_copy]:
        copy.start()
    len_copy.wait()
    sort_rows(lengths, order)
    up_copy.wait()
    columns = up_columns(up_buf)
    pair[0, tiles, :, : columns.shape[1]] = columns
    for copy in copies + [q_copy]:
        copy.wait()


def begin(down, up, lengths, queries):
    count, rank, depth = down.shape
    tiles = depth // 128
    scalars = pltpu.SMEM(lengths.shape, jnp.int32)
    return pl.pallas_call(
        begin_all,
        out_shape=(
            pltpu.VMEM((2, tiles + 1, rank, 128), down.dtype),
            pltpu.VMEM((2, tiles, rank, 128), down.dtype),
            scalars,
            scalars,
            pltpu.VMEM(queries.shape, queries.dtype),
        ),
        in_specs=[HBM] * 4,
        out_specs=(VMEM, VMEM, SMEM, SMEM, VMEM),
        scratch_shapes=[
            pltpu.VMEM(up.shape, up.dtype),
            pltpu.SemaphoreType.DMA((count, tiles)),
            pltpu.SemaphoreType.DMA((3,)),
        ],
        compiler_params=pltpu.CompilerParams(vmem_limit_bytes=2 * MIB),
        cost_estimate=TYPICAL,
        name="begin",
    )(pinned(down), pinned(up), pinned(lengths), pinned(queries))


def pack_other(down, up, _, __, pair, rest):
    lanes = pair.shape[3]
    tiles = down.shape[2] // lanes
    part = plane_part()
    for i in range(tiles):
        cols = slice(i * lanes, (i + 1) * lanes)
        pair[1, i] = down[part, :, cols]
        rest[1, i] = down[1 - part, :, cols]
    columns = up_columns(up)
    pair[1, tiles, :, : columns.shape[1]] = columns


def pack(down, up, pair, rest):
    return pl.pallas_call(
        pack_other,
        out_shape=(like(pair), like(rest)),
        in_specs=[VMEM] * 4,
        out_specs=(VMEM, VMEM),
        input_output_aliases={2: 0, 3: 1},
        compiler_params=pltpu.CompilerParams(vmem_limit_bytes=2 * MIB),
        cost_estimate=TYPICAL,
        name="pack_other",
    )(down, up, pinned(pair, pltpu.VMEM), pinned(rest, pltpu.VMEM))


def attend_cache(pairs, ready, sizes, scale, *refs):
    lengths, order, q_ref, k_hbm, v_hbm = refs[:5]
    k_buf, v_buf, *outs, sems = refs[-5:]
    done = pairs[0]
    o_ref, lse_ref = outs[:2]
    steps, _, heads, size = q_ref.shape
    kv = k_hbm.shape[1] // sizes[-1]
    lanes = steps * heads

    def copies(which, pair, slots):
        span = pl.ds(0, slots * kv)
        hbm, buf = ((k_hbm, k_buf), (v_hbm, v_buf))[which]
        return [
            pltpu.make_async_copy(
                hbm.at[order[2 * pair + i], span],
                buf.at[2 * pair + i, span],
                sems.at[pair, i, which],
            )
            for i in range(2)
        ]

    def start(pair, slots):
        for copy in copies(0, pair, slots) + copies(1, pair, slots):
            copy.start()

    def finish(which, pair, slots):
        for i in which:
            for copy in copies(i, pair, slots):
                copy.wait()

    for pair in range(*ready):
        by_length(lengths[order[2 * pair]], sizes, functools.partial(start, pair))

    row_head = over(within(lax.broadcasted_iota(jnp.int32, (lanes, size), 0), heads), heads // kv)
    slot_head = within(lax.broadcasted_iota(jnp.int32, (lanes, size), 1), kv)
    head_bias = jnp.where(row_head == slot_head, 0.0, -jnp.inf)

    def attend(pair):
        def compute(slots):
            def wait(which):
                @pl.when(pair >= ready[0])
                def _():
                    finish((which,), pair, slots)

            n = slots * kv
            bias = jnp.concatenate([head_bias[:, : min(n, size)]] * max(n // size, 1), axis=1)
            column = lax.broadcasted_iota(jnp.int32, (1, n), 1)
            wait(0)
            scores = []
            for i in range(2):
                row = order[2 * pair + i]
                q = q_ref[:, row].reshape(lanes, size)
                s = lax.dot_general(
                    q,
                    k_buf[2 * pair + i, :n],
                    (((1,), (1,)), ((), ())),
                    preferred_element_type=jnp.float32,
                )
                closed = jnp.where(column < lengths[row] * kv, 0.0, -jnp.inf)
                scores.append(s + (bias + closed))
            highest = [jnp.max(s, axis=1, keepdims=True) * scale for s in scores]
            weights = [jnp.exp2(s * scale - h) for s, h in zip(scores, highest)]
            totals = [jnp.sum(p, axis=1, keepdims=True) for p in weights]
            wait(1)
            for i in range(2):
                o = jnp.dot(
                    weights[i].astype(jnp.bfloat16),
                    v_buf[2 * pair + i, :n],
                    preferred_element_type=jnp.float32,
                )
                spot = 2 * (pair - done) + i
                o_ref[spot] = o / totals[i]
                lse = highest[i] + jnp.log(totals[i]) * LOG2E
                lse_ref[spot] = jnp.broadcast_to(lse, (lanes, size))

        by_length(lengths[order[2 * pair]], sizes, compute)

    if pairs[1] - pairs[0] == 1:
        attend(pairs[0])
    else:
        pl.loop(*pairs)(attend)
    for pair in range(max(pairs[1], ready[0]), ready[1]):
        by_length(lengths[order[2 * pair]], sizes, functools.partial(finish, (0, 1), pair))


def like(x):
    return pltpu.VMEM(x.shape, x.dtype)


def cache_attention(pairs, ready, rows_args, caches, buffers, sizes, after):
    lengths, order, queries = rows_args
    keys, values = caches
    rows, steps, _, heads, size = (keys.shape[0], *queries.shape)
    slots = sizes[-1]
    scale = LOG2E / math.sqrt(size)
    count = 2 * (pairs[1] - pairs[0])
    piece = pltpu.VMEM((count, steps * heads, size), jnp.float32)
    operands = [pinned(x, pltpu.SMEM) for x in (lengths, order)]
    operands += [pinned(queries, pltpu.VMEM)]
    operands += [pinned(keys), pinned(values)]
    aliases = {len(operands) + i: i for i in range(len(buffers))}
    specs = [SMEM, SMEM, VMEM, HBM, HBM] + [VMEM] * len(buffers) + [ANY] * len(after)
    operands += [pinned(b, pltpu.VMEM) for b in buffers] + after
    out_shape = [like(keys), like(values), piece, piece]
    return pl.pallas_call(
        functools.partial(attend_cache, pairs, ready, sizes, scale),
        out_shape=out_shape,
        in_specs=specs,
        out_specs=[VMEM] * len(out_shape),
        input_output_aliases=aliases,
        scratch_shapes=[
            pltpu.SemaphoreType.DMA((rows // 2, 2, 2)),
        ],
        compiler_params=pltpu.CompilerParams(vmem_limit_bytes=8 * MIB),
        cost_estimate=TYPICAL,
        name="cache_attention",
    )(*operands)


def project_old(part, lay, n_hidden, *refs):
    w_ref = refs[0]
    if part == 0:
        out_ref, h_ref = refs[-2:]
        tp = lax.axis_index("tp")
        for i, h in enumerate(refs[1 : 1 + n_hidden]):
            h_ref[lax.rem(tp + i, lay.tp)] = h[...]
    else:
        h_ref, out_ref = refs[1], refs[-1]
    features = h_ref.shape[2]
    chunk = min(features, 1024)
    total = jnp.zeros(out_ref.shape, jnp.float32)
    for t in range(lay.tp):
        for low in range(0, features, chunk):
            start = t * features + low
            total += jnp.dot(
                h_ref[t, :, low : low + chunk],
                w_ref[part, start : start + chunk, :],
                preferred_element_type=jnp.float32,
            )
    out_ref[...] = total


def project(part, lay, weights, hidden, after):
    tokens, features = hidden[0].shape[-2:]
    out_shape = [pltpu.VMEM((tokens, weights.shape[2]), jnp.float32)]
    if part == 0:
        out_shape.append(pltpu.VMEM((lay.tp, tokens, features), jnp.bfloat16))
    else:
        hidden = [pinned(h, pltpu.VMEM) for h in hidden]
    return pl.pallas_call(
        functools.partial(project_old, part, lay, len(hidden)),
        out_shape=out_shape,
        in_specs=[VMEM] * (1 + len(hidden)) + [ANY] * len(after),
        out_specs=[VMEM] * len(out_shape),
        compiler_params=pltpu.CompilerParams(vmem_limit_bytes=4 * MIB),
        cost_estimate=TYPICAL,
        name="project",
    )(pinned(weights, pltpu.VMEM), *hidden, *after)


class Place:
    def __init__(self, lay):
        fsdp, self.grp, self.tp = (lax.axis_index(a) for a in AXES)
        self.z, self.core = fsdp // 2, lax.rem(fsdp, 2)
        self.lay = lay
        there = jnp.where(lax.rem(self.grp, 2) == 0, self.z, lay.depth - 1 - self.z)
        self.own = self.grp * lay.depth + there
        self.per_lane = lay.fsdp * lay.grp // lay.tp
        self.part = plane_part()

    def find(self, plan, downs):
        lay, found = self.lay, []
        for (step, flip, other), down in zip(plan, downs):
            towards = (1 - 2 * self.core if flip else 2 * self.core - 1) * step
            spot = lax.rem(self.own + (lay.ring + towards), lay.ring)
            g = spot // lay.depth
            along = lax.rem(spot, lay.depth)
            zz = jnp.where(lax.rem(g, 2) == 0, along, lay.depth - 1 - along)
            for i in range(2):
                core = lax.rem(self.core + (i + flip), 2)
                index = (zz * 2 + core) * lay.grp + g
                found.append((down.at[i], index, 1 - self.part if other else self.part))
        return found

    def low(self, shards, h_ref, tiles):
        total = jnp.zeros((h_ref.shape[1], shards[0][0].shape[1]), jnp.float32) if shards else 0.0
        for down, index, _ in shards:
            depth = tiles * down.shape[-1]
            column = pl.multiple_of(lax.rem(index, self.per_lane) * depth, depth)
            term = lax.dot_general(
                h_ref[index // self.per_lane, :, pl.ds(column, depth)],
                jnp.concatenate([down[i] for i in range(tiles)], axis=1),
                (((1,), (1,)), ((), ())),
                preferred_element_type=jnp.float32,
            )
            total += term
        return total


def by_projection(place, plan, shards):
    crossed = [other for _, _, other in plan for _ in range(2)]
    return [
        (place.part, [s for s, other in zip(shards, crossed) if not other]),
        (1 - place.part, [s for s, other in zip(shards, crossed) if other]),
    ]


def low_some(lay, plan, tiles, *refs):
    downs, h_ref, out_ref = refs[: len(plan)], refs[len(plan)], refs[-1]
    place = Place(lay)
    for part, group in by_projection(place, plan, place.find(plan, downs)):
        out_ref[part] = place.low(group, h_ref, tiles)


def project_low(lay, entries, states, pairs, tiles, after):
    return pl.pallas_call(
        functools.partial(low_some, lay, [e[:3] for e in entries], tiles),
        out_shape=pltpu.VMEM((pairs, states.shape[1], entries[0][3].shape[-2]), jnp.float32),
        in_specs=[VMEM] * (len(entries) + 1) + [ANY] * len(after),
        out_specs=VMEM,
        compiler_params=pltpu.CompilerParams(vmem_limit_bytes=2 * MIB),
        cost_estimate=TYPICAL,
        name="project_low",
    )(*[e[3] for e in entries], pinned(states, pltpu.VMEM), *after)


def merge_some(lay, plan, has_low, first, n_caches, scale, *refs):
    refs = list(refs)

    def take(n):
        out = refs[:n]
        del refs[:n]
        return out

    last = n_caches > 0
    downs = take(len(plan))
    h_buf, weights = take(2)
    if last:
        old = take(2)
        order, q_ref = take(2)
        caches = [take(2) for _ in range(n_caches)]
        u_buf, low_in, _ = take(3)
        m_hbm, out_hbm, m_buf, sems, low, out_buf, out_sem = refs[-7:]
    elif first:
        (low_in,) = take(1)
        m_hbm, u_buf, low, m_buf, sems, u_parts = refs[-6:]
    else:
        u_buf, low_in, _ = take(3)
        m_hbm, low, m_buf, sems = refs[-4:]
    depth, width = m_buf.shape[1:]
    pairs = weights.shape[0]
    cut = min(width, 256)
    lanes = downs[0].shape[-1]
    tiles = depth // lanes
    place = Place(lay)
    shards = place.find(plan, downs)
    groups = by_projection(place, plan, shards)

    if last:
        low[...] = low_in[...]
        for part, group in groups:
            low[part] += place.low(group, h_buf, tiles)
        new = []
        for k in range(pairs):
            high = low[k].astype(jnp.bfloat16)
            rest = (low[k] - high.astype(jnp.float32)).astype(jnp.bfloat16)
            new.append(
                (
                    old[k][...]
                    + jnp.dot(high, u_buf[k], preferred_element_type=jnp.float32)
                    + jnp.dot(rest, u_buf[k], preferred_element_type=jnp.float32)
                ).astype(jnp.bfloat16)
            )
        add_new_tokens(q_ref, order, caches, new, out_buf, scale)
        out_copy = pltpu.make_async_copy(out_buf, out_hbm, out_sem)
        out_copy.start()
    elif first:
        columns = width // place.per_lane
        for down, index, _ in groups[0][1]:

            @pl.when(index // place.per_lane == place.tp)
            def _():
                u_parts[lax.rem(index, place.per_lane)] = down[tiles, :, : pairs * columns]

        for k in range(pairs):
            u_buf[k] = ADAPTER_SCALING * jnp.concatenate(
                [
                    u_parts[i, :, k * columns : (k + 1) * columns]
                    for i in range(place.per_lane)
                ],
                axis=1,
            )

    chunk = min(depth, 256)
    copies = []
    for j, (down, index, k) in enumerate(shards):
        start = pl.multiple_of(index * depth, depth)
        for begin in range(0, depth, chunk):
            rows = slice(begin, begin + chunk)
            tile = begin // lanes
            d = jnp.concatenate([down[tile + i] for i in range(chunk // lanes)], axis=1)
            for side in range(width // cut):
                cols = slice(side * cut, (side + 1) * cut)
                added = lax.dot_general(
                    d,
                    u_buf[k, :, cols],
                    (((0,), (0,)), ((), ())),
                    preferred_element_type=jnp.float32,
                )
                w = weights[k, pl.ds(start + begin, chunk), cols]
                m_buf[j, rows, cols] = (w.astype(jnp.float32) + added).astype(jnp.bfloat16)
        copy = pltpu.make_async_copy(m_buf.at[j], m_hbm.at[k, pl.ds(start, depth), :], sems.at[j])
        copy.start()
        copies.append(copy)

    if not last:
        low[...] = low_in[...]
        for part, group in by_projection(
            place,
            [e for e, done in zip(plan, has_low) if not done],
            [s for i, s in enumerate(shards) if not has_low[i // 2]],
        ):
            if group:
                low[part] += place.low(group, h_buf, tiles)
    for copy in copies + ([out_copy] if last else []):
        copy.wait()


def add_new_tokens(q_ref, order, caches, new, out_buf, scale):
    steps, rows, heads, size = q_ref.shape
    kv = new[0].shape[1] // size
    new = [
        jnp.concatenate([x[:, g * size : (g + 1) * size] for g in range(kv)], axis=0) for x in new
    ]
    n = kv * steps * rows
    lanes = steps * heads
    left = lax.broadcasted_iota(jnp.int32, (lanes, n), 0)
    right = lax.broadcasted_iota(jnp.int32, (lanes, n), 1)
    same_head = over(within(left, heads), heads // kv) == over(right, steps * rows)
    earlier = within(over(right, rows), steps) <= over(left, heads)
    right_row = jnp.where(same_head & earlier, within(right, rows), -1)

    def all_rows(pieces):
        return jnp.concatenate(list(pieces), axis=0)

    q = all_rows(q_ref[:, order[spot]].reshape(lanes, size) for spot in range(rows))
    s = lax.dot_general(q, new[0], (((1,), (1,)), ((), ())), preferred_element_type=jnp.float32)
    bias = all_rows(
        jnp.where(right_row == order[spot], 0.0, -jnp.inf) for spot in range(rows)
    )
    s = s * scale + bias
    lse = all_rows(ref[i] for _, ref in caches for i in range(ref.shape[0]))
    highest = jnp.maximum(jnp.max(s, axis=1, keepdims=True), lse)
    p = jnp.exp2(s - highest[:, :n])
    old = jnp.exp2(lse - highest)
    divisor = jnp.sum(p, axis=1, keepdims=True) + old
    o = old * all_rows(ref[i] for ref, _ in caches for i in range(ref.shape[0]))
    o = (o + jnp.dot(p.astype(jnp.bfloat16), new[1], preferred_element_type=jnp.float32)) / divisor
    for spot in range(rows):
        piece = o[spot * lanes : (spot + 1) * lanes].astype(out_buf.dtype)
        out_buf[:, order[spot]] = piece.reshape(steps, heads, size)


def merge(lay, shape, entries, has_low, states, weights, state, final, after):
    pairs, total, width = shape
    tokens, rank = states.shape[1], entries[0][3].shape[-2]
    depth = total // (lay.fsdp * lay.grp)
    per_lane = lay.fsdp * lay.grp // lay.tp
    n = 2 * len(entries)
    merged = pltpu.HBM(shape, jnp.bfloat16)
    low_shape = (pairs, tokens, rank)
    operands = [e[3] for e in entries] + [pinned(states, pltpu.VMEM), pinned(weights, pltpu.VMEM)]
    specs = [VMEM] * len(operands)
    scratch = [pltpu.VMEM((n, depth, width), jnp.bfloat16), pltpu.SemaphoreType.DMA((n,))]
    aliases = {}
    n_caches, scale = 0, 0.0
    if isinstance(state, list) and final is None:
        m_prev, u_buf, low = state
        operands += [pinned(u_buf, pltpu.VMEM), pinned(low, pltpu.VMEM), pinned(m_prev)]
        specs += [VMEM, VMEM, HBM]
        aliases = {len(operands) - 1: 0}
        out_shape = [merged, pltpu.VMEM(low_shape, jnp.float32)]
        out_specs = [HBM, VMEM]
    elif final is None:
        operands.append(pinned(state, pltpu.VMEM))
        specs.append(VMEM)
        out_shape = [
            merged,
            pltpu.VMEM((pairs, rank, width), jnp.bfloat16),
            pltpu.VMEM(low_shape, jnp.float32),
        ]
        out_specs = [HBM, VMEM, VMEM]
        scratch.append(pltpu.VMEM((per_lane, rank, pairs * width // per_lane), jnp.bfloat16))
    else:
        olds, order, queries, caches = final
        m_prev, u_buf, low = state
        operands += [*olds, pinned(order, pltpu.SMEM), pinned(queries, pltpu.VMEM), *caches]
        specs += [VMEM, VMEM, SMEM, VMEM] + [VMEM] * len(caches)
        operands += [pinned(u_buf, pltpu.VMEM), pinned(low, pltpu.VMEM), pinned(m_prev)]
        specs += [VMEM, VMEM, HBM]
        aliases = {len(operands) - 1: 0}
        out_shape = [merged, pltpu.HBM(queries.shape, jnp.bfloat16)]
        out_specs = [HBM, HBM]
        scratch += [
            pltpu.VMEM(low_shape, jnp.float32),
            pltpu.VMEM(queries.shape, jnp.bfloat16),
            pltpu.SemaphoreType.DMA,
        ]
        n_caches, scale = len(caches) // 2, LOG2E / math.sqrt(queries.shape[3])
    return pl.pallas_call(
        functools.partial(
            merge_some,
            lay,
            [e[:3] for e in entries],
            has_low,
            not isinstance(state, list),
            n_caches,
            scale,
        ),
        out_shape=out_shape,
        in_specs=specs + [ANY] * len(after),
        out_specs=out_specs,
        input_output_aliases=aliases,
        scratch_shapes=scratch,
        compiler_params=pltpu.CompilerParams(vmem_limit_bytes=20 * MIB),
        cost_estimate=TYPICAL,
        name="merge",
    )(*operands, *after)


def shards(
    lay,
    hidden_states,
    queries,
    cache_keys,
    cache_values,
    cache_lengths,
    projection_weight_matrices,
    factor_down,
    factor_up,
):
    send = functools.partial(lax.ppermute, axis_name=AXES)
    steps, rows, features = hidden_states.shape
    slots, kv, size = cache_keys.shape[1:]
    shape = projection_weight_matrices.shape
    sizes = tuple(slots * i // 24 for i in (1, 4, 8, 16, 24))
    own = jnp.swapaxes(factor_down, 1, 2)
    tokens = hidden_states.reshape(steps * rows, features)
    keys = cache_keys.reshape(rows, slots * kv, size)
    values = cache_values.reshape(rows, slots * kv, size)
    swap, ring, planes = lay.core_swap(), lay.ring_step(), lay.plane_swap()
    pair_count = rows // 2
    last_step = lay.ring // 2
    buffers, caches = [], []

    other, other_up = send(own, perm=swap), send(factor_up, perm=swap)
    pair, rest, *rows_args = begin(own, factor_up, cache_lengths, queries)
    pair, rest = pack(other, other_up, pair, rest)

    def attention(pairs, ready, after):
        nonlocal buffers
        out = cache_attention(pairs, ready, rows_args, (keys, values), buffers, sizes, after)
        buffers = list(out[:2])
        caches.extend(out[2:])
        return out[2]

    entries = [(0, 0, 0, pair), (0, 0, 1, rest)]
    sent = send(pair, perm=ring)
    hidden = [tokens] + [send(tokens, perm=lay.feature_step(i)) for i in range(1, lay.tp)]
    token = attention((0, 1), (0, 2), [pair])
    came, token = after_all(sent, token)
    crossing, crossed = [], []
    for step in range(1, last_step):
        entries.append((step, 0, 0, came))
        over_there = [(s, send(x, perm=swap)) for s, x in crossed]
        across = [(step, send(came, perm=planes))]
        swapped = send(came, perm=swap)
        sent = send(came, perm=ring)
        if step == 1:
            token = attention((1, 2), (2, pair_count), [token])
        elif step == 2:
            token = attention((2, pair_count), (pair_count, pair_count), [token])
            old_keys, states = project(0, lay, projection_weight_matrices, hidden, [token])
            token = old_keys
        elif step == 3:
            (token,) = project(1, lay, projection_weight_matrices, [states], [token])
            olds = [old_keys, token]
            n_low = len(entries)
            tiles = own.shape[2] // 128
            token = low = project_low(lay, entries, states, shape[0], tiles, [token])
        (came, hidden, arrived, swapped, held), token = after_all(
            (sent, hidden, [x for _, x in crossing], swapped, [x for _, x in over_there]), token
        )
        entries.append((step, 1, 0, swapped))
        entries += [(s, 1, 1, x) for (s, _), x in zip(over_there, held)]
        crossed = [(s, x) for (s, _), x in zip(crossing, arrived)]
        entries += [(s, 0, 1, x) for s, x in crossed]
        crossing = across
    weights = projection_weight_matrices
    entries.append((last_step, 0, 0, came))
    own_plane = [i for i, e in enumerate(entries) if not e[2]]
    others = [i for i, e in enumerate(entries) if e[2]]

    def some(chosen):
        return [entries[i] for i in chosen], [i < n_low for i in chosen]

    late = [(last_step, 0, 1, send(came, perm=planes))]
    late += [(s, 1, 1, send(x, perm=swap)) for s, x in crossed]
    m, u, low = merge(lay, shape, *some(own_plane), states, weights, low, None, [token])
    (step, x), = crossing
    x, low = after_all(x, low)
    late.append((step, 1, 1, send(x, perm=swap)))
    others.append(len(entries))
    entries.append((step, 0, 1, x))
    m, low = merge(lay, shape, *some(others), states, weights, [m, u, low], None, [])
    arrived, low = after_all([x for _, _, _, x in late], low)
    late = [(*e[:3], x) for e, x in zip(late, arrived)]
    _, order, q = rows_args
    final = (olds, order, q, caches)
    return tuple(merge(lay, shape, late, None, states, weights, [m, u, low], final, []))


def solution(mesh):
    return jax.shard_map(
        functools.partial(shards, Layout(mesh)),
        mesh=mesh,
        in_specs=(
            P(None, ("fsdp", "grp"), "tp"),
            P(None, ("fsdp", "grp"), "tp", None),
            P(("fsdp", "grp"), None, "tp", None),
            P(("fsdp", "grp"), None, "tp", None),
            P(("fsdp", "grp")),
            P(None, None, "tp"),
            P(None, ("fsdp", "grp"), None),
            P(None, None, ("fsdp", "grp")),
        ),
        out_specs=(P(None, None, "tp"), P(None, ("fsdp", "grp"), "tp", None)),
        check_vma=False,
    )
```

```python
import functools
import math

import jax
import jax.numpy as jnp
from jax import lax
from jax.experimental import pallas as pl
from jax.experimental.pallas import tpu as pltpu
from jax.sharding import PartitionSpec as P

AXES = ("fsdp", "grp", "tp")
ADAPTER_SCALING = 2.0
LOG2E = math.log2(math.e)
MIB = 1024 * 1024
ANY = pl.BlockSpec(memory_space=pl.ANY)
HBM = pl.BlockSpec(memory_space=pltpu.HBM)
VMEM = pl.BlockSpec(memory_space=pltpu.VMEM)
SMEM = pl.BlockSpec(memory_space=pltpu.SMEM)


class Layout:
    def __init__(self, mesh):
        self.fsdp, self.grp, self.tp = (mesh.shape[a] for a in AXES)
        self.depth = self.fsdp // 2
        self.ring = self.depth * self.grp
        self.block = self.depth // self.tp

    def flat(self, z, core, g, t):
        return ((z * 2 + core) * self.grp + g) * self.tp + t

    def devices(self):
        for z in range(self.depth):
            for core in range(2):
                for g in range(self.grp):
                    for t in range(self.tp):
                        yield z, core, g, t

    def place(self, z, g):
        return g * self.depth + (z if g % 2 == 0 else self.depth - 1 - z)

    def at(self, position):
        g, z = divmod(position, self.depth)
        return (z if g % 2 == 0 else self.depth - 1 - z), g

    def ring_step(self):
        pairs = []
        for z, core, g, t in self.devices():
            to_z, to_g = self.at((self.place(z, g) + (1 - 2 * core)) % self.ring)
            pairs.append((self.flat(z, core, g, t), self.flat(to_z, core, to_g, t)))
        return pairs

    def plane_swap(self):
        return [(self.flat(z, c, g, t), self.flat(z, c, g, t ^ 1)) for z, c, g, t in self.devices()]

    def core_swap(self):
        return [
            (self.flat(z, c, g, t), self.flat(z, 1 - c, g, t)) for z, c, g, t in self.devices()
        ]

    def feature_step(self, step):
        return [
            (self.flat(z, c, g, (t + step) % self.tp), self.flat(z, c, g, t))
            for z, c, g, t in self.devices()
        ]


TYPICAL = pl.CostEstimate(flops=6 * 10**8, bytes_accessed=10**7, transcendentals=0)


def over(x, n):
    return x >> (n.bit_length() - 1) if n & (n - 1) == 0 else x // n


def within(x, n):
    return x & (n - 1) if n & (n - 1) == 0 else x % n


def after_all(arrays, token):
    return lax.optimization_barrier((arrays, token))


def pinned(x, space=pltpu.HBM):
    return pltpu.with_memory_space_constraint(x, space)


def sort_rows(lengths, order):
    rows = lengths.shape[0]
    held = [lengths[r] for r in range(rows)]
    for r in range(rows):
        rank = jnp.int32(0)
        for other in range(rows):
            if other != r:
                ahead = held[other] >= held[r] if other < r else held[other] > held[r]
                rank = rank + ahead.astype(jnp.int32)
        order[rank] = r


def by_length(length, sizes, act):
    below = 0
    for slots in sizes:

        @pl.when((length > below) & (length <= slots))
        def _():
            act(slots)

        below = slots


def up_columns(up):
    return jnp.concatenate([up[k] for k in range(up.shape[0])], axis=1)


def plane_part():
    return lax.rem(lax.axis_index("tp"), 2)


def begin_all(down, up, len_hbm, q_hbm, pair, rest, lengths, order, q_ref, up_buf, sems, more):
    lanes = pair.shape[3]
    depth = down.shape[2]
    tiles = depth // lanes
    part = plane_part()
    copies = [
        pltpu.make_async_copy(
            down.at[k, :, pl.ds(i * lanes, lanes)], array.at[0, i], sems.at[which, i]
        )
        for which, (k, array) in enumerate(((part, pair), (1 - part, rest)))
        for i in range(tiles)
    ]
    up_copy = pltpu.make_async_copy(up, up_buf, more.at[0])
    len_copy = pltpu.make_async_copy(len_hbm, lengths, more.at[1])
    q_copy = pltpu.make_async_copy(q_hbm, q_ref, more.at[2])
    for copy in [len_copy, up_copy] + copies + [q_copy]:
        copy.start()
    len_copy.wait()
    sort_rows(lengths, order)
    up_copy.wait()
    columns = up_columns(up_buf)
    pair[0, tiles, :, : columns.shape[1]] = columns
    for copy in copies + [q_copy]:
        copy.wait()


def begin(down, up, lengths, queries):
    count, rank, depth = down.shape
    tiles = depth // 128
    scalars = pltpu.SMEM(lengths.shape, jnp.int32)
    return pl.pallas_call(
        begin_all,
        out_shape=(
            pltpu.VMEM((2, tiles + 1, rank, 128), down.dtype),
            pltpu.VMEM((2, tiles, rank, 128), down.dtype),
            scalars,
            scalars,
            pltpu.VMEM(queries.shape, queries.dtype),
        ),
        in_specs=[HBM] * 4,
        out_specs=(VMEM, VMEM, SMEM, SMEM, VMEM),
        scratch_shapes=[
            pltpu.VMEM(up.shape, up.dtype),
            pltpu.SemaphoreType.DMA((count, tiles)),
            pltpu.SemaphoreType.DMA((3,)),
        ],
        compiler_params=pltpu.CompilerParams(vmem_limit_bytes=2 * MIB),
        cost_estimate=TYPICAL,
        name="begin",
    )(pinned(down), pinned(up), pinned(lengths), pinned(queries))


def pack_other(down, up, _, __, pair, rest):
    lanes = pair.shape[3]
    tiles = down.shape[2] // lanes
    part = plane_part()
    for i in range(tiles):
        cols = slice(i * lanes, (i + 1) * lanes)
        pair[1, i] = down[part, :, cols]
        rest[1, i] = down[1 - part, :, cols]
    columns = up_columns(up)
    pair[1, tiles, :, : columns.shape[1]] = columns


def pack(down, up, pair, rest):
    return pl.pallas_call(
        pack_other,
        out_shape=(like(pair), like(rest)),
        in_specs=[VMEM] * 4,
        out_specs=(VMEM, VMEM),
        input_output_aliases={2: 0, 3: 1},
        compiler_params=pltpu.CompilerParams(vmem_limit_bytes=2 * MIB),
        cost_estimate=TYPICAL,
        name="pack_other",
    )(down, up, pinned(pair, pltpu.VMEM), pinned(rest, pltpu.VMEM))


def attend_cache(pairs, ready, sizes, scale, *refs):
    lengths, order, q_ref, k_hbm, v_hbm = refs[:5]
    k_buf, v_buf, *outs, sems = refs[-5:]
    done = pairs[0]
    o_ref, lse_ref = outs[:2]
    steps, _, heads, size = q_ref.shape
    kv = k_hbm.shape[1] // sizes[-1]
    lanes = steps * heads

    def copies(which, pair, slots):
        span = pl.ds(0, slots * kv)
        hbm, buf = ((k_hbm, k_buf), (v_hbm, v_buf))[which]
        return [
            pltpu.make_async_copy(
                hbm.at[order[2 * pair + i], span],
                buf.at[2 * pair + i, span],
                sems.at[pair, i, which],
            )
            for i in range(2)
        ]

    def start(pair, slots):
        for copy in copies(0, pair, slots) + copies(1, pair, slots):
            copy.start()

    def finish(which, pair, slots):
        for i in which:
            for copy in copies(i, pair, slots):
                copy.wait()

    for pair in range(*ready):
        by_length(lengths[order[2 * pair]], sizes, functools.partial(start, pair))

    row_head = over(within(lax.broadcasted_iota(jnp.int32, (lanes, size), 0), heads), heads // kv)
    slot_head = within(lax.broadcasted_iota(jnp.int32, (lanes, size), 1), kv)
    head_bias = jnp.where(row_head == slot_head, 0.0, -jnp.inf)

    def attend(pair):
        def compute(slots):
            def wait(which):
                @pl.when(pair >= ready[0])
                def _():
                    finish((which,), pair, slots)

            n = slots * kv
            bias = jnp.concatenate([head_bias[:, : min(n, size)]] * max(n // size, 1), axis=1)
            column = lax.broadcasted_iota(jnp.int32, (1, n), 1)
            wait(0)
            scores = []
            for i in range(2):
                row = order[2 * pair + i]
                q = q_ref[:, row].reshape(lanes, size)
                s = lax.dot_general(
                    q,
                    k_buf[2 * pair + i, :n],
                    (((1,), (1,)), ((), ())),
                    preferred_element_type=jnp.float32,
                )
                closed = jnp.where(column < lengths[row] * kv, 0.0, -jnp.inf)
                scores.append(s + (bias + closed))
            highest = [jnp.max(s, axis=1, keepdims=True) * scale for s in scores]
            weights = [jnp.exp2(s * scale - h) for s, h in zip(scores, highest)]
            totals = [jnp.sum(p, axis=1, keepdims=True) for p in weights]
            wait(1)
            for i in range(2):
                o = jnp.dot(
                    weights[i].astype(jnp.bfloat16),
                    v_buf[2 * pair + i, :n],
                    preferred_element_type=jnp.float32,
                )
                spot = 2 * (pair - done) + i
                o_ref[spot] = o / totals[i]
                lse = highest[i] + jnp.log(totals[i]) * LOG2E
                lse_ref[spot] = jnp.broadcast_to(lse, (lanes, size))

        by_length(lengths[order[2 * pair]], sizes, compute)

    if pairs[1] - pairs[0] == 1:
        attend(pairs[0])
    else:
        pl.loop(*pairs)(attend)
    for pair in range(max(pairs[1], ready[0]), ready[1]):
        by_length(lengths[order[2 * pair]], sizes, functools.partial(finish, (0, 1), pair))


def like(x):
    return pltpu.VMEM(x.shape, x.dtype)


def cache_attention(pairs, ready, rows_args, caches, buffers, sizes, after):
    lengths, order, queries = rows_args
    keys, values = caches
    rows, steps, _, heads, size = (keys.shape[0], *queries.shape)
    slots = sizes[-1]
    scale = LOG2E / math.sqrt(size)
    count = 2 * (pairs[1] - pairs[0])
    piece = pltpu.VMEM((count, steps * heads, size), jnp.float32)
    operands = [pinned(x, pltpu.SMEM) for x in (lengths, order)]
    operands += [pinned(queries, pltpu.VMEM)]
    operands += [pinned(keys), pinned(values)]
    aliases = {len(operands) + i: i for i in range(len(buffers))}
    specs = [SMEM, SMEM, VMEM, HBM, HBM] + [VMEM] * len(buffers) + [ANY] * len(after)
    operands += [pinned(b, pltpu.VMEM) for b in buffers] + after
    out_shape = [like(keys), like(values), piece, piece]
    return pl.pallas_call(
        functools.partial(attend_cache, pairs, ready, sizes, scale),
        out_shape=out_shape,
        in_specs=specs,
        out_specs=[VMEM] * len(out_shape),
        input_output_aliases=aliases,
        scratch_shapes=[
            pltpu.SemaphoreType.DMA((rows // 2, 2, 2)),
        ],
        compiler_params=pltpu.CompilerParams(vmem_limit_bytes=8 * MIB),
        cost_estimate=TYPICAL,
        name="cache_attention",
    )(*operands)


def project_old(lay, n_hidden, *refs):
    w_buf, *hidden = refs[: 1 + n_hidden]
    out_ref, h_ref = refs[-2:]
    tp = lax.axis_index("tp")
    for i, h in enumerate(hidden):
        h_ref[lax.rem(tp + i, lay.tp)] = h[...]
    features = h_ref.shape[2]
    chunk = min(features, 1024)
    for k in range(2):
        total = jnp.zeros(out_ref.shape[1:], jnp.float32)
        for t in range(lay.tp):
            for low in range(0, features, chunk):
                start = t * features + low
                total += jnp.dot(
                    h_ref[t, :, low : low + chunk],
                    w_buf[k, start : start + chunk, :],
                    preferred_element_type=jnp.float32,
                )
        out_ref[k] = total


def project(lay, w_buf, hidden, after):
    tokens, features = hidden[0].shape
    return pl.pallas_call(
        functools.partial(project_old, lay, len(hidden)),
        out_shape=(
            pltpu.VMEM((2, tokens, w_buf.shape[2]), jnp.float32),
            pltpu.VMEM((lay.tp, tokens, features), jnp.bfloat16),
        ),
        in_specs=[VMEM] * (1 + len(hidden)) + [ANY] * len(after),
        out_specs=(VMEM, VMEM),
        compiler_params=pltpu.CompilerParams(vmem_limit_bytes=4 * MIB),
        cost_estimate=TYPICAL,
        name="project",
    )(pinned(w_buf, pltpu.VMEM), *hidden, *after)


class Place:
    def __init__(self, lay):
        fsdp, self.grp, self.tp = (lax.axis_index(a) for a in AXES)
        self.z, self.core = fsdp // 2, lax.rem(fsdp, 2)
        self.lay = lay
        there = jnp.where(lax.rem(self.grp, 2) == 0, self.z, lay.depth - 1 - self.z)
        self.own = self.grp * lay.depth + there
        self.per_lane = lay.fsdp * lay.grp // lay.tp
        self.part = plane_part()

    def find(self, plan, downs):
        lay, found = self.lay, []
        for (step, flip, other), down in zip(plan, downs):
            towards = (1 - 2 * self.core if flip else 2 * self.core - 1) * step
            spot = lax.rem(self.own + (lay.ring + towards), lay.ring)
            g = spot // lay.depth
            along = lax.rem(spot, lay.depth)
            zz = jnp.where(lax.rem(g, 2) == 0, along, lay.depth - 1 - along)
            for i in range(2):
                core = lax.rem(self.core + (i + flip), 2)
                index = (zz * 2 + core) * lay.grp + g
                found.append((down.at[i], index, 1 - self.part if other else self.part))
        return found

    def low(self, shards, h_ref, tiles):
        total = jnp.zeros((h_ref.shape[1], shards[0][0].shape[1]), jnp.float32) if shards else 0.0
        for down, index, _ in shards:
            depth = tiles * down.shape[-1]
            column = pl.multiple_of(lax.rem(index, self.per_lane) * depth, depth)
            term = lax.dot_general(
                h_ref[index // self.per_lane, :, pl.ds(column, depth)],
                jnp.concatenate([down[i] for i in range(tiles)], axis=1),
                (((1,), (1,)), ((), ())),
                preferred_element_type=jnp.float32,
            )
            total += term
        return total


def by_projection(place, plan, shards):
    crossed = [other for _, _, other in plan for _ in range(2)]
    return [
        (place.part, [s for s, other in zip(shards, crossed) if not other]),
        (1 - place.part, [s for s, other in zip(shards, crossed) if other]),
    ]


def merge_some(lay, plan, first, n_caches, scale, *refs):
    refs = list(refs)

    def take(n):
        out = refs[:n]
        del refs[:n]
        return out

    last = n_caches > 0
    downs = take(len(plan))
    h_buf, weights = take(2)
    if last:
        old, order, q_ref = take(3)
        caches = [take(2) for _ in range(n_caches)]
        u_buf, low_in, _ = take(3)
        m_hbm, out_hbm, m_buf, sems, low, out_buf, out_sem = refs[-7:]
    elif first:
        m_hbm, u_buf, low, m_buf, sems, u_parts = refs[-6:]
    else:
        u_buf, low_in, _ = take(3)
        m_hbm, low, m_buf, sems = refs[-4:]
    depth, width = m_buf.shape[1:]
    pairs = weights.shape[0]
    cut = min(width, 256)
    lanes = downs[0].shape[-1]
    tiles = depth // lanes
    place = Place(lay)
    shards = place.find(plan, downs)
    groups = by_projection(place, plan, shards)

    if last:
        low[...] = low_in[...]
        for part, group in groups:
            low[part] += place.low(group, h_buf, tiles)
        new = []
        for k in range(pairs):
            high = low[k].astype(jnp.bfloat16)
            rest = (low[k] - high.astype(jnp.float32)).astype(jnp.bfloat16)
            new.append(
                (
                    old[k]
                    + jnp.dot(high, u_buf[k], preferred_element_type=jnp.float32)
                    + jnp.dot(rest, u_buf[k], preferred_element_type=jnp.float32)
                ).astype(jnp.bfloat16)
            )
        add_new_tokens(q_ref, order, caches, new, out_buf, scale)
        out_copy = pltpu.make_async_copy(out_buf, out_hbm, out_sem)
        out_copy.start()
    elif first:
        columns = width // place.per_lane
        for down, index, _ in groups[0][1]:

            @pl.when(index // place.per_lane == place.tp)
            def _():
                u_parts[lax.rem(index, place.per_lane)] = down[tiles, :, : pairs * columns]

        for k in range(pairs):
            u_buf[k] = ADAPTER_SCALING * jnp.concatenate(
                [
                    u_parts[i, :, k * columns : (k + 1) * columns]
                    for i in range(place.per_lane)
                ],
                axis=1,
            )

    chunk = min(depth, 256)
    copies = []
    for j, (down, index, k) in enumerate(shards):
        start = pl.multiple_of(index * depth, depth)
        for begin in range(0, depth, chunk):
            rows = slice(begin, begin + chunk)
            tile = begin // lanes
            d = jnp.concatenate([down[tile + i] for i in range(chunk // lanes)], axis=1)
            for side in range(width // cut):
                cols = slice(side * cut, (side + 1) * cut)
                added = lax.dot_general(
                    d,
                    u_buf[k, :, cols],
                    (((0,), (0,)), ((), ())),
                    preferred_element_type=jnp.float32,
                )
                w = weights[k, pl.ds(start + begin, chunk), cols]
                m_buf[j, rows, cols] = (w.astype(jnp.float32) + added).astype(jnp.bfloat16)
        copy = pltpu.make_async_copy(m_buf.at[j], m_hbm.at[k, pl.ds(start, depth), :], sems.at[j])
        copy.start()
        copies.append(copy)

    if not last:
        low[...] = jnp.zeros_like(low) if first else low_in[...]
        for part, group in groups:
            low[part] += place.low(group, h_buf, tiles)
    for copy in copies + ([out_copy] if last else []):
        copy.wait()


def add_new_tokens(q_ref, order, caches, new, out_buf, scale):
    steps, rows, heads, size = q_ref.shape
    kv = new[0].shape[1] // size
    new = [
        jnp.concatenate([x[:, g * size : (g + 1) * size] for g in range(kv)], axis=0) for x in new
    ]
    n = kv * steps * rows
    lanes = steps * heads
    left = lax.broadcasted_iota(jnp.int32, (lanes, n), 0)
    right = lax.broadcasted_iota(jnp.int32, (lanes, n), 1)
    same_head = over(within(left, heads), heads // kv) == over(right, steps * rows)
    earlier = within(over(right, rows), steps) <= over(left, heads)
    right_row = jnp.where(same_head & earlier, within(right, rows), -1)

    def all_rows(pieces):
        return jnp.concatenate(list(pieces), axis=0)

    q = all_rows(q_ref[:, order[spot]].reshape(lanes, size) for spot in range(rows))
    s = lax.dot_general(q, new[0], (((1,), (1,)), ((), ())), preferred_element_type=jnp.float32)
    bias = all_rows(
        jnp.where(right_row == order[spot], 0.0, -jnp.inf) for spot in range(rows)
    )
    s = s * scale + bias
    lse = all_rows(ref[i] for _, ref in caches for i in range(ref.shape[0]))
    highest = jnp.maximum(jnp.max(s, axis=1, keepdims=True), lse)
    p = jnp.exp2(s - highest[:, :n])
    old = jnp.exp2(lse - highest)
    divisor = jnp.sum(p, axis=1, keepdims=True) + old
    o = old * all_rows(ref[i] for ref, _ in caches for i in range(ref.shape[0]))
    o = (o + jnp.dot(p.astype(jnp.bfloat16), new[1], preferred_element_type=jnp.float32)) / divisor
    for spot in range(rows):
        piece = o[spot * lanes : (spot + 1) * lanes].astype(out_buf.dtype)
        out_buf[:, order[spot]] = piece.reshape(steps, heads, size)


def merge(lay, shape, entries, states, weights, state, final, after):
    pairs, total, width = shape
    tokens, rank = states.shape[1], entries[0][3].shape[-2]
    depth = total // (lay.fsdp * lay.grp)
    per_lane = lay.fsdp * lay.grp // lay.tp
    n = 2 * len(entries)
    merged = pltpu.HBM(shape, jnp.bfloat16)
    low_shape = (pairs, tokens, rank)
    operands = [e[3] for e in entries] + [pinned(states, pltpu.VMEM), pinned(weights, pltpu.VMEM)]
    specs = [VMEM] * len(operands)
    scratch = [pltpu.VMEM((n, depth, width), jnp.bfloat16), pltpu.SemaphoreType.DMA((n,))]
    aliases = {}
    n_caches, scale = 0, 0.0
    if state is not None and final is None:
        m_prev, u_buf, low = state
        operands += [pinned(u_buf, pltpu.VMEM), pinned(low, pltpu.VMEM), pinned(m_prev)]
        specs += [VMEM, VMEM, HBM]
        aliases = {len(operands) - 1: 0}
        out_shape = [merged, pltpu.VMEM(low_shape, jnp.float32)]
        out_specs = [HBM, VMEM]
    elif final is None:
        out_shape = [
            merged,
            pltpu.VMEM((pairs, rank, width), jnp.bfloat16),
            pltpu.VMEM(low_shape, jnp.float32),
        ]
        out_specs = [HBM, VMEM, VMEM]
        scratch.append(pltpu.VMEM((per_lane, rank, pairs * width // per_lane), jnp.bfloat16))
    else:
        olds, order, queries, caches = final
        m_prev, u_buf, low = state
        operands += [olds, pinned(order, pltpu.SMEM), pinned(queries, pltpu.VMEM), *caches]
        specs += [VMEM, SMEM, VMEM] + [VMEM] * len(caches)
        operands += [pinned(u_buf, pltpu.VMEM), pinned(low, pltpu.VMEM), pinned(m_prev)]
        specs += [VMEM, VMEM, HBM]
        aliases = {len(operands) - 1: 0}
        out_shape = [merged, pltpu.HBM(queries.shape, jnp.bfloat16)]
        out_specs = [HBM, HBM]
        scratch += [
            pltpu.VMEM(low_shape, jnp.float32),
            pltpu.VMEM(queries.shape, jnp.bfloat16),
            pltpu.SemaphoreType.DMA,
        ]
        n_caches, scale = len(caches) // 2, LOG2E / math.sqrt(queries.shape[3])
    return pl.pallas_call(
        functools.partial(merge_some, lay, [e[:3] for e in entries], state is None, n_caches, scale),
        out_shape=out_shape,
        in_specs=specs + [ANY] * len(after),
        out_specs=out_specs,
        input_output_aliases=aliases,
        scratch_shapes=scratch,
        compiler_params=pltpu.CompilerParams(vmem_limit_bytes=20 * MIB),
        cost_estimate=TYPICAL,
        name="merge",
    )(*operands, *after)


def shards(
    lay,
    hidden_states,
    queries,
    cache_keys,
    cache_values,
    cache_lengths,
    projection_weight_matrices,
    factor_down,
    factor_up,
):
    send = functools.partial(lax.ppermute, axis_name=AXES)
    steps, rows, features = hidden_states.shape
    slots, kv, size = cache_keys.shape[1:]
    shape = projection_weight_matrices.shape
    sizes = tuple(slots * i // 24 for i in (1, 4, 8, 16, 24))
    own = jnp.swapaxes(factor_down, 1, 2)
    tokens = hidden_states.reshape(steps * rows, features)
    keys = cache_keys.reshape(rows, slots * kv, size)
    values = cache_values.reshape(rows, slots * kv, size)
    swap, ring, planes = lay.core_swap(), lay.ring_step(), lay.plane_swap()
    pair_count = rows // 2
    last_step = lay.ring // 2
    buffers, caches = [], []

    other, other_up = send(own, perm=swap), send(factor_up, perm=swap)
    pair, rest, *rows_args = begin(own, factor_up, cache_lengths, queries)
    pair, rest = pack(other, other_up, pair, rest)

    def attention(pairs, ready, after):
        nonlocal buffers
        out = cache_attention(pairs, ready, rows_args, (keys, values), buffers, sizes, after)
        buffers = list(out[:2])
        caches.extend(out[2:])
        return out[2]

    entries = [(0, 0, 0, pair), (0, 0, 1, rest)]
    sent = send(pair, perm=ring)
    hidden = [tokens] + [send(tokens, perm=lay.feature_step(i)) for i in range(1, lay.tp)]
    token = attention((0, 1), (0, 2), [pair])
    came, token = after_all(sent, token)
    crossing, crossed = [], []
    for step in range(1, last_step):
        entries.append((step, 0, 0, came))
        over_there = [(s, send(x, perm=swap)) for s, x in crossed]
        across = [(step, send(came, perm=planes))]
        swapped = send(came, perm=swap)
        sent = send(came, perm=ring)
        if step == 1:
            token = attention((1, 2), (2, pair_count), [token])
        elif step == 2:
            token = attention((2, pair_count), (pair_count, pair_count), [token])
        elif step == 3:
            olds, states = project(lay, projection_weight_matrices, hidden, [token])
            token = olds
        arrived = [x for _, x in crossing]
        if step + 1 == last_step:
            (sent, arrived), token = after_all((sent, arrived), token)
        (came, hidden, arrived, swapped, held), token = after_all(
            (sent, hidden, arrived, swapped, [x for _, x in over_there]), token
        )
        entries.append((step, 1, 0, swapped))
        entries += [(s, 1, 1, x) for (s, _), x in zip(over_there, held)]
        crossed = [(s, x) for (s, _), x in zip(crossing, arrived)]
        entries += [(s, 0, 1, x) for s, x in crossed]
        crossing = across
    weights = projection_weight_matrices
    entries.append((last_step, 0, 0, came))
    own_plane = [e for e in entries if not e[2]]
    others = [e for e in entries if e[2]]
    late = [(last_step, 0, 1, send(came, perm=planes))]
    late += [(s, 1, 1, send(x, perm=swap)) for s, x in crossed]
    m, u, low = merge(lay, shape, own_plane, states, weights, None, None, [token])
    (step, x), = crossing
    x, low = after_all(x, low)
    late.append((step, 1, 1, send(x, perm=swap)))
    others.append((step, 0, 1, x))
    m, low = merge(lay, shape, others, states, weights, [m, u, low], None, [])
    arrived, low = after_all([x for _, _, _, x in late], low)
    late = [(*e[:3], x) for e, x in zip(late, arrived)]
    _, order, q = rows_args
    final = (olds, order, q, caches)
    return tuple(merge(lay, shape, late, states, weights, [m, u, low], final, []))


def solution(mesh):
    return jax.shard_map(
        functools.partial(shards, Layout(mesh)),
        mesh=mesh,
        in_specs=(
            P(None, ("fsdp", "grp"), "tp"),
            P(None, ("fsdp", "grp"), "tp", None),
            P(("fsdp", "grp"), None, "tp", None),
            P(("fsdp", "grp"), None, "tp", None),
            P(("fsdp", "grp")),
            P(None, None, "tp"),
            P(None, ("fsdp", "grp"), None),
            P(None, None, ("fsdp", "grp")),
        ),
        out_specs=(P(None, None, "tp"), P(None, ("fsdp", "grp"), "tp", None)),
        check_vma=False,
    )
```

```python
import functools
import math

import jax
import jax.numpy as jnp
from jax import lax
from jax.experimental import pallas as pl
from jax.experimental.pallas import tpu as pltpu
from jax.sharding import PartitionSpec as P

AXES = ("fsdp", "grp", "tp")
ADAPTER_SCALING = 2.0
LOG2E = math.log2(math.e)
MIB = 1024 * 1024
ANY = pl.BlockSpec(memory_space=pl.ANY)
HBM = pl.BlockSpec(memory_space=pltpu.HBM)
VMEM = pl.BlockSpec(memory_space=pltpu.VMEM)
SMEM = pl.BlockSpec(memory_space=pltpu.SMEM)


class Layout:
    def __init__(self, mesh):
        self.fsdp, self.grp, self.tp = (mesh.shape[a] for a in AXES)
        self.depth = self.fsdp // 2
        self.ring = self.depth * self.grp
        self.block = self.depth // self.tp

    def flat(self, z, core, g, t):
        return ((z * 2 + core) * self.grp + g) * self.tp + t

    def devices(self):
        for z in range(self.depth):
            for core in range(2):
                for g in range(self.grp):
                    for t in range(self.tp):
                        yield z, core, g, t

    def place(self, z, g):
        return g * self.depth + (z if g % 2 == 0 else self.depth - 1 - z)

    def at(self, position):
        g, z = divmod(position, self.depth)
        return (z if g % 2 == 0 else self.depth - 1 - z), g

    def ring_step(self):
        pairs = []
        for z, core, g, t in self.devices():
            to_z, to_g = self.at((self.place(z, g) + (1 - 2 * core)) % self.ring)
            pairs.append((self.flat(z, core, g, t), self.flat(to_z, core, to_g, t)))
        return pairs

    def plane_swap(self):
        return [(self.flat(z, c, g, t), self.flat(z, c, g, t ^ 1)) for z, c, g, t in self.devices()]

    def core_swap(self):
        return [
            (self.flat(z, c, g, t), self.flat(z, 1 - c, g, t)) for z, c, g, t in self.devices()
        ]

    def feature_step(self, step):
        return [
            (self.flat(z, c, g, (t + step) % self.tp), self.flat(z, c, g, t))
            for z, c, g, t in self.devices()
        ]


TYPICAL = pl.CostEstimate(flops=6 * 10**8, bytes_accessed=10**7, transcendentals=0)


def over(x, n):
    return x >> (n.bit_length() - 1) if n & (n - 1) == 0 else x // n


def within(x, n):
    return x & (n - 1) if n & (n - 1) == 0 else x % n


def after_all(arrays, token):
    return lax.optimization_barrier((arrays, token))


def pinned(x, space=pltpu.HBM):
    return pltpu.with_memory_space_constraint(x, space)


def sort_rows(lengths, order):
    rows = lengths.shape[0]
    held = [lengths[r] for r in range(rows)]
    for r in range(rows):
        rank = jnp.int32(0)
        for other in range(rows):
            if other != r:
                ahead = held[other] >= held[r] if other < r else held[other] > held[r]
                rank = rank + ahead.astype(jnp.int32)
        order[rank] = r


def by_length(length, sizes, act):
    below = 0
    for slots in sizes:

        @pl.when((length > below) & (length <= slots))
        def _():
            act(slots)

        below = slots


def up_columns(up):
    return jnp.concatenate([up[k] for k in range(up.shape[0])], axis=1)


def plane_part():
    return lax.rem(lax.axis_index("tp"), 2)


def begin_all(down, up, len_hbm, q_hbm, pair, rest, lengths, order, q_ref, up_buf, sems, more):
    lanes = pair.shape[3]
    depth = down.shape[2]
    tiles = depth // lanes
    part = plane_part()
    copies = [
        pltpu.make_async_copy(
            down.at[k, :, pl.ds(i * lanes, lanes)], array.at[0, i], sems.at[which, i]
        )
        for which, (k, array) in enumerate(((part, pair), (1 - part, rest)))
        for i in range(tiles)
    ]
    up_copy = pltpu.make_async_copy(up, up_buf, more.at[0])
    len_copy = pltpu.make_async_copy(len_hbm, lengths, more.at[1])
    q_copy = pltpu.make_async_copy(q_hbm, q_ref, more.at[2])
    for copy in [len_copy, up_copy] + copies + [q_copy]:
        copy.start()
    len_copy.wait()
    sort_rows(lengths, order)
    up_copy.wait()
    columns = up_columns(up_buf)
    pair[0, tiles, :, : columns.shape[1]] = columns
    for copy in copies + [q_copy]:
        copy.wait()


def begin(down, up, lengths, queries):
    count, rank, depth = down.shape
    tiles = depth // 128
    scalars = pltpu.SMEM(lengths.shape, jnp.int32)
    return pl.pallas_call(
        begin_all,
        out_shape=(
            pltpu.VMEM((2, tiles + 1, rank, 128), down.dtype),
            pltpu.VMEM((2, tiles, rank, 128), down.dtype),
            scalars,
            scalars,
            pltpu.VMEM(queries.shape, queries.dtype),
        ),
        in_specs=[HBM] * 4,
        out_specs=(VMEM, VMEM, SMEM, SMEM, VMEM),
        scratch_shapes=[
            pltpu.VMEM(up.shape, up.dtype),
            pltpu.SemaphoreType.DMA((count, tiles)),
            pltpu.SemaphoreType.DMA((3,)),
        ],
        compiler_params=pltpu.CompilerParams(vmem_limit_bytes=2 * MIB),
        cost_estimate=TYPICAL,
        name="begin",
    )(pinned(down), pinned(up), pinned(lengths), pinned(queries))


def pack_other(down, up, _, __, pair, rest):
    lanes = pair.shape[3]
    tiles = down.shape[2] // lanes
    part = plane_part()
    for i in range(tiles):
        cols = slice(i * lanes, (i + 1) * lanes)
        pair[1, i] = down[part, :, cols]
        rest[1, i] = down[1 - part, :, cols]
    columns = up_columns(up)
    pair[1, tiles, :, : columns.shape[1]] = columns


def pack(down, up, pair, rest):
    return pl.pallas_call(
        pack_other,
        out_shape=(like(pair), like(rest)),
        in_specs=[VMEM] * 4,
        out_specs=(VMEM, VMEM),
        input_output_aliases={2: 0, 3: 1},
        compiler_params=pltpu.CompilerParams(vmem_limit_bytes=2 * MIB),
        cost_estimate=TYPICAL,
        name="pack_other",
    )(down, up, pinned(pair, pltpu.VMEM), pinned(rest, pltpu.VMEM))


def attend_cache(pairs, ready, sizes, scale, *refs):
    lengths, order, q_ref, k_hbm, v_hbm = refs[:5]
    k_buf, v_buf, *outs, sems = refs[-5:]
    done = pairs[0]
    o_ref, lse_ref = outs[:2]
    steps, _, heads, size = q_ref.shape
    kv = k_hbm.shape[1] // sizes[-1]
    lanes = steps * heads

    def copies(which, pair, slots):
        span = pl.ds(0, slots * kv)
        hbm, buf = ((k_hbm, k_buf), (v_hbm, v_buf))[which]
        return [
            pltpu.make_async_copy(
                hbm.at[order[2 * pair + i], span],
                buf.at[2 * pair + i, span],
                sems.at[pair, i, which],
            )
            for i in range(2)
        ]

    def start(pair, slots):
        for copy in copies(0, pair, slots) + copies(1, pair, slots):
            copy.start()

    def finish(which, pair, slots):
        for i in which:
            for copy in copies(i, pair, slots):
                copy.wait()

    for pair in range(*ready):
        by_length(lengths[order[2 * pair]], sizes, functools.partial(start, pair))

    row_head = over(within(lax.broadcasted_iota(jnp.int32, (lanes, size), 0), heads), heads // kv)
    slot_head = within(lax.broadcasted_iota(jnp.int32, (lanes, size), 1), kv)
    head_bias = jnp.where(row_head == slot_head, 0.0, -jnp.inf)

    def attend(pair):
        def compute(slots):
            def wait(which):
                @pl.when(pair >= ready[0])
                def _():
                    finish((which,), pair, slots)

            n = slots * kv
            bias = jnp.concatenate([head_bias[:, : min(n, size)]] * max(n // size, 1), axis=1)
            column = lax.broadcasted_iota(jnp.int32, (1, n), 1)
            wait(0)
            scores = []
            for i in range(2):
                row = order[2 * pair + i]
                q = q_ref[:, row].reshape(lanes, size)
                s = lax.dot_general(
                    q,
                    k_buf[2 * pair + i, :n],
                    (((1,), (1,)), ((), ())),
                    preferred_element_type=jnp.float32,
                )
                closed = jnp.where(column < lengths[row] * kv, 0.0, -jnp.inf)
                scores.append(s + (bias + closed))
            highest = [jnp.max(s, axis=1, keepdims=True) * scale for s in scores]
            weights = [jnp.exp2(s * scale - h) for s, h in zip(scores, highest)]
            totals = [jnp.sum(p, axis=1, keepdims=True) for p in weights]
            wait(1)
            for i in range(2):
                o = jnp.dot(
                    weights[i].astype(jnp.bfloat16),
                    v_buf[2 * pair + i, :n],
                    preferred_element_type=jnp.float32,
                )
                spot = 2 * (pair - done) + i
                o_ref[spot] = o / totals[i]
                lse = highest[i] + jnp.log(totals[i]) * LOG2E
                lse_ref[spot] = jnp.broadcast_to(lse, (lanes, size))

        by_length(lengths[order[2 * pair]], sizes, compute)

    if pairs[1] - pairs[0] == 1:
        attend(pairs[0])
    else:
        pl.loop(*pairs)(attend)
    for pair in range(max(pairs[1], ready[0]), ready[1]):
        by_length(lengths[order[2 * pair]], sizes, functools.partial(finish, (0, 1), pair))


def like(x):
    return pltpu.VMEM(x.shape, x.dtype)


def cache_attention(pairs, ready, rows_args, caches, buffers, sizes, after):
    lengths, order, queries = rows_args
    keys, values = caches
    rows, steps, _, heads, size = (keys.shape[0], *queries.shape)
    slots = sizes[-1]
    scale = LOG2E / math.sqrt(size)
    count = 2 * (pairs[1] - pairs[0])
    piece = pltpu.VMEM((count, steps * heads, size), jnp.float32)
    operands = [pinned(x, pltpu.SMEM) for x in (lengths, order)]
    operands += [pinned(queries, pltpu.VMEM)]
    operands += [pinned(keys), pinned(values)]
    aliases = {len(operands) + i: i for i in range(len(buffers))}
    specs = [SMEM, SMEM, VMEM, HBM, HBM] + [VMEM] * len(buffers) + [ANY] * len(after)
    operands += [pinned(b, pltpu.VMEM) for b in buffers] + after
    out_shape = [like(keys), like(values), piece, piece]
    return pl.pallas_call(
        functools.partial(attend_cache, pairs, ready, sizes, scale),
        out_shape=out_shape,
        in_specs=specs,
        out_specs=[VMEM] * len(out_shape),
        input_output_aliases=aliases,
        scratch_shapes=[
            pltpu.SemaphoreType.DMA((rows // 2, 2, 2)),
        ],
        compiler_params=pltpu.CompilerParams(vmem_limit_bytes=8 * MIB),
        cost_estimate=TYPICAL,
        name="cache_attention",
    )(*operands)


def project_old(lay, n_hidden, *refs):
    w_buf, *hidden = refs[: 1 + n_hidden]
    out_ref, h_ref = refs[-2:]
    tp = lax.axis_index("tp")
    for i, h in enumerate(hidden):
        h_ref[lax.rem(tp + i, lay.tp)] = h[...]
    features = h_ref.shape[2]
    chunk = min(features, 1024)
    for k in range(2):
        total = jnp.zeros(out_ref.shape[1:], jnp.float32)
        for t in range(lay.tp):
            for low in range(0, features, chunk):
                start = t * features + low
                total += jnp.dot(
                    h_ref[t, :, low : low + chunk],
                    w_buf[k, start : start + chunk, :],
                    preferred_element_type=jnp.float32,
                )
        out_ref[k] = total


def project(lay, w_buf, hidden, after):
    tokens, features = hidden[0].shape
    return pl.pallas_call(
        functools.partial(project_old, lay, len(hidden)),
        out_shape=(
            pltpu.VMEM((2, tokens, w_buf.shape[2]), jnp.float32),
            pltpu.VMEM((lay.tp, tokens, features), jnp.bfloat16),
        ),
        in_specs=[VMEM] * (1 + len(hidden)) + [ANY] * len(after),
        out_specs=(VMEM, VMEM),
        compiler_params=pltpu.CompilerParams(vmem_limit_bytes=4 * MIB),
        cost_estimate=TYPICAL,
        name="project",
    )(pinned(w_buf, pltpu.VMEM), *hidden, *after)


class Place:
    def __init__(self, lay):
        fsdp, self.grp, self.tp = (lax.axis_index(a) for a in AXES)
        self.z, self.core = fsdp // 2, lax.rem(fsdp, 2)
        self.lay = lay
        there = jnp.where(lax.rem(self.grp, 2) == 0, self.z, lay.depth - 1 - self.z)
        self.own = self.grp * lay.depth + there
        self.per_lane = lay.fsdp * lay.grp // lay.tp
        self.part = plane_part()

    def find(self, plan, downs):
        lay, found = self.lay, []
        for (step, flip, other), down in zip(plan, downs):
            towards = (1 - 2 * self.core if flip else 2 * self.core - 1) * step
            spot = lax.rem(self.own + (lay.ring + towards), lay.ring)
            g = spot // lay.depth
            along = lax.rem(spot, lay.depth)
            zz = jnp.where(lax.rem(g, 2) == 0, along, lay.depth - 1 - along)
            for i in range(2):
                core = lax.rem(self.core + (i + flip), 2)
                index = (zz * 2 + core) * lay.grp + g
                found.append((down.at[i], index, 1 - self.part if other else self.part))
        return found

    def low(self, shards, h_ref, tiles):
        total = jnp.zeros((h_ref.shape[1], shards[0][0].shape[1]), jnp.float32) if shards else 0.0
        for down, index, _ in shards:
            depth = tiles * down.shape[-1]
            column = pl.multiple_of(lax.rem(index, self.per_lane) * depth, depth)
            term = lax.dot_general(
                h_ref[index // self.per_lane, :, pl.ds(column, depth)],
                jnp.concatenate([down[i] for i in range(tiles)], axis=1),
                (((1,), (1,)), ((), ())),
                preferred_element_type=jnp.float32,
            )
            total += term
        return total


def by_projection(place, plan, shards):
    crossed = [other for _, _, other in plan for _ in range(2)]
    return [
        (place.part, [s for s, other in zip(shards, crossed) if not other]),
        (1 - place.part, [s for s, other in zip(shards, crossed) if other]),
    ]


def merge_some(lay, plan, first, n_caches, scale, *refs):
    refs = list(refs)

    def take(n):
        out = refs[:n]
        del refs[:n]
        return out

    last = n_caches > 0
    downs = take(len(plan))
    h_buf, weights = take(2)
    if last:
        old, order, q_ref = take(3)
        caches = [take(2) for _ in range(n_caches)]
        u_buf, low_in, _ = take(3)
        m_hbm, out_hbm, m_buf, sems, low, out_buf, out_sem = refs[-7:]
    elif first:
        m_hbm, u_buf, low, m_buf, sems, u_parts = refs[-6:]
    else:
        u_buf, low_in, _ = take(3)
        m_hbm, low, m_buf, sems = refs[-4:]
    depth, width = m_buf.shape[1:]
    pairs = weights.shape[0]
    cut = min(width, 256)
    lanes = downs[0].shape[-1]
    tiles = depth // lanes
    place = Place(lay)
    shards = place.find(plan, downs)
    groups = by_projection(place, plan, shards)

    if last:
        low[...] = low_in[...]
        for part, group in groups:
            low[part] += place.low(group, h_buf, tiles)
        new = []
        for k in range(pairs):
            high = low[k].astype(jnp.bfloat16)
            rest = (low[k] - high.astype(jnp.float32)).astype(jnp.bfloat16)
            new.append(
                (
                    old[k]
                    + jnp.dot(high, u_buf[k], preferred_element_type=jnp.float32)
                    + jnp.dot(rest, u_buf[k], preferred_element_type=jnp.float32)
                ).astype(jnp.bfloat16)
            )
        add_new_tokens(q_ref, order, caches, new, out_buf, scale)
        out_copy = pltpu.make_async_copy(out_buf, out_hbm, out_sem)
        out_copy.start()
    elif first:
        columns = width // place.per_lane
        for down, index, _ in groups[0][1]:

            @pl.when(index // place.per_lane == place.tp)
            def _():
                u_parts[lax.rem(index, place.per_lane)] = down[tiles, :, : pairs * columns]

        for k in range(pairs):
            u_buf[k] = ADAPTER_SCALING * jnp.concatenate(
                [
                    u_parts[i, :, k * columns : (k + 1) * columns]
                    for i in range(place.per_lane)
                ],
                axis=1,
            )

    chunk = min(depth, 256)
    copies = []
    for j, (down, index, k) in enumerate(shards):
        start = pl.multiple_of(index * depth, depth)
        for begin in range(0, depth, chunk):
            rows = slice(begin, begin + chunk)
            tile = begin // lanes
            d = jnp.concatenate([down[tile + i] for i in range(chunk // lanes)], axis=1)
            for side in range(width // cut):
                cols = slice(side * cut, (side + 1) * cut)
                added = lax.dot_general(
                    d,
                    u_buf[k, :, cols],
                    (((0,), (0,)), ((), ())),
                    preferred_element_type=jnp.float32,
                )
                w = weights[k, pl.ds(start + begin, chunk), cols]
                m_buf[j, rows, cols] = (w.astype(jnp.float32) + added).astype(jnp.bfloat16)
            copy = pltpu.make_async_copy(
                m_buf.at[j, pl.ds(begin, chunk)],
                m_hbm.at[k, pl.ds(start + begin, chunk), :],
                sems.at[j, begin // chunk],
            )
            copy.start()
            copies.append(copy)

    if not last:
        low[...] = jnp.zeros_like(low) if first else low_in[...]
        for part, group in groups:
            low[part] += place.low(group, h_buf, tiles)
    for copy in copies + ([out_copy] if last else []):
        copy.wait()


def add_new_tokens(q_ref, order, caches, new, out_buf, scale):
    steps, rows, heads, size = q_ref.shape
    kv = new[0].shape[1] // size
    new = [
        jnp.concatenate([x[:, g * size : (g + 1) * size] for g in range(kv)], axis=0) for x in new
    ]
    n = kv * steps * rows
    lanes = steps * heads
    left = lax.broadcasted_iota(jnp.int32, (lanes, n), 0)
    right = lax.broadcasted_iota(jnp.int32, (lanes, n), 1)
    same_head = over(within(left, heads), heads // kv) == over(right, steps * rows)
    earlier = within(over(right, rows), steps) <= over(left, heads)
    right_row = jnp.where(same_head & earlier, within(right, rows), -1)

    def all_rows(pieces):
        return jnp.concatenate(list(pieces), axis=0)

    q = all_rows(q_ref[:, order[spot]].reshape(lanes, size) for spot in range(rows))
    s = lax.dot_general(q, new[0], (((1,), (1,)), ((), ())), preferred_element_type=jnp.float32)
    bias = all_rows(
        jnp.where(right_row == order[spot], 0.0, -jnp.inf) for spot in range(rows)
    )
    s = s * scale + bias
    lse = all_rows(ref[i] for _, ref in caches for i in range(ref.shape[0]))
    highest = jnp.maximum(jnp.max(s, axis=1, keepdims=True), lse)
    p = jnp.exp2(s - highest[:, :n])
    old = jnp.exp2(lse - highest)
    divisor = jnp.sum(p, axis=1, keepdims=True) + old
    o = old * all_rows(ref[i] for ref, _ in caches for i in range(ref.shape[0]))
    o = (o + jnp.dot(p.astype(jnp.bfloat16), new[1], preferred_element_type=jnp.float32)) / divisor
    for spot in range(rows):
        piece = o[spot * lanes : (spot + 1) * lanes].astype(out_buf.dtype)
        out_buf[:, order[spot]] = piece.reshape(steps, heads, size)


def merge(lay, shape, entries, states, weights, state, final, after):
    pairs, total, width = shape
    tokens, rank = states.shape[1], entries[0][3].shape[-2]
    depth = total // (lay.fsdp * lay.grp)
    per_lane = lay.fsdp * lay.grp // lay.tp
    n = 2 * len(entries)
    merged = pltpu.HBM(shape, jnp.bfloat16)
    low_shape = (pairs, tokens, rank)
    operands = [e[3] for e in entries] + [pinned(states, pltpu.VMEM), pinned(weights, pltpu.VMEM)]
    specs = [VMEM] * len(operands)
    scratch = [pltpu.VMEM((n, depth, width), jnp.bfloat16)]
    scratch.append(pltpu.SemaphoreType.DMA((n, max(1, depth // 256))))
    aliases = {}
    n_caches, scale = 0, 0.0
    if state is not None and final is None:
        m_prev, u_buf, low = state
        operands += [pinned(u_buf, pltpu.VMEM), pinned(low, pltpu.VMEM), pinned(m_prev)]
        specs += [VMEM, VMEM, HBM]
        aliases = {len(operands) - 1: 0}
        out_shape = [merged, pltpu.VMEM(low_shape, jnp.float32)]
        out_specs = [HBM, VMEM]
    elif final is None:
        out_shape = [
            merged,
            pltpu.VMEM((pairs, rank, width), jnp.bfloat16),
            pltpu.VMEM(low_shape, jnp.float32),
        ]
        out_specs = [HBM, VMEM, VMEM]
        scratch.append(pltpu.VMEM((per_lane, rank, pairs * width // per_lane), jnp.bfloat16))
    else:
        olds, order, queries, caches = final
        m_prev, u_buf, low = state
        operands += [olds, pinned(order, pltpu.SMEM), pinned(queries, pltpu.VMEM), *caches]
        specs += [VMEM, SMEM, VMEM] + [VMEM] * len(caches)
        operands += [pinned(u_buf, pltpu.VMEM), pinned(low, pltpu.VMEM), pinned(m_prev)]
        specs += [VMEM, VMEM, HBM]
        aliases = {len(operands) - 1: 0}
        out_shape = [merged, pltpu.HBM(queries.shape, jnp.bfloat16)]
        out_specs = [HBM, HBM]
        scratch += [
            pltpu.VMEM(low_shape, jnp.float32),
            pltpu.VMEM(queries.shape, jnp.bfloat16),
            pltpu.SemaphoreType.DMA,
        ]
        n_caches, scale = len(caches) // 2, LOG2E / math.sqrt(queries.shape[3])
    return pl.pallas_call(
        functools.partial(merge_some, lay, [e[:3] for e in entries], state is None, n_caches, scale),
        out_shape=out_shape,
        in_specs=specs + [ANY] * len(after),
        out_specs=out_specs,
        input_output_aliases=aliases,
        scratch_shapes=scratch,
        compiler_params=pltpu.CompilerParams(vmem_limit_bytes=20 * MIB),
        cost_estimate=TYPICAL,
        name="merge",
    )(*operands, *after)


def shards(
    lay,
    hidden_states,
    queries,
    cache_keys,
    cache_values,
    cache_lengths,
    projection_weight_matrices,
    factor_down,
    factor_up,
):
    send = functools.partial(lax.ppermute, axis_name=AXES)
    steps, rows, features = hidden_states.shape
    slots, kv, size = cache_keys.shape[1:]
    shape = projection_weight_matrices.shape
    sizes = tuple(slots * i // 24 for i in (1, 4, 8, 16, 24))
    own = jnp.swapaxes(factor_down, 1, 2)
    tokens = hidden_states.reshape(steps * rows, features)
    keys = cache_keys.reshape(rows, slots * kv, size)
    values = cache_values.reshape(rows, slots * kv, size)
    swap, ring, planes = lay.core_swap(), lay.ring_step(), lay.plane_swap()
    pair_count = rows // 2
    last_step = lay.ring // 2
    buffers, caches = [], []

    other, other_up = send(own, perm=swap), send(factor_up, perm=swap)
    pair, rest, *rows_args = begin(own, factor_up, cache_lengths, queries)
    pair, rest = pack(other, other_up, pair, rest)

    def attention(pairs, ready, after):
        nonlocal buffers
        out = cache_attention(pairs, ready, rows_args, (keys, values), buffers, sizes, after)
        buffers = list(out[:2])
        caches.extend(out[2:])
        return out[2]

    entries = [(0, 0, 0, pair), (0, 0, 1, rest)]
    sent = send(pair, perm=ring)
    hidden = [tokens] + [send(tokens, perm=lay.feature_step(i)) for i in range(1, lay.tp)]
    token = attention((0, 1), (0, 2), [pair])
    came, token = after_all(sent, token)
    crossing, crossed = [], []
    for step in range(1, last_step):
        entries.append((step, 0, 0, came))
        over_there = [(s, send(x, perm=swap)) for s, x in crossed]
        across = [(step, send(came, perm=planes))]
        swapped = send(came, perm=swap)
        sent = send(came, perm=ring)
        if step == 1:
            token = attention((1, 2), (2, pair_count), [token])
        elif step == 2:
            token = attention((2, pair_count), (pair_count, pair_count), [token])
        elif step == 3:
            olds, states = project(lay, projection_weight_matrices, hidden, [token])
            token = olds
        arrived = [x for _, x in crossing]
        if step + 1 == last_step:
            (sent, arrived), token = after_all((sent, arrived), token)
        (came, hidden, arrived, swapped, held), token = after_all(
            (sent, hidden, arrived, swapped, [x for _, x in over_there]), token
        )
        entries.append((step, 1, 0, swapped))
        entries += [(s, 1, 1, x) for (s, _), x in zip(over_there, held)]
        crossed = [(s, x) for (s, _), x in zip(crossing, arrived)]
        entries += [(s, 0, 1, x) for s, x in crossed]
        crossing = across
    weights = projection_weight_matrices
    entries.append((last_step, 0, 0, came))
    own_plane = [e for e in entries if not e[2]]
    others = [e for e in entries if e[2]]
    late = [(last_step, 0, 1, send(came, perm=planes))]
    late += [(s, 1, 1, send(x, perm=swap)) for s, x in crossed]
    m, u, low = merge(lay, shape, own_plane, states, weights, None, None, [token])
    (step, x), = crossing
    x, low = after_all(x, low)
    late.append((step, 1, 1, send(x, perm=swap)))
    others.append((step, 0, 1, x))
    m, low = merge(lay, shape, others, states, weights, [m, u, low], None, [])
    arrived, low = after_all([x for _, _, _, x in late], low)
    late = [(*e[:3], x) for e, x in zip(late, arrived)]
    _, order, q = rows_args
    final = (olds, order, q, caches)
    return tuple(merge(lay, shape, late, states, weights, [m, u, low], final, []))


def solution(mesh):
    return jax.shard_map(
        functools.partial(shards, Layout(mesh)),
        mesh=mesh,
        in_specs=(
            P(None, ("fsdp", "grp"), "tp"),
            P(None, ("fsdp", "grp"), "tp", None),
            P(("fsdp", "grp"), None, "tp", None),
            P(("fsdp", "grp"), None, "tp", None),
            P(("fsdp", "grp")),
            P(None, None, "tp"),
            P(None, ("fsdp", "grp"), None),
            P(None, None, ("fsdp", "grp")),
        ),
        out_specs=(P(None, None, "tp"), P(None, ("fsdp", "grp"), "tp", None)),
        check_vma=False,
    )
```

```python
import functools
import math

import jax
import jax.numpy as jnp
from jax import lax
from jax.experimental import pallas as pl
from jax.experimental.pallas import tpu as pltpu
from jax.sharding import PartitionSpec as P

AXES = ("fsdp", "grp", "tp")
ADAPTER_SCALING = 2.0
LOG2E = math.log2(math.e)
MIB = 1024 * 1024
ANY = pl.BlockSpec(memory_space=pl.ANY)
HBM = pl.BlockSpec(memory_space=pltpu.HBM)
VMEM = pl.BlockSpec(memory_space=pltpu.VMEM)
SMEM = pl.BlockSpec(memory_space=pltpu.SMEM)


class Layout:
    def __init__(self, mesh):
        self.fsdp, self.grp, self.tp = (mesh.shape[a] for a in AXES)
        self.depth = self.fsdp // 2
        self.ring = self.depth * self.grp
        self.block = self.depth // self.tp

    def flat(self, z, core, g, t):
        return ((z * 2 + core) * self.grp + g) * self.tp + t

    def devices(self):
        for z in range(self.depth):
            for core in range(2):
                for g in range(self.grp):
                    for t in range(self.tp):
                        yield z, core, g, t

    def place(self, z, g):
        return g * self.depth + (z if g % 2 == 0 else self.depth - 1 - z)

    def at(self, position):
        g, z = divmod(position, self.depth)
        return (z if g % 2 == 0 else self.depth - 1 - z), g

    def ring_step(self):
        pairs = []
        for z, core, g, t in self.devices():
            to_z, to_g = self.at((self.place(z, g) + (1 - 2 * core)) % self.ring)
            pairs.append((self.flat(z, core, g, t), self.flat(to_z, core, to_g, t)))
        return pairs

    def plane_swap(self):
        return [(self.flat(z, c, g, t), self.flat(z, c, g, t ^ 1)) for z, c, g, t in self.devices()]

    def core_swap(self):
        return [
            (self.flat(z, c, g, t), self.flat(z, 1 - c, g, t)) for z, c, g, t in self.devices()
        ]

    def feature_step(self, step):
        return [
            (self.flat(z, c, g, (t + step) % self.tp), self.flat(z, c, g, t))
            for z, c, g, t in self.devices()
        ]


TYPICAL = pl.CostEstimate(flops=6 * 10**8, bytes_accessed=10**7, transcendentals=0)


def over(x, n):
    return x >> (n.bit_length() - 1) if n & (n - 1) == 0 else x // n


def within(x, n):
    return x & (n - 1) if n & (n - 1) == 0 else x % n


def after_all(arrays, token):
    return lax.optimization_barrier((arrays, token))


def pinned(x, space=pltpu.HBM):
    return pltpu.with_memory_space_constraint(x, space)


def sort_rows(lengths, order):
    rows = lengths.shape[0]
    held = [lengths[r] for r in range(rows)]
    for r in range(rows):
        rank = jnp.int32(0)
        for other in range(rows):
            if other != r:
                ahead = held[other] >= held[r] if other < r else held[other] > held[r]
                rank = rank + ahead.astype(jnp.int32)
        order[rank] = r


def by_length(length, sizes, act):
    below = 0
    for slots in sizes:

        @pl.when((length > below) & (length <= slots))
        def _():
            act(slots)

        below = slots


def up_columns(up):
    return jnp.concatenate([up[k] for k in range(up.shape[0])], axis=1)


def plane_part():
    return lax.rem(lax.axis_index("tp"), 2)


def begin_all(down, up, len_hbm, q_hbm, pair, rest, lengths, order, q_ref, up_buf, sems, more):
    lanes = pair.shape[3]
    depth = down.shape[2]
    tiles = depth // lanes
    part = plane_part()
    copies = [
        pltpu.make_async_copy(
            down.at[k, :, pl.ds(i * lanes, lanes)], array.at[0, i], sems.at[which, i]
        )
        for which, (k, array) in enumerate(((part, pair), (1 - part, rest)))
        for i in range(tiles)
    ]
    up_copy = pltpu.make_async_copy(up, up_buf, more.at[0])
    len_copy = pltpu.make_async_copy(len_hbm, lengths, more.at[1])
    q_copy = pltpu.make_async_copy(q_hbm, q_ref, more.at[2])
    for copy in [len_copy, up_copy] + copies + [q_copy]:
        copy.start()
    len_copy.wait()
    sort_rows(lengths, order)
    up_copy.wait()
    columns = up_columns(up_buf)
    pair[0, tiles, :, : columns.shape[1]] = columns
    for copy in copies + [q_copy]:
        copy.wait()


def begin(down, up, lengths, queries):
    count, rank, depth = down.shape
    tiles = depth // 128
    scalars = pltpu.SMEM(lengths.shape, jnp.int32)
    return pl.pallas_call(
        begin_all,
        out_shape=(
            pltpu.VMEM((2, tiles + 1, rank, 128), down.dtype),
            pltpu.VMEM((2, tiles, rank, 128), down.dtype),
            scalars,
            scalars,
            pltpu.VMEM(queries.shape, queries.dtype),
        ),
        in_specs=[HBM] * 4,
        out_specs=(VMEM, VMEM, SMEM, SMEM, VMEM),
        scratch_shapes=[
            pltpu.VMEM(up.shape, up.dtype),
            pltpu.SemaphoreType.DMA((count, tiles)),
            pltpu.SemaphoreType.DMA((3,)),
        ],
        compiler_params=pltpu.CompilerParams(vmem_limit_bytes=2 * MIB),
        cost_estimate=TYPICAL,
        name="begin",
    )(pinned(down), pinned(up), pinned(lengths), pinned(queries))


def pack_other(down, up, _, __, pair, rest):
    lanes = pair.shape[3]
    tiles = down.shape[2] // lanes
    part = plane_part()
    for i in range(tiles):
        cols = slice(i * lanes, (i + 1) * lanes)
        pair[1, i] = down[part, :, cols]
        rest[1, i] = down[1 - part, :, cols]
    columns = up_columns(up)
    pair[1, tiles, :, : columns.shape[1]] = columns


def pack(down, up, pair, rest):
    return pl.pallas_call(
        pack_other,
        out_shape=(like(pair), like(rest)),
        in_specs=[VMEM] * 4,
        out_specs=(VMEM, VMEM),
        input_output_aliases={2: 0, 3: 1},
        compiler_params=pltpu.CompilerParams(vmem_limit_bytes=2 * MIB),
        cost_estimate=TYPICAL,
        name="pack_other",
    )(down, up, pinned(pair, pltpu.VMEM), pinned(rest, pltpu.VMEM))


def attend_cache(pairs, ready, sizes, scale, *refs):
    lengths, order, q_ref, k_hbm, v_hbm = refs[:5]
    k_buf, v_buf, *outs, sems = refs[-5:]
    done = pairs[0]
    o_ref, lse_ref = outs[:2]
    steps, _, heads, size = q_ref.shape
    kv = k_hbm.shape[1] // sizes[-1]
    lanes = steps * heads

    def copies(which, pair, slots):
        span = pl.ds(0, slots * kv)
        hbm, buf = ((k_hbm, k_buf), (v_hbm, v_buf))[which]
        return [
            pltpu.make_async_copy(
                hbm.at[order[2 * pair + i], span],
                buf.at[2 * pair + i, span],
                sems.at[pair, i, which],
            )
            for i in range(2)
        ]

    def start(pair, slots):
        for copy in copies(0, pair, slots) + copies(1, pair, slots):
            copy.start()

    def finish(which, pair, slots):
        for i in which:
            for copy in copies(i, pair, slots):
                copy.wait()

    for pair in range(*ready):
        by_length(lengths[order[2 * pair]], sizes, functools.partial(start, pair))

    row_head = over(within(lax.broadcasted_iota(jnp.int32, (lanes, size), 0), heads), heads // kv)
    slot_head = within(lax.broadcasted_iota(jnp.int32, (lanes, size), 1), kv)
    head_bias = jnp.where(row_head == slot_head, 0.0, -jnp.inf)

    def attend(pair):
        def compute(slots):
            def wait(which):
                @pl.when(pair >= ready[0])
                def _():
                    finish((which,), pair, slots)

            n = slots * kv
            bias = jnp.concatenate([head_bias[:, : min(n, size)]] * max(n // size, 1), axis=1)
            column = lax.broadcasted_iota(jnp.int32, (1, n), 1)
            wait(0)
            scores = []
            for i in range(2):
                row = order[2 * pair + i]
                q = q_ref[:, row].reshape(lanes, size)
                s = lax.dot_general(
                    q,
                    k_buf[2 * pair + i, :n],
                    (((1,), (1,)), ((), ())),
                    preferred_element_type=jnp.float32,
                )
                closed = jnp.where(column < lengths[row] * kv, 0.0, -jnp.inf)
                scores.append(s + (bias + closed))
            highest = [jnp.max(s, axis=1, keepdims=True) * scale for s in scores]
            weights = [jnp.exp2(s * scale - h) for s, h in zip(scores, highest)]
            totals = [jnp.sum(p, axis=1, keepdims=True) for p in weights]
            wait(1)
            for i in range(2):
                o = jnp.dot(
                    weights[i].astype(jnp.bfloat16),
                    v_buf[2 * pair + i, :n],
                    preferred_element_type=jnp.float32,
                )
                spot = 2 * (pair - done) + i
                o_ref[spot] = o / totals[i]
                lse = highest[i] + jnp.log(totals[i]) * LOG2E
                lse_ref[spot] = jnp.broadcast_to(lse, (lanes, size))

        by_length(lengths[order[2 * pair]], sizes, compute)

    if pairs[1] - pairs[0] == 1:
        attend(pairs[0])
    else:
        pl.loop(*pairs)(attend)
    for pair in range(max(pairs[1], ready[0]), ready[1]):
        by_length(lengths[order[2 * pair]], sizes, functools.partial(finish, (0, 1), pair))


def like(x):
    return pltpu.VMEM(x.shape, x.dtype)


def cache_attention(pairs, ready, rows_args, caches, buffers, sizes, after):
    lengths, order, queries = rows_args
    keys, values = caches
    rows, steps, _, heads, size = (keys.shape[0], *queries.shape)
    slots = sizes[-1]
    scale = LOG2E / math.sqrt(size)
    count = 2 * (pairs[1] - pairs[0])
    piece = pltpu.VMEM((count, steps * heads, size), jnp.float32)
    operands = [pinned(x, pltpu.SMEM) for x in (lengths, order)]
    operands += [pinned(queries, pltpu.VMEM)]
    operands += [pinned(keys), pinned(values)]
    aliases = {len(operands) + i: i for i in range(len(buffers))}
    specs = [SMEM, SMEM, VMEM, HBM, HBM] + [VMEM] * len(buffers) + [ANY] * len(after)
    operands += [pinned(b, pltpu.VMEM) for b in buffers] + after
    out_shape = [like(keys), like(values), piece, piece]
    return pl.pallas_call(
        functools.partial(attend_cache, pairs, ready, sizes, scale),
        out_shape=out_shape,
        in_specs=specs,
        out_specs=[VMEM] * len(out_shape),
        input_output_aliases=aliases,
        scratch_shapes=[
            pltpu.SemaphoreType.DMA((rows // 2, 2, 2)),
        ],
        compiler_params=pltpu.CompilerParams(vmem_limit_bytes=8 * MIB),
        cost_estimate=TYPICAL,
        name="cache_attention",
    )(*operands)


def project_old(lay, n_hidden, *refs):
    w_buf, *hidden = refs[: 1 + n_hidden]
    out_ref, h_ref = refs[-2:]
    tp = lax.axis_index("tp")
    for i, h in enumerate(hidden):
        h_ref[lax.rem(tp + i, lay.tp)] = h[...]
    features = h_ref.shape[2]
    chunk = min(features, 1024)
    for k in range(2):
        total = jnp.zeros(out_ref.shape[1:], jnp.float32)
        for t in range(lay.tp):
            for low in range(0, features, chunk):
                start = t * features + low
                total += jnp.dot(
                    h_ref[t, :, low : low + chunk],
                    w_buf[k, start : start + chunk, :],
                    preferred_element_type=jnp.float32,
                )
        out_ref[k] = total


def project(lay, w_buf, hidden, after):
    tokens, features = hidden[0].shape
    return pl.pallas_call(
        functools.partial(project_old, lay, len(hidden)),
        out_shape=(
            pltpu.VMEM((2, tokens, w_buf.shape[2]), jnp.float32),
            pltpu.VMEM((lay.tp, tokens, features), jnp.bfloat16),
        ),
        in_specs=[VMEM] * (1 + len(hidden)) + [ANY] * len(after),
        out_specs=(VMEM, VMEM),
        compiler_params=pltpu.CompilerParams(vmem_limit_bytes=4 * MIB),
        cost_estimate=TYPICAL,
        name="project",
    )(pinned(w_buf, pltpu.VMEM), *hidden, *after)


class Place:
    def __init__(self, lay):
        fsdp, self.grp, self.tp = (lax.axis_index(a) for a in AXES)
        self.z, self.core = fsdp // 2, lax.rem(fsdp, 2)
        self.lay = lay
        there = jnp.where(lax.rem(self.grp, 2) == 0, self.z, lay.depth - 1 - self.z)
        self.own = self.grp * lay.depth + there
        self.per_lane = lay.fsdp * lay.grp // lay.tp
        self.part = plane_part()

    def find(self, plan, downs):
        lay, found = self.lay, []
        for (step, flip, other), down in zip(plan, downs):
            towards = (1 - 2 * self.core if flip else 2 * self.core - 1) * step
            spot = lax.rem(self.own + (lay.ring + towards), lay.ring)
            g = spot // lay.depth
            along = lax.rem(spot, lay.depth)
            zz = jnp.where(lax.rem(g, 2) == 0, along, lay.depth - 1 - along)
            for i in range(2):
                core = lax.rem(self.core + (i + flip), 2)
                index = (zz * 2 + core) * lay.grp + g
                found.append((down.at[i], index, 1 - self.part if other else self.part))
        return found

    def low(self, shards, h_ref, tiles):
        total = jnp.zeros((h_ref.shape[1], shards[0][0].shape[1]), jnp.float32) if shards else 0.0
        for down, index, _ in shards:
            depth = tiles * down.shape[-1]
            column = pl.multiple_of(lax.rem(index, self.per_lane) * depth, depth)
            term = lax.dot_general(
                h_ref[index // self.per_lane, :, pl.ds(column, depth)],
                jnp.concatenate([down[i] for i in range(tiles)], axis=1),
                (((1,), (1,)), ((), ())),
                preferred_element_type=jnp.float32,
            )
            total += term
        return total


def by_projection(place, plan, shards):
    crossed = [other for _, _, other in plan for _ in range(2)]
    return [
        (place.part, [s for s, other in zip(shards, crossed) if not other]),
        (1 - place.part, [s for s, other in zip(shards, crossed) if other]),
    ]


def merge_some(lay, plan, up_plan, first, n_caches, scale, *refs):
    refs = list(refs)

    def take(n):
        out = refs[:n]
        del refs[:n]
        return out

    last = n_caches > 0
    downs, up_only = take(len(plan)), take(len(up_plan))
    h_buf, weights = take(2)
    if last:
        old, order, q_ref = take(3)
        caches = [take(2) for _ in range(n_caches)]
        u_buf, low_in, _ = take(3)
        m_hbm, out_hbm, m_buf, sems, low, out_buf, out_sem = refs[-7:]
    elif first:
        m_hbm, u_buf, low, m_buf, sems, u_parts = refs[-6:]
    else:
        u_buf, low_in, _ = take(3)
        m_hbm, low, m_buf, sems = refs[-4:]
    depth, width = m_buf.shape[1:]
    pairs = weights.shape[0]
    cut = min(width, 256)
    lanes = downs[0].shape[-1]
    tiles = depth // lanes
    place = Place(lay)
    shards = place.find(plan, downs)
    groups = by_projection(place, plan, shards)

    if last:
        low[...] = low_in[...]
        for part, group in groups:
            low[part] += place.low(group, h_buf, tiles)
        new = []
        for k in range(pairs):
            high = low[k].astype(jnp.bfloat16)
            rest = (low[k] - high.astype(jnp.float32)).astype(jnp.bfloat16)
            new.append(
                (
                    old[k]
                    + jnp.dot(high, u_buf[k], preferred_element_type=jnp.float32)
                    + jnp.dot(rest, u_buf[k], preferred_element_type=jnp.float32)
                ).astype(jnp.bfloat16)
            )
        add_new_tokens(q_ref, order, caches, new, out_buf, scale)
        out_copy = pltpu.make_async_copy(out_buf, out_hbm, out_sem)
        out_copy.start()
    elif first:
        columns = width // place.per_lane
        for down, index, _ in groups[0][1] + place.find(up_plan, up_only):

            @pl.when(index // place.per_lane == place.tp)
            def _():
                u_parts[lax.rem(index, place.per_lane)] = down[tiles, :, : pairs * columns]

        for k in range(pairs):
            u_buf[k] = ADAPTER_SCALING * jnp.concatenate(
                [
                    u_parts[i, :, k * columns : (k + 1) * columns]
                    for i in range(place.per_lane)
                ],
                axis=1,
            )

    chunk = min(depth, 256)
    both = min(len(group) for _, group in groups)
    turns = [list(pair) for pair in zip(*(group[:both] for _, group in groups))]
    turns += [[shard] for _, group in groups for shard in group[both:]]
    copies = []
    j = 0
    for turn in turns:
        for begin in range(0, depth, chunk):
            rows = slice(begin, begin + chunk)
            tile = begin // lanes
            for i, (down, index, k) in enumerate(turn):
                start = pl.multiple_of(index * depth, depth)
                d = jnp.concatenate([down[tile + i] for i in range(chunk // lanes)], axis=1)
                for side in range(width // cut):
                    cols = slice(side * cut, (side + 1) * cut)
                    added = lax.dot_general(
                        d,
                        u_buf[k, :, cols],
                        (((0,), (0,)), ((), ())),
                        preferred_element_type=jnp.float32,
                    )
                    w = weights[k, pl.ds(start + begin, chunk), cols]
                    m_buf[j + i, rows, cols] = (w.astype(jnp.float32) + added).astype(jnp.bfloat16)
        for down, index, k in turn:
            start = pl.multiple_of(index * depth, depth)
            copy = pltpu.make_async_copy(
                m_buf.at[j], m_hbm.at[k, pl.ds(start, depth), :], sems.at[j]
            )
            copy.start()
            copies.append(copy)
            j += 1

    if not last:
        low[...] = jnp.zeros_like(low) if first else low_in[...]
        for part, group in groups:
            low[part] += place.low(group, h_buf, tiles)
    for copy in copies + ([out_copy] if last else []):
        copy.wait()


def add_new_tokens(q_ref, order, caches, new, out_buf, scale):
    steps, rows, heads, size = q_ref.shape
    kv = new[0].shape[1] // size
    new = [
        jnp.concatenate([x[:, g * size : (g + 1) * size] for g in range(kv)], axis=0) for x in new
    ]
    n = kv * steps * rows
    lanes = steps * heads
    left = lax.broadcasted_iota(jnp.int32, (lanes, n), 0)
    right = lax.broadcasted_iota(jnp.int32, (lanes, n), 1)
    same_head = over(within(left, heads), heads // kv) == over(right, steps * rows)
    earlier = within(over(right, rows), steps) <= over(left, heads)
    right_row = jnp.where(same_head & earlier, within(right, rows), -1)

    def all_rows(pieces):
        return jnp.concatenate(list(pieces), axis=0)

    q = all_rows(q_ref[:, order[spot]].reshape(lanes, size) for spot in range(rows))
    s = lax.dot_general(q, new[0], (((1,), (1,)), ((), ())), preferred_element_type=jnp.float32)
    bias = all_rows(
        jnp.where(right_row == order[spot], 0.0, -jnp.inf) for spot in range(rows)
    )
    s = s * scale + bias
    lse = all_rows(ref[i] for _, ref in caches for i in range(ref.shape[0]))
    highest = jnp.maximum(jnp.max(s, axis=1, keepdims=True), lse)
    p = jnp.exp2(s - highest[:, :n])
    old = jnp.exp2(lse - highest)
    divisor = jnp.sum(p, axis=1, keepdims=True) + old
    o = old * all_rows(ref[i] for ref, _ in caches for i in range(ref.shape[0]))
    o = (o + jnp.dot(p.astype(jnp.bfloat16), new[1], preferred_element_type=jnp.float32)) / divisor
    for spot in range(rows):
        piece = o[spot * lanes : (spot + 1) * lanes].astype(out_buf.dtype)
        out_buf[:, order[spot]] = piece.reshape(steps, heads, size)


def merge(lay, shape, entries, up_only, states, weights, state, final, after):
    pairs, total, width = shape
    tokens, rank = states.shape[1], entries[0][3].shape[-2]
    depth = total // (lay.fsdp * lay.grp)
    per_lane = lay.fsdp * lay.grp // lay.tp
    n = 2 * len(entries)
    merged = pltpu.HBM(shape, jnp.bfloat16)
    low_shape = (pairs, tokens, rank)
    operands = [e[3] for e in entries + up_only]
    operands += [pinned(states, pltpu.VMEM), pinned(weights, pltpu.VMEM)]
    specs = [VMEM] * len(operands)
    scratch = [pltpu.VMEM((n, depth, width), jnp.bfloat16), pltpu.SemaphoreType.DMA((n,))]
    aliases = {}
    n_caches, scale = 0, 0.0
    if state is not None and final is None:
        m_prev, u_buf, low = state
        operands += [pinned(u_buf, pltpu.VMEM), pinned(low, pltpu.VMEM), pinned(m_prev)]
        specs += [VMEM, VMEM, HBM]
        aliases = {len(operands) - 1: 0}
        out_shape = [merged, pltpu.VMEM(low_shape, jnp.float32)]
        out_specs = [HBM, VMEM]
    elif final is None:
        out_shape = [
            merged,
            pltpu.VMEM((pairs, rank, width), jnp.bfloat16),
            pltpu.VMEM(low_shape, jnp.float32),
        ]
        out_specs = [HBM, VMEM, VMEM]
        scratch.append(pltpu.VMEM((per_lane, rank, pairs * width // per_lane), jnp.bfloat16))
    else:
        olds, order, queries, caches = final
        m_prev, u_buf, low = state
        operands += [olds, pinned(order, pltpu.SMEM), pinned(queries, pltpu.VMEM), *caches]
        specs += [VMEM, SMEM, VMEM] + [VMEM] * len(caches)
        operands += [pinned(u_buf, pltpu.VMEM), pinned(low, pltpu.VMEM), pinned(m_prev)]
        specs += [VMEM, VMEM, HBM]
        aliases = {len(operands) - 1: 0}
        out_shape = [merged, pltpu.HBM(queries.shape, jnp.bfloat16)]
        out_specs = [HBM, HBM]
        scratch += [
            pltpu.VMEM(low_shape, jnp.float32),
            pltpu.VMEM(queries.shape, jnp.bfloat16),
            pltpu.SemaphoreType.DMA,
        ]
        n_caches, scale = len(caches) // 2, LOG2E / math.sqrt(queries.shape[3])
    return pl.pallas_call(
        functools.partial(
            merge_some,
            lay,
            [e[:3] for e in entries],
            [e[:3] for e in up_only],
            state is None,
            n_caches,
            scale,
        ),
        out_shape=out_shape,
        in_specs=specs + [ANY] * len(after),
        out_specs=out_specs,
        input_output_aliases=aliases,
        scratch_shapes=scratch,
        compiler_params=pltpu.CompilerParams(vmem_limit_bytes=20 * MIB),
        cost_estimate=TYPICAL,
        name="merge",
    )(*operands, *after)


def shards(
    lay,
    hidden_states,
    queries,
    cache_keys,
    cache_values,
    cache_lengths,
    projection_weight_matrices,
    factor_down,
    factor_up,
):
    send = functools.partial(lax.ppermute, axis_name=AXES)
    steps, rows, features = hidden_states.shape
    slots, kv, size = cache_keys.shape[1:]
    shape = projection_weight_matrices.shape
    sizes = tuple(slots * i // 24 for i in (1, 4, 8, 16, 24))
    own = jnp.swapaxes(factor_down, 1, 2)
    tokens = hidden_states.reshape(steps * rows, features)
    keys = cache_keys.reshape(rows, slots * kv, size)
    values = cache_values.reshape(rows, slots * kv, size)
    swap, ring, planes = lay.core_swap(), lay.ring_step(), lay.plane_swap()
    pair_count = rows // 2
    last_step = lay.ring // 2
    buffers, caches = [], []

    other, other_up = send(own, perm=swap), send(factor_up, perm=swap)
    pair, rest, *rows_args = begin(own, factor_up, cache_lengths, queries)
    pair, rest = pack(other, other_up, pair, rest)

    def attention(pairs, ready, after):
        nonlocal buffers
        out = cache_attention(pairs, ready, rows_args, (keys, values), buffers, sizes, after)
        buffers = list(out[:2])
        caches.extend(out[2:])
        return out[2]

    entries = [(0, 0, 0, pair), (0, 0, 1, rest)]
    sent = send(pair, perm=ring)
    hidden = [tokens] + [send(tokens, perm=lay.feature_step(i)) for i in range(1, lay.tp)]
    token = attention((0, 1), (0, 2), [pair])
    came, token = after_all(sent, token)
    crossing, crossed = [], []
    for step in range(1, last_step):
        entries.append((step, 0, 0, came))
        over_there = [(s, send(x, perm=swap)) for s, x in crossed]
        across = [(step, send(came, perm=planes))]
        swapped = send(came, perm=swap)
        sent = send(came, perm=ring)
        if step == 1:
            token = attention((1, 2), (2, pair_count), [token])
        elif step == 2:
            token = attention((2, pair_count), (pair_count, pair_count), [token])
        elif step == 3:
            olds, states = project(lay, projection_weight_matrices, hidden, [token])
            token = olds
        arrived = [x for _, x in crossing]
        if step + 1 == last_step:
            (sent, arrived), token = after_all((sent, arrived), token)
        (came, hidden, arrived, swapped, held), token = after_all(
            (sent, hidden, arrived, swapped, [x for _, x in over_there]), token
        )
        entries.append((step, 1, 0, swapped))
        entries += [(s, 1, 1, x) for (s, _), x in zip(over_there, held)]
        crossed = [(s, x) for (s, _), x in zip(crossing, arrived)]
        entries += [(s, 0, 1, x) for s, x in crossed]
        crossing = across
    weights = projection_weight_matrices
    entries.append((last_step, 0, 0, came))
    other_plane = [e for e in entries if e[2]]
    own_plane = [e for e in entries if not e[2]]
    own_plane = own_plane[-1:] + own_plane[:-1]
    others = own_plane[len(other_plane) :]
    now = own_plane[: len(other_plane)] + other_plane
    late = [(last_step, 0, 1, send(came, perm=planes))]
    late += [(s, 1, 1, send(x, perm=swap)) for s, x in crossed]
    m, u, low = merge(lay, shape, now, others, states, weights, None, None, [token])
    (step, x), = crossing
    x, low = after_all(x, low)
    late.append((step, 1, 1, send(x, perm=swap)))
    others.append((step, 0, 1, x))
    m, low = merge(lay, shape, others, [], states, weights, [m, u, low], None, [])
    arrived, low = after_all([x for _, _, _, x in late], low)
    late = [(*e[:3], x) for e, x in zip(late, arrived)]
    _, order, q = rows_args
    final = (olds, order, q, caches)
    return tuple(merge(lay, shape, late, [], states, weights, [m, u, low], final, []))


def solution(mesh):
    return jax.shard_map(
        functools.partial(shards, Layout(mesh)),
        mesh=mesh,
        in_specs=(
            P(None, ("fsdp", "grp"), "tp"),
            P(None, ("fsdp", "grp"), "tp", None),
            P(("fsdp", "grp"), None, "tp", None),
            P(("fsdp", "grp"), None, "tp", None),
            P(("fsdp", "grp")),
            P(None, None, "tp"),
            P(None, ("fsdp", "grp"), None),
            P(None, None, ("fsdp", "grp")),
        ),
        out_specs=(P(None, None, "tp"), P(None, ("fsdp", "grp"), "tp", None)),
        check_vma=False,
    )
```

```python
import functools
import math

import jax
import jax.numpy as jnp
from jax import lax
from jax.experimental import pallas as pl
from jax.experimental.pallas import tpu as pltpu
from jax.sharding import PartitionSpec as P

AXES = ("fsdp", "grp", "tp")
ADAPTER_SCALING = 2.0
LOG2E = math.log2(math.e)
MIB = 1024 * 1024
ANY = pl.BlockSpec(memory_space=pl.ANY)
HBM = pl.BlockSpec(memory_space=pltpu.HBM)
VMEM = pl.BlockSpec(memory_space=pltpu.VMEM)
SMEM = pl.BlockSpec(memory_space=pltpu.SMEM)


class Layout:
    def __init__(self, mesh):
        self.fsdp, self.grp, self.tp = (mesh.shape[a] for a in AXES)
        self.depth = self.fsdp // 2
        self.ring = self.depth * self.grp
        self.block = self.depth // self.tp

    def flat(self, z, core, g, t):
        return ((z * 2 + core) * self.grp + g) * self.tp + t

    def devices(self):
        for z in range(self.depth):
            for core in range(2):
                for g in range(self.grp):
                    for t in range(self.tp):
                        yield z, core, g, t

    def place(self, z, g):
        return g * self.depth + (z if g % 2 == 0 else self.depth - 1 - z)

    def at(self, position):
        g, z = divmod(position, self.depth)
        return (z if g % 2 == 0 else self.depth - 1 - z), g

    def ring_step(self):
        pairs = []
        for z, core, g, t in self.devices():
            to_z, to_g = self.at((self.place(z, g) + (1 - 2 * core)) % self.ring)
            pairs.append((self.flat(z, core, g, t), self.flat(to_z, core, to_g, t)))
        return pairs

    def plane_swap(self):
        return [(self.flat(z, c, g, t), self.flat(z, c, g, t ^ 1)) for z, c, g, t in self.devices()]

    def core_swap(self):
        return [
            (self.flat(z, c, g, t), self.flat(z, 1 - c, g, t)) for z, c, g, t in self.devices()
        ]

    def feature_step(self, step):
        return [
            (self.flat(z, c, g, (t + step) % self.tp), self.flat(z, c, g, t))
            for z, c, g, t in self.devices()
        ]


TYPICAL = pl.CostEstimate(flops=6 * 10**8, bytes_accessed=10**7, transcendentals=0)


def over(x, n):
    return x >> (n.bit_length() - 1) if n & (n - 1) == 0 else x // n


def within(x, n):
    return x & (n - 1) if n & (n - 1) == 0 else x % n


def after_all(arrays, token):
    return lax.optimization_barrier((arrays, token))


def pinned(x, space=pltpu.HBM):
    return pltpu.with_memory_space_constraint(x, space)


def sort_rows(lengths, order):
    rows = lengths.shape[0]
    held = [lengths[r] for r in range(rows)]
    for r in range(rows):
        rank = jnp.int32(0)
        for other in range(rows):
            if other != r:
                ahead = held[other] >= held[r] if other < r else held[other] > held[r]
                rank = rank + ahead.astype(jnp.int32)
        order[rank] = r


def by_length(length, sizes, act):
    below = 0
    for slots in sizes:

        @pl.when((length > below) & (length <= slots))
        def _():
            act(slots)

        below = slots


def up_columns(up):
    return jnp.concatenate([up[k] for k in range(up.shape[0])], axis=1)


def plane_part():
    return lax.rem(lax.axis_index("tp"), 2)


def begin_all(down, up, len_hbm, q_hbm, pair, rest, lengths, order, q_ref, up_buf, sems, more):
    lanes = pair.shape[3]
    depth = down.shape[2]
    tiles = depth // lanes
    part = plane_part()
    copies = [
        pltpu.make_async_copy(
            down.at[k, :, pl.ds(i * lanes, lanes)], array.at[0, i], sems.at[which, i]
        )
        for which, (k, array) in enumerate(((part, pair), (1 - part, rest)))
        for i in range(tiles)
    ]
    up_copy = pltpu.make_async_copy(up, up_buf, more.at[0])
    len_copy = pltpu.make_async_copy(len_hbm, lengths, more.at[1])
    q_copy = pltpu.make_async_copy(q_hbm, q_ref, more.at[2])
    for copy in [len_copy, up_copy] + copies + [q_copy]:
        copy.start()
    len_copy.wait()
    sort_rows(lengths, order)
    up_copy.wait()
    columns = up_columns(up_buf)
    pair[0, tiles, :, : columns.shape[1]] = columns
    for copy in copies + [q_copy]:
        copy.wait()


def begin(down, up, lengths, queries):
    count, rank, depth = down.shape
    tiles = depth // 128
    scalars = pltpu.SMEM(lengths.shape, jnp.int32)
    return pl.pallas_call(
        begin_all,
        out_shape=(
            pltpu.VMEM((2, tiles + 1, rank, 128), down.dtype),
            pltpu.VMEM((2, tiles, rank, 128), down.dtype),
            scalars,
            scalars,
            pltpu.VMEM(queries.shape, queries.dtype),
        ),
        in_specs=[HBM] * 4,
        out_specs=(VMEM, VMEM, SMEM, SMEM, VMEM),
        scratch_shapes=[
            pltpu.VMEM(up.shape, up.dtype),
            pltpu.SemaphoreType.DMA((count, tiles)),
            pltpu.SemaphoreType.DMA((3,)),
        ],
        compiler_params=pltpu.CompilerParams(vmem_limit_bytes=2 * MIB),
        cost_estimate=TYPICAL,
        name="begin",
    )(pinned(down), pinned(up), pinned(lengths), pinned(queries))


def pack_other(down, up, _, __, pair, rest):
    lanes = pair.shape[3]
    tiles = down.shape[2] // lanes
    part = plane_part()
    for i in range(tiles):
        cols = slice(i * lanes, (i + 1) * lanes)
        pair[1, i] = down[part, :, cols]
        rest[1, i] = down[1 - part, :, cols]
    columns = up_columns(up)
    pair[1, tiles, :, : columns.shape[1]] = columns


def pack(down, up, pair, rest):
    return pl.pallas_call(
        pack_other,
        out_shape=(like(pair), like(rest)),
        in_specs=[VMEM] * 4,
        out_specs=(VMEM, VMEM),
        input_output_aliases={2: 0, 3: 1},
        compiler_params=pltpu.CompilerParams(vmem_limit_bytes=2 * MIB),
        cost_estimate=TYPICAL,
        name="pack_other",
    )(down, up, pinned(pair, pltpu.VMEM), pinned(rest, pltpu.VMEM))


def attend_cache(pairs, ready, sizes, scale, *refs):
    lengths, order, q_ref, k_hbm, v_hbm = refs[:5]
    k_buf, v_buf, *outs, sems = refs[-5:]
    done = pairs[0]
    o_ref, lse_ref = outs[:2]
    steps, _, heads, size = q_ref.shape
    kv = k_hbm.shape[1] // sizes[-1]
    lanes = steps * heads

    def copies(which, pair, slots):
        span = pl.ds(0, slots * kv)
        hbm, buf = ((k_hbm, k_buf), (v_hbm, v_buf))[which]
        return [
            pltpu.make_async_copy(
                hbm.at[order[2 * pair + i], span],
                buf.at[2 * pair + i, span],
                sems.at[pair, i, which],
            )
            for i in range(2)
        ]

    def start(pair, slots):
        for copy in copies(0, pair, slots) + copies(1, pair, slots):
            copy.start()

    def finish(which, pair, slots):
        for i in which:
            for copy in copies(i, pair, slots):
                copy.wait()

    for pair in range(*ready):
        by_length(lengths[order[2 * pair]], sizes, functools.partial(start, pair))

    row_head = over(within(lax.broadcasted_iota(jnp.int32, (lanes, size), 0), heads), heads // kv)
    slot_head = within(lax.broadcasted_iota(jnp.int32, (lanes, size), 1), kv)
    head_bias = jnp.where(row_head == slot_head, 0.0, -jnp.inf)

    def attend(pair):
        def compute(slots):
            def wait(which):
                @pl.when(pair >= ready[0])
                def _():
                    finish((which,), pair, slots)

            n = slots * kv
            bias = jnp.concatenate([head_bias[:, : min(n, size)]] * max(n // size, 1), axis=1)
            column = lax.broadcasted_iota(jnp.int32, (1, n), 1)
            wait(0)
            scores = []
            for i in range(2):
                row = order[2 * pair + i]
                q = q_ref[:, row].reshape(lanes, size)
                s = lax.dot_general(
                    q,
                    k_buf[2 * pair + i, :n],
                    (((1,), (1,)), ((), ())),
                    preferred_element_type=jnp.float32,
                )
                closed = jnp.where(column < lengths[row] * kv, 0.0, -jnp.inf)
                scores.append(s + (bias + closed))
            highest = [jnp.max(s, axis=1, keepdims=True) * scale for s in scores]
            weights = [jnp.exp2(s * scale - h) for s, h in zip(scores, highest)]
            totals = [jnp.sum(p, axis=1, keepdims=True) for p in weights]
            wait(1)
            for i in range(2):
                o = jnp.dot(
                    weights[i].astype(jnp.bfloat16),
                    v_buf[2 * pair + i, :n],
                    preferred_element_type=jnp.float32,
                )
                spot = 2 * (pair - done) + i
                o_ref[spot] = o / totals[i]
                lse = highest[i] + jnp.log(totals[i]) * LOG2E
                lse_ref[spot] = jnp.broadcast_to(lse, (lanes, size))

        by_length(lengths[order[2 * pair]], sizes, compute)

    if pairs[1] - pairs[0] == 1:
        attend(pairs[0])
    else:
        pl.loop(*pairs)(attend)
    for pair in range(max(pairs[1], ready[0]), ready[1]):
        by_length(lengths[order[2 * pair]], sizes, functools.partial(finish, (0, 1), pair))


def like(x):
    return pltpu.VMEM(x.shape, x.dtype)


def cache_attention(pairs, ready, rows_args, caches, buffers, sizes, after):
    lengths, order, queries = rows_args
    keys, values = caches
    rows, steps, _, heads, size = (keys.shape[0], *queries.shape)
    slots = sizes[-1]
    scale = LOG2E / math.sqrt(size)
    count = 2 * (pairs[1] - pairs[0])
    piece = pltpu.VMEM((count, steps * heads, size), jnp.float32)
    operands = [pinned(x, pltpu.SMEM) for x in (lengths, order)]
    operands += [pinned(queries, pltpu.VMEM)]
    operands += [pinned(keys), pinned(values)]
    aliases = {len(operands) + i: i for i in range(len(buffers))}
    specs = [SMEM, SMEM, VMEM, HBM, HBM] + [VMEM] * len(buffers) + [ANY] * len(after)
    operands += [pinned(b, pltpu.VMEM) for b in buffers] + after
    out_shape = [like(keys), like(values), piece, piece]
    return pl.pallas_call(
        functools.partial(attend_cache, pairs, ready, sizes, scale),
        out_shape=out_shape,
        in_specs=specs,
        out_specs=[VMEM] * len(out_shape),
        input_output_aliases=aliases,
        scratch_shapes=[
            pltpu.SemaphoreType.DMA((rows // 2, 2, 2)),
        ],
        compiler_params=pltpu.CompilerParams(vmem_limit_bytes=8 * MIB),
        cost_estimate=TYPICAL,
        name="cache_attention",
    )(*operands)


def project_old(lay, n_hidden, *refs):
    w_buf, *hidden = refs[: 1 + n_hidden]
    out_ref, h_ref = refs[-2:]
    tp = lax.axis_index("tp")
    for i, h in enumerate(hidden):
        h_ref[lax.rem(tp + i, lay.tp)] = h[...]
    features = h_ref.shape[2]
    chunk = min(features, 1024)
    for k in range(2):
        total = jnp.zeros(out_ref.shape[1:], jnp.float32)
        for t in range(lay.tp):
            for low in range(0, features, chunk):
                start = t * features + low
                total += jnp.dot(
                    h_ref[t, :, low : low + chunk],
                    w_buf[k, start : start + chunk, :],
                    preferred_element_type=jnp.float32,
                )
        out_ref[k] = total


def project(lay, w_buf, hidden, after):
    tokens, features = hidden[0].shape
    return pl.pallas_call(
        functools.partial(project_old, lay, len(hidden)),
        out_shape=(
            pltpu.VMEM((2, tokens, w_buf.shape[2]), jnp.float32),
            pltpu.VMEM((lay.tp, tokens, features), jnp.bfloat16),
        ),
        in_specs=[VMEM] * (1 + len(hidden)) + [ANY] * len(after),
        out_specs=(VMEM, VMEM),
        compiler_params=pltpu.CompilerParams(vmem_limit_bytes=4 * MIB),
        cost_estimate=TYPICAL,
        name="project",
    )(pinned(w_buf, pltpu.VMEM), *hidden, *after)


class Place:
    def __init__(self, lay):
        fsdp, self.grp, self.tp = (lax.axis_index(a) for a in AXES)
        self.z, self.core = fsdp // 2, lax.rem(fsdp, 2)
        self.lay = lay
        there = jnp.where(lax.rem(self.grp, 2) == 0, self.z, lay.depth - 1 - self.z)
        self.own = self.grp * lay.depth + there
        self.per_lane = lay.fsdp * lay.grp // lay.tp
        self.part = plane_part()

    def find(self, plan, downs):
        lay, found = self.lay, []
        for (step, flip, other), down in zip(plan, downs):
            towards = (1 - 2 * self.core if flip else 2 * self.core - 1) * step
            spot = lax.rem(self.own + (lay.ring + towards), lay.ring)
            g = spot // lay.depth
            along = lax.rem(spot, lay.depth)
            zz = jnp.where(lax.rem(g, 2) == 0, along, lay.depth - 1 - along)
            for i in range(2):
                core = lax.rem(self.core + (i + flip), 2)
                index = (zz * 2 + core) * lay.grp + g
                found.append((down.at[i], index, 1 - self.part if other else self.part))
        return found

    def low(self, shards, h_ref, tiles):
        total = jnp.zeros((h_ref.shape[1], shards[0][0].shape[1]), jnp.float32) if shards else 0.0
        for down, index, _ in shards:
            depth = tiles * down.shape[-1]
            column = pl.multiple_of(lax.rem(index, self.per_lane) * depth, depth)
            term = lax.dot_general(
                h_ref[index // self.per_lane, :, pl.ds(column, depth)],
                jnp.concatenate([down[i] for i in range(tiles)], axis=1),
                (((1,), (1,)), ((), ())),
                preferred_element_type=jnp.float32,
            )
            total += term
        return total


def by_projection(place, plan, shards):
    crossed = [other for _, _, other in plan for _ in range(2)]
    return [
        (place.part, [s for s, other in zip(shards, crossed) if not other]),
        (1 - place.part, [s for s, other in zip(shards, crossed) if other]),
    ]


def merge_some(lay, plan, first, n_caches, scale, *refs):
    refs = list(refs)

    def take(n):
        out = refs[:n]
        del refs[:n]
        return out

    last = n_caches > 0
    downs = take(len(plan))
    h_buf, weights = take(2)
    if last:
        old, order, q_ref = take(3)
        caches = [take(2) for _ in range(n_caches)]
        u_buf, low_in, _ = take(3)
        m_hbm, out_hbm, m_buf, sems, low, out_buf, out_sem = refs[-7:]
    elif first:
        m_hbm, u_buf, low, m_buf, sems, u_parts = refs[-6:]
    else:
        u_buf, low_in, _ = take(3)
        m_hbm, low, m_buf, sems = refs[-4:]
    depth, width = m_buf.shape[1:]
    pairs = weights.shape[0]
    cut = min(width, 256)
    lanes = downs[0].shape[-1]
    tiles = depth // lanes
    place = Place(lay)
    shards = place.find(plan, downs)
    groups = by_projection(place, plan, shards)

    if first:
        columns = width // place.per_lane
        for down, index, _ in groups[0][1]:

            @pl.when(index // place.per_lane == place.tp)
            def _():
                u_parts[lax.rem(index, place.per_lane)] = down[tiles, :, : pairs * columns]

        for k in range(pairs):
            u_buf[k] = ADAPTER_SCALING * jnp.concatenate(
                [
                    u_parts[i, :, k * columns : (k + 1) * columns]
                    for i in range(place.per_lane)
                ],
                axis=1,
            )

    chunk = min(depth, 256)
    copies = []
    for j, (down, index, k) in enumerate(shards):
        start = pl.multiple_of(index * depth, depth)
        for begin in range(0, depth, chunk):
            rows = slice(begin, begin + chunk)
            tile = begin // lanes
            d = jnp.concatenate([down[tile + i] for i in range(chunk // lanes)], axis=1)
            for side in range(width // cut):
                cols = slice(side * cut, (side + 1) * cut)
                added = lax.dot_general(
                    d,
                    u_buf[k, :, cols],
                    (((0,), (0,)), ((), ())),
                    preferred_element_type=jnp.float32,
                )
                w = weights[k, pl.ds(start + begin, chunk), cols]
                m_buf[j, rows, cols] = (w.astype(jnp.float32) + added).astype(jnp.bfloat16)
        copy = pltpu.make_async_copy(m_buf.at[j], m_hbm.at[k, pl.ds(start, depth), :], sems.at[j])
        copy.start()
        copies.append(copy)

    if not last:
        low[...] = jnp.zeros_like(low) if first else low_in[...]
        for part, group in groups:
            low[part] += place.low(group, h_buf, tiles)
    if last:
        low[...] = low_in[...]
        for part, group in groups:
            low[part] += place.low(group, h_buf, tiles)
        new = []
        for k in range(pairs):
            high = low[k].astype(jnp.bfloat16)
            rest = (low[k] - high.astype(jnp.float32)).astype(jnp.bfloat16)
            new.append(
                (
                    old[k]
                    + jnp.dot(high, u_buf[k], preferred_element_type=jnp.float32)
                    + jnp.dot(rest, u_buf[k], preferred_element_type=jnp.float32)
                ).astype(jnp.bfloat16)
            )
        add_new_tokens(q_ref, order, caches, new, out_buf, scale)
        out_copy = pltpu.make_async_copy(out_buf, out_hbm, out_sem)
        out_copy.start()
    for copy in copies + ([out_copy] if last else []):
        copy.wait()


def add_new_tokens(q_ref, order, caches, new, out_buf, scale):
    steps, rows, heads, size = q_ref.shape
    kv = new[0].shape[1] // size
    new = [
        jnp.concatenate([x[:, g * size : (g + 1) * size] for g in range(kv)], axis=0) for x in new
    ]
    n = kv * steps * rows
    lanes = steps * heads
    left = lax.broadcasted_iota(jnp.int32, (lanes, n), 0)
    right = lax.broadcasted_iota(jnp.int32, (lanes, n), 1)
    same_head = over(within(left, heads), heads // kv) == over(right, steps * rows)
    earlier = within(over(right, rows), steps) <= over(left, heads)
    right_row = jnp.where(same_head & earlier, within(right, rows), -1)

    def all_rows(pieces):
        return jnp.concatenate(list(pieces), axis=0)

    q = all_rows(q_ref[:, order[spot]].reshape(lanes, size) for spot in range(rows))
    s = lax.dot_general(q, new[0], (((1,), (1,)), ((), ())), preferred_element_type=jnp.float32)
    bias = all_rows(
        jnp.where(right_row == order[spot], 0.0, -jnp.inf) for spot in range(rows)
    )
    s = s * scale + bias
    lse = all_rows(ref[i] for _, ref in caches for i in range(ref.shape[0]))
    highest = jnp.maximum(jnp.max(s, axis=1, keepdims=True), lse)
    p = jnp.exp2(s - highest[:, :n])
    old = jnp.exp2(lse - highest)
    divisor = jnp.sum(p, axis=1, keepdims=True) + old
    o = old * all_rows(ref[i] for ref, _ in caches for i in range(ref.shape[0]))
    o = (o + jnp.dot(p.astype(jnp.bfloat16), new[1], preferred_element_type=jnp.float32)) / divisor
    for spot in range(rows):
        piece = o[spot * lanes : (spot + 1) * lanes].astype(out_buf.dtype)
        out_buf[:, order[spot]] = piece.reshape(steps, heads, size)


def merge(lay, shape, entries, states, weights, state, final, after):
    pairs, total, width = shape
    tokens, rank = states.shape[1], entries[0][3].shape[-2]
    depth = total // (lay.fsdp * lay.grp)
    per_lane = lay.fsdp * lay.grp // lay.tp
    n = 2 * len(entries)
    merged = pltpu.HBM(shape, jnp.bfloat16)
    low_shape = (pairs, tokens, rank)
    operands = [e[3] for e in entries] + [pinned(states, pltpu.VMEM), pinned(weights, pltpu.VMEM)]
    specs = [VMEM] * len(operands)
    scratch = [pltpu.VMEM((n, depth, width), jnp.bfloat16), pltpu.SemaphoreType.DMA((n,))]
    aliases = {}
    n_caches, scale = 0, 0.0
    if state is not None and final is None:
        m_prev, u_buf, low = state
        operands += [pinned(u_buf, pltpu.VMEM), pinned(low, pltpu.VMEM), pinned(m_prev)]
        specs += [VMEM, VMEM, HBM]
        aliases = {len(operands) - 1: 0}
        out_shape = [merged, pltpu.VMEM(low_shape, jnp.float32)]
        out_specs = [HBM, VMEM]
    elif final is None:
        out_shape = [
            merged,
            pltpu.VMEM((pairs, rank, width), jnp.bfloat16),
            pltpu.VMEM(low_shape, jnp.float32),
        ]
        out_specs = [HBM, VMEM, VMEM]
        scratch.append(pltpu.VMEM((per_lane, rank, pairs * width // per_lane), jnp.bfloat16))
    else:
        olds, order, queries, caches = final
        m_prev, u_buf, low = state
        operands += [olds, pinned(order, pltpu.SMEM), pinned(queries, pltpu.VMEM), *caches]
        specs += [VMEM, SMEM, VMEM] + [VMEM] * len(caches)
        operands += [pinned(u_buf, pltpu.VMEM), pinned(low, pltpu.VMEM), pinned(m_prev)]
        specs += [VMEM, VMEM, HBM]
        aliases = {len(operands) - 1: 0}
        out_shape = [merged, pltpu.HBM(queries.shape, jnp.bfloat16)]
        out_specs = [HBM, HBM]
        scratch += [
            pltpu.VMEM(low_shape, jnp.float32),
            pltpu.VMEM(queries.shape, jnp.bfloat16),
            pltpu.SemaphoreType.DMA,
        ]
        n_caches, scale = len(caches) // 2, LOG2E / math.sqrt(queries.shape[3])
    return pl.pallas_call(
        functools.partial(merge_some, lay, [e[:3] for e in entries], state is None, n_caches, scale),
        out_shape=out_shape,
        in_specs=specs + [ANY] * len(after),
        out_specs=out_specs,
        input_output_aliases=aliases,
        scratch_shapes=scratch,
        compiler_params=pltpu.CompilerParams(vmem_limit_bytes=20 * MIB),
        cost_estimate=TYPICAL,
        name="merge",
    )(*operands, *after)


def shards(
    lay,
    hidden_states,
    queries,
    cache_keys,
    cache_values,
    cache_lengths,
    projection_weight_matrices,
    factor_down,
    factor_up,
):
    send = functools.partial(lax.ppermute, axis_name=AXES)
    steps, rows, features = hidden_states.shape
    slots, kv, size = cache_keys.shape[1:]
    shape = projection_weight_matrices.shape
    sizes = tuple(slots * i // 24 for i in (1, 4, 8, 16, 24))
    own = jnp.swapaxes(factor_down, 1, 2)
    tokens = hidden_states.reshape(steps * rows, features)
    keys = cache_keys.reshape(rows, slots * kv, size)
    values = cache_values.reshape(rows, slots * kv, size)
    swap, ring, planes = lay.core_swap(), lay.ring_step(), lay.plane_swap()
    pair_count = rows // 2
    last_step = lay.ring // 2
    buffers, caches = [], []

    other, other_up = send(own, perm=swap), send(factor_up, perm=swap)
    pair, rest, *rows_args = begin(own, factor_up, cache_lengths, queries)
    pair, rest = pack(other, other_up, pair, rest)

    def attention(pairs, ready, after):
        nonlocal buffers
        out = cache_attention(pairs, ready, rows_args, (keys, values), buffers, sizes, after)
        buffers = list(out[:2])
        caches.extend(out[2:])
        return out[2]

    entries = [(0, 0, 0, pair), (0, 0, 1, rest)]
    sent = send(pair, perm=ring)
    hidden = [tokens] + [send(tokens, perm=lay.feature_step(i)) for i in range(1, lay.tp)]
    token = attention((0, 1), (0, 2), [pair])
    came, token = after_all(sent, token)
    crossing, crossed = [], []
    for step in range(1, last_step):
        entries.append((step, 0, 0, came))
        over_there = [(s, send(x, perm=swap)) for s, x in crossed]
        across = [(step, send(came, perm=planes))]
        swapped = send(came, perm=swap)
        sent = send(came, perm=ring)
        if step == 1:
            token = attention((1, 2), (2, pair_count), [token])
        elif step == 2:
            token = attention((2, pair_count), (pair_count, pair_count), [token])
        elif step == 3:
            olds, states = project(lay, projection_weight_matrices, hidden, [token])
            token = olds
        arrived = [x for _, x in crossing]
        if step + 1 == last_step:
            (sent, arrived), token = after_all((sent, arrived), token)
        (came, hidden, arrived, swapped, held), token = after_all(
            (sent, hidden, arrived, swapped, [x for _, x in over_there]), token
        )
        entries.append((step, 1, 0, swapped))
        entries += [(s, 1, 1, x) for (s, _), x in zip(over_there, held)]
        crossed = [(s, x) for (s, _), x in zip(crossing, arrived)]
        entries += [(s, 0, 1, x) for s, x in crossed]
        crossing = across
    weights = projection_weight_matrices
    entries.append((last_step, 0, 0, came))
    own_plane = [e for e in entries if not e[2]]
    others = [e for e in entries if e[2]]
    late = [(last_step, 0, 1, send(came, perm=planes))]
    late += [(s, 1, 1, send(x, perm=swap)) for s, x in crossed]
    m, u, low = merge(lay, shape, own_plane, states, weights, None, None, [token])
    (step, x), = crossing
    x, low = after_all(x, low)
    late.append((step, 1, 1, send(x, perm=swap)))
    others.append((step, 0, 1, x))
    m, low = merge(lay, shape, others, states, weights, [m, u, low], None, [])
    arrived, low = after_all([x for _, _, _, x in late], low)
    late = [(*e[:3], x) for e, x in zip(late, arrived)]
    _, order, q = rows_args
    final = (olds, order, q, caches)
    return tuple(merge(lay, shape, late, states, weights, [m, u, low], final, []))


def solution(mesh):
    return jax.shard_map(
        functools.partial(shards, Layout(mesh)),
        mesh=mesh,
        in_specs=(
            P(None, ("fsdp", "grp"), "tp"),
            P(None, ("fsdp", "grp"), "tp", None),
            P(("fsdp", "grp"), None, "tp", None),
            P(("fsdp", "grp"), None, "tp", None),
            P(("fsdp", "grp")),
            P(None, None, "tp"),
            P(None, ("fsdp", "grp"), None),
            P(None, None, ("fsdp", "grp")),
        ),
        out_specs=(P(None, None, "tp"), P(None, ("fsdp", "grp"), "tp", None)),
        check_vma=False,
    )
```
